32 devices in a mesh: gx: 4 (over x, core), gy: 4 (over z), gz: 2 (over y).
Axes of the slice: x: 2, y: 2, z: 4, core: 2. Of those that a mesh axis runs over, the one named last changes fastest.
Arguments:
- state: float32 [7, 16, 16, 32, 128], P(None, 'gx', 'gy', 'gz'), may hold values from -6 to 6, as said below
- arms: float32 [3, 16, 16, 32, 128], P(None, 'gx', 'gy', 'gz'), may hold values from -6 to 6
- sphere_frag: int32 [16, 16, 32, 128], P('gx', 'gy', 'gz'), may hold values from 0 to 63
- frag_owner: int32 [2048, 1], P(('gx', 'gy', 'gz')), may hold values from 0 to 31; in each aligned block of 64 rows (0 to 63, 64 to 127, ...) at most 2 rows name the same one
- frag_clump: int32 [2048], P(('gx', 'gy', 'gz')), may hold values from 0 to 47
- tiles: int32 [32, 2048], P(('gx', 'gy', 'gz')), may hold values from 0 to 6911, as said below
- clump_motion: float32 [6, 1536], P(None, ('gx', 'gy', 'gz')), may hold values from -6 to 6
- inv_mass: float32 [1536], P(('gx', 'gy', 'gz')), may hold values from 0.3 to 3
- inv_moment: float32 [1536], P(('gx', 'gy', 'gz')), may hold values from 0.1 to 1
Outputs:
- sphere_next: float32 [6, 16, 16, 32, 128], P(None, 'gx', 'gy', 'gz')
- clump_next: float32 [6, 1536], P(None, ('gx', 'gy', 'gz'))
The draws below stay inside these ranges and needn't reach their ends.
Inputs may be any that keep to these rules, and one draw needn't show every extreme that they name: `state`: rows 0 to 2 lie in [0, 1), rows 3 to 5 in [-6, 6], row 6 in [0.08, 0.14]. `tiles`: the 2048 codes of one brick are distinct. `frag_owner`: among the 64 fragments of one brick at most 2 name the same owner.
All inputs are finite; a program needn't handle non-finite values.
Results may differ from the reference program's by a relative error of at most 0.0003.
Values sent between devices are 32-bit elements; how exact they have to be, the bound alone decides.
No kernel may reach another device: no remote copies, remote signals or barrier semaphores. Data moves between devices by JAX's collectives and lax.ppermute only.
A program may use at most 64 MiB of HBM per device.

```python
import math
import jax
import jax.numpy as jnp
import numpy as np
from jax import lax

SLOT = 128
CX = 4
CY = 4
CZ = 16
HELD = 64
OWN = 48
CAP = 2
BRICKS = 32
TILES_DEV = 2048
CLUMPS = 1536
NX = 16
NY = 16
NZ = 32
N_GX = 4
N_GY = 4
N_GZ = 2


def sphere_world(key):
    base = jax.random.fold_in(key, 23)
    keys = jax.random.split(base, 5)
    grid = (NX, NY, NZ, SLOT)
    position = jax.random.uniform(keys[0], (3,) + grid, jnp.float32, 0.0, 0.999)
    velocity = jnp.clip(jax.random.normal(keys[1], (3,) + grid, jnp.float32), -6.0, 6.0)
    radius = jax.random.uniform(keys[2], (1,) + grid, jnp.float32, 0.08, 0.14)
    state = jnp.concatenate([position, velocity, radius], axis=0)
    index_x = lax.broadcasted_iota(jnp.int32, grid, 0)
    index_y = lax.broadcasted_iota(jnp.int32, grid, 1)
    index_z = lax.broadcasted_iota(jnp.int32, grid, 2)
    slot_index = lax.broadcasted_iota(jnp.int32, grid, 3)
    local_x = index_x % CX
    local_y = index_y % CY
    local_z = index_z % CZ
    spheres = CX * CY * CZ * SLOT
    linear = ((local_x * CY + local_y) * CZ + local_z) * SLOT + slot_index
    home = linear * HELD // spheres
    side = jax.random.randint(keys[3], grid, 0, 2) * 2 - 1
    stray = jax.random.randint(keys[4], grid, 0, 4) == 0
    target_z = local_z + side
    inside = (target_z >= 0) & (target_z < CZ)
    other = (linear + side * SLOT) * HELD // spheres
    edge = (slot_index == 0) | (slot_index == SLOT - 1)
    frag = jnp.where(stray & inside & jnp.logical_not(edge), other, home).astype(jnp.int32)
    brick = (index_x // CX * N_GY + index_y // CY) * N_GZ + index_z // CZ
    global_frag = (brick * HELD + frag).reshape(-1)
    place = jnp.stack([index_x.astype(jnp.float32) + position[0], index_y.astype(jnp.float32) + position[1], index_z.astype(jnp.float32) + position[2]])
    flat = place.reshape(3, -1).T
    segments = N_GX * N_GY * N_GZ * HELD
    total = jax.ops.segment_sum(flat, global_frag, num_segments=segments)
    count = jax.ops.segment_sum(jnp.ones((flat.shape[0],), jnp.float32), global_frag, num_segments=segments)
    centre = total / jnp.maximum(count, 1.0)[:, None]
    arms = place - jnp.take(centre, global_frag, axis=0).T.reshape((3,) + grid)
    return (state, frag, arms)


def draw_state(key, part):
    return sphere_world(key)[0]


def draw_sphere_frag(key, part):
    return sphere_world(key)[1]


def draw_arms(key, part):
    return sphere_world(key)[2]


def draw_tiles(key, part):
    base = jax.random.fold_in(key, 7)
    brick_keys = jax.random.split(base, N_GX * N_GY * N_GZ)

    def one_brick(brick_key):
        return jax.random.permutation(brick_key, 27 * CX * CY * CZ)[:TILES_DEV]
    return jax.vmap(one_brick)(brick_keys).astype(jnp.int32)


def with_ends(values, stream_key, least, top_value):
    shape = values.shape
    spot = [jax.random.randint(jax.random.fold_in(stream_key, axis), (), 0, shape[axis]) for axis in range(len(shape))]
    values = values.at[tuple(spot)].set(least)
    longest = shape.index(max(shape))
    spot[longest] = (spot[longest] + 1) % shape[longest]
    return values.at[tuple(spot)].set(top_value)


def level_of(own_key, shape, cuts, smallest, high):
    def one(axis_at, shards_of):
        draws = jax.random.uniform(jax.random.fold_in(jax.random.fold_in(own_key, 6), axis_at), (shards_of,), jnp.float32, smallest / len(cuts), high / len(cuts))
        return jnp.repeat(jnp.exp(draws), shape[axis_at] // shards_of).reshape((-1,) + (1,) * (len(shape) - axis_at - 1))

    level = one(*cuts[0])
    for cut in cuts[1:]:
        level = level * one(*cut)
    return level


def routed_block(own_key, own, number, rows, number_of, top, reach, lean):
    ranking = jax.random.permutation(own_key, number_of)
    crowded, ordinary = portions_of(number_of, rows * top, reach, lean, True), portions_of(number_of, rows * top, reach, lean, False)
    places = jnp.arange(number_of)

    def named(tallies, offset_by):
        used = int((tallies > 0).sum())
        fixed = max(1, used // 4)
        moved = fixed + (places - fixed + offset_by * (used - fixed)) % max(1, number_of - fixed)
        return jnp.zeros((number_of,), jnp.int32).at[ranking[jnp.where(places < fixed, places, moved)]].set(jnp.asarray(tallies, jnp.int32))

    tallies = jnp.where(number % 4 == 0, named(crowded, number // 4), named(ordinary, number - number // 4 - 1))
    mixed = jax.random.permutation(jax.random.fold_in(own, 3), number_of)
    donor, sink = mixed[0:number_of // 2 * 2:2], mixed[1:number_of // 2 * 2:2]
    room = jnp.minimum(tallies[donor] - 1, reach - tallies[sink]) // 2
    room = jnp.where((donor == ranking[0]) | (sink == ranking[0]) | (tallies[sink] == 0), 0, jnp.maximum(room, 0))
    moved = jax.random.randint(jax.random.fold_in(own, 4), (number_of // 2,), 0, 1 << 20) % (room + 1)
    tallies = tallies.at[donor].add(-moved).at[sink].add(moved)
    members = jnp.searchsorted(jnp.cumsum(tallies), jnp.arange(rows * top), side="right").astype(jnp.int32)
    table = members.reshape(top, rows).T
    table = table[jax.random.permutation(jax.random.fold_in(own, 1), rows)]
    offset_by = jax.random.randint(jax.random.fold_in(own, 2), (rows, 1), 0, top)
    return jnp.take_along_axis(table, (jnp.arange(top)[None, :] + offset_by) % top, axis=1)


def portions_of(number_of, total, most, slope, full):
    weights = [(1 << 20) // math.isqrt(rank ** slope) + 1 for rank in range(1, number_of + 1)]
    largest = most if full else min(most, max(-(-total // number_of), total * weights[0] // sum(weights)))
    least = 1 if total - largest >= number_of - 1 else 0
    counts, spare = [largest] + [least] * (number_of - 1), total - largest - least * (number_of - 1)
    while spare > 0:
        candidates = [i for i in range(1, number_of) if counts[i] < largest] or [i for i in range(1, number_of) if counts[i] < most]
        pool, budget = sum([weights[i] for i in candidates]), spare
        for i in candidates:
            addition = min(most - counts[i], max(1, budget * weights[i] // pool), spare)
            counts[i] = counts[i] + addition
            spare = spare - addition
    return np.array(counts)


def gaussian(key, extent, spread, bound, cuts=(), kind=jnp.bfloat16):
    result = jax.random.normal(key, extent, jnp.float32) * spread
    if len(cuts) > 0:
        result = level_of(key, extent, cuts, -0.22, 0.18) * result
    return jnp.clip(result, min=-bound, max=bound).astype(kind)


def setup_inputs(seed: int = 0) -> dict:
    splits = jax.random.split(jax.random.key(seed), 10)
    state = draw_state(jax.random.fold_in(splits[9], 71), 0)
    arms = draw_arms(jax.random.fold_in(splits[9], 71), 0)
    sphere_frag = draw_sphere_frag(jax.random.fold_in(splits[9], 71), 0)
    frag_owner_keys = jax.random.split(jax.random.fold_in(splits[3], 1), (BRICKS * HELD) // HELD)
    frag_owner_turns = jax.random.permutation(jax.random.fold_in(splits[3], 3), (BRICKS * HELD) // HELD)
    frag_owner = jax.vmap(lambda own, number: routed_block(jax.random.fold_in(splits[3], 2), own, number, HELD, BRICKS, 1, CAP, 2))(frag_owner_keys, frag_owner_turns).reshape((BRICKS * HELD, 1))
    frag_clump = with_ends(jax.random.randint(splits[4], (BRICKS * HELD,), 0, OWN), jax.random.fold_in(splits[4], 1), 0, OWN - 1).astype(jnp.int32)
    tiles = draw_tiles(jax.random.fold_in(splits[9], 71), 0)
    clump_motion = gaussian(splits[6], (6, CLUMPS), 1.0, 6.0, ((1, 32),), jnp.float32)
    inv_mass = jnp.clip(jnp.exp(math.log(3.0) - 2.3025851 * jax.random.uniform(splits[7], (CLUMPS,), jnp.float32) ** level_of(splits[7], (CLUMPS,), ((0, 32),), -0.2, 0.2)), 0.3, 3.0)
    inv_moment = jnp.clip(jnp.exp(math.log(1.0) - 2.3025851 * jax.random.uniform(splits[8], (CLUMPS,), jnp.float32) ** level_of(splits[8], (CLUMPS,), ((0, 32),), -0.2, 0.2)), 0.1, 1.0)
    return {"state": state, "arms": arms, "sphere_frag": sphere_frag, "frag_owner": frag_owner, "frag_clump": frag_clump, "tiles": tiles, "clump_motion": clump_motion, "inv_mass": inv_mass, "inv_moment": inv_moment}


stiffness = 100.0
damping = 2.0
time_step = 0.01
gravity = 9.81
epsilon_sq = 1e-08

def cross_rows(first, second):
    return jnp.stack([first[1] * second[2] - first[2] * second[1], first[2] * second[0] - first[0] * second[2], first[0] * second[1] - first[1] * second[0]])

def pair_forces(own_block, neighbor_block, cell_shift):
    separation = [neighbor_block[axis_k][:, None, :] + cell_shift[axis_k][:, None, None] - own_block[axis_k][:, :, None] for axis_k in range(3)]
    distance = jnp.sqrt(separation[0] * separation[0] + separation[1] * separation[1] + separation[2] * separation[2] + epsilon_sq)
    radius_own = own_block[6][:, :, None]
    radius_other = neighbor_block[6][:, None, :]
    distinct = (own_block[7][:, :, None] != neighbor_block[7][:, None, :]).astype(jnp.float32)
    intersection = jnp.maximum(radius_own + radius_other - distance, 0.0) * distinct
    reduced = radius_own * radius_other / (radius_own + radius_other)
    closing = sum(((neighbor_block[3 + axis_k][:, None, :] - own_block[3 + axis_k][:, :, None]) * separation[axis_k] for axis_k in range(3))) / distance
    magnitude = stiffness * jnp.sqrt(reduced) * intersection * jnp.sqrt(intersection) - damping * jnp.sqrt(reduced * intersection) * closing
    factor = magnitude / distance
    return jnp.stack([-lax.optimization_barrier(jnp.sum(factor * separation[axis_k], axis=2)) for axis_k in range(3)])

def decode_tiles(codes, cells_y, cells_z):
    own_cell = codes // 27
    offset = codes % 27
    step_x = offset // 9 - 1
    step_y = offset // 3 % 3 - 1
    step_z = offset % 3 - 1
    cell_x = own_cell // (cells_y * cells_z)
    cell_y = own_cell // cells_z % cells_y
    cell_z = own_cell % cells_z
    return (own_cell, cell_x, cell_y, cell_z, step_x, step_y, step_z)

def advance(motion, sums, inv_mass, inv_moment):
    pull = jnp.array([0.0, 0.0, gravity], jnp.float32)[:, None]
    velocity = motion[0:3] + time_step * (sums[0:3] * inv_mass[None, :] - pull)
    spin = motion[3:6] + time_step * sums[3:6] * inv_moment[None, :]
    return jnp.concatenate([velocity, spin], axis=0)

def move_spheres(state, arms, motion):
    velocity = motion[0:3]
    spin = motion[3:6]
    half = 0.5 * time_step * spin
    turned = cross_rows(half, arms)
    twice = cross_rows(half, turned)
    scale = 2.0 / (1.0 + half[0] * half[0] + half[1] * half[1] + half[2] * half[2])
    new_arm = arms + scale * (turned + twice)
    position = state[0:3] + time_step * velocity + (new_arm - arms)
    moving = velocity + cross_rows(spin, new_arm)
    return jnp.concatenate([position, moving], axis=0)

def to_bricks(values):
    comps = values.shape[0]
    shaped = values.reshape(comps, N_GX, CX, N_GY, CY, N_GZ, CZ, SLOT)
    shaped = shaped.transpose(1, 3, 5, 0, 2, 4, 6, 7)
    return shaped.reshape(N_GX * N_GY * N_GZ, comps, CX * CY * CZ, SLOT)

def reference(state, arms, sphere_frag, frag_owner, frag_clump, tiles, clump_motion, inv_mass, inv_moment):
    bricks = N_GX * N_GY * N_GZ
    owner = frag_owner[:, 0]
    grid = (NX, NY, NZ, SLOT)
    index_x = lax.broadcasted_iota(jnp.int32, grid, 0)
    index_y = lax.broadcasted_iota(jnp.int32, grid, 1)
    index_z = lax.broadcasted_iota(jnp.int32, grid, 2)
    brick = (index_x // CX * N_GY + index_y // CY) * N_GZ + index_z // CZ
    frag_global = brick * HELD + sphere_frag
    sphere_clump = owner[frag_global] * OWN + frag_clump[frag_global]
    full = jnp.concatenate([state, sphere_clump.astype(jnp.float32)[None]], axis=0).reshape(8, NX * NY * NZ, SLOT)

    def brick_forces(index):
        codes = tiles[index]
        brick_x = index // (N_GY * N_GZ)
        brick_y = index // N_GZ % N_GY
        brick_z = index % N_GZ
        own_cell, cell_x, cell_y, cell_z, step_x, step_y, step_z = decode_tiles(codes, CY, CZ)
        global_x = brick_x * CX + cell_x
        global_y = brick_y * CY + cell_y
        global_z = brick_z * CZ + cell_z
        own_glob = ((global_x * NY + global_y) * NZ + global_z).astype(jnp.int32)
        other_x = (global_x + step_x) % NX
        other_y = (global_y + step_y) % NY
        other_z = (global_z + step_z) % NZ
        other_glob = ((other_x * NY + other_y) * NZ + other_z).astype(jnp.int32)
        cell_shift = jnp.stack([step_x, step_y, step_z]).astype(jnp.float32)
        forces = pair_forces(jnp.take(full, own_glob, axis=1), jnp.take(full, other_glob, axis=1), cell_shift)
        return jnp.zeros((3, CX * CY * CZ, SLOT), jnp.float32).at[:, own_cell].add(forces)
    per_brick = lax.map(brick_forces, jnp.arange(bricks, dtype=jnp.int32))
    force = per_brick.transpose(1, 0, 2, 3)
    lever = to_bricks(arms).transpose(1, 0, 2, 3)
    torque = cross_rows(lever, force)
    loads = jnp.concatenate([force, torque], axis=0).reshape(6, -1)
    frag_blocks = to_bricks(sphere_frag[None])[:, 0]
    frag_index = (frag_blocks + (jnp.arange(bricks, dtype=jnp.int32) * HELD)[:, None, None]).reshape(-1)
    frag_sums = jax.ops.segment_sum(loads.T, frag_index, num_segments=bricks * HELD)
    clump_index = owner * OWN + frag_clump
    clump_sums = jax.ops.segment_sum(frag_sums, clump_index, num_segments=OWN * bricks).T
    clump_next = advance(clump_motion, clump_sums, inv_mass, inv_moment)
    sphere_motion = jnp.take(clump_next, sphere_clump, axis=1)
    return (move_spheres(state, arms, sphere_motion), clump_next)
```

```python
import functools

import jax
import jax.numpy as jnp
from jax import lax
from jax.experimental import pallas as pl
from jax.experimental.pallas import tpu as pltpu
from jax.sharding import PartitionSpec as P

stiffness = 100.0
damping = 2.0
time_step = 0.01
gravity = 9.81
epsilon_sq = 1e-08
radius_top = 0.14

GROUP = 32
GROUP_BITS = GROUP.bit_length() - 1
UNITS = 4
VMEM = 56 * 1024 * 1024


def lanes_of(values, index):
    return jnp.take_along_axis(values, index, axis=1, mode="promise_in_bounds")


def split_rows(values):
    high = values.astype(jnp.bfloat16).astype(jnp.float32)
    rest = values - high
    middle = rest.astype(jnp.bfloat16).astype(jnp.float32)
    low = rest - middle
    return jnp.concatenate([high, middle, low], axis=0).astype(jnp.bfloat16)


def joined_rows(stacked):
    rows = stacked.shape[0] // 3
    return stacked[0:rows] + stacked[rows : 2 * rows] + stacked[2 * rows :]


def dot_lanes(first, second):
    return lax.dot_general(
        first, second, (((1,), (1,)), ((), ())), preferred_element_type=jnp.float32
    )


def with_halo(x, sides, width):
    for axis, dim in sides:
        devices, length = (lax.axis_size(axis), x.shape[dim])
        up = [(i, (i + 1) % devices) for i in range(devices)]
        down = [(j, i) for i, j in up]
        last = lax.slice_in_dim(x, length - width, length, axis=dim)
        initial = lax.slice_in_dim(x, 0, width, axis=dim)
        before = lax.ppermute(last, axis, up)
        after = lax.ppermute(initial, axis, down)
        x = jnp.concatenate([before, x, after], axis=dim)
    return x


def pack_kernel(state_ref, frag_ref, key_ref, out_ref):
    cells = frag_ref.shape[0]
    for comp in range(7):
        out_ref[:, comp, :] = state_ref[comp]
    keys = jnp.broadcast_to(key_ref[0:1, :], (8, key_ref.shape[1]))
    for block in range(cells // 8):
        rows = pl.ds(block * 8, 8)
        out_ref[rows, 7, :] = lanes_of(keys, frag_ref[rows, :])


def list_kernel(near_smem, need_smem, table_ref, slots_ref, count_ref, class_ref, member_ref):
    tiles = slots_ref.shape[0]
    lanes = slots_ref.shape[1]
    radius = table_ref[:, 6, :] + (radius_top + 1e-5)
    classes = jnp.zeros(class_ref.shape, jnp.int32)
    for axis in range(3):
        place = table_ref[:, axis, :]
        classes = classes | jnp.where(place < radius, 1 << (2 * axis), 0)
        classes = classes | jnp.where(place > 1.0 - radius, 2 << (2 * axis), 0)
    class_ref[...] = classes

    def copy_rows(block, unused):
        for unit in range(8):
            tile = block * 8 + unit
            need = need_smem[tile]
            row = class_ref[pl.ds(near_smem[tile], 1), :]
            member_ref[pl.ds(tile, 1), :] = jnp.where((row & need) == need, 1, 0)
        return unused

    lax.fori_loop(0, tiles // 8, copy_rows, 0)

    before = lax.broadcasted_iota(jnp.int32, (lanes, lanes), 0)
    after = lax.broadcasted_iota(jnp.int32, (lanes, lanes), 1)
    earlier = (before < after).astype(jnp.bfloat16)
    ones = jnp.ones((8, lanes), jnp.bfloat16)
    step_rows = 64

    def compact(block, unused):
        rows = pl.ds(pl.multiple_of(block * step_rows, step_rows), step_rows)
        member = member_ref[rows, :]
        flags = member.astype(jnp.float32).astype(jnp.bfloat16)
        rank = jnp.dot(flags, earlier, preferred_element_type=jnp.float32)
        slot = lax.broadcasted_iota(jnp.int32, (step_rows, lanes), 1)
        moves = slot - rank.astype(jnp.int32)
        word = jnp.where(member != 0, slot + lanes * moves, 0)
        bit = 1
        while bit < lanes:
            keep = jnp.where((word & (bit * lanes)) != 0, 0, word)
            gone = word ^ keep
            word = keep | pltpu.roll(gone, lanes - bit, 1)
            bit *= 2
        slots_ref[rows, :] = word & (lanes - 1)
        return unused

    lax.fori_loop(0, tiles // step_rows, compact, 0)
    for block in range(tiles // lanes):
        flags = member_ref[pl.ds(block * lanes, lanes), :].astype(jnp.float32).astype(jnp.bfloat16)
        count_ref[:, pl.ds(block * lanes, lanes)] = dot_lanes(ones, flags).astype(jnp.int32)


def force_kernel(
    near_smem,
    shift_smem,
    own_smem,
    first_smem,
    count_smem,
    place_smem,
    table_ref,
    slots_ref,
    shift_ref,
    arms_ref,
    frag_ref,
    out_ref,
    list_ref,
    turned_ref,
    force_ref,
    loads_ref,
    cell_smem,
):
    tiles = slots_ref.shape[0]
    lanes = slots_ref.shape[1]
    cells = frag_ref.shape[0]
    held = out_ref.shape[1]
    lane_bits = lanes.bit_length() - 1
    lane = lax.broadcasted_iota(jnp.int32, (8, lanes), 1)
    row = lax.broadcasted_iota(jnp.int32, (8, lanes), 0)
    absent = jnp.where(row == 6, -10.0, 0.0)

    force_ref[...] = jnp.zeros(force_ref.shape, jnp.float32)

    def fill(block, carry):
        end, last_chunk, last_new, last_held = carry
        for unit in range(8):
            tile = block * 8 + unit
            align = first_smem[tile]
            own = own_smem[tile]
            start = (end + align) & ~align
            amount = count_smem[0, tile]
            chunk = start >> lane_bits
            offset = start & (lanes - 1)
            for piece in range(lanes // GROUP + 1):
                cell_smem[(start >> GROUP_BITS) + piece] = own
            slots = jnp.broadcast_to(slots_ref[pl.ds(tile, 1), :], (8, lanes))
            slots = pltpu.roll(slots, offset, 1)
            found = lanes_of(table_ref[near_smem[tile]], slots) + shift_ref[shift_smem[tile]]
            new = jnp.where(((lane - offset) & (lanes - 1)) < amount, found, absent)
            held_row = jnp.where(chunk != last_chunk, last_new, last_held)
            held_row = jnp.where(lane >= offset, new, held_row)
            new = jnp.where(lane >= offset, absent, new)
            list_ref[pl.ds(pl.multiple_of(chunk * 8, 8), 8), :] = held_row
            list_ref[pl.ds(pl.multiple_of(chunk * 8 + 8, 8), 8), :] = new
            end, last_chunk, last_new, last_held = start + amount, chunk, new, held_row
        return end, last_chunk, last_new, last_held

    start = (jnp.int32(0), jnp.int32(0), absent, absent)
    end = lax.fori_loop(0, tiles // 8, fill, start)[0]
    groups = (end + GROUP - 1) >> GROUP_BITS
    for extra in range(UNITS):
        cell_smem[groups + extra] = cells

    def turn(block, unused):
        rows = pl.ds(pl.multiple_of(block * lanes, lanes), lanes)
        turned_ref[rows, :] = list_ref[rows, :].T
        return unused

    lax.fori_loop(0, (end + 16 * lanes - 1) >> (lane_bits + 4), turn, 0)

    def pairs(step, unused):
        totals = []
        for unit in range(UNITS):
            group = step * UNITS + unit
            cell = cell_smem[group]
            own = place_smem[cell]
            begin = group * GROUP
            chunk = begin >> lane_bits
            at = (chunk >> 4) * lanes + (begin & (lanes - 1))
            block = turned_ref[pl.ds(pl.multiple_of(at, GROUP), GROUP), :]
            column = (chunk & 15) * 8
            other = [
                lanes_of(block, jnp.full((GROUP, lanes), column + comp, jnp.int32))
                for comp in range(8)
            ]
            mine = [table_ref[own, pl.ds(comp, 1), :] for comp in range(8)]
            apart = [other[axis] - mine[axis] for axis in range(3)]
            square = apart[0] * apart[0] + apart[1] * apart[1] + apart[2] * apart[2] + epsilon_sq
            inverse = lax.rsqrt(square)
            reach = other[6] + mine[6]
            overlap = jnp.maximum(reach - square * inverse, 0.0)
            overlap = jnp.where(other[7] != mine[7], overlap, 0.0)
            closing = (
                (other[3] - mine[3]) * apart[0]
                + (other[4] - mine[4]) * apart[1]
                + (other[5] - mine[5]) * apart[2]
            )
            scaled = overlap * (other[6] * mine[6])
            root = scaled * lax.rsqrt(jnp.maximum(scaled * reach, 1e-30))
            factor = (
                root * inverse * (stiffness / damping * overlap - closing * inverse)
            )
            totals.append(
                (
                    cell,
                    [
                        jnp.sum((factor * apart[axis]).reshape(GROUP // 8, 8, lanes), axis=0)
                        for axis in range(3)
                    ],
                )
            )
        for cell, parts in totals:
            for axis in range(3):
                force_ref[axis, cell] += parts[axis]
        return unused

    lax.fori_loop(0, lax.div(groups + (UNITS - 1), UNITS), pairs, 0)

    label = lax.broadcasted_iota(jnp.int32, (held, lanes), 0)

    def gather_sums(block, total):
        rows = pl.ds(pl.multiple_of(block * 8, 8), 8)
        force = [-damping * jnp.sum(force_ref[axis, rows], axis=1) for axis in range(3)]
        lever = [arms_ref[axis, rows, :] for axis in range(3)]
        torque = [
            lever[1] * force[2] - lever[2] * force[1],
            lever[2] * force[0] - lever[0] * force[2],
            lever[0] * force[1] - lever[1] * force[0],
        ]
        loads = force + torque + [jnp.zeros_like(force[0])] * 2
        for comp in range(8):
            loads_ref[:, comp, :] = loads[comp]
        frags = frag_ref[rows, :]
        for unit in range(8):
            hits = (frags[unit : unit + 1, :] == label).astype(jnp.float32).astype(jnp.bfloat16)
            total = total + dot_lanes(split_rows(loads_ref[unit]), hits)
        return total

    total = lax.fori_loop(0, cells // 8, gather_sums, jnp.zeros((24, held), jnp.float32))
    out_ref[...] = joined_rows(total)


def move_kernel(
    owned, target_ref, fixed_ref, sums_ref, state_ref, arms_ref, frag_ref, spheres_ref, clumps_ref
):
    bricks, _, held = sums_ref.shape
    lanes = frag_ref.shape[1]
    cells = frag_ref.shape[0]
    targets = jnp.broadcast_to(target_ref[...], (lanes, held))
    lane = lax.broadcasted_iota(jnp.int32, (1, held), 1)

    def match(brick, carry):
        sums, base = carry
        fixed = fixed_ref[brick]
        hits = (targets == fixed[8:9, :]).astype(jnp.float32).astype(jnp.bfloat16)
        sums = sums + dot_lanes(split_rows(sums_ref[brick]), hits)
        number = jnp.where(lane < owned, brick * owned + lane, -1).astype(jnp.float32)
        hits = (targets == number).astype(jnp.float32).astype(jnp.bfloat16)
        base = base + dot_lanes(split_rows(fixed[0:8, :]), hits)
        return sums, base

    zero = jnp.zeros((24, lanes), jnp.float32)
    sums, base = lax.fori_loop(0, bricks, match, (zero, zero))
    sums = joined_rows(sums)
    base = joined_rows(base)
    rows = []
    for axis in range(3):
        pull = gravity if axis == 2 else 0.0
        rows.append(
            base[axis : axis + 1]
            + time_step * (sums[axis : axis + 1] * base[6:7] - pull)
        )
    for axis in range(3, 6):
        rows.append(base[axis : axis + 1] + time_step * sums[axis : axis + 1] * base[7:8])
    for comp in range(6):
        clumps_ref[comp : comp + 1, :] = rows[comp]
    wide = [jnp.broadcast_to(value, (8, lanes)) for value in rows]

    def cross(first, second):
        return [
            first[1] * second[2] - first[2] * second[1],
            first[2] * second[0] - first[0] * second[2],
            first[0] * second[1] - first[1] * second[0],
        ]

    def move(block, unused):
        at = pl.ds(pl.multiple_of(block * 8, 8), 8)
        index = frag_ref[at, :] + (lanes - held)
        motion = [lanes_of(value, index) for value in wide]
        velocity, spin = motion[0:3], motion[3:6]
        arm = [arms_ref[axis, at, :] for axis in range(3)]
        half = [0.5 * time_step * value for value in spin]
        turned = cross(half, arm)
        twice = cross(half, turned)
        scale = 2.0 / (1.0 + half[0] * half[0] + half[1] * half[1] + half[2] * half[2])
        change = [scale * (turned[axis] + twice[axis]) for axis in range(3)]
        new_arm = [arm[axis] + change[axis] for axis in range(3)]
        swing = cross(spin, new_arm)
        for axis in range(3):
            spheres_ref[axis, at, :] = (
                state_ref[axis, at, :] + time_step * velocity[axis] + (new_arm[axis] - arm[axis])
            )
            spheres_ref[3 + axis, at, :] = velocity[axis] + swing[axis]
        return unused

    lax.fori_loop(0, cells // 8, move, 0)


def local(
    state, arms, sphere_frag, frag_owner, frag_clump, tiles, clump_motion, inv_mass, inv_moment
):
    cells_x, cells_y, cells_z = (state.shape[1], state.shape[2], state.shape[3])
    lanes = state.shape[4]
    cells = cells_x * cells_y * cells_z
    owned = inv_mass.shape[0]
    held = frag_clump.shape[0]
    names = ("gx", "gy", "gz")
    vmem = pl.BlockSpec(memory_space=pltpu.VMEM)
    smem = pl.BlockSpec(memory_space=pltpu.SMEM)
    params = pltpu.CompilerParams(vmem_limit_bytes=VMEM)

    frag_key = (frag_owner[:, 0] * owned + frag_clump).astype(jnp.float32)
    flat_state = state.reshape(7, cells, lanes)
    flat_arms = arms.reshape(3, cells, lanes)
    flat_frag = sphere_frag.reshape(cells, lanes)

    fixed = jnp.concatenate(
        [
            jnp.pad(
                jnp.concatenate([clump_motion, inv_mass[None], inv_moment[None]], axis=0),
                ((0, 0), (0, held - owned)),
            ),
            frag_key[None],
            jnp.zeros((7, held), jnp.float32),
        ],
        axis=0,
    )
    fixed = lax.all_gather(fixed, names, axis=0, tiled=False)

    table = pl.pallas_call(
        pack_kernel,
        out_shape=jax.ShapeDtypeStruct((cells, 8, lanes), jnp.float32),
        in_specs=[vmem] * 3,
        out_specs=vmem,
        compiler_params=params,
    )(flat_state, flat_frag, jnp.pad(frag_key, (0, lanes - held))[None])
    padded = with_halo(
        table.reshape(cells_x, cells_y, cells_z, 8, lanes), (("gx", 0), ("gy", 1), ("gz", 2)), 1
    )
    span_y, span_z = (cells_y + 2, cells_z + 2)
    span = (cells_x + 2) * span_y * span_z
    padded = padded.reshape(span, 8, lanes)

    codes = jnp.sort(tiles[0])
    total = codes.shape[0]
    own = codes // 27
    offset = codes % 27
    steps = (offset // 9 - 1, offset // 3 % 3 - 1, offset % 3 - 1)

    def pad_place(cell):
        x = cell // (cells_y * cells_z) + 1
        y = cell // cells_z % cells_y + 1
        z = cell % cells_z + 1
        return (x * span_y + y) * span_z + z

    near = pad_place(own) + (steps[0] * span_y + steps[1]) * span_z + steps[2]
    need = sum(
        jnp.where(steps[axis] == 1, 1, jnp.where(steps[axis] == -1, 2, 0)) << (2 * axis)
        for axis in range(3)
    )
    first = jnp.where(own != jnp.roll(own, 1), GROUP - 1, 0).at[0].set(GROUP - 1)
    place = pad_place(jnp.arange(cells + 1, dtype=jnp.int32) % cells)
    kinds = jnp.arange(27, dtype=jnp.int32)
    moves = jnp.stack([kinds // 9 - 1, kinds // 3 % 3 - 1, kinds % 3 - 1], axis=1)
    shift = jnp.pad(moves.astype(jnp.float32), ((0, 0), (0, 5)))
    shift = jnp.broadcast_to(shift[:, :, None], (27, 8, lanes))

    slots, count = pl.pallas_call(
        list_kernel,
        out_shape=(
            jax.ShapeDtypeStruct((total, lanes), jnp.int32),
            jax.ShapeDtypeStruct((8, total), jnp.int32),
        ),
        in_specs=[smem, smem, vmem],
        out_specs=(vmem, vmem),
        scratch_shapes=[
            pltpu.VMEM((span, lanes), jnp.int32),
            pltpu.VMEM((total, lanes), jnp.int32),
        ],
        compiler_params=params,
    )(near, need, padded)

    chunks = total + cells * GROUP // lanes + 2
    chunks = -(-chunks // 16) * 16
    sums = pl.pallas_call(
        force_kernel,
        out_shape=jax.ShapeDtypeStruct((8, held), jnp.float32),
        in_specs=[smem] * 6 + [vmem] * 5,
        out_specs=vmem,
        scratch_shapes=[
            pltpu.VMEM((chunks * 8, lanes), jnp.float32),
            pltpu.VMEM((chunks * 8, lanes), jnp.float32),
            pltpu.VMEM((3, cells + 8, 8, lanes), jnp.float32),
            pltpu.VMEM((8, 8, lanes), jnp.float32),
            pltpu.SMEM((chunks * (lanes // GROUP) + 16,), jnp.int32),
        ],
        compiler_params=params,
    )(near, offset, own, first, count[0:1], place, padded, slots, shift, flat_arms, flat_frag)

    sums = lax.all_gather(sums, names, axis=0, tiled=False)

    brick = lax.axis_index(names)
    mine = jnp.where(
        jnp.arange(lanes - held) < owned, brick * owned + jnp.arange(lanes - held), -2
    ).astype(jnp.float32)
    target = jnp.concatenate([mine, frag_key])[:, None]
    spheres, clumps = pl.pallas_call(
        functools.partial(move_kernel, owned),
        out_shape=(
            jax.ShapeDtypeStruct((6, cells, lanes), jnp.float32),
            jax.ShapeDtypeStruct((6, lanes), jnp.float32),
        ),
        in_specs=[vmem] * 6,
        out_specs=(vmem, vmem),
        compiler_params=params,
    )(target, fixed, sums, flat_state, flat_arms, flat_frag)
    return (spheres.reshape((6,) + state.shape[1:]), clumps[:, :owned])


def solution(mesh):
    return jax.shard_map(
        local,
        mesh=mesh,
        in_specs=(
            P(None, "gx", "gy", "gz", None),
            P(None, "gx", "gy", "gz", None),
            P("gx", "gy", "gz", None),
            P(("gx", "gy", "gz"), None),
            P(("gx", "gy", "gz")),
            P(("gx", "gy", "gz"), None),
            P(None, ("gx", "gy", "gz")),
            P(("gx", "gy", "gz")),
            P(("gx", "gy", "gz")),
        ),
        out_specs=(P(None, "gx", "gy", "gz", None), P(None, ("gx", "gy", "gz"))),
        check_vma=False,
    )
```

```python
import functools

import jax
import jax.numpy as jnp
from jax import lax
from jax.experimental import pallas as pl
from jax.experimental.pallas import tpu as pltpu
from jax.sharding import PartitionSpec as P

stiffness = 100.0
damping = 2.0
time_step = 0.01
gravity = 9.81
epsilon_sq = 1e-08
radius_top = 0.14

GROUP = 32
GROUP_BITS = GROUP.bit_length() - 1
UNITS = 4
VMEM = 56 * 1024 * 1024


def lanes_of(values, index):
    return jnp.take_along_axis(values, index, axis=1, mode="promise_in_bounds")


def split_rows(values):
    high = values.astype(jnp.bfloat16).astype(jnp.float32)
    rest = values - high
    middle = rest.astype(jnp.bfloat16).astype(jnp.float32)
    low = rest - middle
    return jnp.concatenate([high, middle, low], axis=0).astype(jnp.bfloat16)


def joined_rows(stacked):
    rows = stacked.shape[0] // 3
    return stacked[0:rows] + stacked[rows : 2 * rows] + stacked[2 * rows :]


def dot_lanes(first, second):
    return lax.dot_general(
        first, second, (((1,), (1,)), ((), ())), preferred_element_type=jnp.float32
    )


def everywhere(x, names):
    devices = lax.axis_size(names)
    copies = jnp.broadcast_to(x[None], (devices,) + x.shape)
    return lax.all_to_all(copies, names, split_axis=0, concat_axis=0, tiled=True)


def with_halo(x, sides, width):
    for axis, dim in sides:
        devices, length = (lax.axis_size(axis), x.shape[dim])
        up = [(i, (i + 1) % devices) for i in range(devices)]
        down = [(j, i) for i, j in up]
        last = lax.slice_in_dim(x, length - width, length, axis=dim)
        initial = lax.slice_in_dim(x, 0, width, axis=dim)
        before = lax.ppermute(last, axis, up)
        after = lax.ppermute(initial, axis, down)
        x = jnp.concatenate([before, x, after], axis=dim)
    return x


def pack_kernel(state_ref, frag_ref, key_ref, out_ref):
    cells = frag_ref.shape[0]
    for comp in range(7):
        out_ref[:, comp, :] = state_ref[comp]
    keys = jnp.broadcast_to(key_ref[0:1, :], (8, key_ref.shape[1]))
    for block in range(cells // 8):
        rows = pl.ds(block * 8, 8)
        out_ref[rows, 7, :] = lanes_of(keys, frag_ref[rows, :])


def list_kernel(near_smem, need_smem, table_ref, slots_ref, count_ref, class_ref, member_ref):
    tiles = slots_ref.shape[0]
    lanes = slots_ref.shape[1]
    span = class_ref.shape[0]

    def plane(comp):
        return table_ref[pl.ds(comp, span, stride=8), :]

    radius = plane(6) + (radius_top + 1e-5)
    classes = jnp.zeros(class_ref.shape, jnp.int32)
    for axis in range(3):
        place = plane(axis)
        classes = classes | jnp.where(place < radius, 1 << (2 * axis), 0)
        classes = classes | jnp.where(place > 1.0 - radius, 2 << (2 * axis), 0)
    class_ref[...] = classes

    def copy_rows(block, unused):
        for unit in range(8):
            tile = block * 8 + unit
            need = need_smem[tile]
            row = class_ref[pl.ds(near_smem[tile], 1), :]
            member_ref[pl.ds(tile, 1), :] = jnp.where((row & need) == need, 1, 0)
        return unused

    lax.fori_loop(0, tiles // 8, copy_rows, 0)

    before = lax.broadcasted_iota(jnp.int32, (lanes, lanes), 0)
    after = lax.broadcasted_iota(jnp.int32, (lanes, lanes), 1)
    earlier = (before < after).astype(jnp.bfloat16)
    ones = jnp.ones((8, lanes), jnp.bfloat16)
    step_rows = 256

    def compact(block, unused):
        rows = pl.ds(pl.multiple_of(block * step_rows, step_rows), step_rows)
        member = member_ref[rows, :]
        flags = member.astype(jnp.float32).astype(jnp.bfloat16)
        rank = jnp.dot(flags, earlier, preferred_element_type=jnp.float32)
        slot = lax.broadcasted_iota(jnp.int32, (step_rows, lanes), 1)
        moves = slot - rank.astype(jnp.int32)
        word = jnp.where(member != 0, slot + lanes * moves, 0)
        bit = 1
        while bit < lanes:
            keep = jnp.where((word & (bit * lanes)) != 0, 0, word)
            gone = word ^ keep
            word = keep | pltpu.roll(gone, lanes - bit, 1)
            bit *= 2
        slots_ref[rows, :] = word & (lanes - 1)
        return unused

    lax.fori_loop(0, tiles // step_rows, compact, 0)
    for block in range(tiles // lanes):
        flags = member_ref[pl.ds(block * lanes, lanes), :].astype(jnp.float32).astype(jnp.bfloat16)
        count_ref[:, pl.ds(block * lanes, lanes)] = dot_lanes(ones, flags).astype(jnp.int32)


def fill_kernel(
    near_smem, shift_smem, own_smem, first_smem, count_smem, table_ref, slots_ref, shift_ref,
    turned_ref, cell_smem, groups_smem, list_ref,
):
    tiles = slots_ref.shape[0]
    lanes = slots_ref.shape[1]
    lane_bits = lanes.bit_length() - 1
    lane = lax.broadcasted_iota(jnp.int32, (8, lanes), 1)
    row = lax.broadcasted_iota(jnp.int32, (8, lanes), 0)
    absent = jnp.where(row == 6, -10.0, 0.0)
    def fill(block, carry):
        end, last_chunk, last_new, last_held = carry
        for unit in range(8):
            tile = block * 8 + unit
            align = first_smem[tile]
            own = own_smem[tile]
            start = (end + align) & ~align
            amount = count_smem[0, tile]
            chunk = start >> lane_bits
            offset = start & (lanes - 1)
            for piece in range(lanes // GROUP + 1):
                cell_smem[(start >> GROUP_BITS) + piece] = own
            slots = jnp.broadcast_to(slots_ref[pl.ds(tile, 1), :], (8, lanes))
            slots = pltpu.roll(slots, offset, 1)
            found = lanes_of(table_ref[near_smem[tile]], slots) + shift_ref[shift_smem[tile]]
            new = jnp.where(((lane - offset) & (lanes - 1)) < amount, found, absent)
            held_row = jnp.where(chunk != last_chunk, last_new, last_held)
            held_row = jnp.where(lane >= offset, new, held_row)
            new = jnp.where(lane >= offset, absent, new)
            list_ref[pl.ds(pl.multiple_of(chunk * 8, 8), 8), :] = held_row
            list_ref[pl.ds(pl.multiple_of(chunk * 8 + 8, 8), 8), :] = new
            end, last_chunk, last_new, last_held = start + amount, chunk, new, held_row
        return end, last_chunk, last_new, last_held

    start = (jnp.int32(0), jnp.int32(0), absent, absent)
    end = lax.fori_loop(0, tiles // 8, fill, start)[0]
    groups = (end + GROUP - 1) >> GROUP_BITS
    for extra in range(UNITS):
        cell_smem[groups + extra] = -1
    groups_smem[0] = groups

    def turn(block, unused):
        rows = pl.ds(pl.multiple_of(block * lanes, lanes), lanes)
        turned_ref[rows, :] = list_ref[rows, :].T
        return unused

    lax.fori_loop(0, (end + 16 * lanes - 1) >> (lane_bits + 4), turn, 0)


def pair_kernel(cell_smem, groups_smem, place_smem, table_ref, turned_ref, force_ref):
    lanes = table_ref.shape[2]
    lane_bits = lanes.bit_length() - 1
    cells = place_smem.shape[0]
    groups = groups_smem[0]
    force_ref[...] = jnp.zeros(force_ref.shape, jnp.float32)

    def pairs(step, unused):
        totals = []
        for unit in range(UNITS):
            group = step * UNITS + unit
            cell = cell_smem[group]
            target = jnp.where(cell < 0, cells, cell)
            own = place_smem[jnp.maximum(cell, 0)]
            begin = group * GROUP
            chunk = begin >> lane_bits
            at = (chunk >> 4) * lanes + (begin & (lanes - 1))
            block = turned_ref[pl.ds(pl.multiple_of(at, GROUP), GROUP), :]
            column = (chunk & 15) * 8
            other = [
                lanes_of(block, jnp.full((GROUP, lanes), column + comp, jnp.int32))
                for comp in range(8)
            ]
            mine = [table_ref[own, pl.ds(comp, 1), :] for comp in range(8)]
            apart = [other[axis] - mine[axis] for axis in range(3)]
            square = apart[0] * apart[0] + apart[1] * apart[1] + apart[2] * apart[2] + epsilon_sq
            inverse = lax.rsqrt(square)
            reach = other[6] + mine[6]
            overlap = jnp.maximum(reach - square * inverse, 0.0)
            overlap = jnp.where(other[7] != mine[7], overlap, 0.0)
            closing = (
                (other[3] - mine[3]) * apart[0]
                + (other[4] - mine[4]) * apart[1]
                + (other[5] - mine[5]) * apart[2]
            )
            scaled = overlap * (other[6] * mine[6])
            root = scaled * lax.rsqrt(jnp.maximum(scaled * reach, 1e-30))
            factor = (
                root * inverse * (stiffness / damping * overlap - closing * inverse)
            )
            totals.append(
                (
                    target,
                    [
                        jnp.sum((factor * apart[axis]).reshape(GROUP // 8, 8, lanes), axis=0)
                        for axis in range(3)
                    ],
                )
            )
        for cell, parts in totals:
            for axis in range(3):
                force_ref[axis, cell] += parts[axis]
        return unused

    lax.fori_loop(0, lax.div(groups + (UNITS - 1), UNITS), pairs, 0)


def sums_kernel(force_ref, arms_ref, frag_ref, out_ref, loads_ref):
    cells, lanes = frag_ref.shape
    held = out_ref.shape[1]
    label = lax.broadcasted_iota(jnp.int32, (held, lanes), 0)

    def gather_sums(block, total):
        rows = pl.ds(pl.multiple_of(block * 8, 8), 8)
        force = [-damping * jnp.sum(force_ref[axis, rows], axis=1) for axis in range(3)]
        lever = [arms_ref[axis, rows, :] for axis in range(3)]
        torque = [
            lever[1] * force[2] - lever[2] * force[1],
            lever[2] * force[0] - lever[0] * force[2],
            lever[0] * force[1] - lever[1] * force[0],
        ]
        loads = force + torque + [jnp.zeros_like(force[0])] * 2
        for comp in range(8):
            loads_ref[:, comp, :] = loads[comp]
        frags = frag_ref[rows, :]
        for unit in range(8):
            hits = (frags[unit : unit + 1, :] == label).astype(jnp.float32).astype(jnp.bfloat16)
            total = total + dot_lanes(split_rows(loads_ref[unit]), hits)
        return total

    total = lax.fori_loop(0, cells // 8, gather_sums, jnp.zeros((24, held), jnp.float32))
    out_ref[...] = joined_rows(total)


def add_over(bricks, dots, rows, lanes):
    def step(block, total):
        parts = [dots(block * 8 + unit) for unit in range(8)]
        while len(parts) > 1:
            parts = [first + second for first, second in zip(parts[::2], parts[1::2])]
        return total + parts[0]

    return joined_rows(lax.fori_loop(0, bricks // 8, step, jnp.zeros((rows, lanes), jnp.float32)))


def base_kernel(owned, target_ref, fixed_ref, base_ref):
    bricks, _, held = fixed_ref.shape
    lanes = target_ref.shape[0]
    targets = jnp.broadcast_to(target_ref[...], (lanes, held))
    lane = lax.broadcasted_iota(jnp.int32, (1, held), 1)

    def dots(brick):
        number = jnp.where(lane < owned, brick * owned + lane, -1).astype(jnp.float32)
        hits = (targets == number).astype(jnp.float32).astype(jnp.bfloat16)
        return dot_lanes(split_rows(fixed_ref[brick, 0:8, :]), hits)

    base_ref[...] = add_over(bricks, dots, 24, lanes)


def move_kernel(
    target_ref, fixed_ref, base_ref, sums_ref, state_ref, arms_ref, frag_ref, spheres_ref, clumps_ref
):
    bricks, _, held = sums_ref.shape
    lanes = frag_ref.shape[1]
    cells = frag_ref.shape[0]
    targets = jnp.broadcast_to(target_ref[...], (lanes, held))

    def dots(brick):
        hits = (targets == fixed_ref[brick, 8:9, :]).astype(jnp.float32).astype(jnp.bfloat16)
        return dot_lanes(split_rows(sums_ref[brick]), hits)

    sums = add_over(bricks, dots, 24, lanes)
    base = base_ref[...]
    rows = []
    for axis in range(3):
        pull = gravity if axis == 2 else 0.0
        rows.append(
            base[axis : axis + 1]
            + time_step * (sums[axis : axis + 1] * base[6:7] - pull)
        )
    for axis in range(3, 6):
        rows.append(base[axis : axis + 1] + time_step * sums[axis : axis + 1] * base[7:8])
    for comp in range(6):
        clumps_ref[comp : comp + 1, :] = rows[comp]
    tall = 32
    wide = [jnp.broadcast_to(value, (tall, lanes)) for value in rows]

    def cross(first, second):
        return [
            first[1] * second[2] - first[2] * second[1],
            first[2] * second[0] - first[0] * second[2],
            first[0] * second[1] - first[1] * second[0],
        ]

    def move(block, unused):
        at = pl.ds(pl.multiple_of(block * tall, tall), tall)
        index = frag_ref[at, :] + (lanes - held)
        motion = [lanes_of(value, index) for value in wide]
        velocity, spin = motion[0:3], motion[3:6]
        arm = [arms_ref[axis, at, :] for axis in range(3)]
        half = [0.5 * time_step * value for value in spin]
        turned = cross(half, arm)
        twice = cross(half, turned)
        scale = 2.0 / (1.0 + half[0] * half[0] + half[1] * half[1] + half[2] * half[2])
        change = [scale * (turned[axis] + twice[axis]) for axis in range(3)]
        new_arm = [arm[axis] + change[axis] for axis in range(3)]
        swing = cross(spin, new_arm)
        for axis in range(3):
            spheres_ref[axis, at, :] = (
                state_ref[axis, at, :] + time_step * velocity[axis] + (new_arm[axis] - arm[axis])
            )
            spheres_ref[3 + axis, at, :] = velocity[axis] + swing[axis]
        return unused

    lax.fori_loop(0, cells // tall, move, 0)


def local(
    state, arms, sphere_frag, frag_owner, frag_clump, tiles, clump_motion, inv_mass, inv_moment
):
    cells_x, cells_y, cells_z = (state.shape[1], state.shape[2], state.shape[3])
    lanes = state.shape[4]
    cells = cells_x * cells_y * cells_z
    owned = inv_mass.shape[0]
    held = frag_clump.shape[0]
    names = ("gx", "gy", "gz")
    vmem = pl.BlockSpec(memory_space=pltpu.VMEM)
    smem = pl.BlockSpec(memory_space=pltpu.SMEM)
    params = pltpu.CompilerParams(vmem_limit_bytes=VMEM)

    frag_key = (frag_owner[:, 0] * owned + frag_clump).astype(jnp.float32)
    flat_state = state.reshape(7, cells, lanes)
    flat_arms = arms.reshape(3, cells, lanes)
    flat_frag = sphere_frag.reshape(cells, lanes)

    fixed = jnp.concatenate(
        [
            jnp.pad(
                jnp.concatenate([clump_motion, inv_mass[None], inv_moment[None]], axis=0),
                ((0, 0), (0, held - owned)),
            ),
            frag_key[None],
            jnp.zeros((7, held), jnp.float32),
        ],
        axis=0,
    )
    fixed = everywhere(fixed, names)

    table = pl.pallas_call(
        pack_kernel,
        out_shape=jax.ShapeDtypeStruct((cells, 8, lanes), jnp.float32),
        in_specs=[vmem] * 3,
        out_specs=vmem,
        compiler_params=params,
    )(flat_state, flat_frag, jnp.pad(frag_key, (0, lanes - held))[None])
    padded = with_halo(
        table.reshape(cells_x, cells_y, cells_z, 8, lanes), (("gx", 0), ("gy", 1), ("gz", 2)), 1
    )
    span_y, span_z = (cells_y + 2, cells_z + 2)
    span = (cells_x + 2) * span_y * span_z
    padded = padded.reshape(span, 8, lanes)

    codes = jnp.sort(tiles[0])
    total = codes.shape[0]
    own = codes // 27
    offset = codes % 27
    steps = (offset // 9 - 1, offset // 3 % 3 - 1, offset % 3 - 1)

    def pad_place(cell):
        x = cell // (cells_y * cells_z) + 1
        y = cell // cells_z % cells_y + 1
        z = cell % cells_z + 1
        return (x * span_y + y) * span_z + z

    near = pad_place(own) + (steps[0] * span_y + steps[1]) * span_z + steps[2]
    need = sum(
        jnp.where(steps[axis] == 1, 1, jnp.where(steps[axis] == -1, 2, 0)) << (2 * axis)
        for axis in range(3)
    )
    first = jnp.where(own != jnp.roll(own, 1), GROUP - 1, 0).at[0].set(GROUP - 1)
    place = pad_place(jnp.arange(cells, dtype=jnp.int32))
    kinds = jnp.arange(27, dtype=jnp.int32)
    moves = jnp.stack([kinds // 9 - 1, kinds // 3 % 3 - 1, kinds % 3 - 1], axis=1)
    shift = jnp.pad(moves.astype(jnp.float32), ((0, 0), (0, 5)))
    shift = jnp.broadcast_to(shift[:, :, None], (27, 8, lanes))

    slots, count = pl.pallas_call(
        list_kernel,
        out_shape=(
            jax.ShapeDtypeStruct((total, lanes), jnp.int32),
            jax.ShapeDtypeStruct((8, total), jnp.int32),
        ),
        in_specs=[smem, smem, vmem],
        out_specs=(vmem, vmem),
        scratch_shapes=[
            pltpu.VMEM((span, lanes), jnp.int32),
            pltpu.VMEM((total, lanes), jnp.int32),
        ],
        compiler_params=params,
    )(near, need, padded.reshape(span * 8, lanes))

    chunks = total + cells * GROUP // lanes + 2
    chunks = -(-chunks // 16) * 16
    turned, cell_of, groups = pl.pallas_call(
        fill_kernel,
        out_shape=(
            jax.ShapeDtypeStruct((chunks * 8, lanes), jnp.float32),
            jax.ShapeDtypeStruct((chunks * (lanes // GROUP) + 16,), jnp.int32),
            jax.ShapeDtypeStruct((1,), jnp.int32),
        ),
        in_specs=[smem] * 5 + [vmem] * 3,
        out_specs=(vmem, smem, smem),
        scratch_shapes=[pltpu.VMEM((chunks * 8, lanes), jnp.float32)],
        compiler_params=params,
    )(near, offset, own, first, count[0:1], padded, slots, shift)
    force = pl.pallas_call(
        pair_kernel,
        out_shape=jax.ShapeDtypeStruct((3, cells + 8, 8, lanes), jnp.float32),
        in_specs=[smem] * 3 + [vmem] * 2,
        out_specs=vmem,
        compiler_params=params,
    )(cell_of, groups, place, padded, turned)
    sums = pl.pallas_call(
        sums_kernel,
        out_shape=jax.ShapeDtypeStruct((8, held), jnp.float32),
        in_specs=[vmem] * 3,
        out_specs=vmem,
        scratch_shapes=[pltpu.VMEM((8, 8, lanes), jnp.float32)],
        compiler_params=params,
    )(force, flat_arms, flat_frag)

    sums = everywhere(sums, names)

    brick = lax.axis_index(names)
    mine = jnp.where(
        jnp.arange(lanes - held) < owned, brick * owned + jnp.arange(lanes - held), -2
    ).astype(jnp.float32)
    target = jnp.concatenate([mine, frag_key])[:, None]
    base = pl.pallas_call(
        functools.partial(base_kernel, owned),
        out_shape=jax.ShapeDtypeStruct((8, lanes), jnp.float32),
        in_specs=[vmem] * 2,
        out_specs=vmem,
        compiler_params=params,
    )(target, fixed)
    spheres, clumps = pl.pallas_call(
        move_kernel,
        out_shape=(
            jax.ShapeDtypeStruct((6, cells, lanes), jnp.float32),
            jax.ShapeDtypeStruct((6, lanes), jnp.float32),
        ),
        in_specs=[vmem] * 7,
        out_specs=(vmem, vmem),
        compiler_params=params,
    )(target, fixed, base, sums, flat_state, flat_arms, flat_frag)
    return (spheres.reshape((6,) + state.shape[1:]), clumps[:, :owned])


def solution(mesh):
    return jax.shard_map(
        local,
        mesh=mesh,
        in_specs=(
            P(None, "gx", "gy", "gz", None),
            P(None, "gx", "gy", "gz", None),
            P("gx", "gy", "gz", None),
            P(("gx", "gy", "gz"), None),
            P(("gx", "gy", "gz")),
            P(("gx", "gy", "gz"), None),
            P(None, ("gx", "gy", "gz")),
            P(("gx", "gy", "gz")),
            P(("gx", "gy", "gz")),
        ),
        out_specs=(P(None, "gx", "gy", "gz", None), P(None, ("gx", "gy", "gz"))),
        check_vma=False,
    )
```

```python
import functools

import jax
import jax.numpy as jnp
from jax import lax
from jax.experimental import pallas as pl
from jax.experimental.pallas import tpu as pltpu
from jax.sharding import PartitionSpec as P

stiffness = 100.0
damping = 2.0
time_step = 0.01
gravity = 9.81
epsilon_sq = 1e-08
radius_top = 0.14

GROUP = 32
GROUP_BITS = GROUP.bit_length() - 1
FILL = 16
UNITS = 4
VMEM = 56 * 1024 * 1024


def lanes_of(values, index):
    return jnp.take_along_axis(values, index, axis=1, mode="promise_in_bounds")


def split_rows(values):
    high = values.astype(jnp.bfloat16).astype(jnp.float32)
    rest = values - high
    middle = rest.astype(jnp.bfloat16).astype(jnp.float32)
    low = rest - middle
    return jnp.concatenate([high, middle, low], axis=0).astype(jnp.bfloat16)


def joined_rows(stacked):
    rows = stacked.shape[0] // 3
    return stacked[0:rows] + stacked[rows : 2 * rows] + stacked[2 * rows :]


def dot_lanes(first, second):
    return lax.dot_general(
        first, second, (((1,), (1,)), ((), ())), preferred_element_type=jnp.float32
    )


def everywhere(x, names):
    devices = lax.axis_size(names)
    copies = jnp.broadcast_to(x[None], (devices,) + x.shape)
    return lax.all_to_all(copies, names, split_axis=0, concat_axis=0, tiled=True)


def with_halo(x, sides, width):
    for axis, dim in sides:
        devices, length = (lax.axis_size(axis), x.shape[dim])
        up = [(i, (i + 1) % devices) for i in range(devices)]
        down = [(j, i) for i, j in up]
        last = lax.slice_in_dim(x, length - width, length, axis=dim)
        initial = lax.slice_in_dim(x, 0, width, axis=dim)
        before = lax.ppermute(last, axis, up)
        after = lax.ppermute(initial, axis, down)
        x = jnp.concatenate([before, x, after], axis=dim)
    return x


def pack_kernel(state_ref, frag_ref, key_ref, out_ref):
    cells = frag_ref.shape[0]
    for comp in range(7):
        out_ref[:, comp, :] = state_ref[comp]
    keys = jnp.broadcast_to(key_ref[0:1, :], (8, key_ref.shape[1]))
    for block in range(cells // 8):
        rows = pl.ds(block * 8, 8)
        out_ref[rows, 7, :] = lanes_of(keys, frag_ref[rows, :])


def list_kernel(near_ref, need_ref, table_ref, slots_ref, count_ref, class_ref):
    tiles, lanes = slots_ref.shape
    span = table_ref.shape[0] // 8
    padded = class_ref.shape[0]

    def plane(comp):
        return table_ref[pl.ds(comp, span, stride=8), :]

    radius = plane(6) + (radius_top + 1e-5)
    classes = jnp.zeros((span, lanes), jnp.float32)
    for axis in range(3):
        place = plane(axis)
        classes = classes + jnp.where(place < radius, 1.0 * (1 << (2 * axis)), 0.0)
        classes = classes + jnp.where(place > 1.0 - radius, 1.0 * (2 << (2 * axis)), 0.0)
    class_ref[pl.ds(span // 8 * 8, padded - span // 8 * 8), :] = jnp.zeros(
        (padded - span // 8 * 8, lanes), jnp.float32
    )
    class_ref[pl.ds(0, span), :] = classes
    codes = jnp.concatenate(
        [class_ref[pl.ds(at, lanes), :].T for at in range(0, padded, lanes)], axis=1
    ).astype(jnp.bfloat16)
    before = lax.broadcasted_iota(jnp.int32, (lanes, lanes), 1)
    after = lax.broadcasted_iota(jnp.int32, (lanes, lanes), 0)
    earlier = (before < after).astype(jnp.float32).astype(jnp.bfloat16)
    ones = jnp.ones((8, lanes), jnp.bfloat16)
    wide = 256

    def compact(block, unused):
        at = pl.ds(pl.multiple_of(block * wide, wide), wide)
        cell = lax.broadcasted_iota(jnp.int32, (padded, wide), 0)
        hits = (cell == near_ref[:, at]).astype(jnp.float32).astype(jnp.bfloat16)
        found = jnp.dot(codes, hits, preferred_element_type=jnp.float32).astype(jnp.int32)
        need = need_ref[:, at]
        member = (found & need) == need
        flags = member.astype(jnp.float32).astype(jnp.bfloat16)
        count_ref[:, at] = jnp.dot(ones, flags, preferred_element_type=jnp.float32).astype(jnp.int32)
        rank = jnp.dot(earlier, flags, preferred_element_type=jnp.float32)
        slot = lax.broadcasted_iota(jnp.int32, (lanes, wide), 0)
        moves = slot - rank.astype(jnp.int32)
        word = jnp.where(member, slot + lanes * moves, 0)
        bit = 1
        while bit < lanes:
            keep = jnp.where((word & (bit * lanes)) != 0, 0, word)
            gone = word ^ keep
            word = keep | jnp.concatenate([gone[bit:], gone[:bit]], axis=0)
            bit *= 2
        word = word & (lanes - 1)
        for part in range(wide // lanes):
            rows = pl.ds(pl.multiple_of(block * wide + part * lanes, lanes), lanes)
            slots_ref[rows, :] = word[:, part * lanes : (part + 1) * lanes].T
        return unused

    lax.fori_loop(0, tiles // wide, compact, 0)


def fill_kernel(
    near_smem, shift_smem, own_smem, first_smem, count_smem, table_ref, slots_ref, shift_ref,
    turned_ref, cell_smem, until_smem, groups_smem, list_ref,
):
    tiles, lanes = slots_ref.shape
    cells = cell_smem.shape[0] - 8
    lane_bits = lanes.bit_length() - 1
    lane = lax.broadcasted_iota(jnp.int32, (8, lanes), 1)
    row = lax.broadcasted_iota(jnp.int32, (8, lanes), 0)
    absent = jnp.where(row == 6, -10.0, 0.0)

    def fill(block, carry):
        end, entry, last_chunk, last_new, last_held = carry
        units = range(FILL)
        first = [first_smem[block * FILL + unit] for unit in units]
        own = [own_smem[block * FILL + unit] for unit in units]
        near = [near_smem[block * FILL + unit] for unit in units]
        shift = [shift_smem[block * FILL + unit] for unit in units]
        amounts = [count_smem[0, block * FILL + unit] for unit in units]
        starts, ends, entries = [], [], []
        for unit in units:
            align = first[unit] * (GROUP - 1)
            start = (end + align) & ~align
            end = start + jnp.maximum(amounts[unit], first[unit])
            entry = entry + first[unit]
            starts.append(start)
            ends.append(end)
            entries.append(entry)
        found = []
        for unit in units:
            slots = jnp.broadcast_to(slots_ref[pl.ds(block * FILL + unit, 1), :], (8, lanes))
            slots = pltpu.roll(slots, starts[unit] & (lanes - 1), 1)
            found.append(lanes_of(table_ref[near[unit]], slots) + shift_ref[shift[unit]])
        for unit in units:
            chunk = starts[unit] >> lane_bits
            offset = starts[unit] & (lanes - 1)
            new = jnp.where(((lane - offset) & (lanes - 1)) < amounts[unit], found[unit], absent)
            held_row = jnp.where(chunk != last_chunk, last_new, last_held)
            held_row = jnp.where(lane >= offset, new, held_row)
            new = jnp.where(lane >= offset, absent, new)
            list_ref[chunk] = held_row
            list_ref[chunk + 1] = new
            last_chunk, last_new, last_held = chunk, new, held_row
        for unit in units:
            cell_smem[entries[unit]] = own[unit]
            until_smem[entries[unit]] = (ends[unit] + (GROUP - 1)) >> GROUP_BITS
        return end, entry, last_chunk, last_new, last_held

    start = (jnp.int32(0), jnp.int32(-1), jnp.int32(0), absent, absent)
    end, entry = lax.fori_loop(0, tiles // FILL, fill, start)[0:2]
    groups_smem[0] = (end + (GROUP - 1)) >> GROUP_BITS
    cell_smem[entry + 1] = cells
    until_smem[entry + 1] = 1 << 30

    def turn(block, unused):
        rows = pl.ds(pl.multiple_of(block * lanes, lanes), lanes)
        chunks = pl.ds(pl.multiple_of(block * 16, 16), 16)
        turned_ref[rows, :] = list_ref[chunks].reshape(lanes, lanes).T
        return unused

    lax.fori_loop(0, (end + 16 * lanes - 1) >> (lane_bits + 4), turn, 0)


def pair_kernel(cell_smem, until_smem, groups_smem, place_smem, table_ref, turned_ref, force_ref):
    lanes = table_ref.shape[2]
    lane_bits = lanes.bit_length() - 1
    groups = groups_smem[0]
    force_ref[...] = jnp.zeros(force_ref.shape, jnp.float32)

    def pairs(step, entry):
        totals = []
        for unit in range(UNITS):
            group = step * UNITS + unit
            entry = entry + jnp.where(group >= until_smem[entry], 1, 0)
            cell = cell_smem[entry]
            own = place_smem[cell]
            begin = group * GROUP
            chunk = begin >> lane_bits
            at = (chunk >> 4) * lanes + (begin & (lanes - 1))
            block = turned_ref[pl.ds(pl.multiple_of(at, GROUP), GROUP), :]
            block = pltpu.roll(block, (lanes - (chunk & 15) * 8) & (lanes - 1), 1)
            other = [block[:, comp : comp + 1] for comp in range(8)]
            mine = [table_ref[own, pl.ds(comp, 1), :] for comp in range(8)]
            apart = [other[axis] - mine[axis] for axis in range(3)]
            square = apart[0] * apart[0] + apart[1] * apart[1] + apart[2] * apart[2] + epsilon_sq
            inverse = lax.rsqrt(square)
            reach = other[6] + mine[6]
            overlap = jnp.maximum(reach - square * inverse, 0.0)
            overlap = jnp.where(other[7] != mine[7], overlap, 0.0)
            closing = (
                (other[3] - mine[3]) * apart[0]
                + (other[4] - mine[4]) * apart[1]
                + (other[5] - mine[5]) * apart[2]
            )
            scaled = overlap * (other[6] * mine[6])
            root = scaled * lax.rsqrt(jnp.maximum(scaled * reach, 1e-30))
            factor = (
                root * inverse * (stiffness / damping * overlap - closing * inverse)
            )
            totals.append(
                (
                    cell,
                    [
                        jnp.sum((factor * apart[axis]).reshape(GROUP // 8, 8, lanes), axis=0)
                        for axis in range(3)
                    ],
                )
            )
        for cell, parts in totals:
            for axis in range(3):
                force_ref[axis, cell] += parts[axis]
        return entry

    lax.fori_loop(0, lax.div(groups + (UNITS - 1), UNITS), pairs, 0)


def sums_kernel(force_ref, arms_ref, frag_ref, out_ref, loads_ref):
    cells, lanes = frag_ref.shape
    held = out_ref.shape[1]
    label = lax.broadcasted_iota(jnp.int32, (held, lanes), 0)

    def gather_sums(block, total):
        rows = pl.ds(pl.multiple_of(block * 8, 8), 8)
        force = [-damping * jnp.sum(force_ref[axis, rows], axis=1) for axis in range(3)]
        lever = [arms_ref[axis, rows, :] for axis in range(3)]
        torque = [
            lever[1] * force[2] - lever[2] * force[1],
            lever[2] * force[0] - lever[0] * force[2],
            lever[0] * force[1] - lever[1] * force[0],
        ]
        loads = force + torque + [jnp.zeros_like(force[0])] * 2
        for comp in range(8):
            loads_ref[:, comp, :] = loads[comp]
        frags = frag_ref[rows, :]
        for unit in range(8):
            hits = (frags[unit : unit + 1, :] == label).astype(jnp.float32).astype(jnp.bfloat16)
            total = total + dot_lanes(split_rows(loads_ref[unit]), hits)
        return total

    total = lax.fori_loop(0, cells // 8, gather_sums, jnp.zeros((24, held), jnp.float32))
    out_ref[...] = joined_rows(total)


def add_over(bricks, dots, rows, lanes):
    def step(block, total):
        parts = [dots(block * 8 + unit) for unit in range(8)]
        while len(parts) > 1:
            parts = [first + second for first, second in zip(parts[::2], parts[1::2])]
        return total + parts[0]

    return joined_rows(lax.fori_loop(0, bricks // 8, step, jnp.zeros((rows, lanes), jnp.float32)))


def base_kernel(owned, target_ref, fixed_ref, base_ref):
    bricks, _, held = fixed_ref.shape
    lanes = target_ref.shape[0]
    targets = jnp.broadcast_to(target_ref[...], (lanes, held))
    lane = lax.broadcasted_iota(jnp.int32, (1, held), 1)

    def dots(brick):
        number = jnp.where(lane < owned, brick * owned + lane, -1).astype(jnp.float32)
        hits = (targets == number).astype(jnp.float32).astype(jnp.bfloat16)
        return dot_lanes(split_rows(fixed_ref[brick, 0:8, :]), hits)

    base_ref[...] = add_over(bricks, dots, 24, lanes)


def move_kernel(
    target_ref, fixed_ref, base_ref, sums_ref, state_ref, arms_ref, frag_ref, spheres_ref, clumps_ref
):
    bricks, _, held = sums_ref.shape
    lanes = frag_ref.shape[1]
    cells = frag_ref.shape[0]
    targets = jnp.broadcast_to(target_ref[...], (lanes, held))

    def dots(brick):
        hits = (targets == fixed_ref[brick, 8:9, :]).astype(jnp.float32).astype(jnp.bfloat16)
        return dot_lanes(split_rows(sums_ref[brick]), hits)

    sums = add_over(bricks, dots, 24, lanes)
    base = base_ref[...]
    rows = []
    for axis in range(3):
        pull = gravity if axis == 2 else 0.0
        rows.append(
            base[axis : axis + 1]
            + time_step * (sums[axis : axis + 1] * base[6:7] - pull)
        )
    for axis in range(3, 6):
        rows.append(base[axis : axis + 1] + time_step * sums[axis : axis + 1] * base[7:8])
    for comp in range(6):
        clumps_ref[comp : comp + 1, :] = rows[comp]
    tall = 32
    wide = [jnp.broadcast_to(value, (tall, lanes)) for value in rows]

    def cross(first, second):
        return [
            first[1] * second[2] - first[2] * second[1],
            first[2] * second[0] - first[0] * second[2],
            first[0] * second[1] - first[1] * second[0],
        ]

    def move(block, unused):
        at = pl.ds(pl.multiple_of(block * tall, tall), tall)
        index = frag_ref[at, :] + (lanes - held)
        motion = [lanes_of(value, index) for value in wide]
        velocity, spin = motion[0:3], motion[3:6]
        arm = [arms_ref[axis, at, :] for axis in range(3)]
        half = [0.5 * time_step * value for value in spin]
        turned = cross(half, arm)
        twice = cross(half, turned)
        scale = 2.0 / (1.0 + half[0] * half[0] + half[1] * half[1] + half[2] * half[2])
        change = [scale * (turned[axis] + twice[axis]) for axis in range(3)]
        new_arm = [arm[axis] + change[axis] for axis in range(3)]
        swing = cross(spin, new_arm)
        for axis in range(3):
            spheres_ref[axis, at, :] = (
                state_ref[axis, at, :] + time_step * velocity[axis] + (new_arm[axis] - arm[axis])
            )
            spheres_ref[3 + axis, at, :] = velocity[axis] + swing[axis]
        return unused

    lax.fori_loop(0, cells // tall, move, 0)


def local(
    state, arms, sphere_frag, frag_owner, frag_clump, tiles, clump_motion, inv_mass, inv_moment
):
    cells_x, cells_y, cells_z = (state.shape[1], state.shape[2], state.shape[3])
    lanes = state.shape[4]
    cells = cells_x * cells_y * cells_z
    owned = inv_mass.shape[0]
    held = frag_clump.shape[0]
    names = ("gx", "gy", "gz")
    vmem = pl.BlockSpec(memory_space=pltpu.VMEM)
    smem = pl.BlockSpec(memory_space=pltpu.SMEM)
    params = pltpu.CompilerParams(vmem_limit_bytes=VMEM)

    frag_key = (frag_owner[:, 0] * owned + frag_clump).astype(jnp.float32)
    flat_state = state.reshape(7, cells, lanes)
    flat_arms = arms.reshape(3, cells, lanes)
    flat_frag = sphere_frag.reshape(cells, lanes)

    fixed = jnp.concatenate(
        [
            jnp.pad(
                jnp.concatenate([clump_motion, inv_mass[None], inv_moment[None]], axis=0),
                ((0, 0), (0, held - owned)),
            ),
            frag_key[None],
            jnp.zeros((7, held), jnp.float32),
        ],
        axis=0,
    )
    fixed = everywhere(fixed, names)

    table = pl.pallas_call(
        pack_kernel,
        out_shape=jax.ShapeDtypeStruct((cells, 8, lanes), jnp.float32),
        in_specs=[vmem] * 3,
        out_specs=vmem,
        compiler_params=params,
    )(flat_state, flat_frag, jnp.pad(frag_key, (0, lanes - held))[None])
    padded = with_halo(
        table.reshape(cells_x, cells_y, cells_z, 8, lanes), (("gx", 0), ("gy", 1), ("gz", 2)), 1
    )
    span_y, span_z = (cells_y + 2, cells_z + 2)
    span = (cells_x + 2) * span_y * span_z
    padded = padded.reshape(span, 8, lanes)

    codes = jnp.sort(tiles[0])
    total = codes.shape[0]
    own = codes // 27
    offset = codes % 27
    steps = (offset // 9 - 1, offset // 3 % 3 - 1, offset % 3 - 1)

    def pad_place(cell):
        x = cell // (cells_y * cells_z) + 1
        y = cell // cells_z % cells_y + 1
        z = cell % cells_z + 1
        return (x * span_y + y) * span_z + z

    near = pad_place(own) + (steps[0] * span_y + steps[1]) * span_z + steps[2]
    need = sum(
        jnp.where(steps[axis] == 1, 1, jnp.where(steps[axis] == -1, 2, 0)) << (2 * axis)
        for axis in range(3)
    )
    first = jnp.concatenate([jnp.ones((1,), jnp.int32), (own[1:] != own[:-1]).astype(jnp.int32)])
    place = pad_place(jnp.arange(cells + 1, dtype=jnp.int32) % cells)
    kinds = jnp.arange(27, dtype=jnp.int32)
    moves = jnp.stack([kinds // 9 - 1, kinds // 3 % 3 - 1, kinds % 3 - 1], axis=1)
    shift = jnp.pad(moves.astype(jnp.float32), ((0, 0), (0, 5)))
    shift = jnp.broadcast_to(shift[:, :, None], (27, 8, lanes))

    slots, count = pl.pallas_call(
        list_kernel,
        out_shape=(
            jax.ShapeDtypeStruct((total, lanes), jnp.int32),
            jax.ShapeDtypeStruct((8, total), jnp.int32),
        ),
        in_specs=[vmem] * 3,
        out_specs=(vmem, vmem),
        scratch_shapes=[pltpu.VMEM((-(-span // lanes) * lanes, lanes), jnp.float32)],
        compiler_params=params,
    )(near[None], need[None], padded.reshape(span * 8, lanes))

    chunks = total + cells * GROUP // lanes + 2
    chunks = -(-chunks // 16) * 16
    turned, cell_of, until, groups = pl.pallas_call(
        fill_kernel,
        out_shape=(
            jax.ShapeDtypeStruct((chunks * 8, lanes), jnp.float32),
            jax.ShapeDtypeStruct((cells + 8,), jnp.int32),
            jax.ShapeDtypeStruct((cells + 8,), jnp.int32),
            jax.ShapeDtypeStruct((1,), jnp.int32),
        ),
        in_specs=[smem] * 5 + [vmem] * 3,
        out_specs=(vmem, smem, smem, smem),
        scratch_shapes=[pltpu.VMEM((chunks, 8, lanes), jnp.float32)],
        compiler_params=params,
    )(near, offset, own, first, count[0:1], padded, slots, shift)
    force = pl.pallas_call(
        pair_kernel,
        out_shape=jax.ShapeDtypeStruct((3, cells + 8, 8, lanes), jnp.float32),
        in_specs=[smem] * 4 + [vmem] * 2,
        out_specs=vmem,
        compiler_params=params,
    )(cell_of, until, groups, place, padded, turned)
    sums = pl.pallas_call(
        sums_kernel,
        out_shape=jax.ShapeDtypeStruct((8, held), jnp.float32),
        in_specs=[vmem] * 3,
        out_specs=vmem,
        scratch_shapes=[pltpu.VMEM((8, 8, lanes), jnp.float32)],
        compiler_params=params,
    )(force, flat_arms, flat_frag)

    sums = everywhere(sums, names)

    brick = lax.axis_index(names)
    mine = jnp.where(
        jnp.arange(lanes - held) < owned, brick * owned + jnp.arange(lanes - held), -2
    ).astype(jnp.float32)
    target = jnp.concatenate([mine, frag_key])[:, None]
    base = pl.pallas_call(
        functools.partial(base_kernel, owned),
        out_shape=jax.ShapeDtypeStruct((8, lanes), jnp.float32),
        in_specs=[vmem] * 2,
        out_specs=vmem,
        compiler_params=params,
    )(target, fixed)
    spheres, clumps = pl.pallas_call(
        move_kernel,
        out_shape=(
            jax.ShapeDtypeStruct((6, cells, lanes), jnp.float32),
            jax.ShapeDtypeStruct((6, lanes), jnp.float32),
        ),
        in_specs=[vmem] * 7,
        out_specs=(vmem, vmem),
        compiler_params=params,
    )(target, fixed, base, sums, flat_state, flat_arms, flat_frag)
    return (spheres.reshape((6,) + state.shape[1:]), clumps[:, :owned])


def solution(mesh):
    return jax.shard_map(
        local,
        mesh=mesh,
        in_specs=(
            P(None, "gx", "gy", "gz", None),
            P(None, "gx", "gy", "gz", None),
            P("gx", "gy", "gz", None),
            P(("gx", "gy", "gz"), None),
            P(("gx", "gy", "gz")),
            P(("gx", "gy", "gz"), None),
            P(None, ("gx", "gy", "gz")),
            P(("gx", "gy", "gz")),
            P(("gx", "gy", "gz")),
        ),
        out_specs=(P(None, "gx", "gy", "gz", None), P(None, ("gx", "gy", "gz"))),
        check_vma=False,
    )
```

```python
import functools

import jax
import jax.numpy as jnp
from jax import lax
from jax.experimental import pallas as pl
from jax.experimental.pallas import tpu as pltpu
from jax.sharding import PartitionSpec as P

stiffness = 100.0
damping = 2.0
time_step = 0.01
gravity = 9.81
epsilon_sq = 1e-08
radius_top = 0.14

GROUP = 32
FILL = 16
SPREAD = 2
VMEM = 56 * 1024 * 1024


def lanes_of(values, index):
    return jnp.take_along_axis(values, index, axis=1, mode="promise_in_bounds")


def split_rows(values):
    high = values.astype(jnp.bfloat16).astype(jnp.float32)
    rest = values - high
    middle = rest.astype(jnp.bfloat16).astype(jnp.float32)
    low = rest - middle
    return jnp.concatenate([high, middle, low], axis=0).astype(jnp.bfloat16)


def joined_rows(stacked):
    rows = stacked.shape[0] // 3
    return stacked[0:rows] + stacked[rows : 2 * rows] + stacked[2 * rows :]


def dot_lanes(first, second):
    return lax.dot_general(
        first, second, (((1,), (1,)), ((), ())), preferred_element_type=jnp.float32
    )


def everywhere(x, names):
    devices = lax.axis_size(names)
    copies = jnp.broadcast_to(x[None], (devices,) + x.shape)
    return lax.all_to_all(copies, names, split_axis=0, concat_axis=0, tiled=True)


def with_halo(x, sides, width):
    for axis, dim in sides:
        devices, length = (lax.axis_size(axis), x.shape[dim])
        up = [(i, (i + 1) % devices) for i in range(devices)]
        down = [(j, i) for i, j in up]
        last = lax.slice_in_dim(x, length - width, length, axis=dim)
        initial = lax.slice_in_dim(x, 0, width, axis=dim)
        before = lax.ppermute(last, axis, up)
        after = lax.ppermute(initial, axis, down)
        x = jnp.concatenate([before, x, after], axis=dim)
    return x


def pack_kernel(state_ref, frag_ref, key_ref, out_ref):
    cells = frag_ref.shape[0]
    for comp in range(7):
        out_ref[:, comp, :] = state_ref[comp]
    keys = jnp.broadcast_to(key_ref[0:1, :], (8, key_ref.shape[1]))
    for block in range(cells // 8):
        rows = pl.ds(block * 8, 8)
        out_ref[rows, 7, :] = lanes_of(keys, frag_ref[rows, :])


def list_kernel(
    near_ref, need_ref, own_ref, table_ref, slots_ref, where_ref, cell_ref, class_ref, member_ref, count_ref
):
    tiles, lanes = slots_ref.shape
    span = table_ref.shape[0] // 8
    padded = class_ref.shape[0]
    cells = count_ref.shape[0]
    wide = 256

    def plane(comp):
        return table_ref[pl.ds(comp, span, stride=8), :]

    def flag(value):
        return value.astype(jnp.float32).astype(jnp.bfloat16)

    def dot(first, second):
        return jnp.dot(first, second, preferred_element_type=jnp.float32)

    def ramp(shape, axis):
        return lax.broadcasted_iota(jnp.int32, shape, axis)

    radius = plane(6) + (radius_top + 1e-5)
    classes = jnp.zeros((span, lanes), jnp.float32)
    for axis in range(3):
        place = plane(axis)
        classes = classes + jnp.where(place < radius, 1.0 * (1 << (2 * axis)), 0.0)
        classes = classes + jnp.where(place > 1.0 - radius, 1.0 * (2 << (2 * axis)), 0.0)
    class_ref[pl.ds(span // 8 * 8, padded - span // 8 * 8), :] = jnp.zeros(
        (padded - span // 8 * 8, lanes), jnp.float32
    )
    class_ref[pl.ds(0, span), :] = classes
    codes = jnp.concatenate(
        [class_ref[pl.ds(at, lanes), :].T for at in range(0, padded, lanes)], axis=1
    ).astype(jnp.bfloat16)
    ones = jnp.ones((lanes, lanes), jnp.bfloat16)
    count_ref[...] = jnp.zeros(count_ref.shape, jnp.float32)

    def choose(block, unused):
        at = pl.ds(pl.multiple_of(block * wide, wide), wide)
        hits = flag(ramp((padded, wide), 0) == near_ref[:, at])
        found = dot(codes, hits).astype(jnp.int32)
        need = need_ref[:, at]
        member = ((found & need) == need).astype(jnp.float32)
        member_ref[:, at] = member
        count = dot(ones, member.astype(jnp.bfloat16))
        mine = flag(ramp((cells, wide), 0) == own_ref[:, at])
        count_ref[...] += dot_lanes(mine, count.astype(jnp.bfloat16))
        return unused

    lax.fori_loop(0, tiles // wide, choose, 0)

    held = count_ref[...]
    high = jnp.floor(held * (1.0 / lanes))
    low = held - lanes * high
    taken = jnp.floor((held + (GROUP - 1)) * (1.0 / GROUP))
    upto = flag(ramp((cells, cells), 1) <= ramp((cells, cells), 0))
    ends = dot(upto, taken.astype(jnp.bfloat16))
    cell_ones = jnp.ones((8, cells), jnp.bfloat16)
    group_blocks = cell_ref.shape[1] // lanes - 1

    def name_groups(block, unused):
        group = (ramp((cells, lanes), 1) + block * lanes).astype(jnp.float32)
        over = dot(cell_ones, flag(ends <= group))
        at = pl.ds(pl.multiple_of(block * lanes, lanes), lanes)
        cell_ref[:, at] = over[0:1].astype(jnp.int32)
        return unused

    lax.fori_loop(0, group_blocks, name_groups, 0)
    cell_ref[:, pl.ds(group_blocks * lanes, lanes)] = ends[cells - 1 : cells].astype(jnp.int32)
    before_cell = jnp.concatenate(
        [value.T[0:8] for value in (taken, high, low)], axis=0
    ).astype(jnp.bfloat16)

    earlier = flag(ramp((lanes, lanes), 1) < ramp((lanes, lanes), 0))
    earlier_tile = flag(ramp((wide, wide), 0) < ramp((wide, wide), 1))

    def place(block, done):
        at = pl.ds(pl.multiple_of(block * wide, wide), wide)
        member = member_ref[:, at]
        flags = member.astype(jnp.bfloat16)
        count = dot(ones, flags)
        lower = flag(ramp((cells, wide), 0) < own_ref[:, at])
        before = dot(before_cell, lower)
        so_far = dot(count[0:8].astype(jnp.bfloat16), earlier_tile) + done
        start = (GROUP * before[0:8] + so_far - (lanes * before[8:16] + before[16:24]))
        start = start.astype(jnp.int32)[0:1]
        where_ref[:, at] = start * 256 + count[0:1].astype(jnp.int32)
        rank = dot(earlier, flags)
        slot = ramp((lanes, wide), 0)
        word = jnp.where(member > 0.0, slot + lanes * (slot - rank.astype(jnp.int32)), 0)
        bit = 1
        while bit < lanes:
            keep = jnp.where((word & (bit * lanes)) != 0, 0, word)
            gone = word ^ keep
            word = keep | jnp.concatenate([gone[bit:], gone[:bit]], axis=0)
            bit *= 2
        word = word & (lanes - 1)
        turn = jnp.broadcast_to(start, (lanes, wide))
        bit = 1
        while bit < lanes:
            moved = jnp.concatenate([word[lanes - bit :], word[: lanes - bit]], axis=0)
            word = jnp.where((turn & bit) != 0, moved, word)
            bit *= 2
        for part in range(wide // lanes):
            rows = pl.ds(pl.multiple_of(block * wide + part * lanes, lanes), lanes)
            slots_ref[rows, :] = word[:, part * lanes : (part + 1) * lanes].T
        total = jnp.sum(count[0:8], axis=1, keepdims=True)
        return done + total

    lax.fori_loop(0, tiles // wide, place, jnp.zeros((8, 1), jnp.float32))


def fill_kernel(where_smem, near_smem, table_ref, slots_ref, shift_ref, list_ref):
    tiles, lanes = slots_ref.shape
    lane_bits = lanes.bit_length() - 1
    lane = lax.broadcasted_iota(jnp.int32, (8, lanes), 1)
    row = lax.broadcasted_iota(jnp.int32, (8, lanes), 0)
    absent = jnp.where(row == 6, -10.0, 0.0)

    def fill(block, carry):
        last_chunk, last_new, last_held = carry
        units = range(FILL)
        where = [where_smem[0, block * FILL + unit] for unit in units]
        near = [near_smem[block * FILL + unit] for unit in units]
        found = []
        for unit in units:
            slots = slots_ref[pl.ds(block * FILL + unit, 8, stride=0), :]
            cell = table_ref[near[unit] >> 5]
            found.append(lanes_of(cell, slots) + shift_ref[near[unit] & 31])
        for unit in units:
            amount = where[unit] & 255
            chunk = where[unit] >> (8 + lane_bits)
            offset = (where[unit] >> 8) & (lanes - 1)
            new = jnp.where(((lane - offset) & (lanes - 1)) < amount, found[unit], absent)
            held_row = jnp.where(chunk != last_chunk, last_new, last_held)
            held_row = jnp.where(lane >= offset, new, held_row)
            new = jnp.where(lane >= offset, absent, new)
            list_ref[chunk] = held_row
            list_ref[chunk + 1] = new
            last_chunk, last_new, last_held = chunk, new, held_row
        return last_chunk, last_new, last_held

    lax.fori_loop(0, tiles // FILL, fill, (jnp.int32(0), absent, absent))


def pair_kernel(cell_smem, place_smem, table_ref, list_ref, force_ref, even_ref, odd_ref):
    lanes = table_ref.shape[1]
    rows = even_ref.shape[0]
    chunks = rows // lanes
    units = rows // GROUP
    groups = cell_smem[0, cell_smem.shape[1] - lanes]
    force_ref[...] = jnp.zeros(force_ref.shape, jnp.float32)
    part = lax.broadcasted_iota(jnp.int32, (32, 8 * lanes), 0)
    comp = lax.broadcasted_iota(jnp.int32, (32, 8 * lanes), 1) // lanes
    weights = jnp.where((part < 24) & (part % 8 == comp), 1.0, 0.0).astype(jnp.bfloat16)

    def spread(step, out_ref):
        turned = []
        for piece in range(chunks):
            values = list_ref[step * chunks + piece]
            high = values.astype(jnp.bfloat16).astype(jnp.float32)
            rest = values - high
            middle = rest.astype(jnp.bfloat16).astype(jnp.float32)
            parts = jnp.concatenate([high, middle, rest - middle, jnp.zeros_like(values)], axis=0)
            turned.append(parts.T.astype(jnp.bfloat16))
        turned = jnp.concatenate(turned, axis=0)
        out_ref[...] = jnp.dot(turned, weights, preferred_element_type=jnp.float32)

    def pairs(step, wide_ref):
        totals = []
        for unit in range(units):
            cell = cell_smem[0, step * units + unit]
            own = place_smem[cell] * 8
            other = [
                wide_ref[pl.ds(unit * GROUP, GROUP), pl.ds(value * lanes, lanes)].reshape(
                    GROUP // 8, 8, lanes
                )
                for value in range(8)
            ]
            mine = [table_ref[pl.ds(own + value, 8, stride=0), :][None] for value in range(8)]
            apart = [other[axis] - mine[axis] for axis in range(3)]
            square = apart[0] * apart[0] + apart[1] * apart[1] + apart[2] * apart[2] + epsilon_sq
            inverse = lax.rsqrt(square)
            reach = other[6] + mine[6]
            overlap = jnp.maximum(reach - square * inverse, 0.0)
            overlap = jnp.where(other[7] != mine[7], overlap, 0.0)
            closing = (
                (other[3] - mine[3]) * apart[0]
                + (other[4] - mine[4]) * apart[1]
                + (other[5] - mine[5]) * apart[2]
            )
            scaled = overlap * (other[6] * mine[6])
            root = scaled * lax.rsqrt(jnp.maximum(scaled * reach, 1e-30))
            factor = root * inverse * (stiffness / damping * overlap - closing * inverse)
            totals.append((cell, [jnp.sum(factor * apart[axis], axis=0) for axis in range(3)]))
        for cell, parts in totals:
            for axis in range(3):
                force_ref[axis, cell] += parts[axis]

    spread(0, even_ref)

    def both(step, unused):
        spread(2 * step + 1, odd_ref)
        pairs(2 * step, even_ref)
        spread(2 * step + 2, even_ref)
        pairs(2 * step + 1, odd_ref)
        return unused

    lax.fori_loop(0, lax.div(groups + (2 * units - 1), 2 * units), both, 0)


def sums_kernel(force_ref, arms_ref, frag_ref, out_ref, loads_ref):
    cells, lanes = frag_ref.shape
    held = out_ref.shape[1]
    tall = loads_ref.shape[0]
    label = lax.broadcasted_iota(jnp.int32, (held, lanes), 0)

    def gather_sums(block, total):
        rows = pl.ds(pl.multiple_of(block * tall, tall), tall)
        force = [-damping * jnp.sum(force_ref[axis, rows], axis=1) for axis in range(3)]
        lever = [arms_ref[axis, rows, :] for axis in range(3)]
        torque = [
            lever[1] * force[2] - lever[2] * force[1],
            lever[2] * force[0] - lever[0] * force[2],
            lever[0] * force[1] - lever[1] * force[0],
        ]
        loads = force + torque + [jnp.zeros_like(force[0])] * 2
        for comp in range(8):
            loads_ref[:, comp, :] = loads[comp]
        frags = frag_ref[rows, :]
        hits = [
            (frags[unit : unit + 1, :] == label).astype(jnp.float32).astype(jnp.bfloat16)
            for unit in range(tall)
        ]
        values = [split_rows(loads_ref[unit]) for unit in range(tall)]
        return total + dot_lanes(jnp.concatenate(values, axis=1), jnp.concatenate(hits, axis=1))

    total = lax.fori_loop(0, cells // tall, gather_sums, jnp.zeros((24, held), jnp.float32))
    out_ref[...] = joined_rows(total)


def add_over(bricks, dots, rows, lanes):
    def step(block, total):
        parts = [dots(block * 8 + unit) for unit in range(8)]
        while len(parts) > 1:
            parts = [first + second for first, second in zip(parts[::2], parts[1::2])]
        return total + parts[0]

    return joined_rows(lax.fori_loop(0, bricks // 8, step, jnp.zeros((rows, lanes), jnp.float32)))


def base_kernel(owned, target_ref, fixed_ref, base_ref):
    bricks, _, held = fixed_ref.shape
    lanes = target_ref.shape[0]
    targets = jnp.broadcast_to(target_ref[...], (lanes, held))
    lane = lax.broadcasted_iota(jnp.int32, (1, held), 1)

    def dots(brick):
        number = jnp.where(lane < owned, brick * owned + lane, -1).astype(jnp.float32)
        hits = (targets == number).astype(jnp.float32).astype(jnp.bfloat16)
        return dot_lanes(split_rows(fixed_ref[brick, 0:8, :]), hits)

    base_ref[...] = add_over(bricks, dots, 24, lanes)


def move_kernel(
    target_ref, fixed_ref, base_ref, sums_ref, state_ref, arms_ref, frag_ref, spheres_ref, clumps_ref
):
    bricks, _, held = sums_ref.shape
    lanes = frag_ref.shape[1]
    cells = frag_ref.shape[0]
    targets = jnp.broadcast_to(target_ref[...], (lanes, held))

    def dots(brick):
        hits = (targets == fixed_ref[brick, 8:9, :]).astype(jnp.float32).astype(jnp.bfloat16)
        return dot_lanes(split_rows(sums_ref[brick]), hits)

    sums = add_over(bricks, dots, 24, lanes)
    base = base_ref[...]
    rows = []
    for axis in range(3):
        pull = gravity if axis == 2 else 0.0
        rows.append(
            base[axis : axis + 1]
            + time_step * (sums[axis : axis + 1] * base[6:7] - pull)
        )
    for axis in range(3, 6):
        rows.append(base[axis : axis + 1] + time_step * sums[axis : axis + 1] * base[7:8])
    for comp in range(6):
        clumps_ref[comp : comp + 1, :] = rows[comp]
    tall = 32
    wide = [jnp.broadcast_to(value, (tall, lanes)) for value in rows]

    def cross(first, second):
        return [
            first[1] * second[2] - first[2] * second[1],
            first[2] * second[0] - first[0] * second[2],
            first[0] * second[1] - first[1] * second[0],
        ]

    def move(block, unused):
        at = pl.ds(pl.multiple_of(block * tall, tall), tall)
        index = frag_ref[at, :] + (lanes - held)
        motion = [lanes_of(value, index) for value in wide]
        velocity, spin = motion[0:3], motion[3:6]
        arm = [arms_ref[axis, at, :] for axis in range(3)]
        half = [0.5 * time_step * value for value in spin]
        turned = cross(half, arm)
        twice = cross(half, turned)
        scale = 2.0 / (1.0 + half[0] * half[0] + half[1] * half[1] + half[2] * half[2])
        change = [scale * (turned[axis] + twice[axis]) for axis in range(3)]
        new_arm = [arm[axis] + change[axis] for axis in range(3)]
        swing = cross(spin, new_arm)
        for axis in range(3):
            spheres_ref[axis, at, :] = (
                state_ref[axis, at, :] + time_step * velocity[axis] + (new_arm[axis] - arm[axis])
            )
            spheres_ref[3 + axis, at, :] = velocity[axis] + swing[axis]
        return unused

    lax.fori_loop(0, cells // tall, move, 0)


def local(
    state, arms, sphere_frag, frag_owner, frag_clump, tiles, clump_motion, inv_mass, inv_moment
):
    cells_x, cells_y, cells_z = (state.shape[1], state.shape[2], state.shape[3])
    lanes = state.shape[4]
    cells = cells_x * cells_y * cells_z
    owned = inv_mass.shape[0]
    held = frag_clump.shape[0]
    names = ("gx", "gy", "gz")
    vmem = pl.BlockSpec(memory_space=pltpu.VMEM)
    smem = pl.BlockSpec(memory_space=pltpu.SMEM)
    params = pltpu.CompilerParams(vmem_limit_bytes=VMEM)

    frag_key = (frag_owner[:, 0] * owned + frag_clump).astype(jnp.float32)
    flat_state = state.reshape(7, cells, lanes)
    flat_arms = arms.reshape(3, cells, lanes)
    flat_frag = sphere_frag.reshape(cells, lanes)

    fixed = jnp.concatenate(
        [
            jnp.pad(
                jnp.concatenate([clump_motion, inv_mass[None], inv_moment[None]], axis=0),
                ((0, 0), (0, held - owned)),
            ),
            frag_key[None],
            jnp.zeros((7, held), jnp.float32),
        ],
        axis=0,
    )
    fixed = everywhere(fixed, names)

    table = pl.pallas_call(
        pack_kernel,
        out_shape=jax.ShapeDtypeStruct((cells, 8, lanes), jnp.float32),
        in_specs=[vmem] * 3,
        out_specs=vmem,
        compiler_params=params,
    )(flat_state, flat_frag, jnp.pad(frag_key, (0, lanes - held))[None])
    padded = with_halo(
        table.reshape(cells_x, cells_y, cells_z, 8, lanes), (("gx", 0), ("gy", 1), ("gz", 2)), 1
    )
    span_y, span_z = (cells_y + 2, cells_z + 2)
    span = (cells_x + 2) * span_y * span_z
    padded = padded.reshape(span, 8, lanes)
    flat = padded.reshape(span * 8, lanes)

    codes = jnp.sort(tiles[0])
    total = codes.shape[0]
    own = codes // 27
    offset = codes % 27
    steps = (offset // 9 - 1, offset // 3 % 3 - 1, offset % 3 - 1)

    def pad_place(cell):
        x = cell // (cells_y * cells_z) + 1
        y = cell // cells_z % cells_y + 1
        z = cell % cells_z + 1
        return (x * span_y + y) * span_z + z

    near = pad_place(own) + (steps[0] * span_y + steps[1]) * span_z + steps[2]
    need = sum(
        jnp.where(steps[axis] == 1, 1, jnp.where(steps[axis] == -1, 2, 0)) << (2 * axis)
        for axis in range(3)
    )
    place = pad_place(jnp.arange(cells + 1, dtype=jnp.int32) % cells)
    kinds = jnp.arange(27, dtype=jnp.int32)
    moves = jnp.stack([kinds // 9 - 1, kinds // 3 % 3 - 1, kinds % 3 - 1], axis=1)
    shift = jnp.pad(moves.astype(jnp.float32), ((0, 0), (0, 5)))
    shift = jnp.broadcast_to(shift[:, :, None], (27, 8, lanes))

    chunks = -(-(total + cells * GROUP // lanes) // 16) * 16 + 8
    group_top = chunks * (lanes // GROUP)
    slots, where, cell_of = pl.pallas_call(
        list_kernel,
        out_shape=(
            jax.ShapeDtypeStruct((total, lanes), jnp.int32),
            jax.ShapeDtypeStruct((1, total), jnp.int32),
            jax.ShapeDtypeStruct((1, -(-group_top // lanes) * lanes + lanes), jnp.int32),
        ),
        in_specs=[vmem] * 4,
        out_specs=(vmem, vmem, vmem),
        scratch_shapes=[
            pltpu.VMEM((-(-span // lanes) * lanes, lanes), jnp.float32),
            pltpu.VMEM((lanes, total), jnp.float32),
            pltpu.VMEM((cells, lanes), jnp.float32),
        ],
        compiler_params=params,
    )(near[None], need[None], own[None], flat)
    lists = pl.pallas_call(
        fill_kernel,
        out_shape=jax.ShapeDtypeStruct((chunks, 8, lanes), jnp.float32),
        in_specs=[smem] * 2 + [vmem] * 3,
        out_specs=vmem,
        compiler_params=params,
    )(where, near * 32 + offset, padded, slots, shift)
    force = pl.pallas_call(
        pair_kernel,
        out_shape=jax.ShapeDtypeStruct((3, cells + 8, 8, lanes), jnp.float32),
        in_specs=[smem] * 2 + [vmem] * 2,
        out_specs=vmem,
        scratch_shapes=[pltpu.VMEM((SPREAD * lanes, 8 * lanes), jnp.float32)] * 2,
        compiler_params=params,
    )(cell_of, place, flat, lists)
    sums = pl.pallas_call(
        sums_kernel,
        out_shape=jax.ShapeDtypeStruct((8, held), jnp.float32),
        in_specs=[vmem] * 3,
        out_specs=vmem,
        scratch_shapes=[pltpu.VMEM((16, 8, lanes), jnp.float32)],
        compiler_params=params,
    )(force, flat_arms, flat_frag)

    sums = everywhere(sums, names)

    brick = lax.axis_index(names)
    mine = jnp.where(
        jnp.arange(lanes - held) < owned, brick * owned + jnp.arange(lanes - held), -2
    ).astype(jnp.float32)
    target = jnp.concatenate([mine, frag_key])[:, None]
    base = pl.pallas_call(
        functools.partial(base_kernel, owned),
        out_shape=jax.ShapeDtypeStruct((8, lanes), jnp.float32),
        in_specs=[vmem] * 2,
        out_specs=vmem,
        compiler_params=params,
    )(target, fixed)
    spheres, clumps = pl.pallas_call(
        move_kernel,
        out_shape=(
            jax.ShapeDtypeStruct((6, cells, lanes), jnp.float32),
            jax.ShapeDtypeStruct((6, lanes), jnp.float32),
        ),
        in_specs=[vmem] * 7,
        out_specs=(vmem, vmem),
        compiler_params=params,
    )(target, fixed, base, sums, flat_state, flat_arms, flat_frag)
    return (spheres.reshape((6,) + state.shape[1:]), clumps[:, :owned])


def solution(mesh):
    return jax.shard_map(
        local,
        mesh=mesh,
        in_specs=(
            P(None, "gx", "gy", "gz", None),
            P(None, "gx", "gy", "gz", None),
            P("gx", "gy", "gz", None),
            P(("gx", "gy", "gz"), None),
            P(("gx", "gy", "gz")),
            P(("gx", "gy", "gz"), None),
            P(None, ("gx", "gy", "gz")),
            P(("gx", "gy", "gz")),
            P(("gx", "gy", "gz")),
        ),
        out_specs=(P(None, "gx", "gy", "gz", None), P(None, ("gx", "gy", "gz"))),
        check_vma=False,
    )
```

```python
import functools

import jax
import jax.numpy as jnp
from jax import lax
from jax.experimental import pallas as pl
from jax.experimental.pallas import tpu as pltpu
from jax.sharding import PartitionSpec as P

stiffness = 100.0
damping = 2.0
time_step = 0.01
gravity = 9.81
epsilon_sq = 1e-08
radius_top = 0.14

GROUP = 32
FILL = 16
SPREAD = 2
VMEM = 56 * 1024 * 1024


def lanes_of(values, index):
    return jnp.take_along_axis(values, index, axis=1, mode="promise_in_bounds")


def split_rows(values):
    high = values.astype(jnp.bfloat16).astype(jnp.float32)
    rest = values - high
    middle = rest.astype(jnp.bfloat16).astype(jnp.float32)
    low = rest - middle
    return jnp.concatenate([high, middle, low], axis=0).astype(jnp.bfloat16)


def joined_rows(stacked):
    rows = stacked.shape[0] // 3
    return stacked[0:rows] + stacked[rows : 2 * rows] + stacked[2 * rows :]


def dot_lanes(first, second):
    return lax.dot_general(
        first, second, (((1,), (1,)), ((), ())), preferred_element_type=jnp.float32
    )


def exchange(last, initial, axis):
    devices = lax.axis_size(axis)
    up = [(i, (i + 1) % devices) for i in range(devices)]
    down = [(j, i) for i, j in up]
    return lax.ppermute(last, axis, up), lax.ppermute(initial, axis, down)


def pack_kernel(state_ref, frag_ref, key_ref, out_ref):
    cells = frag_ref.shape[0]
    for comp in range(7):
        out_ref[:, comp, :] = state_ref[comp]
    keys = jnp.broadcast_to(key_ref[0:1, :], (8, key_ref.shape[1]))
    for block in range(cells // 8):
        rows = pl.ds(block * 8, 8)
        out_ref[rows, 7, :] = lanes_of(keys, frag_ref[rows, :])


def list_kernel(
    amount_smem, near_ref, need_ref, own_ref, table_ref, slots_ref, where_ref, cell_ref, class_ref, member_ref, count_ref
):
    tiles, lanes = slots_ref.shape
    span = table_ref.shape[0] // 8
    padded = class_ref.shape[0]
    cells = count_ref.shape[0]
    wide = 256

    def plane(comp):
        return table_ref[pl.ds(comp, span, stride=8), :]

    def flag(value):
        return value.astype(jnp.float32).astype(jnp.bfloat16)

    def dot(first, second):
        return jnp.dot(first, second, preferred_element_type=jnp.float32)

    def ramp(shape, axis):
        return lax.broadcasted_iota(jnp.int32, shape, axis)

    radius = plane(6) + (radius_top + 1e-5)
    classes = jnp.zeros((span, lanes), jnp.float32)
    for axis in range(3):
        place = plane(axis)
        classes = classes + jnp.where(place < radius, 1.0 * (1 << (2 * axis)), 0.0)
        classes = classes + jnp.where(place > 1.0 - radius, 1.0 * (2 << (2 * axis)), 0.0)
    class_ref[...] = jnp.zeros(class_ref.shape, jnp.float32)
    class_ref[pl.ds(0, span), :] = classes
    codes = jnp.concatenate(
        [class_ref[pl.ds(at, lanes), :].T for at in range(0, padded, lanes)], axis=1
    ).astype(jnp.bfloat16)
    ones = jnp.ones((lanes, lanes), jnp.bfloat16)
    count_ref[...] = jnp.zeros(count_ref.shape, jnp.float32)

    pair = 2 * wide
    blocks = lax.div(amount_smem[0] + (pair - 1), pair)

    def choose(block, unused):
        held = []
        for half in range(2):
            at = pl.ds(pl.multiple_of(block * pair + half * wide, wide), wide)
            hits = flag(ramp((padded, wide), 0) == near_ref[:, at])
            found = dot(codes, hits).astype(jnp.int32)
            need = need_ref[:, at]
            member = ((found & need) == need).astype(jnp.float32)
            member_ref[:, at] = member
            count = dot(ones, member.astype(jnp.bfloat16))
            mine = flag(ramp((cells, wide), 0) == own_ref[:, at])
            held.append(dot_lanes(mine, count.astype(jnp.bfloat16)))
        count_ref[...] += held[0] + held[1]
        return unused

    lax.fori_loop(0, blocks, choose, 0)

    held = count_ref[...]
    high = jnp.floor(held * (1.0 / lanes))
    low = held - lanes * high
    taken = jnp.floor((held + (GROUP - 1)) * (1.0 / GROUP))
    upto = flag(ramp((cells, cells), 1) <= ramp((cells, cells), 0))
    ends = dot(upto, taken.astype(jnp.bfloat16))
    cell_ones = jnp.ones((8, cells), jnp.bfloat16)
    group_blocks = cell_ref.shape[1] // lanes - 1

    def name_groups(block, unused):
        group = (ramp((cells, lanes), 1) + block * lanes).astype(jnp.float32)
        over = dot(cell_ones, flag(ends <= group))
        at = pl.ds(pl.multiple_of(block * lanes, lanes), lanes)
        cell_ref[:, at] = over[0:1].astype(jnp.int32)
        return unused

    used = jnp.max(ends).astype(jnp.int32)
    needed = jnp.minimum((used >> (lanes.bit_length() - 1)) + 2, group_blocks)
    lax.fori_loop(0, needed, name_groups, 0)
    cell_ref[:, pl.ds(group_blocks * lanes, lanes)] = ends[cells - 1 : cells].astype(jnp.int32)
    before_cell = jnp.concatenate(
        [value.T[0:8] for value in (taken, high, low)], axis=0
    ).astype(jnp.bfloat16)

    earlier = flag(ramp((lanes, lanes), 1) < ramp((lanes, lanes), 0))
    earlier_tile = flag(ramp((wide, wide), 0) < ramp((wide, wide), 1))

    def place(block, done):
        for half in range(2):
            at = pl.ds(pl.multiple_of(block * pair + half * wide, wide), wide)
            flags = member_ref[:, at].astype(jnp.bfloat16)
            count = dot(ones, flags)
            lower = flag(ramp((cells, wide), 0) < own_ref[:, at])
            before = dot(before_cell, lower)
            so_far = dot(count[0:8].astype(jnp.bfloat16), earlier_tile) + done
            start = GROUP * before[0:8] + so_far - (lanes * before[8:16] + before[16:24])
            start = start.astype(jnp.int32)[0:1]
            where_ref[:, at] = start * 256 + count[0:1].astype(jnp.int32)
            rank = dot(earlier, flags)
            slot = ramp((lanes, wide), 0)
            moves = slot - rank.astype(jnp.int32)
            word = jnp.where(member_ref[:, at] > 0.0, slot + lanes * moves, 0)
            bit = 1
            while bit < lanes:
                keep = jnp.where((word & (bit * lanes)) != 0, 0, word)
                gone = word ^ keep
                word = keep | jnp.concatenate([gone[bit:], gone[:bit]], axis=0)
                bit *= 2
            word = word & (lanes - 1)
            turn = jnp.broadcast_to(start, (lanes, wide))
            bit = 1
            while bit < lanes:
                moved = jnp.concatenate([word[lanes - bit :], word[: lanes - bit]], axis=0)
                word = jnp.where((turn & bit) != 0, moved, word)
                bit *= 2
            for part in range(wide // lanes):
                first = block * pair + half * wide + part * lanes
                rows = pl.ds(pl.multiple_of(first, lanes), lanes)
                slots_ref[rows, :] = word[:, part * lanes : (part + 1) * lanes].T
            done = done + jnp.sum(count[0:8], axis=1, keepdims=True)
        return done

    lax.fori_loop(0, blocks, place, jnp.zeros((8, 1), jnp.float32))


def fill_lists(amount, where_smem, near_smem, table_ref, slots_ref, shift_ref, list_ref):
    tiles, lanes = slots_ref.shape
    lane_bits = lanes.bit_length() - 1
    lane = lax.broadcasted_iota(jnp.int32, (8, lanes), 1)
    row = lax.broadcasted_iota(jnp.int32, (8, lanes), 0)
    absent = jnp.where(row == 6, -10.0, 0.0)

    def fill(block, carry):
        last_chunk, last_new, last_held = carry
        units = range(FILL)
        where = [where_smem[0, block * FILL + unit] for unit in units]
        near = [near_smem[block * FILL + unit] for unit in units]
        found = []
        for unit in units:
            slots = slots_ref[pl.ds(block * FILL + unit, 8, stride=0), :]
            cell = table_ref[near[unit] >> 5]
            found.append(lanes_of(cell, slots) + shift_ref[near[unit] & 31])
        for unit in units:
            amount = where[unit] & 255
            chunk = where[unit] >> (8 + lane_bits)
            offset = (where[unit] >> 8) & (lanes - 1)
            new = jnp.where(((lane - offset) & (lanes - 1)) < amount, found[unit], absent)
            held_row = jnp.where(chunk != last_chunk, last_new, last_held)
            held_row = jnp.where(lane >= offset, new, held_row)
            new = jnp.where(lane >= offset, absent, new)
            list_ref[chunk] = held_row
            list_ref[chunk + 1] = new
            last_chunk, last_new, last_held = chunk, new, held_row
        return last_chunk, last_new, last_held

    blocks = lax.div(amount + (FILL - 1), FILL)
    lax.fori_loop(0, blocks, fill, (jnp.int32(0), absent, absent))


def pair_forces(cell_smem, table_ref, list_ref, force_ref, even_ref, odd_ref):
    lanes = table_ref.shape[1]
    cells = table_ref.shape[0] // 8
    rows = even_ref.shape[0]
    chunks = rows // lanes
    units = rows // GROUP
    groups = cell_smem[0, cell_smem.shape[1] - lanes]
    force_ref[...] = jnp.zeros(force_ref.shape, jnp.float32)
    part = lax.broadcasted_iota(jnp.int32, (32, 8 * lanes), 0)
    comp = lax.broadcasted_iota(jnp.int32, (32, 8 * lanes), 1) // lanes
    weights = jnp.where((part < 24) & (part % 8 == comp), 1.0, 0.0).astype(jnp.bfloat16)

    def spread(step, out_ref):
        turned = []
        for piece in range(chunks):
            values = list_ref[step * chunks + piece]
            high = values.astype(jnp.bfloat16).astype(jnp.float32)
            rest = values - high
            middle = rest.astype(jnp.bfloat16).astype(jnp.float32)
            parts = jnp.concatenate([high, middle, rest - middle, jnp.zeros_like(values)], axis=0)
            turned.append(parts.T.astype(jnp.bfloat16))
        turned = jnp.concatenate(turned, axis=0)
        out_ref[...] = jnp.dot(turned, weights, preferred_element_type=jnp.float32)

    def pairs(step, wide_ref, carry):
        last, running = carry
        for unit in range(units):
            cell = cell_smem[0, step * units + unit]
            own = jnp.minimum(cell, cells - 1) * 8
            other = [
                wide_ref[pl.ds(unit * GROUP, GROUP), pl.ds(value * lanes, lanes)].reshape(
                    GROUP // 8, 8, lanes
                )
                for value in range(8)
            ]
            mine = [table_ref[pl.ds(own + value, 8, stride=0), :][None] for value in range(8)]
            apart = [other[axis] - mine[axis] for axis in range(3)]
            square = apart[0] * apart[0] + apart[1] * apart[1] + apart[2] * apart[2] + epsilon_sq
            inverse = lax.rsqrt(square)
            reach = other[6] + mine[6]
            overlap = jnp.maximum(reach - square * inverse, 0.0)
            overlap = jnp.where(other[7] != mine[7], overlap, 0.0)
            closing = (
                (other[3] - mine[3]) * apart[0]
                + (other[4] - mine[4]) * apart[1]
                + (other[5] - mine[5]) * apart[2]
            )
            scaled = overlap * (other[6] * mine[6])
            root = scaled * lax.rsqrt(jnp.maximum(scaled * reach, 1e-30))
            factor = root * inverse * (stiffness / damping * overlap - closing * inverse)
            running = [
                jnp.sum(factor * apart[axis], axis=0)
                + jnp.where(cell == last, running[axis], 0.0)
                for axis in range(3)
            ]
            last = cell
            for axis in range(3):
                force_ref[cell, axis] = running[axis]
        return last, running

    spread(0, even_ref)

    def both(step, carry):
        spread(2 * step + 1, odd_ref)
        carry = pairs(2 * step, even_ref, carry)
        spread(2 * step + 2, even_ref)
        return pairs(2 * step + 1, odd_ref, carry)

    zero = jnp.zeros((8, lanes), jnp.float32)
    steps = lax.div(groups + (2 * units - 1), 2 * units)
    lax.fori_loop(0, steps, both, (jnp.int32(-1), [zero] * 3))


def inner_kernel(
    amount_smem, where_smem, near_smem, cell_smem, table_ref, slots_ref, shift_ref,
    force_ref, list_ref, even_ref, odd_ref,
):
    cells = table_ref.shape[0]
    fill_lists(amount_smem[0], where_smem, near_smem, table_ref, slots_ref, shift_ref, list_ref)
    flat = table_ref.reshape(cells * 8, table_ref.shape[2])
    pair_forces(cell_smem, flat, list_ref, force_ref, even_ref, odd_ref)


def outer_kernel(
    amount_smem, where_smem, near_smem, cell_smem, table_ref, halo_ref, slots_ref, shift_ref,
    inner_ref, arms_ref, frag_ref, fixed_ref, out_ref, list_ref, even_ref, odd_ref, force_ref, loads_ref,
):
    held = fixed_ref.shape[1] // 2
    fill_lists(amount_smem[0], where_smem, near_smem, halo_ref, slots_ref, shift_ref, list_ref)
    pair_forces(cell_smem, table_ref, list_ref, force_ref, even_ref, odd_ref)
    sums = fragment_sums(inner_ref, force_ref, arms_ref, frag_ref, loads_ref, held)
    out = fixed_ref[...] + jnp.concatenate([sums, jnp.zeros_like(sums)], axis=1)
    for brick in range(out_ref.shape[0]):
        out_ref[brick] = out


def fragment_sums(inner_ref, outer_ref, arms_ref, frag_ref, loads_ref, held):
    cells, lanes = frag_ref.shape
    tall = loads_ref.shape[0]
    label = lax.broadcasted_iota(jnp.int32, (held, lanes), 0)

    def gather_sums(block, total):
        rows = pl.ds(pl.multiple_of(block * tall, tall), tall)
        force = [
            -damping * jnp.sum(inner_ref[rows, axis] + outer_ref[rows, axis], axis=1)
            for axis in range(3)
        ]
        lever = [arms_ref[axis, rows, :] for axis in range(3)]
        torque = [
            lever[1] * force[2] - lever[2] * force[1],
            lever[2] * force[0] - lever[0] * force[2],
            lever[0] * force[1] - lever[1] * force[0],
        ]
        loads = force + torque + [jnp.zeros_like(force[0])] * 2
        for comp in range(8):
            loads_ref[:, comp, :] = loads[comp]
        frags = frag_ref[rows, :]
        hits = [
            (frags[unit : unit + 1, :] == label).astype(jnp.float32).astype(jnp.bfloat16)
            for unit in range(tall)
        ]
        values = [split_rows(loads_ref[unit]) for unit in range(tall)]
        return total + dot_lanes(jnp.concatenate(values, axis=1), jnp.concatenate(hits, axis=1))

    total = lax.fori_loop(0, cells // tall, gather_sums, jnp.zeros((24, held), jnp.float32))
    return joined_rows(total)


def move_kernel(
    owned, target_ref, known_ref, state_ref, arms_ref, frag_ref, spheres_ref, clumps_ref
):
    bricks, _, lanes = known_ref.shape
    held = lanes // 2
    cells = frag_ref.shape[0]
    targets = jnp.broadcast_to(target_ref[...], (lanes, lanes))
    lane = lax.broadcasted_iota(jnp.int32, (1, lanes), 1)

    def match(block, carry):
        sums, base = carry
        for unit in range(8):
            brick = block * 8 + unit
            known = known_ref[brick]
            values = split_rows(known)
            key = jnp.where(lane < held, known[6:7], -1.0)
            number = jnp.where(
                (lane >= held) & (lane < held + owned), brick * owned + lane - held, -1
            ).astype(jnp.float32)
            sums = sums + dot_lanes(values, (targets == key).astype(jnp.float32).astype(jnp.bfloat16))
            base = base + dot_lanes(values, (targets == number).astype(jnp.float32).astype(jnp.bfloat16))
        return sums, base

    zero = jnp.zeros((24, lanes), jnp.float32)
    sums, base = lax.fori_loop(0, bricks // 8, match, (zero, zero))
    sums = joined_rows(sums)
    base = joined_rows(base)
    rows = []
    for axis in range(3):
        pull = gravity if axis == 2 else 0.0
        rows.append(
            base[axis : axis + 1]
            + time_step * (sums[axis : axis + 1] * base[6:7] - pull)
        )
    for axis in range(3, 6):
        rows.append(base[axis : axis + 1] + time_step * sums[axis : axis + 1] * base[7:8])
    for comp in range(6):
        clumps_ref[comp : comp + 1, :] = rows[comp]
    tall = 32
    wide = [jnp.broadcast_to(value, (tall, lanes)) for value in rows]

    def cross(first, second):
        return [
            first[1] * second[2] - first[2] * second[1],
            first[2] * second[0] - first[0] * second[2],
            first[0] * second[1] - first[1] * second[0],
        ]

    def move(block, unused):
        at = pl.ds(pl.multiple_of(block * tall, tall), tall)
        index = frag_ref[at, :] + (lanes - held)
        motion = [lanes_of(value, index) for value in wide]
        velocity, spin = motion[0:3], motion[3:6]
        arm = [arms_ref[axis, at, :] for axis in range(3)]
        half = [0.5 * time_step * value for value in spin]
        turned = cross(half, arm)
        twice = cross(half, turned)
        scale = 2.0 / (1.0 + half[0] * half[0] + half[1] * half[1] + half[2] * half[2])
        change = [scale * (turned[axis] + twice[axis]) for axis in range(3)]
        new_arm = [arm[axis] + change[axis] for axis in range(3)]
        swing = cross(spin, new_arm)
        for axis in range(3):
            spheres_ref[axis, at, :] = (
                state_ref[axis, at, :] + time_step * velocity[axis] + (new_arm[axis] - arm[axis])
            )
            spheres_ref[3 + axis, at, :] = velocity[axis] + swing[axis]
        return unused

    lax.fori_loop(0, cells // tall, move, 0)


def local(
    state, arms, sphere_frag, frag_owner, frag_clump, tiles, clump_motion, inv_mass, inv_moment
):
    cells_x, cells_y, cells_z = (state.shape[1], state.shape[2], state.shape[3])
    lanes = state.shape[4]
    cells = cells_x * cells_y * cells_z
    owned = inv_mass.shape[0]
    held = frag_clump.shape[0]
    names = ("gx", "gy", "gz")
    vmem = pl.BlockSpec(memory_space=pltpu.VMEM)
    smem = pl.BlockSpec(memory_space=pltpu.SMEM)
    params = pltpu.CompilerParams(vmem_limit_bytes=VMEM)

    frag_key = (frag_owner[:, 0] * owned + frag_clump).astype(jnp.float32)
    flat_state = state.reshape(7, cells, lanes)
    flat_arms = arms.reshape(3, cells, lanes)
    flat_frag = sphere_frag.reshape(cells, lanes)

    fixed = jnp.concatenate(
        [
            jnp.concatenate([jnp.zeros((6, held)), frag_key[None], jnp.zeros((1, held))], axis=0),
            jnp.concatenate([clump_motion, inv_mass[None], inv_moment[None]], axis=0),
            jnp.zeros((8, lanes - held - owned)),
        ],
        axis=1,
    )

    table = pl.pallas_call(
        pack_kernel,
        out_shape=jax.ShapeDtypeStruct((cells, 8, lanes), jnp.float32),
        in_specs=[vmem] * 3,
        out_specs=vmem,
        compiler_params=params,
    )(flat_state, flat_frag, jnp.pad(frag_key, (0, lanes - held))[None])
    grid = table.reshape(cells_x, cells_y, cells_z, 8, lanes)
    z_before, z_after = exchange(grid[:, :, -1:], grid[:, :, :1], "gz")

    kinds = jnp.arange(27, dtype=jnp.int32)
    moves = jnp.stack([kinds // 9 - 1, kinds // 3 % 3 - 1, kinds % 3 - 1], axis=1)
    shift = jnp.pad(moves.astype(jnp.float32), ((0, 0), (0, 5)))
    shift = jnp.broadcast_to(shift[:, :, None], (27, 8, lanes))

    outside = 1 << 20
    span_z = cells_z + 2
    starts = [0, cells_x * cells_y, 2 * cells_x * cells_y]
    starts += [starts[-1] + cells_y * span_z, starts[-1] + 2 * cells_y * span_z]
    starts += [starts[-1] + (cells_x + 2) * span_z]

    def decode(codes):
        own, offset = (codes // 27, codes % 27)
        steps = (offset // 9 - 1, offset // 3 % 3 - 1, offset % 3 - 1)
        x = own // (cells_y * cells_z) + steps[0]
        y = own // cells_z % cells_y + steps[1]
        z = own % cells_z + steps[2]
        need = sum(
            jnp.where(steps[axis] == 1, 1, jnp.where(steps[axis] == -1, 2, 0)) << (2 * axis)
            for axis in range(3)
        )
        return own, offset, need, x, y, z

    def inside(x, y, z):
        inner = (x >= 0) & (x < cells_x) & (y >= 0) & (y < cells_y)
        return inner & (z >= 0) & (z < cells_z)

    codes = tiles[0]
    total = codes.shape[0]
    codes = jnp.sort(codes + jnp.where(inside(*decode(codes)[3:]), 0, outside))
    inner_amount = jnp.sum((codes < outside).astype(jnp.int32))
    order = jnp.arange(total, dtype=jnp.int32)

    def listed(codes, amount, want_inside):
        own, offset, need, x, y, z = decode(codes & (outside - 1))
        if want_inside:
            near = (x * cells_y + y) * cells_z + z
        else:
            in_y = jnp.where(y < 0, starts[4], starts[5]) + (x + 1) * span_z + z + 1
            in_x = jnp.where(x < 0, starts[2], starts[3]) + y * span_z + z + 1
            in_z = jnp.where(z < 0, starts[0], starts[1]) + x * cells_y + y
            near = jnp.where(
                (y < 0) | (y >= cells_y), in_y, jnp.where((x < 0) | (x >= cells_x), in_x, in_z)
            )
        live = order < amount
        near = jnp.where(live, near, 0)
        return (
            near,
            near * 32 + jnp.where(live, offset, 0),
            jnp.where(live, need, 64),
            jnp.where(live, own, cells),
        )

    chunks = -(-(total + cells * GROUP // lanes) // 16) * 16 + 8
    group_top = chunks * (lanes // GROUP)

    def lists(near, need, own, amount, source):
        span = source.shape[0]
        return pl.pallas_call(
            list_kernel,
            out_shape=(
                jax.ShapeDtypeStruct((total, lanes), jnp.int32),
                jax.ShapeDtypeStruct((1, total), jnp.int32),
                jax.ShapeDtypeStruct((1, -(-group_top // lanes) * lanes + lanes), jnp.int32),
            ),
            in_specs=[smem] + [vmem] * 4,
            out_specs=(vmem, vmem, vmem),
            scratch_shapes=[
                pltpu.VMEM((-(-span // lanes) * lanes, lanes), jnp.float32),
                pltpu.VMEM((lanes, total), jnp.float32),
                pltpu.VMEM((cells, lanes), jnp.float32),
            ],
            compiler_params=params,
        )(amount[None], near[None], need[None], own[None], source.reshape(span * 8, lanes))

    force_shape = (cells + 8, 3, 8, lanes)
    scratch = [
        pltpu.VMEM((chunks, 8, lanes), jnp.float32),
        pltpu.VMEM((SPREAD * lanes, 8 * lanes), jnp.float32),
        pltpu.VMEM((SPREAD * lanes, 8 * lanes), jnp.float32),
    ]

    near, word, need, own = listed(codes, inner_amount, True)
    z_before, z_after, near, need, own = lax.optimization_barrier(
        (z_before, z_after, near, need, own)
    )
    x_before, x_after = exchange(
        jnp.concatenate([z_before[-1:], grid[-1:], z_after[-1:]], axis=2),
        jnp.concatenate([z_before[:1], grid[:1], z_after[:1]], axis=2),
        "gx",
    )
    slots, where, cell_of = lists(near, need, own, inner_amount, table)
    x_before, x_after, slots, where, cell_of = lax.optimization_barrier(
        (x_before, x_after, slots, where, cell_of)
    )

    def face(at):
        middle = jnp.concatenate([z_before[:, at], grid[:, at], z_after[:, at]], axis=2)
        return jnp.concatenate([x_before[:, at], middle, x_after[:, at]], axis=0)

    y_before, y_after = exchange(face(slice(-1, None)), face(slice(0, 1)), "gy")
    inner = pl.pallas_call(
        inner_kernel,
        out_shape=jax.ShapeDtypeStruct(force_shape, jnp.float32),
        in_specs=[smem] * 4 + [vmem] * 3,
        out_specs=vmem,
        scratch_shapes=scratch,
        compiler_params=params,
    )(inner_amount[None], where, word, cell_of, table, slots, shift)

    outer_amount = total - inner_amount
    codes = lax.dynamic_slice(jnp.concatenate([codes, codes]), (inner_amount,), (total,))
    near, word, need, own = listed(codes, outer_amount, False)
    halo = jnp.concatenate(
        [
            part.reshape(-1, 8, lanes)
            for part in (z_before, z_after, x_before, x_after, y_before, y_after)
        ],
        axis=0,
    )
    slots, where, cell_of = lists(near, need, own, outer_amount, halo)
    bricks = lax.axis_size(names)
    known = pl.pallas_call(
        outer_kernel,
        out_shape=jax.ShapeDtypeStruct((bricks, 8, lanes), jnp.float32),
        in_specs=[smem] * 4 + [vmem] * 8,
        out_specs=vmem,
        scratch_shapes=scratch
        + [pltpu.VMEM(force_shape, jnp.float32), pltpu.VMEM((16, 8, lanes), jnp.float32)],
        compiler_params=params,
    )(
        outer_amount[None],
        where,
        word,
        cell_of,
        table.reshape(cells * 8, lanes),
        halo,
        slots,
        shift,
        inner,
        flat_arms,
        flat_frag,
        fixed,
    )
    known = lax.all_to_all(known, names, split_axis=0, concat_axis=0, tiled=True)

    brick = lax.axis_index(names)
    mine = jnp.where(
        jnp.arange(lanes - held) < owned, brick * owned + jnp.arange(lanes - held), -2
    ).astype(jnp.float32)
    target = jnp.concatenate([mine, frag_key])[:, None]
    spheres, clumps = pl.pallas_call(
        functools.partial(move_kernel, owned),
        out_shape=(
            jax.ShapeDtypeStruct((6, cells, lanes), jnp.float32),
            jax.ShapeDtypeStruct((6, lanes), jnp.float32),
        ),
        in_specs=[vmem] * 5,
        out_specs=(vmem, vmem),
        compiler_params=params,
    )(target, known, flat_state, flat_arms, flat_frag)
    return (spheres.reshape((6,) + state.shape[1:]), clumps[:, :owned])


def solution(mesh):
    return jax.shard_map(
        local,
        mesh=mesh,
        in_specs=(
            P(None, "gx", "gy", "gz", None),
            P(None, "gx", "gy", "gz", None),
            P("gx", "gy", "gz", None),
            P(("gx", "gy", "gz"), None),
            P(("gx", "gy", "gz")),
            P(("gx", "gy", "gz"), None),
            P(None, ("gx", "gy", "gz")),
            P(("gx", "gy", "gz")),
            P(("gx", "gy", "gz")),
        ),
        out_specs=(P(None, "gx", "gy", "gz", None), P(None, ("gx", "gy", "gz"))),
        check_vma=False,
    )
```

```python
import functools

import jax
import jax.numpy as jnp
from jax import lax
from jax.experimental import pallas as pl
from jax.experimental.pallas import tpu as pltpu
from jax.sharding import PartitionSpec as P

stiffness = 100.0
damping = 2.0
time_step = 0.01
gravity = 9.81
epsilon_sq = 1e-08
radius_top = 0.14

GROUP = 32
FILL = 32
SPREAD = 4
VMEM = 56 * 1024 * 1024


def lanes_of(values, index):
    return jnp.take_along_axis(values, index, axis=1, mode="promise_in_bounds")


def split_rows(values):
    high = values.astype(jnp.bfloat16).astype(jnp.float32)
    rest = values - high
    middle = rest.astype(jnp.bfloat16).astype(jnp.float32)
    low = rest - middle
    return jnp.concatenate([high, middle, low], axis=0).astype(jnp.bfloat16)


def joined_rows(stacked):
    rows = stacked.shape[0] // 3
    return stacked[0:rows] + stacked[rows : 2 * rows] + stacked[2 * rows :]


def dot_lanes(first, second):
    return lax.dot_general(
        first, second, (((1,), (1,)), ((), ())), preferred_element_type=jnp.float32
    )


def exchange(last, initial, axis):
    devices = lax.axis_size(axis)
    up = [(i, (i + 1) % devices) for i in range(devices)]
    down = [(j, i) for i, j in up]
    return lax.ppermute(last, axis, up), lax.ppermute(initial, axis, down)


def pack_kernel(state_ref, frag_ref, key_ref, out_ref):
    cells = frag_ref.shape[0]
    for comp in range(7):
        out_ref[:, comp, :] = state_ref[comp]
    keys = jnp.broadcast_to(key_ref[0:1, :], (8, key_ref.shape[1]))
    for block in range(cells // 8):
        rows = pl.ds(block * 8, 8)
        out_ref[rows, 7, :] = lanes_of(keys, frag_ref[rows, :])


def list_kernel(
    amount_smem, near_ref, need_ref, own_ref, table_ref, slots_ref, where_ref, cell_ref, class_ref, member_ref, count_ref
):
    tiles, lanes = slots_ref.shape
    span = table_ref.shape[0] // 8
    padded = class_ref.shape[0]
    cells = count_ref.shape[0]
    wide = 256

    def plane(comp):
        return table_ref[pl.ds(comp, span, stride=8), :]

    def flag(value):
        return value.astype(jnp.float32).astype(jnp.bfloat16)

    def dot(first, second):
        return jnp.dot(first, second, preferred_element_type=jnp.float32)

    def ramp(shape, axis):
        return lax.broadcasted_iota(jnp.int32, shape, axis)

    radius = plane(6) + (radius_top + 1e-5)
    classes = jnp.zeros((span, lanes), jnp.float32)
    for axis in range(3):
        place = plane(axis)
        classes = classes + jnp.where(place < radius, 1.0 * (1 << (2 * axis)), 0.0)
        classes = classes + jnp.where(place > 1.0 - radius, 1.0 * (2 << (2 * axis)), 0.0)
    class_ref[...] = jnp.zeros(class_ref.shape, jnp.float32)
    class_ref[pl.ds(0, span), :] = classes
    codes = jnp.concatenate(
        [class_ref[pl.ds(at, lanes), :].T for at in range(0, padded, lanes)], axis=1
    ).astype(jnp.bfloat16)
    ones = jnp.ones((lanes, lanes), jnp.bfloat16)
    count_ref[...] = jnp.zeros(count_ref.shape, jnp.float32)

    pair = 2 * wide
    blocks = lax.div(amount_smem[0] + (pair - 1), pair)

    def choose(block, unused):
        held = []
        for half in range(2):
            at = pl.ds(pl.multiple_of(block * pair + half * wide, wide), wide)
            hits = flag(ramp((padded, wide), 0) == near_ref[:, at])
            found = dot(codes, hits).astype(jnp.int32)
            need = need_ref[:, at]
            member = ((found & need) == need).astype(jnp.float32)
            member_ref[:, at] = member
            count = dot(ones, member.astype(jnp.bfloat16))
            mine = flag(ramp((cells, wide), 0) == own_ref[:, at])
            held.append(dot_lanes(mine, count.astype(jnp.bfloat16)))
        count_ref[...] += held[0] + held[1]
        return unused

    lax.fori_loop(0, blocks, choose, 0)

    held = count_ref[...]
    high = jnp.floor(held * (1.0 / lanes))
    low = held - lanes * high
    taken = jnp.floor((held + (GROUP - 1)) * (1.0 / GROUP))
    upto = flag(ramp((cells, cells), 1) <= ramp((cells, cells), 0))
    ends = dot(upto, taken.astype(jnp.bfloat16))
    cell_ones = jnp.ones((8, cells), jnp.bfloat16)
    group_blocks = cell_ref.shape[1] // lanes - 1

    def name_groups(block, unused):
        group = (ramp((cells, lanes), 1) + block * lanes).astype(jnp.float32)
        over = dot(cell_ones, flag(ends <= group))
        at = pl.ds(pl.multiple_of(block * lanes, lanes), lanes)
        cell_ref[:, at] = over[0:1].astype(jnp.int32)
        return unused

    used = jnp.max(ends).astype(jnp.int32)
    needed = jnp.minimum((used >> (lanes.bit_length() - 1)) + 2, group_blocks)
    lax.fori_loop(0, needed, name_groups, 0)
    cell_ref[:, pl.ds(group_blocks * lanes, lanes)] = ends[cells - 1 : cells].astype(jnp.int32)
    before_cell = jnp.concatenate(
        [value.T[0:8] for value in (taken, high, low)], axis=0
    ).astype(jnp.bfloat16)

    earlier = flag(ramp((lanes, lanes), 1) < ramp((lanes, lanes), 0))
    earlier_tile = flag(ramp((wide, wide), 0) < ramp((wide, wide), 1))

    def place(block, done):
        for half in range(2):
            at = pl.ds(pl.multiple_of(block * pair + half * wide, wide), wide)
            flags = member_ref[:, at].astype(jnp.bfloat16)
            count = dot(ones, flags)
            lower = flag(ramp((cells, wide), 0) < own_ref[:, at])
            before = dot(before_cell, lower)
            so_far = dot(count[0:8].astype(jnp.bfloat16), earlier_tile) + done
            start = GROUP * before[0:8] + so_far - (lanes * before[8:16] + before[16:24])
            start = start.astype(jnp.int32)[0:1]
            where_ref[:, at] = start * 256 + count[0:1].astype(jnp.int32)
            rank = dot(earlier, flags)
            slot = ramp((lanes, wide), 0)
            moves = slot - rank.astype(jnp.int32)
            word = jnp.where(member_ref[:, at] > 0.0, slot + lanes * moves, 0)
            bit = 1
            while bit < lanes:
                keep = jnp.where((word & (bit * lanes)) != 0, 0, word)
                gone = word ^ keep
                word = keep | jnp.concatenate([gone[bit:], gone[:bit]], axis=0)
                bit *= 2
            word = word & (lanes - 1)
            turn = jnp.broadcast_to(start, (lanes, wide))
            bit = 1
            while bit < lanes:
                moved = jnp.concatenate([word[lanes - bit :], word[: lanes - bit]], axis=0)
                word = jnp.where((turn & bit) != 0, moved, word)
                bit *= 2
            for part in range(wide // lanes):
                first = block * pair + half * wide + part * lanes
                rows = pl.ds(pl.multiple_of(first, lanes), lanes)
                slots_ref[rows, :] = word[:, part * lanes : (part + 1) * lanes].T
            done = done + jnp.sum(count[0:8], axis=1, keepdims=True)
        return done

    lax.fori_loop(0, blocks, place, jnp.zeros((8, 1), jnp.float32))


def fill_lists(amount, where_smem, near_smem, table_ref, slots_ref, shift_ref, list_ref):
    tiles, lanes = slots_ref.shape
    lane_bits = lanes.bit_length() - 1
    lane = lax.broadcasted_iota(jnp.int32, (8, lanes), 1)
    row = lax.broadcasted_iota(jnp.int32, (8, lanes), 0)
    absent = jnp.where(row == 6, -10.0, 0.0)

    def fill(block, carry):
        last_chunk, last_new, last_held = carry
        units = range(FILL)
        where = [where_smem[0, block * FILL + unit] for unit in units]
        near = [near_smem[block * FILL + unit] for unit in units]
        found = []
        for unit in units:
            slots = slots_ref[pl.ds(block * FILL + unit, 8, stride=0), :]
            cell = table_ref[near[unit] >> 5]
            found.append(lanes_of(cell, slots) + shift_ref[near[unit] & 31])
        for unit in units:
            amount = where[unit] & 255
            chunk = where[unit] >> (8 + lane_bits)
            offset = (where[unit] >> 8) & (lanes - 1)
            new = jnp.where(((lane - offset) & (lanes - 1)) < amount, found[unit], absent)
            held_row = jnp.where(chunk != last_chunk, last_new, last_held)
            held_row = jnp.where(lane >= offset, new, held_row)
            new = jnp.where(lane >= offset, absent, new)
            list_ref[chunk] = held_row
            list_ref[chunk + 1] = new
            last_chunk, last_new, last_held = chunk, new, held_row
        return last_chunk, last_new, last_held

    blocks = lax.div(amount + (FILL - 1), FILL)
    lax.fori_loop(0, blocks, fill, (jnp.int32(0), absent, absent))


def pair_forces(cell_smem, table_ref, list_ref, force_ref, even_ref, odd_ref):
    lanes = table_ref.shape[1]
    cells = table_ref.shape[0] // 8
    rows = even_ref.shape[0]
    chunks = rows // lanes
    units = rows // GROUP
    groups = cell_smem[0, cell_smem.shape[1] - lanes]
    force_ref[...] = jnp.zeros(force_ref.shape, jnp.float32)
    part = lax.broadcasted_iota(jnp.int32, (32, 8 * lanes), 0)
    comp = lax.broadcasted_iota(jnp.int32, (32, 8 * lanes), 1) // lanes
    weights = jnp.where((part < 24) & (part % 8 == comp), 1.0, 0.0).astype(jnp.bfloat16)

    def spread(step, out_ref):
        turned = []
        for piece in range(chunks):
            values = list_ref[step * chunks + piece]
            high = values.astype(jnp.bfloat16).astype(jnp.float32)
            rest = values - high
            middle = rest.astype(jnp.bfloat16).astype(jnp.float32)
            parts = jnp.concatenate([high, middle, rest - middle, jnp.zeros_like(values)], axis=0)
            turned.append(parts.astype(jnp.bfloat16).T)
        turned = jnp.concatenate(turned, axis=0)
        out_ref[...] = jnp.dot(turned, weights, preferred_element_type=jnp.float32)

    def pairs(step, wide_ref, carry):
        last, running = carry
        for unit in range(units):
            cell = cell_smem[0, step * units + unit]
            own = jnp.minimum(cell, cells - 1) * 8
            other = [
                wide_ref[pl.ds(unit * GROUP, GROUP), pl.ds(value * lanes, lanes)].reshape(
                    GROUP // 8, 8, lanes
                )
                for value in range(8)
            ]
            mine = [table_ref[pl.ds(own + value, 8, stride=0), :][None] for value in range(8)]
            apart = [other[axis] - mine[axis] for axis in range(3)]
            square = apart[0] * apart[0] + apart[1] * apart[1] + apart[2] * apart[2] + epsilon_sq
            inverse = lax.rsqrt(square)
            reach = other[6] + mine[6]
            overlap = jnp.maximum(reach - square * inverse, 0.0)
            overlap = jnp.where(other[7] != mine[7], overlap, 0.0)
            closing = (
                (other[3] - mine[3]) * apart[0]
                + (other[4] - mine[4]) * apart[1]
                + (other[5] - mine[5]) * apart[2]
            )
            scaled = overlap * (other[6] * mine[6])
            root = scaled * lax.rsqrt(jnp.maximum(scaled * reach, 1e-30))
            factor = root * inverse * (stiffness / damping * overlap - closing * inverse)
            running = [
                jnp.sum(factor * apart[axis], axis=0)
                + jnp.where(cell == last, running[axis], 0.0)
                for axis in range(3)
            ]
            last = cell
            for axis in range(3):
                force_ref[cell, axis] = running[axis]
        return last, running

    spread(0, even_ref)

    def both(step, carry):
        spread(2 * step + 1, odd_ref)
        carry = pairs(2 * step, even_ref, carry)
        spread(2 * step + 2, even_ref)
        return pairs(2 * step + 1, odd_ref, carry)

    zero = jnp.zeros((8, lanes), jnp.float32)
    steps = lax.div(groups + (2 * units - 1), 2 * units)
    lax.fori_loop(0, steps, both, (jnp.int32(-1), [zero] * 3))


def inner_kernel(
    amount_smem, where_smem, near_smem, cell_smem, table_ref, slots_ref, shift_ref,
    force_ref, list_ref, even_ref, odd_ref,
):
    cells = table_ref.shape[0]
    fill_lists(amount_smem[0], where_smem, near_smem, table_ref, slots_ref, shift_ref, list_ref)
    flat = table_ref.reshape(cells * 8, table_ref.shape[2])
    pair_forces(cell_smem, flat, list_ref, force_ref, even_ref, odd_ref)


def outer_kernel(
    amount_smem, where_smem, near_smem, cell_smem, table_ref, halo_ref, slots_ref, shift_ref,
    inner_ref, arms_ref, frag_ref, fixed_ref, out_ref, list_ref, even_ref, odd_ref, force_ref, loads_ref,
):
    held = fixed_ref.shape[1] // 2
    fill_lists(amount_smem[0], where_smem, near_smem, halo_ref, slots_ref, shift_ref, list_ref)
    pair_forces(cell_smem, table_ref, list_ref, force_ref, even_ref, odd_ref)
    sums = fragment_sums(inner_ref, force_ref, arms_ref, frag_ref, loads_ref, held)
    out = fixed_ref[...] + jnp.concatenate([sums, jnp.zeros_like(sums)], axis=1)
    for brick in range(out_ref.shape[0]):
        out_ref[brick] = out


def fragment_sums(inner_ref, outer_ref, arms_ref, frag_ref, loads_ref, held):
    cells, lanes = frag_ref.shape
    tall = loads_ref.shape[0]
    label = lax.broadcasted_iota(jnp.int32, (held, lanes), 0)

    def gather_sums(block, total):
        rows = pl.ds(pl.multiple_of(block * tall, tall), tall)
        force = [
            -damping * jnp.sum(inner_ref[rows, axis] + outer_ref[rows, axis], axis=1)
            for axis in range(3)
        ]
        lever = [arms_ref[axis, rows, :] for axis in range(3)]
        torque = [
            lever[1] * force[2] - lever[2] * force[1],
            lever[2] * force[0] - lever[0] * force[2],
            lever[0] * force[1] - lever[1] * force[0],
        ]
        loads = force + torque + [jnp.zeros_like(force[0])] * 2
        for comp in range(8):
            loads_ref[:, comp, :] = loads[comp]
        frags = frag_ref[rows, :]
        hits = [
            (frags[unit : unit + 1, :] == label).astype(jnp.float32).astype(jnp.bfloat16)
            for unit in range(tall)
        ]
        values = [split_rows(loads_ref[unit]) for unit in range(tall)]
        return total + dot_lanes(jnp.concatenate(values, axis=1), jnp.concatenate(hits, axis=1))

    total = lax.fori_loop(0, cells // tall, gather_sums, jnp.zeros((24, held), jnp.float32))
    return joined_rows(total)


def move_kernel(
    owned, target_ref, known_ref, state_ref, arms_ref, frag_ref, spheres_ref, clumps_ref
):
    bricks, _, lanes = known_ref.shape
    held = lanes // 2
    cells = frag_ref.shape[0]
    targets = jnp.broadcast_to(target_ref[...], (lanes, lanes))
    lane = lax.broadcasted_iota(jnp.int32, (1, lanes), 1)

    def match(block, carry):
        sums, base = carry
        for unit in range(8):
            brick = block * 8 + unit
            known = known_ref[brick]
            values = split_rows(known)
            key = jnp.where(lane < held, known[6:7], -1.0)
            number = jnp.where(
                (lane >= held) & (lane < held + owned), brick * owned + lane - held, -1
            ).astype(jnp.float32)
            sums = sums + dot_lanes(values, (targets == key).astype(jnp.float32).astype(jnp.bfloat16))
            base = base + dot_lanes(values, (targets == number).astype(jnp.float32).astype(jnp.bfloat16))
        return sums, base

    zero = jnp.zeros((24, lanes), jnp.float32)
    sums, base = lax.fori_loop(0, bricks // 8, match, (zero, zero))
    sums = joined_rows(sums)
    base = joined_rows(base)
    rows = []
    for axis in range(3):
        pull = gravity if axis == 2 else 0.0
        rows.append(
            base[axis : axis + 1]
            + time_step * (sums[axis : axis + 1] * base[6:7] - pull)
        )
    for axis in range(3, 6):
        rows.append(base[axis : axis + 1] + time_step * sums[axis : axis + 1] * base[7:8])
    for comp in range(6):
        clumps_ref[comp : comp + 1, :] = rows[comp]
    tall = 32
    wide = [jnp.broadcast_to(value, (tall, lanes)) for value in rows]

    def cross(first, second):
        return [
            first[1] * second[2] - first[2] * second[1],
            first[2] * second[0] - first[0] * second[2],
            first[0] * second[1] - first[1] * second[0],
        ]

    def move(block, unused):
        at = pl.ds(pl.multiple_of(block * tall, tall), tall)
        index = frag_ref[at, :] + (lanes - held)
        motion = [lanes_of(value, index) for value in wide]
        velocity, spin = motion[0:3], motion[3:6]
        arm = [arms_ref[axis, at, :] for axis in range(3)]
        half = [0.5 * time_step * value for value in spin]
        turned = cross(half, arm)
        twice = cross(half, turned)
        scale = 2.0 / (1.0 + half[0] * half[0] + half[1] * half[1] + half[2] * half[2])
        change = [scale * (turned[axis] + twice[axis]) for axis in range(3)]
        new_arm = [arm[axis] + change[axis] for axis in range(3)]
        swing = cross(spin, new_arm)
        for axis in range(3):
            spheres_ref[axis, at, :] = (
                state_ref[axis, at, :] + time_step * velocity[axis] + (new_arm[axis] - arm[axis])
            )
            spheres_ref[3 + axis, at, :] = velocity[axis] + swing[axis]
        return unused

    lax.fori_loop(0, cells // tall, move, 0)


def local(
    state, arms, sphere_frag, frag_owner, frag_clump, tiles, clump_motion, inv_mass, inv_moment
):
    cells_x, cells_y, cells_z = (state.shape[1], state.shape[2], state.shape[3])
    lanes = state.shape[4]
    cells = cells_x * cells_y * cells_z
    owned = inv_mass.shape[0]
    held = frag_clump.shape[0]
    names = ("gx", "gy", "gz")
    vmem = pl.BlockSpec(memory_space=pltpu.VMEM)
    smem = pl.BlockSpec(memory_space=pltpu.SMEM)
    params = pltpu.CompilerParams(vmem_limit_bytes=VMEM)

    frag_key = (frag_owner[:, 0] * owned + frag_clump).astype(jnp.float32)
    flat_state = state.reshape(7, cells, lanes)
    flat_arms = arms.reshape(3, cells, lanes)
    flat_frag = sphere_frag.reshape(cells, lanes)

    fixed = jnp.concatenate(
        [
            jnp.concatenate([jnp.zeros((6, held)), frag_key[None], jnp.zeros((1, held))], axis=0),
            jnp.concatenate([clump_motion, inv_mass[None], inv_moment[None]], axis=0),
            jnp.zeros((8, lanes - held - owned)),
        ],
        axis=1,
    )

    table = pl.pallas_call(
        pack_kernel,
        out_shape=jax.ShapeDtypeStruct((cells, 8, lanes), jnp.float32),
        in_specs=[vmem] * 3,
        out_specs=vmem,
        compiler_params=params,
    )(flat_state, flat_frag, jnp.pad(frag_key, (0, lanes - held))[None])
    grid = table.reshape(cells_x, cells_y, cells_z, 8, lanes)
    z_before, z_after = exchange(grid[:, :, -1:], grid[:, :, :1], "gz")

    kinds = jnp.arange(27, dtype=jnp.int32)
    moves = jnp.stack([kinds // 9 - 1, kinds // 3 % 3 - 1, kinds % 3 - 1], axis=1)
    shift = jnp.pad(moves.astype(jnp.float32), ((0, 0), (0, 5)))
    shift = jnp.broadcast_to(shift[:, :, None], (27, 8, lanes))

    outside = 1 << 20
    span_z = cells_z + 2
    starts = [0, cells_x * cells_y, 2 * cells_x * cells_y]
    starts += [starts[-1] + cells_y * span_z, starts[-1] + 2 * cells_y * span_z]
    starts += [starts[-1] + (cells_x + 2) * span_z]

    def decode(codes):
        own, offset = (codes // 27, codes % 27)
        steps = (offset // 9 - 1, offset // 3 % 3 - 1, offset % 3 - 1)
        x = own // (cells_y * cells_z) + steps[0]
        y = own // cells_z % cells_y + steps[1]
        z = own % cells_z + steps[2]
        need = sum(
            jnp.where(steps[axis] == 1, 1, jnp.where(steps[axis] == -1, 2, 0)) << (2 * axis)
            for axis in range(3)
        )
        return own, offset, need, x, y, z

    def inside(x, y, z):
        inner = (x >= 0) & (x < cells_x) & (y >= 0) & (y < cells_y)
        return inner & (z >= 0) & (z < cells_z)

    codes = tiles[0]
    total = codes.shape[0]
    codes = jnp.sort(codes + jnp.where(inside(*decode(codes)[3:]), 0, outside))
    inner_amount = jnp.sum((codes < outside).astype(jnp.int32))
    order = jnp.arange(total, dtype=jnp.int32)

    def listed(codes, amount, want_inside):
        own, offset, need, x, y, z = decode(codes & (outside - 1))
        if want_inside:
            near = (x * cells_y + y) * cells_z + z
        else:
            in_y = jnp.where(y < 0, starts[4], starts[5]) + (x + 1) * span_z + z + 1
            in_x = jnp.where(x < 0, starts[2], starts[3]) + y * span_z + z + 1
            in_z = jnp.where(z < 0, starts[0], starts[1]) + x * cells_y + y
            near = jnp.where(
                (y < 0) | (y >= cells_y), in_y, jnp.where((x < 0) | (x >= cells_x), in_x, in_z)
            )
        live = order < amount
        near = jnp.where(live, near, 0)
        return (
            near,
            near * 32 + jnp.where(live, offset, 0),
            jnp.where(live, need, 64),
            jnp.where(live, own, cells),
        )

    chunks = total + cells * GROUP // lanes + 3 * SPREAD
    group_top = chunks * (lanes // GROUP)

    def lists(near, need, own, amount, source):
        span = source.shape[0]
        return pl.pallas_call(
            list_kernel,
            out_shape=(
                jax.ShapeDtypeStruct((total, lanes), jnp.int32),
                jax.ShapeDtypeStruct((1, total), jnp.int32),
                jax.ShapeDtypeStruct((1, -(-group_top // lanes) * lanes + lanes), jnp.int32),
            ),
            in_specs=[smem] + [vmem] * 4,
            out_specs=(vmem, vmem, vmem),
            scratch_shapes=[
                pltpu.VMEM((-(-span // lanes) * lanes, lanes), jnp.float32),
                pltpu.VMEM((lanes, total), jnp.float32),
                pltpu.VMEM((cells, lanes), jnp.float32),
            ],
            compiler_params=params,
        )(amount[None], near[None], need[None], own[None], source.reshape(span * 8, lanes))

    force_shape = (cells + 8, 3, 8, lanes)
    scratch = [
        pltpu.VMEM((chunks, 8, lanes), jnp.float32),
        pltpu.VMEM((SPREAD * lanes, 8 * lanes), jnp.float32),
        pltpu.VMEM((SPREAD * lanes, 8 * lanes), jnp.float32),
    ]

    near, word, need, own = listed(codes, inner_amount, True)
    z_before, z_after, near, need, own = lax.optimization_barrier(
        (z_before, z_after, near, need, own)
    )
    x_before, x_after = exchange(
        jnp.concatenate([z_before[-1:], grid[-1:], z_after[-1:]], axis=2),
        jnp.concatenate([z_before[:1], grid[:1], z_after[:1]], axis=2),
        "gx",
    )
    slots, where, cell_of = lists(near, need, own, inner_amount, table)
    x_before, x_after, slots, where, cell_of = lax.optimization_barrier(
        (x_before, x_after, slots, where, cell_of)
    )

    def face(at):
        middle = jnp.concatenate([z_before[:, at], grid[:, at], z_after[:, at]], axis=2)
        return jnp.concatenate([x_before[:, at], middle, x_after[:, at]], axis=0)

    y_before, y_after = exchange(face(slice(-1, None)), face(slice(0, 1)), "gy")
    inner = pl.pallas_call(
        inner_kernel,
        out_shape=jax.ShapeDtypeStruct(force_shape, jnp.float32),
        in_specs=[smem] * 4 + [vmem] * 3,
        out_specs=vmem,
        scratch_shapes=scratch,
        compiler_params=params,
    )(inner_amount[None], where, word, cell_of, table, slots, shift)

    outer_amount = total - inner_amount
    codes = lax.dynamic_slice(jnp.concatenate([codes, codes]), (inner_amount,), (total,))
    near, word, need, own = listed(codes, outer_amount, False)
    halo = jnp.concatenate(
        [
            part.reshape(-1, 8, lanes)
            for part in (z_before, z_after, x_before, x_after, y_before, y_after)
        ],
        axis=0,
    )
    slots, where, cell_of = lists(near, need, own, outer_amount, halo)
    bricks = lax.axis_size(names)
    known = pl.pallas_call(
        outer_kernel,
        out_shape=jax.ShapeDtypeStruct((bricks, 8, lanes), jnp.float32),
        in_specs=[smem] * 4 + [vmem] * 8,
        out_specs=vmem,
        scratch_shapes=scratch
        + [pltpu.VMEM(force_shape, jnp.float32), pltpu.VMEM((16, 8, lanes), jnp.float32)],
        compiler_params=params,
    )(
        outer_amount[None],
        where,
        word,
        cell_of,
        table.reshape(cells * 8, lanes),
        halo,
        slots,
        shift,
        inner,
        flat_arms,
        flat_frag,
        fixed,
    )
    known = lax.all_to_all(known, names, split_axis=0, concat_axis=0, tiled=True)

    brick = lax.axis_index(names)
    mine = jnp.where(
        jnp.arange(lanes - held) < owned, brick * owned + jnp.arange(lanes - held), -2
    ).astype(jnp.float32)
    target = jnp.concatenate([mine, frag_key])[:, None]
    spheres, clumps = pl.pallas_call(
        functools.partial(move_kernel, owned),
        out_shape=(
            jax.ShapeDtypeStruct((6, cells, lanes), jnp.float32),
            jax.ShapeDtypeStruct((6, lanes), jnp.float32),
        ),
        in_specs=[vmem] * 5,
        out_specs=(vmem, vmem),
        compiler_params=params,
    )(target, known, flat_state, flat_arms, flat_frag)
    return (spheres.reshape((6,) + state.shape[1:]), clumps[:, :owned])


def solution(mesh):
    return jax.shard_map(
        local,
        mesh=mesh,
        in_specs=(
            P(None, "gx", "gy", "gz", None),
            P(None, "gx", "gy", "gz", None),
            P("gx", "gy", "gz", None),
            P(("gx", "gy", "gz"), None),
            P(("gx", "gy", "gz")),
            P(("gx", "gy", "gz"), None),
            P(None, ("gx", "gy", "gz")),
            P(("gx", "gy", "gz")),
            P(("gx", "gy", "gz")),
        ),
        out_specs=(P(None, "gx", "gy", "gz", None), P(None, ("gx", "gy", "gz"))),
        check_vma=False,
    )
```

```python
import functools

import jax
import jax.numpy as jnp
from jax import lax
from jax.experimental import pallas as pl
from jax.experimental.pallas import tpu as pltpu
from jax.sharding import PartitionSpec as P

stiffness = 100.0
damping = 2.0
time_step = 0.01
gravity = 9.81
epsilon_sq = 1e-08
radius_top = 0.14

GROUP = 32
FILL = 32
SPREAD_VALUES = 6
SPREAD = 4
VMEM = 56 * 1024 * 1024


def lanes_of(values, index):
    return jnp.take_along_axis(values, index, axis=1, mode="promise_in_bounds")


def split_rows(values):
    high = values.astype(jnp.bfloat16).astype(jnp.float32)
    rest = values - high
    middle = rest.astype(jnp.bfloat16).astype(jnp.float32)
    low = rest - middle
    return jnp.concatenate([high, middle, low], axis=0).astype(jnp.bfloat16)


def joined_rows(stacked):
    rows = stacked.shape[0] // 3
    return stacked[0:rows] + stacked[rows : 2 * rows] + stacked[2 * rows :]


def dot_lanes(first, second):
    return lax.dot_general(
        first, second, (((1,), (1,)), ((), ())), preferred_element_type=jnp.float32
    )


def exchange(last, initial, axis):
    devices = lax.axis_size(axis)
    up = [(i, (i + 1) % devices) for i in range(devices)]
    down = [(j, i) for i, j in up]
    return lax.ppermute(last, axis, up), lax.ppermute(initial, axis, down)


def pack_kernel(state_ref, frag_ref, key_ref, out_ref):
    cells = frag_ref.shape[0]
    for comp in range(7):
        out_ref[:, comp, :] = state_ref[comp]
    keys = jnp.broadcast_to(key_ref[0:1, :], (8, key_ref.shape[1]))
    for block in range(cells // 8):
        rows = pl.ds(block * 8, 8)
        out_ref[rows, 7, :] = lanes_of(keys, frag_ref[rows, :])


def list_kernel(
    amount_smem, near_ref, need_ref, own_ref, table_ref, slots_ref, where_ref, cell_ref, class_ref, member_ref, count_ref
):
    tiles, lanes = slots_ref.shape
    span = table_ref.shape[0] // 8
    padded = class_ref.shape[0]
    cells = count_ref.shape[0]
    wide = 256

    def plane(comp):
        return table_ref[pl.ds(comp, span, stride=8), :]

    def flag(value):
        return value.astype(jnp.float32).astype(jnp.bfloat16)

    def dot(first, second):
        return jnp.dot(first, second, preferred_element_type=jnp.float32)

    def ramp(shape, axis):
        return lax.broadcasted_iota(jnp.int32, shape, axis)

    radius = plane(6) + (radius_top + 1e-5)
    classes = jnp.zeros((span, lanes), jnp.float32)
    for axis in range(3):
        place = plane(axis)
        classes = classes + jnp.where(place < radius, 1.0 * (1 << (2 * axis)), 0.0)
        classes = classes + jnp.where(place > 1.0 - radius, 1.0 * (2 << (2 * axis)), 0.0)
    class_ref[...] = jnp.zeros(class_ref.shape, jnp.float32)
    class_ref[pl.ds(0, span), :] = classes
    codes = jnp.concatenate(
        [class_ref[pl.ds(at, lanes), :].T for at in range(0, padded, lanes)], axis=1
    ).astype(jnp.bfloat16)
    ones = jnp.ones((lanes, lanes), jnp.bfloat16)
    count_ref[...] = jnp.zeros(count_ref.shape, jnp.float32)

    pair = 2 * wide
    blocks = lax.div(amount_smem[0] + (pair - 1), pair)

    def choose(block, unused):
        held = []
        for half in range(2):
            at = pl.ds(pl.multiple_of(block * pair + half * wide, wide), wide)
            hits = flag(ramp((padded, wide), 0) == near_ref[:, at])
            found = dot(codes, hits).astype(jnp.int32)
            need = need_ref[:, at]
            member = ((found & need) == need).astype(jnp.float32)
            member_ref[:, at] = member
            count = dot(ones, member.astype(jnp.bfloat16))
            mine = flag(ramp((cells, wide), 0) == own_ref[:, at])
            held.append(dot_lanes(mine, count.astype(jnp.bfloat16)))
        count_ref[...] += held[0] + held[1]
        return unused

    lax.fori_loop(0, blocks, choose, 0)

    held = count_ref[...]
    high = jnp.floor(held * (1.0 / lanes))
    low = held - lanes * high
    taken = jnp.floor((held + (GROUP - 1)) * (1.0 / GROUP))
    upto = flag(ramp((cells, cells), 1) <= ramp((cells, cells), 0))
    ends = dot(upto, taken.astype(jnp.bfloat16))
    cell_ones = jnp.ones((8, cells), jnp.bfloat16)
    group_blocks = cell_ref.shape[1] // lanes - 1

    def name_groups(block, unused):
        group = (ramp((cells, lanes), 1) + block * lanes).astype(jnp.float32)
        over = dot(cell_ones, flag(ends <= group))
        at = pl.ds(pl.multiple_of(block * lanes, lanes), lanes)
        cell_ref[:, at] = over[0:1].astype(jnp.int32)
        return unused

    used = jnp.max(ends).astype(jnp.int32)
    needed = jnp.minimum((used >> (lanes.bit_length() - 1)) + 2, group_blocks)
    lax.fori_loop(0, needed, name_groups, 0)
    cell_ref[:, pl.ds(group_blocks * lanes, lanes)] = ends[cells - 1 : cells].astype(jnp.int32)
    before_cell = jnp.concatenate(
        [value.T[0:8] for value in (taken, high, low)], axis=0
    ).astype(jnp.bfloat16)

    earlier = flag(ramp((lanes, lanes), 1) < ramp((lanes, lanes), 0))
    earlier_tile = flag(ramp((wide, wide), 0) < ramp((wide, wide), 1))

    def place(block, done):
        for half in range(2):
            at = pl.ds(pl.multiple_of(block * pair + half * wide, wide), wide)
            flags = member_ref[:, at].astype(jnp.bfloat16)
            count = dot(ones, flags)
            lower = flag(ramp((cells, wide), 0) < own_ref[:, at])
            before = dot(before_cell, lower)
            so_far = dot(count[0:8].astype(jnp.bfloat16), earlier_tile) + done
            start = GROUP * before[0:8] + so_far - (lanes * before[8:16] + before[16:24])
            start = start.astype(jnp.int32)[0:1]
            where_ref[:, at] = start * 256 + count[0:1].astype(jnp.int32)
            rank = dot(earlier, flags)
            slot = ramp((lanes, wide), 0)
            moves = slot - rank.astype(jnp.int32)
            word = jnp.where(member_ref[:, at] > 0.0, slot + lanes * moves, 0)
            bit = 1
            while bit < lanes:
                keep = jnp.where((word & (bit * lanes)) != 0, 0, word)
                gone = word ^ keep
                word = keep | jnp.concatenate([gone[bit:], gone[:bit]], axis=0)
                bit *= 2
            word = word & (lanes - 1)
            turn = jnp.broadcast_to(start, (lanes, wide))
            bit = 1
            while bit < lanes:
                moved = jnp.concatenate([word[lanes - bit :], word[: lanes - bit]], axis=0)
                word = jnp.where((turn & bit) != 0, moved, word)
                bit *= 2
            for part in range(wide // lanes):
                first = block * pair + half * wide + part * lanes
                rows = pl.ds(pl.multiple_of(first, lanes), lanes)
                slots_ref[rows, :] = word[:, part * lanes : (part + 1) * lanes].T
            done = done + jnp.sum(count[0:8], axis=1, keepdims=True)
        return done

    lax.fori_loop(0, blocks, place, jnp.zeros((8, 1), jnp.float32))


def fill_lists(amount, where_smem, near_smem, table_ref, slots_ref, shift_ref, list_ref):
    tiles, lanes = slots_ref.shape
    lane_bits = lanes.bit_length() - 1
    lane = lax.broadcasted_iota(jnp.int32, (8, lanes), 1)
    row = lax.broadcasted_iota(jnp.int32, (8, lanes), 0)
    absent = jnp.where(row == 6, -10.0, 0.0)
    for kind in range(27):
        steps = (kind // 9 - 1.0, kind // 3 % 3 - 1.0, kind % 3 - 1.0)
        shift_ref[kind] = sum(jnp.where(row == axis, steps[axis], 0.0) for axis in range(3))

    def fill(block, carry):
        last_chunk, last_new, last_held = carry
        units = range(FILL)
        where = [where_smem[0, block * FILL + unit] for unit in units]
        near = [near_smem[block * FILL + unit] for unit in units]
        found = []
        for unit in units:
            slots = slots_ref[pl.ds(block * FILL + unit, 8, stride=0), :]
            cell = table_ref[near[unit] >> 5]
            found.append(lanes_of(cell, slots) + shift_ref[near[unit] & 31])
        for unit in units:
            amount = where[unit] & 255
            chunk = where[unit] >> (8 + lane_bits)
            offset = (where[unit] >> 8) & (lanes - 1)
            new = jnp.where(((lane - offset) & (lanes - 1)) < amount, found[unit], absent)
            held_row = jnp.where(chunk != last_chunk, last_new, last_held)
            held_row = jnp.where(lane >= offset, new, held_row)
            new = jnp.where(lane >= offset, absent, new)
            list_ref[chunk] = held_row
            list_ref[chunk + 1] = new
            last_chunk, last_new, last_held = chunk, new, held_row
        return last_chunk, last_new, last_held

    blocks = lax.div(amount + (FILL - 1), FILL)
    lax.fori_loop(0, blocks, fill, (jnp.int32(0), absent, absent))


def pair_forces(cell_smem, table_ref, list_ref, force_ref, even_ref, odd_ref, turned_ref):
    lanes = table_ref.shape[1]
    cells = table_ref.shape[0] // 8
    rows = even_ref.shape[0]
    chunks = rows // lanes
    units = rows // GROUP
    groups = cell_smem[0, cell_smem.shape[1] - lanes]
    force_ref[...] = jnp.zeros(force_ref.shape, jnp.float32)
    spread_count = even_ref.shape[1] // lanes
    part = lax.broadcasted_iota(jnp.int32, (32, spread_count * lanes), 0)
    comp = lax.broadcasted_iota(jnp.int32, (32, spread_count * lanes), 1) // lanes
    weights = jnp.where((part < 24) & (part % 8 == comp), 1.0, 0.0).astype(jnp.bfloat16)

    def spread(step, out_ref):
        turned = []
        for piece in range(chunks):
            values = list_ref[step * chunks + piece]
            high = values.astype(jnp.bfloat16).astype(jnp.float32)
            rest = values - high
            middle = rest.astype(jnp.bfloat16).astype(jnp.float32)
            parts = jnp.concatenate([high, middle, rest - middle, jnp.zeros_like(values)], axis=0)
            turned.append(parts.astype(jnp.bfloat16).T)
        turned = jnp.concatenate(turned, axis=0)
        out_ref[...] = jnp.dot(turned, weights, preferred_element_type=jnp.float32)

    def pairs(step, wide_ref, carry):
        last, running = carry
        for unit in range(units):
            cell = cell_smem[0, step * units + unit]
            own = jnp.minimum(cell, cells - 1) * 8
            other = [
                wide_ref[pl.ds(unit * GROUP, GROUP), pl.ds(value * lanes, lanes)].reshape(
                    GROUP // 8, 8, lanes
                )
                for value in range(spread_count)
            ]
            chunk = step * chunks + unit // (lanes // GROUP)
            at = (chunk >> 4) * lanes + unit % (lanes // GROUP) * GROUP
            turned = turned_ref[pl.ds(pl.multiple_of(at, GROUP), GROUP), :]
            for value in range(spread_count, 8):
                column = jnp.full((GROUP, lanes), (chunk & 15) * 8 + value, jnp.int32)
                other.append(lanes_of(turned, column).reshape(GROUP // 8, 8, lanes))
            mine = [table_ref[pl.ds(own + value, 8, stride=0), :][None] for value in range(8)]
            apart = [other[axis] - mine[axis] for axis in range(3)]
            square = apart[0] * apart[0] + apart[1] * apart[1] + apart[2] * apart[2] + epsilon_sq
            inverse = lax.rsqrt(square)
            reach = other[6] + mine[6]
            overlap = jnp.maximum(reach - square * inverse, 0.0)
            overlap = jnp.where(other[7] != mine[7], overlap, 0.0)
            closing = (
                (other[3] - mine[3]) * apart[0]
                + (other[4] - mine[4]) * apart[1]
                + (other[5] - mine[5]) * apart[2]
            )
            scaled = overlap * (other[6] * mine[6])
            root = scaled * lax.rsqrt(jnp.maximum(scaled * reach, 1e-30))
            factor = root * inverse * (stiffness / damping * overlap - closing * inverse)
            running = [
                jnp.sum(factor * apart[axis], axis=0)
                + jnp.where(cell == last, running[axis], 0.0)
                for axis in range(3)
            ]
            last = cell
            for axis in range(3):
                force_ref[cell, axis] = running[axis]
        return last, running

    def turn(block, unused):
        rows = pl.ds(pl.multiple_of(block * lanes, lanes), lanes)
        some = pl.ds(pl.multiple_of(block * 16, 16), 16)
        turned_ref[rows, :] = list_ref[some].reshape(lanes, lanes).T
        return unused

    group_bits = (16 * lanes // GROUP).bit_length() - 1
    lax.fori_loop(0, (groups >> group_bits) + 1, turn, 0)
    spread(0, even_ref)

    def both(step, carry):
        spread(2 * step + 1, odd_ref)
        carry = pairs(2 * step, even_ref, carry)
        spread(2 * step + 2, even_ref)
        return pairs(2 * step + 1, odd_ref, carry)

    zero = jnp.zeros((8, lanes), jnp.float32)
    steps = lax.div(groups + (2 * units - 1), 2 * units)
    lax.fori_loop(0, steps, both, (jnp.int32(-1), [zero] * 3))


def inner_kernel(
    amount_smem, where_smem, near_smem, cell_smem, table_ref, slots_ref,
    force_ref, list_ref, even_ref, odd_ref, turned_ref, shift_ref,
):
    cells = table_ref.shape[0]
    fill_lists(amount_smem[0], where_smem, near_smem, table_ref, slots_ref, shift_ref, list_ref)
    flat = table_ref.reshape(cells * 8, table_ref.shape[2])
    pair_forces(cell_smem, flat, list_ref, force_ref, even_ref, odd_ref, turned_ref)


def outer_kernel(
    amount_smem, where_smem, near_smem, cell_smem, table_ref, halo_ref, slots_ref,
    inner_ref, arms_ref, frag_ref, fixed_ref, out_ref, list_ref, even_ref, odd_ref, turned_ref,
    shift_ref, force_ref, loads_ref,
):
    held = fixed_ref.shape[1] // 2
    fill_lists(amount_smem[0], where_smem, near_smem, halo_ref, slots_ref, shift_ref, list_ref)
    pair_forces(cell_smem, table_ref, list_ref, force_ref, even_ref, odd_ref, turned_ref)
    sums = fragment_sums(inner_ref, force_ref, arms_ref, frag_ref, loads_ref, held)
    out = fixed_ref[...] + jnp.concatenate([sums, jnp.zeros_like(sums)], axis=1)
    for brick in range(out_ref.shape[0]):
        out_ref[brick] = out


def fragment_sums(inner_ref, outer_ref, arms_ref, frag_ref, loads_ref, held):
    cells, lanes = frag_ref.shape
    tall = loads_ref.shape[0]
    label = lax.broadcasted_iota(jnp.int32, (held, lanes), 0)

    def gather_sums(block, total):
        rows = pl.ds(pl.multiple_of(block * tall, tall), tall)
        force = [
            -damping * jnp.sum(inner_ref[rows, axis] + outer_ref[rows, axis], axis=1)
            for axis in range(3)
        ]
        lever = [arms_ref[axis, rows, :] for axis in range(3)]
        torque = [
            lever[1] * force[2] - lever[2] * force[1],
            lever[2] * force[0] - lever[0] * force[2],
            lever[0] * force[1] - lever[1] * force[0],
        ]
        loads = force + torque + [jnp.zeros_like(force[0])] * 2
        for comp in range(8):
            loads_ref[:, comp, :] = loads[comp]
        frags = frag_ref[rows, :]
        hits = [
            (frags[unit : unit + 1, :] == label).astype(jnp.float32).astype(jnp.bfloat16)
            for unit in range(tall)
        ]
        values = [split_rows(loads_ref[unit]) for unit in range(tall)]
        return total + dot_lanes(jnp.concatenate(values, axis=1), jnp.concatenate(hits, axis=1))

    total = lax.fori_loop(0, cells // tall, gather_sums, jnp.zeros((24, held), jnp.float32))
    return joined_rows(total)


def move_kernel(
    owned, target_ref, known_ref, state_ref, arms_ref, frag_ref, spheres_ref, clumps_ref
):
    bricks, _, lanes = known_ref.shape
    held = lanes // 2
    cells = frag_ref.shape[0]
    targets = jnp.broadcast_to(target_ref[...], (lanes, lanes))
    lane = lax.broadcasted_iota(jnp.int32, (1, lanes), 1)

    def match(block, carry):
        sums, base = carry
        for unit in range(8):
            brick = block * 8 + unit
            known = known_ref[brick]
            values = split_rows(known)
            key = jnp.where(lane < held, known[6:7], -1.0)
            number = jnp.where(
                (lane >= held) & (lane < held + owned), brick * owned + lane - held, -1
            ).astype(jnp.float32)
            sums = sums + dot_lanes(values, (targets == key).astype(jnp.float32).astype(jnp.bfloat16))
            base = base + dot_lanes(values, (targets == number).astype(jnp.float32).astype(jnp.bfloat16))
        return sums, base

    zero = jnp.zeros((24, lanes), jnp.float32)
    sums, base = lax.fori_loop(0, bricks // 8, match, (zero, zero))
    sums = joined_rows(sums)
    base = joined_rows(base)
    rows = []
    for axis in range(3):
        pull = gravity if axis == 2 else 0.0
        rows.append(
            base[axis : axis + 1]
            + time_step * (sums[axis : axis + 1] * base[6:7] - pull)
        )
    for axis in range(3, 6):
        rows.append(base[axis : axis + 1] + time_step * sums[axis : axis + 1] * base[7:8])
    for comp in range(6):
        clumps_ref[comp : comp + 1, :] = rows[comp]
    tall = 32
    wide = [jnp.broadcast_to(value, (tall, lanes)) for value in rows]

    def cross(first, second):
        return [
            first[1] * second[2] - first[2] * second[1],
            first[2] * second[0] - first[0] * second[2],
            first[0] * second[1] - first[1] * second[0],
        ]

    def move(block, unused):
        at = pl.ds(pl.multiple_of(block * tall, tall), tall)
        index = frag_ref[at, :] + (lanes - held)
        motion = [lanes_of(value, index) for value in wide]
        velocity, spin = motion[0:3], motion[3:6]
        arm = [arms_ref[axis, at, :] for axis in range(3)]
        half = [0.5 * time_step * value for value in spin]
        turned = cross(half, arm)
        twice = cross(half, turned)
        scale = 2.0 / (1.0 + half[0] * half[0] + half[1] * half[1] + half[2] * half[2])
        change = [scale * (turned[axis] + twice[axis]) for axis in range(3)]
        new_arm = [arm[axis] + change[axis] for axis in range(3)]
        swing = cross(spin, new_arm)
        for axis in range(3):
            spheres_ref[axis, at, :] = (
                state_ref[axis, at, :] + time_step * velocity[axis] + (new_arm[axis] - arm[axis])
            )
            spheres_ref[3 + axis, at, :] = velocity[axis] + swing[axis]
        return unused

    lax.fori_loop(0, cells // tall, move, 0)


def local(
    state, arms, sphere_frag, frag_owner, frag_clump, tiles, clump_motion, inv_mass, inv_moment
):
    cells_x, cells_y, cells_z = (state.shape[1], state.shape[2], state.shape[3])
    lanes = state.shape[4]
    cells = cells_x * cells_y * cells_z
    owned = inv_mass.shape[0]
    held = frag_clump.shape[0]
    names = ("gx", "gy", "gz")
    vmem = pl.BlockSpec(memory_space=pltpu.VMEM)
    smem = pl.BlockSpec(memory_space=pltpu.SMEM)
    params = pltpu.CompilerParams(vmem_limit_bytes=VMEM)

    frag_key = (frag_owner[:, 0] * owned + frag_clump).astype(jnp.float32)
    flat_state = state.reshape(7, cells, lanes)
    flat_arms = arms.reshape(3, cells, lanes)
    flat_frag = sphere_frag.reshape(cells, lanes)

    fixed = jnp.concatenate(
        [
            jnp.concatenate([jnp.zeros((6, held)), frag_key[None], jnp.zeros((1, held))], axis=0),
            jnp.concatenate([clump_motion, inv_mass[None], inv_moment[None]], axis=0),
            jnp.zeros((8, lanes - held - owned)),
        ],
        axis=1,
    )

    table = pl.pallas_call(
        pack_kernel,
        out_shape=jax.ShapeDtypeStruct((cells, 8, lanes), jnp.float32),
        in_specs=[vmem] * 3,
        out_specs=vmem,
        compiler_params=params,
    )(flat_state, flat_frag, jnp.pad(frag_key, (0, lanes - held))[None])
    grid = table.reshape(cells_x, cells_y, cells_z, 8, lanes)
    z_before, z_after = exchange(grid[:, :, -1:], grid[:, :, :1], "gz")

    outside = 1 << 20
    span_z = cells_z + 2
    starts = [0, cells_x * cells_y, 2 * cells_x * cells_y]
    starts += [starts[-1] + cells_y * span_z, starts[-1] + 2 * cells_y * span_z]
    starts += [starts[-1] + (cells_x + 2) * span_z]

    def decode(codes):
        own, offset = (codes // 27, codes % 27)
        steps = (offset // 9 - 1, offset // 3 % 3 - 1, offset % 3 - 1)
        x = own // (cells_y * cells_z) + steps[0]
        y = own // cells_z % cells_y + steps[1]
        z = own % cells_z + steps[2]
        need = sum(
            jnp.where(steps[axis] == 1, 1, jnp.where(steps[axis] == -1, 2, 0)) << (2 * axis)
            for axis in range(3)
        )
        return own, offset, need, x, y, z

    def inside(x, y, z):
        inner = (x >= 0) & (x < cells_x) & (y >= 0) & (y < cells_y)
        return inner & (z >= 0) & (z < cells_z)

    codes = tiles[0]
    total = codes.shape[0]
    codes = jnp.sort(codes + jnp.where(inside(*decode(codes)[3:]), 0, outside))
    inner_amount = jnp.sum((codes < outside).astype(jnp.int32))
    order = jnp.arange(total, dtype=jnp.int32)

    def listed(codes, amount, want_inside):
        own, offset, need, x, y, z = decode(codes & (outside - 1))
        if want_inside:
            near = (x * cells_y + y) * cells_z + z
        else:
            in_y = jnp.where(y < 0, starts[4], starts[5]) + (x + 1) * span_z + z + 1
            in_x = jnp.where(x < 0, starts[2], starts[3]) + y * span_z + z + 1
            in_z = jnp.where(z < 0, starts[0], starts[1]) + x * cells_y + y
            near = jnp.where(
                (y < 0) | (y >= cells_y), in_y, jnp.where((x < 0) | (x >= cells_x), in_x, in_z)
            )
        live = order < amount
        near = jnp.where(live, near, 0)
        return (
            near,
            near * 32 + jnp.where(live, offset, 0),
            jnp.where(live, need, 64),
            jnp.where(live, own, cells),
        )

    chunks = -(-(total + cells * GROUP // lanes + 3 * SPREAD) // 16) * 16
    group_top = chunks * (lanes // GROUP)

    def lists(near, need, own, amount, source):
        span = source.shape[0]
        return pl.pallas_call(
            list_kernel,
            out_shape=(
                jax.ShapeDtypeStruct((total, lanes), jnp.int32),
                jax.ShapeDtypeStruct((1, total), jnp.int32),
                jax.ShapeDtypeStruct((1, -(-group_top // lanes) * lanes + lanes), jnp.int32),
            ),
            in_specs=[smem] + [vmem] * 4,
            out_specs=(vmem, vmem, vmem),
            scratch_shapes=[
                pltpu.VMEM((-(-span // lanes) * lanes, lanes), jnp.float32),
                pltpu.VMEM((lanes, total), jnp.float32),
                pltpu.VMEM((cells, lanes), jnp.float32),
            ],
            compiler_params=params,
        )(amount[None], near[None], need[None], own[None], source.reshape(span * 8, lanes))

    force_shape = (cells + 8, 3, 8, lanes)
    scratch = [
        pltpu.VMEM((chunks, 8, lanes), jnp.float32),
        pltpu.VMEM((SPREAD * lanes, SPREAD_VALUES * lanes), jnp.float32),
        pltpu.VMEM((SPREAD * lanes, SPREAD_VALUES * lanes), jnp.float32),
        pltpu.VMEM((chunks * 8, lanes), jnp.float32),
        pltpu.VMEM((27, 8, lanes), jnp.float32),
    ]

    near, word, need, own = listed(codes, inner_amount, True)
    z_before, z_after, near, need, own = lax.optimization_barrier(
        (z_before, z_after, near, need, own)
    )
    x_before, x_after = exchange(
        jnp.concatenate([z_before[-1:], grid[-1:], z_after[-1:]], axis=2),
        jnp.concatenate([z_before[:1], grid[:1], z_after[:1]], axis=2),
        "gx",
    )
    slots, where, cell_of = lists(near, need, own, inner_amount, table)
    x_before, x_after, slots, where, cell_of = lax.optimization_barrier(
        (x_before, x_after, slots, where, cell_of)
    )

    def face(at):
        middle = jnp.concatenate([z_before[:, at], grid[:, at], z_after[:, at]], axis=2)
        return jnp.concatenate([x_before[:, at], middle, x_after[:, at]], axis=0)

    y_before, y_after = exchange(face(slice(-1, None)), face(slice(0, 1)), "gy")
    inner = pl.pallas_call(
        inner_kernel,
        out_shape=jax.ShapeDtypeStruct(force_shape, jnp.float32),
        in_specs=[smem] * 4 + [vmem] * 2,
        out_specs=vmem,
        scratch_shapes=scratch,
        compiler_params=params,
    )(inner_amount[None], where, word, cell_of, table, slots)

    outer_amount = total - inner_amount
    codes = lax.dynamic_slice(jnp.concatenate([codes, codes]), (inner_amount,), (total,))
    near, word, need, own = listed(codes, outer_amount, False)
    halo = jnp.concatenate(
        [
            part.reshape(-1, 8, lanes)
            for part in (z_before, z_after, x_before, x_after, y_before, y_after)
        ],
        axis=0,
    )
    slots, where, cell_of = lists(near, need, own, outer_amount, halo)
    bricks = lax.axis_size(names)
    known = pl.pallas_call(
        outer_kernel,
        out_shape=jax.ShapeDtypeStruct((bricks, 8, lanes), jnp.float32),
        in_specs=[smem] * 4 + [vmem] * 7,
        out_specs=vmem,
        scratch_shapes=scratch
        + [pltpu.VMEM(force_shape, jnp.float32), pltpu.VMEM((16, 8, lanes), jnp.float32)],
        compiler_params=params,
    )(
        outer_amount[None],
        where,
        word,
        cell_of,
        table.reshape(cells * 8, lanes),
        halo,
        slots,
        inner,
        flat_arms,
        flat_frag,
        fixed,
    )
    known = lax.all_to_all(known, names, split_axis=0, concat_axis=0, tiled=True)

    brick = lax.axis_index(names)
    mine = jnp.where(
        jnp.arange(lanes - held) < owned, brick * owned + jnp.arange(lanes - held), -2
    ).astype(jnp.float32)
    target = jnp.concatenate([mine, frag_key])[:, None]
    spheres, clumps = pl.pallas_call(
        functools.partial(move_kernel, owned),
        out_shape=(
            jax.ShapeDtypeStruct((6, cells, lanes), jnp.float32),
            jax.ShapeDtypeStruct((6, lanes), jnp.float32),
        ),
        in_specs=[vmem] * 5,
        out_specs=(vmem, vmem),
        compiler_params=params,
    )(target, known, flat_state, flat_arms, flat_frag)
    return (spheres.reshape((6,) + state.shape[1:]), clumps[:, :owned])


def solution(mesh):
    return jax.shard_map(
        local,
        mesh=mesh,
        in_specs=(
            P(None, "gx", "gy", "gz", None),
            P(None, "gx", "gy", "gz", None),
            P("gx", "gy", "gz", None),
            P(("gx", "gy", "gz"), None),
            P(("gx", "gy", "gz")),
            P(("gx", "gy", "gz"), None),
            P(None, ("gx", "gy", "gz")),
            P(("gx", "gy", "gz")),
            P(("gx", "gy", "gz")),
        ),
        out_specs=(P(None, "gx", "gy", "gz", None), P(None, ("gx", "gy", "gz"))),
        check_vma=False,
    )
```

```python
import functools

import jax
import jax.numpy as jnp
from jax import lax
from jax.experimental import pallas as pl
from jax.experimental.pallas import tpu as pltpu
from jax.sharding import PartitionSpec as P

stiffness = 100.0
damping = 2.0
time_step = 0.01
gravity = 9.81
epsilon_sq = 1e-08
radius_top = 0.14

GROUP = 32
FILL = 32
SPREAD = 4
VMEM = 56 * 1024 * 1024


def lanes_of(values, index):
    return jnp.take_along_axis(values, index, axis=1, mode="promise_in_bounds")


def split_rows(values):
    high = values.astype(jnp.bfloat16).astype(jnp.float32)
    rest = values - high
    middle = rest.astype(jnp.bfloat16).astype(jnp.float32)
    low = rest - middle
    return jnp.concatenate([high, middle, low], axis=0).astype(jnp.bfloat16)


def joined_rows(stacked):
    rows = stacked.shape[0] // 3
    return stacked[0:rows] + stacked[rows : 2 * rows] + stacked[2 * rows :]


def dot_lanes(first, second):
    return lax.dot_general(
        first, second, (((1,), (1,)), ((), ())), preferred_element_type=jnp.float32
    )


def exchange(last, initial, axis):
    devices = lax.axis_size(axis)
    up = [(i, (i + 1) % devices) for i in range(devices)]
    down = [(j, i) for i, j in up]
    return lax.ppermute(last, axis, up), lax.ppermute(initial, axis, down)


def pack_kernel(state_ref, frag_ref, key_ref, out_ref):
    cells = frag_ref.shape[0]
    for comp in range(7):
        out_ref[:, comp, :] = state_ref[comp]
    keys = jnp.broadcast_to(key_ref[0:1, :], (8, key_ref.shape[1]))
    for block in range(cells // 8):
        rows = pl.ds(block * 8, 8)
        out_ref[rows, 7, :] = lanes_of(keys, frag_ref[rows, :])


def list_kernel(
    amount_smem, near_ref, need_ref, own_ref, table_ref, slots_ref, where_ref, cell_ref, class_ref, member_ref, count_ref
):
    tiles, lanes = slots_ref.shape
    span = table_ref.shape[0] // 8
    padded = class_ref.shape[0]
    cells = count_ref.shape[0]
    wide = 256

    def plane(comp):
        return table_ref[pl.ds(comp, span, stride=8), :]

    def flag(value):
        return value.astype(jnp.float32).astype(jnp.bfloat16)

    def dot(first, second):
        return jnp.dot(first, second, preferred_element_type=jnp.float32)

    def ramp(shape, axis):
        return lax.broadcasted_iota(jnp.int32, shape, axis)

    radius = plane(6) + (radius_top + 1e-5)
    classes = jnp.zeros((span, lanes), jnp.float32)
    for axis in range(3):
        place = plane(axis)
        classes = classes + jnp.where(place < radius, 1.0 * (1 << (2 * axis)), 0.0)
        classes = classes + jnp.where(place > 1.0 - radius, 1.0 * (2 << (2 * axis)), 0.0)
    class_ref[...] = jnp.zeros(class_ref.shape, jnp.float32)
    class_ref[pl.ds(0, span), :] = classes
    codes = jnp.concatenate(
        [class_ref[pl.ds(at, lanes), :].T for at in range(0, padded, lanes)], axis=1
    ).astype(jnp.bfloat16)
    ones = jnp.ones((lanes, lanes), jnp.bfloat16)
    count_ref[...] = jnp.zeros(count_ref.shape, jnp.float32)

    pair = 2 * wide
    blocks = lax.div(amount_smem[0] + (pair - 1), pair)

    def choose(block, unused):
        held = []
        for half in range(2):
            at = pl.ds(pl.multiple_of(block * pair + half * wide, wide), wide)
            hits = flag(ramp((padded, wide), 0) == near_ref[:, at])
            found = dot(codes, hits).astype(jnp.int32)
            need = need_ref[:, at]
            member = ((found & need) == need).astype(jnp.float32)
            member_ref[:, at] = member
            count = dot(ones, member.astype(jnp.bfloat16))
            mine = flag(ramp((cells, wide), 0) == own_ref[:, at])
            held.append(dot_lanes(mine, count.astype(jnp.bfloat16)))
        count_ref[...] += held[0] + held[1]
        return unused

    lax.fori_loop(0, blocks, choose, 0)

    held = count_ref[...]
    high = jnp.floor(held * (1.0 / lanes))
    low = held - lanes * high
    taken = jnp.floor((held + (GROUP - 1)) * (1.0 / GROUP))
    upto = flag(ramp((cells, cells), 1) <= ramp((cells, cells), 0))
    ends = dot(upto, taken.astype(jnp.bfloat16))
    cell_ones = jnp.ones((8, cells), jnp.bfloat16)
    group_blocks = cell_ref.shape[1] // lanes - 1

    def name_groups(block, unused):
        group = (ramp((cells, lanes), 1) + block * lanes).astype(jnp.float32)
        over = dot(cell_ones, flag(ends <= group))
        at = pl.ds(pl.multiple_of(block * lanes, lanes), lanes)
        cell_ref[:, at] = over[0:1].astype(jnp.int32)
        return unused

    used = jnp.max(ends).astype(jnp.int32)
    needed = jnp.minimum((used >> (lanes.bit_length() - 1)) + 2, group_blocks)
    lax.fori_loop(0, needed, name_groups, 0)
    cell_ref[:, pl.ds(group_blocks * lanes, lanes)] = ends[cells - 1 : cells].astype(jnp.int32)
    before_cell = jnp.concatenate(
        [value.T[0:8] for value in (taken, high, low)], axis=0
    ).astype(jnp.bfloat16)

    earlier = flag(ramp((lanes, lanes), 1) < ramp((lanes, lanes), 0))
    earlier_tile = flag(ramp((wide, wide), 0) < ramp((wide, wide), 1))

    def place(block, done):
        for half in range(2):
            at = pl.ds(pl.multiple_of(block * pair + half * wide, wide), wide)
            flags = member_ref[:, at].astype(jnp.bfloat16)
            count = dot(ones, flags)
            lower = flag(ramp((cells, wide), 0) < own_ref[:, at])
            before = dot(before_cell, lower)
            so_far = dot(count[0:8].astype(jnp.bfloat16), earlier_tile) + done
            start = GROUP * before[0:8] + so_far - (lanes * before[8:16] + before[16:24])
            start = start.astype(jnp.int32)[0:1]
            where_ref[:, at] = start * 256 + count[0:1].astype(jnp.int32)
            rank = dot(earlier, flags)
            slot = ramp((lanes, wide), 0)
            moves = slot - rank.astype(jnp.int32)
            word = jnp.where(member_ref[:, at] > 0.0, slot + lanes * moves, 0)
            bit = 1
            while bit < lanes:
                keep = jnp.where((word & (bit * lanes)) != 0, 0, word)
                gone = word ^ keep
                word = keep | jnp.concatenate([gone[bit:], gone[:bit]], axis=0)
                bit *= 2
            word = word & (lanes - 1)
            turn = jnp.broadcast_to(start, (lanes, wide))
            bit = 1
            while bit < lanes:
                moved = jnp.concatenate([word[lanes - bit :], word[: lanes - bit]], axis=0)
                word = jnp.where((turn & bit) != 0, moved, word)
                bit *= 2
            for part in range(wide // lanes):
                first = block * pair + half * wide + part * lanes
                rows = pl.ds(pl.multiple_of(first, lanes), lanes)
                slots_ref[rows, :] = word[:, part * lanes : (part + 1) * lanes].T
            done = done + jnp.sum(count[0:8], axis=1, keepdims=True)
        return done

    lax.fori_loop(0, blocks, place, jnp.zeros((8, 1), jnp.float32))


def fill_lists(amount, where_smem, near_smem, table_ref, slots_ref, shift_ref, list_ref):
    tiles, lanes = slots_ref.shape
    lane_bits = lanes.bit_length() - 1
    lane = lax.broadcasted_iota(jnp.int32, (8, lanes), 1)
    row = lax.broadcasted_iota(jnp.int32, (8, lanes), 0)
    absent = jnp.where(row == 6, -10.0, 0.0)
    for kind in range(27):
        steps = (kind // 9 - 1.0, kind // 3 % 3 - 1.0, kind % 3 - 1.0)
        shift_ref[kind] = sum(jnp.where(row == axis, steps[axis], 0.0) for axis in range(3))

    def fill(block, carry):
        last_chunk, last_new, last_held = carry
        units = range(FILL)
        where = [where_smem[0, block * FILL + unit] for unit in units]
        near = [near_smem[block * FILL + unit] for unit in units]
        found = []
        for unit in units:
            slots = slots_ref[pl.ds(block * FILL + unit, 8, stride=0), :]
            cell = table_ref[near[unit] >> 5]
            found.append(lanes_of(cell, slots) + shift_ref[near[unit] & 31])
        for unit in units:
            amount = where[unit] & 255
            chunk = where[unit] >> (8 + lane_bits)
            offset = (where[unit] >> 8) & (lanes - 1)
            new = jnp.where(((lane - offset) & (lanes - 1)) < amount, found[unit], absent)
            held_row = jnp.where(chunk != last_chunk, last_new, last_held)
            held_row = jnp.where(lane >= offset, new, held_row)
            new = jnp.where(lane >= offset, absent, new)
            list_ref[chunk] = held_row
            list_ref[chunk + 1] = new
            last_chunk, last_new, last_held = chunk, new, held_row
        return last_chunk, last_new, last_held

    blocks = lax.div(amount + (FILL - 1), FILL)
    lax.fori_loop(0, blocks, fill, (jnp.int32(0), absent, absent))


def pair_forces(cell_smem, table_ref, list_ref, force_ref, even_ref, odd_ref):
    lanes = table_ref.shape[1]
    cells = table_ref.shape[0] // 8
    rows = even_ref.shape[0]
    chunks = rows // lanes
    units = rows // GROUP
    groups = cell_smem[0, cell_smem.shape[1] - lanes]
    force_ref[...] = jnp.zeros(force_ref.shape, jnp.float32)
    part = lax.broadcasted_iota(jnp.int32, (32, 8 * lanes), 0)
    comp = lax.broadcasted_iota(jnp.int32, (32, 8 * lanes), 1) // lanes
    weights = jnp.where((part < 24) & (part % 8 == comp), 1.0, 0.0).astype(jnp.bfloat16)
    column = 2 * lanes

    def turned(step):
        pieces = []
        for piece in range(chunks):
            values = list_ref[step * chunks + piece]
            high = values.astype(jnp.bfloat16).astype(jnp.float32)
            rest = values - high
            middle = rest.astype(jnp.bfloat16).astype(jnp.float32)
            parts = jnp.concatenate([high, middle, rest - middle, jnp.zeros_like(values)], axis=0)
            pieces.append(parts.astype(jnp.bfloat16).T)
        return jnp.concatenate(pieces, axis=0)

    def spread(rows_in, at, out_ref):
        out_ref[:, at : at + column] = jnp.dot(
            rows_in, weights[:, at : at + column], preferred_element_type=jnp.float32
        )

    def block_force(wide_ref, row, mine):
        other = [wide_ref[pl.ds(row, 8), pl.ds(value * lanes, lanes)] for value in range(8)]
        apart = [other[axis] - mine[axis] for axis in range(3)]
        square = apart[0] * apart[0] + apart[1] * apart[1] + apart[2] * apart[2] + epsilon_sq
        inverse = lax.rsqrt(square)
        reach = other[6] + mine[6]
        overlap = jnp.maximum(reach - square * inverse, 0.0)
        overlap = jnp.where(other[7] != mine[7], overlap, 0.0)
        closing = (
            (other[3] - mine[3]) * apart[0]
            + (other[4] - mine[4]) * apart[1]
            + (other[5] - mine[5]) * apart[2]
        )
        scaled = overlap * (other[6] * mine[6])
        root = scaled * lax.rsqrt(jnp.maximum(scaled * reach, 1e-30))
        factor = root * inverse * (stiffness / damping * overlap - closing * inverse)
        return [factor * apart[axis] for axis in range(3)]

    def pairs(step, wide_ref, next_ref, carry):
        last, running = carry
        rows_in = turned(step + 1)
        for unit in range(units):
            if unit % (units // 4) == 0:
                spread(rows_in, unit // (units // 4) * column, next_ref)
            cell = cell_smem[0, step * units + unit]
            own = jnp.minimum(cell, cells - 1) * 8
            mine = [table_ref[pl.ds(own + value, 8, stride=0), :] for value in range(8)]
            running = [jnp.where(cell == last, running[axis], 0.0) for axis in range(3)]
            for block in range(GROUP // 8):
                force = block_force(wide_ref, unit * GROUP + block * 8, mine)
                running = [running[axis] + force[axis] for axis in range(3)]
            last = cell
            for axis in range(3):
                force_ref[cell, axis] = running[axis]
        return last, running

    first = turned(0)
    for at in range(0, 8 * lanes, column):
        spread(first, at, even_ref)

    def both(step, carry):
        carry = pairs(2 * step, even_ref, odd_ref, carry)
        return pairs(2 * step + 1, odd_ref, even_ref, carry)

    zero = jnp.zeros((8, lanes), jnp.float32)
    steps = lax.div(groups + (2 * units - 1), 2 * units)
    lax.fori_loop(0, steps, both, (jnp.int32(-1), [zero] * 3))


def inner_kernel(
    amount_smem, where_smem, near_smem, cell_smem, table_ref, slots_ref,
    force_ref, list_ref, even_ref, odd_ref, shift_ref,
):
    cells = table_ref.shape[0]
    fill_lists(amount_smem[0], where_smem, near_smem, table_ref, slots_ref, shift_ref, list_ref)
    flat = table_ref.reshape(cells * 8, table_ref.shape[2])
    pair_forces(cell_smem, flat, list_ref, force_ref, even_ref, odd_ref)


def outer_kernel(
    amount_smem, where_smem, near_smem, cell_smem, table_ref, halo_ref, slots_ref,
    inner_ref, arms_ref, frag_ref, fixed_ref, out_ref, list_ref, even_ref, odd_ref,
    shift_ref, force_ref, loads_ref,
):
    held = fixed_ref.shape[1] // 2
    fill_lists(amount_smem[0], where_smem, near_smem, halo_ref, slots_ref, shift_ref, list_ref)
    pair_forces(cell_smem, table_ref, list_ref, force_ref, even_ref, odd_ref)
    sums = fragment_sums(inner_ref, force_ref, arms_ref, frag_ref, loads_ref, held)
    out = fixed_ref[...] + jnp.concatenate([sums, jnp.zeros_like(sums)], axis=1)
    for brick in range(out_ref.shape[0]):
        out_ref[brick] = out


def fragment_sums(inner_ref, outer_ref, arms_ref, frag_ref, loads_ref, held):
    cells, lanes = frag_ref.shape
    tall = loads_ref.shape[0]
    label = lax.broadcasted_iota(jnp.int32, (held, lanes), 0)

    def gather_sums(block, total):
        rows = pl.ds(pl.multiple_of(block * tall, tall), tall)
        force = [
            -damping * jnp.sum(inner_ref[rows, axis] + outer_ref[rows, axis], axis=1)
            for axis in range(3)
        ]
        lever = [arms_ref[axis, rows, :] for axis in range(3)]
        torque = [
            lever[1] * force[2] - lever[2] * force[1],
            lever[2] * force[0] - lever[0] * force[2],
            lever[0] * force[1] - lever[1] * force[0],
        ]
        loads = force + torque + [jnp.zeros_like(force[0])] * 2
        for comp in range(8):
            loads_ref[:, comp, :] = loads[comp]
        frags = frag_ref[rows, :]
        hits = [
            (frags[unit : unit + 1, :] == label).astype(jnp.float32).astype(jnp.bfloat16)
            for unit in range(tall)
        ]
        values = [split_rows(loads_ref[unit]) for unit in range(tall)]
        return total + dot_lanes(jnp.concatenate(values, axis=1), jnp.concatenate(hits, axis=1))

    total = lax.fori_loop(0, cells // tall, gather_sums, jnp.zeros((24, held), jnp.float32))
    return joined_rows(total)


def move_kernel(
    owned, target_ref, known_ref, state_ref, arms_ref, frag_ref, spheres_ref, clumps_ref
):
    bricks, _, lanes = known_ref.shape
    held = lanes // 2
    cells = frag_ref.shape[0]
    targets = jnp.broadcast_to(target_ref[...], (lanes, lanes))
    lane = lax.broadcasted_iota(jnp.int32, (1, lanes), 1)

    def match(block, carry):
        sums, base = carry
        for unit in range(8):
            brick = block * 8 + unit
            known = known_ref[brick]
            values = split_rows(known)
            key = jnp.where(lane < held, known[6:7], -1.0)
            number = jnp.where(
                (lane >= held) & (lane < held + owned), brick * owned + lane - held, -1
            ).astype(jnp.float32)
            sums = sums + dot_lanes(values, (targets == key).astype(jnp.float32).astype(jnp.bfloat16))
            base = base + dot_lanes(values, (targets == number).astype(jnp.float32).astype(jnp.bfloat16))
        return sums, base

    zero = jnp.zeros((24, lanes), jnp.float32)
    sums, base = lax.fori_loop(0, bricks // 8, match, (zero, zero))
    sums = joined_rows(sums)
    base = joined_rows(base)
    rows = []
    for axis in range(3):
        pull = gravity if axis == 2 else 0.0
        rows.append(
            base[axis : axis + 1]
            + time_step * (sums[axis : axis + 1] * base[6:7] - pull)
        )
    for axis in range(3, 6):
        rows.append(base[axis : axis + 1] + time_step * sums[axis : axis + 1] * base[7:8])
    for comp in range(6):
        clumps_ref[comp : comp + 1, :] = rows[comp]
    tall = 32
    wide = [jnp.broadcast_to(value, (tall, lanes)) for value in rows]

    def cross(first, second):
        return [
            first[1] * second[2] - first[2] * second[1],
            first[2] * second[0] - first[0] * second[2],
            first[0] * second[1] - first[1] * second[0],
        ]

    def move(block, unused):
        at = pl.ds(pl.multiple_of(block * tall, tall), tall)
        index = frag_ref[at, :] + (lanes - held)
        motion = [lanes_of(value, index) for value in wide]
        velocity, spin = motion[0:3], motion[3:6]
        arm = [arms_ref[axis, at, :] for axis in range(3)]
        half = [0.5 * time_step * value for value in spin]
        turned = cross(half, arm)
        twice = cross(half, turned)
        scale = 2.0 / (1.0 + half[0] * half[0] + half[1] * half[1] + half[2] * half[2])
        change = [scale * (turned[axis] + twice[axis]) for axis in range(3)]
        new_arm = [arm[axis] + change[axis] for axis in range(3)]
        swing = cross(spin, new_arm)
        for axis in range(3):
            spheres_ref[axis, at, :] = (
                state_ref[axis, at, :] + time_step * velocity[axis] + (new_arm[axis] - arm[axis])
            )
            spheres_ref[3 + axis, at, :] = velocity[axis] + swing[axis]
        return unused

    lax.fori_loop(0, cells // tall, move, 0)


def local(
    state, arms, sphere_frag, frag_owner, frag_clump, tiles, clump_motion, inv_mass, inv_moment
):
    cells_x, cells_y, cells_z = (state.shape[1], state.shape[2], state.shape[3])
    lanes = state.shape[4]
    cells = cells_x * cells_y * cells_z
    owned = inv_mass.shape[0]
    held = frag_clump.shape[0]
    names = ("gx", "gy", "gz")
    vmem = pl.BlockSpec(memory_space=pltpu.VMEM)
    smem = pl.BlockSpec(memory_space=pltpu.SMEM)
    params = pltpu.CompilerParams(vmem_limit_bytes=VMEM)

    frag_key = (frag_owner[:, 0] * owned + frag_clump).astype(jnp.float32)
    flat_state = state.reshape(7, cells, lanes)
    flat_arms = arms.reshape(3, cells, lanes)
    flat_frag = sphere_frag.reshape(cells, lanes)

    fixed = jnp.concatenate(
        [
            jnp.concatenate([jnp.zeros((6, held)), frag_key[None], jnp.zeros((1, held))], axis=0),
            jnp.concatenate([clump_motion, inv_mass[None], inv_moment[None]], axis=0),
            jnp.zeros((8, lanes - held - owned)),
        ],
        axis=1,
    )

    table = pl.pallas_call(
        pack_kernel,
        out_shape=jax.ShapeDtypeStruct((cells, 8, lanes), jnp.float32),
        in_specs=[vmem] * 3,
        out_specs=vmem,
        compiler_params=params,
    )(flat_state, flat_frag, jnp.pad(frag_key, (0, lanes - held))[None])
    grid = table.reshape(cells_x, cells_y, cells_z, 8, lanes)
    z_before, z_after = exchange(grid[:, :, -1:], grid[:, :, :1], "gz")

    outside = 1 << 20
    span_z = cells_z + 2
    starts = [0, cells_x * cells_y, 2 * cells_x * cells_y]
    starts += [starts[-1] + cells_y * span_z, starts[-1] + 2 * cells_y * span_z]
    starts += [starts[-1] + (cells_x + 2) * span_z]

    def decode(codes):
        own, offset = (codes // 27, codes % 27)
        steps = (offset // 9 - 1, offset // 3 % 3 - 1, offset % 3 - 1)
        x = own // (cells_y * cells_z) + steps[0]
        y = own // cells_z % cells_y + steps[1]
        z = own % cells_z + steps[2]
        need = sum(
            jnp.where(steps[axis] == 1, 1, jnp.where(steps[axis] == -1, 2, 0)) << (2 * axis)
            for axis in range(3)
        )
        return own, offset, need, x, y, z

    def inside(x, y, z):
        inner = (x >= 0) & (x < cells_x) & (y >= 0) & (y < cells_y)
        return inner & (z >= 0) & (z < cells_z)

    codes = tiles[0]
    total = codes.shape[0]
    codes = jnp.sort(codes + jnp.where(inside(*decode(codes)[3:]), 0, outside))
    inner_amount = jnp.sum((codes < outside).astype(jnp.int32))
    order = jnp.arange(total, dtype=jnp.int32)

    def listed(codes, amount, want_inside):
        own, offset, need, x, y, z = decode(codes & (outside - 1))
        if want_inside:
            near = (x * cells_y + y) * cells_z + z
        else:
            in_y = jnp.where(y < 0, starts[4], starts[5]) + (x + 1) * span_z + z + 1
            in_x = jnp.where(x < 0, starts[2], starts[3]) + y * span_z + z + 1
            in_z = jnp.where(z < 0, starts[0], starts[1]) + x * cells_y + y
            near = jnp.where(
                (y < 0) | (y >= cells_y), in_y, jnp.where((x < 0) | (x >= cells_x), in_x, in_z)
            )
        live = order < amount
        near = jnp.where(live, near, 0)
        return (
            near,
            near * 32 + jnp.where(live, offset, 0),
            jnp.where(live, need, 64),
            jnp.where(live, own, cells),
        )

    chunks = -(-(total + cells * GROUP // lanes + 3 * SPREAD) // 16) * 16
    group_top = chunks * (lanes // GROUP)

    def lists(near, need, own, amount, source):
        span = source.shape[0]
        return pl.pallas_call(
            list_kernel,
            out_shape=(
                jax.ShapeDtypeStruct((total, lanes), jnp.int32),
                jax.ShapeDtypeStruct((1, total), jnp.int32),
                jax.ShapeDtypeStruct((1, -(-group_top // lanes) * lanes + lanes), jnp.int32),
            ),
            in_specs=[smem] + [vmem] * 4,
            out_specs=(vmem, vmem, vmem),
            scratch_shapes=[
                pltpu.VMEM((-(-span // lanes) * lanes, lanes), jnp.float32),
                pltpu.VMEM((lanes, total), jnp.float32),
                pltpu.VMEM((cells, lanes), jnp.float32),
            ],
            compiler_params=params,
        )(amount[None], near[None], need[None], own[None], source.reshape(span * 8, lanes))

    force_shape = (cells + 8, 3, 8, lanes)
    scratch = [
        pltpu.VMEM((chunks, 8, lanes), jnp.float32),
        pltpu.VMEM((SPREAD * lanes, 8 * lanes), jnp.float32),
        pltpu.VMEM((SPREAD * lanes, 8 * lanes), jnp.float32),
        pltpu.VMEM((27, 8, lanes), jnp.float32),
    ]

    near, word, need, own = listed(codes, inner_amount, True)
    z_before, z_after, near, need, own = lax.optimization_barrier(
        (z_before, z_after, near, need, own)
    )
    x_before, x_after = exchange(
        jnp.concatenate([z_before[-1:], grid[-1:], z_after[-1:]], axis=2),
        jnp.concatenate([z_before[:1], grid[:1], z_after[:1]], axis=2),
        "gx",
    )
    slots, where, cell_of = lists(near, need, own, inner_amount, table)
    x_before, x_after, slots, where, cell_of = lax.optimization_barrier(
        (x_before, x_after, slots, where, cell_of)
    )

    def face(at):
        middle = jnp.concatenate([z_before[:, at], grid[:, at], z_after[:, at]], axis=2)
        return jnp.concatenate([x_before[:, at], middle, x_after[:, at]], axis=0)

    y_before, y_after = exchange(face(slice(-1, None)), face(slice(0, 1)), "gy")
    inner = pl.pallas_call(
        inner_kernel,
        out_shape=jax.ShapeDtypeStruct(force_shape, jnp.float32),
        in_specs=[smem] * 4 + [vmem] * 2,
        out_specs=vmem,
        scratch_shapes=scratch,
        compiler_params=params,
    )(inner_amount[None], where, word, cell_of, table, slots)

    outer_amount = total - inner_amount
    codes = lax.dynamic_slice(jnp.concatenate([codes, codes]), (inner_amount,), (total,))
    near, word, need, own = listed(codes, outer_amount, False)
    halo = jnp.concatenate(
        [
            part.reshape(-1, 8, lanes)
            for part in (z_before, z_after, x_before, x_after, y_before, y_after)
        ],
        axis=0,
    )
    slots, where, cell_of = lists(near, need, own, outer_amount, halo)
    bricks = lax.axis_size(names)
    known = pl.pallas_call(
        outer_kernel,
        out_shape=jax.ShapeDtypeStruct((bricks, 8, lanes), jnp.float32),
        in_specs=[smem] * 4 + [vmem] * 7,
        out_specs=vmem,
        scratch_shapes=scratch
        + [pltpu.VMEM(force_shape, jnp.float32), pltpu.VMEM((16, 8, lanes), jnp.float32)],
        compiler_params=params,
    )(
        outer_amount[None],
        where,
        word,
        cell_of,
        table.reshape(cells * 8, lanes),
        halo,
        slots,
        inner,
        flat_arms,
        flat_frag,
        fixed,
    )
    known = lax.all_to_all(known, names, split_axis=0, concat_axis=0, tiled=True)

    brick = lax.axis_index(names)
    mine = jnp.where(
        jnp.arange(lanes - held) < owned, brick * owned + jnp.arange(lanes - held), -2
    ).astype(jnp.float32)
    target = jnp.concatenate([mine, frag_key])[:, None]
    spheres, clumps = pl.pallas_call(
        functools.partial(move_kernel, owned),
        out_shape=(
            jax.ShapeDtypeStruct((6, cells, lanes), jnp.float32),
            jax.ShapeDtypeStruct((6, lanes), jnp.float32),
        ),
        in_specs=[vmem] * 5,
        out_specs=(vmem, vmem),
        compiler_params=params,
    )(target, known, flat_state, flat_arms, flat_frag)
    return (spheres.reshape((6,) + state.shape[1:]), clumps[:, :owned])


def solution(mesh):
    return jax.shard_map(
        local,
        mesh=mesh,
        in_specs=(
            P(None, "gx", "gy", "gz", None),
            P(None, "gx", "gy", "gz", None),
            P("gx", "gy", "gz", None),
            P(("gx", "gy", "gz"), None),
            P(("gx", "gy", "gz")),
            P(("gx", "gy", "gz"), None),
            P(None, ("gx", "gy", "gz")),
            P(("gx", "gy", "gz")),
            P(("gx", "gy", "gz")),
        ),
        out_specs=(P(None, "gx", "gy", "gz", None), P(None, ("gx", "gy", "gz"))),
        check_vma=False,
    )
```

```python
import functools

import jax
import jax.numpy as jnp
from jax import lax
from jax.experimental import pallas as pl
from jax.experimental.pallas import tpu as pltpu
from jax.sharding import PartitionSpec as P

stiffness = 100.0
damping = 2.0
time_step = 0.01
gravity = 9.81
epsilon_sq = 1e-08
radius_top = 0.14

GROUP = 16
FILL = 32
SLACK = 256
SPREAD = 4
VMEM = 56 * 1024 * 1024


def lanes_of(values, index):
    return jnp.take_along_axis(values, index, axis=1, mode="promise_in_bounds")


def split_rows(values):
    high = values.astype(jnp.bfloat16).astype(jnp.float32)
    rest = values - high
    middle = rest.astype(jnp.bfloat16).astype(jnp.float32)
    low = rest - middle
    return jnp.concatenate([high, middle, low], axis=0).astype(jnp.bfloat16)


def joined_rows(stacked):
    rows = stacked.shape[0] // 3
    return stacked[0:rows] + stacked[rows : 2 * rows] + stacked[2 * rows :]


def dot_lanes(first, second):
    return lax.dot_general(
        first, second, (((1,), (1,)), ((), ())), preferred_element_type=jnp.float32
    )


def exchange(last, initial, axis):
    devices = lax.axis_size(axis)
    up = [(i, (i + 1) % devices) for i in range(devices)]
    down = [(j, i) for i, j in up]
    return lax.ppermute(last, axis, up), lax.ppermute(initial, axis, down)


def pack_kernel(state_ref, frag_ref, key_ref, out_ref):
    cells = frag_ref.shape[0]
    for comp in range(7):
        out_ref[:, comp, :] = state_ref[comp]
    keys = jnp.broadcast_to(key_ref[0:1, :], (8, key_ref.shape[1]))
    for block in range(cells // 8):
        rows = pl.ds(block * 8, 8)
        out_ref[rows, 7, :] = lanes_of(keys, frag_ref[rows, :])


def list_tiles(
    amount, near_of, sizes, code_ref, table_ref, slots_ref, where_ref, word_ref, cell_ref,
    class_ref, member_ref, count_ref, near_ref, need_ref, own_ref,
):
    tiles, lanes = slots_ref.shape
    span = table_ref.shape[0]
    padded = class_ref.shape[0]
    cells = count_ref.shape[0]
    wide = 256
    parts = 4
    flat = table_ref.reshape(span * 8, lanes)

    def plane(comp):
        return flat[pl.ds(comp, span, stride=8), :]

    def flag(value):
        return value.astype(jnp.float32).astype(jnp.bfloat16)

    def dot(first, second):
        return jnp.dot(first, second, preferred_element_type=jnp.float32)

    def ramp(shape, axis):
        return lax.broadcasted_iota(jnp.int32, shape, axis)

    def over(value, by):
        return jnp.floor((value.astype(jnp.float32) + 0.5) * (1.0 / by)).astype(jnp.int32)

    code = code_ref[...]
    own = over(code, 27)
    kind = code - 27 * own
    step_x = over(kind, 9)
    step_y = over(kind, 3) - 3 * step_x
    steps = (step_x - 1, step_y - 1, kind - 9 * step_x - 3 * step_y - 1)
    own_x = over(own, sizes[1] * sizes[2])
    row = over(own, sizes[2])
    near = near_of(
        own_x + steps[0], row - own_x * sizes[1] + steps[1], own - row * sizes[2] + steps[2]
    )
    need = sum(
        jnp.where(steps[axis] == 1, 1, jnp.where(steps[axis] == -1, 2, 0)) * (1 << (2 * axis))
        for axis in range(3)
    )
    live = ramp((1, tiles), 1) < amount
    near = jnp.where(live, near, 0)
    near_ref[...] = near
    word_ref[...] = near * 32 + jnp.where(live, kind, 0)
    need_ref[...] = jnp.where(live, need, 64)
    own_ref[...] = jnp.where(live, own, cells)

    radius = plane(6) + (radius_top + 1e-5)
    classes = jnp.zeros((span, lanes), jnp.float32)
    for axis in range(3):
        place = plane(axis)
        classes = classes + jnp.where(place < radius, 1.0 * (1 << (2 * axis)), 0.0)
        classes = classes + jnp.where(place > 1.0 - radius, 1.0 * (2 << (2 * axis)), 0.0)
    if padded > span:
        class_ref[...] = jnp.zeros(class_ref.shape, jnp.float32)
    class_ref[pl.ds(0, span), :] = classes
    codes = jnp.concatenate(
        [class_ref[pl.ds(at, lanes), :].T for at in range(0, padded, lanes)], axis=1
    ).astype(jnp.bfloat16)
    ones = jnp.ones((lanes, lanes), jnp.bfloat16)
    count_ref[...] = jnp.zeros(count_ref.shape, jnp.float32)
    blocks = lax.div(amount + (parts * wide - 1), parts * wide)

    def choose(block, unused):
        held = []
        for part in range(parts):
            at = pl.ds(pl.multiple_of((block * parts + part) * wide, wide), wide)
            hits = flag(ramp((padded, wide), 0) == near_ref[:, at])
            found = dot(codes, hits).astype(jnp.int32)
            need = need_ref[:, at]
            member = ((found & need) == need).astype(jnp.float32)
            member_ref[:, at] = member
            count = dot(ones, member.astype(jnp.bfloat16))
            mine = flag(ramp((cells, wide), 0) == own_ref[:, at])
            held.append(dot_lanes(mine, count.astype(jnp.bfloat16)))
        count_ref[...] += (held[0] + held[1]) + (held[2] + held[3])
        return unused

    lax.fori_loop(0, blocks, choose, 0)

    held = count_ref[...]
    high = jnp.floor(held * (1.0 / lanes))
    low = held - lanes * high
    taken = jnp.floor((held + (GROUP - 1)) * (1.0 / GROUP))
    upto = flag(ramp((cells, cells), 1) <= ramp((cells, cells), 0))
    ends = dot(upto, taken.astype(jnp.bfloat16))
    cell_ones = jnp.ones((8, cells), jnp.bfloat16)
    many = 8 * lanes
    wide_ends = jnp.concatenate([ends] * 8, axis=1)

    def name_groups(block, unused):
        group = (ramp((cells, many), 1) + block * many).astype(jnp.float32)
        at = pl.ds(pl.multiple_of(block * many, many), many)
        cell_ref[:, at] = dot(cell_ones, flag(wide_ends <= group))[0:1].astype(jnp.int32)
        return unused

    groups = jnp.max(ends).astype(jnp.int32)
    lax.fori_loop(0, lax.div(groups + SLACK, many) + 1, name_groups, 0)
    before_cell = jnp.concatenate(
        [value.T[0:8] for value in (taken, high, low)], axis=0
    ).astype(jnp.bfloat16)

    earlier = flag(ramp((lanes, lanes), 1) < ramp((lanes, lanes), 0))
    earlier_tile = flag(ramp((wide, wide), 0) < ramp((wide, wide), 1))

    def place(block, done):
        for part in range(parts):
            first = pl.multiple_of((block * parts + part) * wide, wide)
            at = pl.ds(first, wide)
            flags = member_ref[:, at].astype(jnp.bfloat16)
            count = dot(ones, flags)
            lower = flag(ramp((cells, wide), 0) < own_ref[:, at])
            before = dot(before_cell, lower)
            so_far = dot(count[0:8].astype(jnp.bfloat16), earlier_tile) + done
            start = GROUP * before[0:8] + so_far - (lanes * before[8:16] + before[16:24])
            start = start.astype(jnp.int32)[0:1]
            where_ref[:, at] = start * 256 + count[0:1].astype(jnp.int32)
            rank = dot(earlier, flags)
            slot = ramp((lanes, wide), 0)
            moves = slot - rank.astype(jnp.int32)
            word = jnp.where(member_ref[:, at] > 0.0, slot + lanes * moves, 0)
            bit = 1
            while bit < lanes:
                keep = jnp.where((word & (bit * lanes)) != 0, 0, word)
                gone = word ^ keep
                word = keep | jnp.concatenate([gone[bit:], gone[:bit]], axis=0)
                bit *= 2
            word = word & (lanes - 1)
            turn = jnp.broadcast_to(start, (lanes, wide))
            bit = 1
            while bit < lanes:
                moved = jnp.concatenate([word[lanes - bit :], word[: lanes - bit]], axis=0)
                word = jnp.where((turn & bit) != 0, moved, word)
                bit *= 2
            for half in range(wide // lanes):
                rows = pl.ds(pl.multiple_of(first + half * lanes, lanes), lanes)
                slots_ref[rows, :] = word[:, half * lanes : (half + 1) * lanes].T
            done = done + jnp.sum(count[0:8], axis=1, keepdims=True)
        return done

    lax.fori_loop(0, blocks, place, jnp.zeros((8, 1), jnp.float32))
    return groups


def fill_lists(amount, where_smem, near_smem, table_ref, slots_ref, shift_ref, list_ref):
    tiles, lanes = slots_ref.shape
    lane_bits = lanes.bit_length() - 1
    lane = lax.broadcasted_iota(jnp.int32, (8, lanes), 1)
    row = lax.broadcasted_iota(jnp.int32, (8, lanes), 0)
    absent = jnp.where(row == 6, -10.0, 0.0)
    for kind in range(27):
        steps = (kind // 9 - 1.0, kind // 3 % 3 - 1.0, kind % 3 - 1.0)
        shift_ref[kind] = sum(jnp.where(row == axis, steps[axis], 0.0) for axis in range(3))

    def fill(block, carry):
        last_chunk, last_new, last_held = carry
        units = range(FILL)
        where = [where_smem[0, block * FILL + unit] for unit in units]
        near = [near_smem[0, block * FILL + unit] for unit in units]
        found = []
        for unit in units:
            slots = slots_ref[pl.ds(block * FILL + unit, 8, stride=0), :]
            cell = table_ref[near[unit] >> 5]
            found.append(lanes_of(cell, slots) + shift_ref[near[unit] & 31])
        for unit in units:
            amount = where[unit] & 255
            chunk = where[unit] >> (8 + lane_bits)
            offset = (where[unit] >> 8) & (lanes - 1)
            new = jnp.where(((lane - offset) & (lanes - 1)) < amount, found[unit], absent)
            held_row = jnp.where(chunk != last_chunk, last_new, last_held)
            held_row = jnp.where(lane >= offset, new, held_row)
            new = jnp.where(lane >= offset, absent, new)
            list_ref[chunk] = held_row
            list_ref[chunk + 1] = new
            last_chunk, last_new, last_held = chunk, new, held_row
        return last_chunk, last_new, last_held

    blocks = lax.div(amount + (FILL - 1), FILL)
    lax.fori_loop(0, blocks, fill, (jnp.int32(0), absent, absent))


def pair_forces(groups, cell_smem, table_ref, list_ref, force_ref, even_ref, odd_ref):
    lanes = table_ref.shape[1]
    cells = table_ref.shape[0] // 8
    rows = even_ref.shape[0]
    chunks = rows // lanes
    units = rows // GROUP
    force_ref[...] = jnp.zeros(force_ref.shape, jnp.float32)
    part = lax.broadcasted_iota(jnp.int32, (32, 8 * lanes), 0)
    comp = lax.broadcasted_iota(jnp.int32, (32, 8 * lanes), 1) // lanes
    weights = jnp.where((part < 24) & (part % 8 == comp), 1.0, 0.0).astype(jnp.bfloat16)

    def turned(step):
        pieces = []
        for piece in range(chunks):
            values = list_ref[step * chunks + piece]
            high = values.astype(jnp.bfloat16).astype(jnp.float32)
            rest = values - high
            middle = rest.astype(jnp.bfloat16).astype(jnp.float32)
            parts = jnp.concatenate([high, middle, rest - middle, jnp.zeros_like(values)], axis=0)
            pieces.append(parts.astype(jnp.bfloat16).T)
        return jnp.concatenate(pieces, axis=0)

    def spread(step, out_ref):
        out_ref[...] = jnp.dot(turned(step), weights, preferred_element_type=jnp.float32)

    def block_force(wide_ref, row, mine):
        other = [wide_ref[pl.ds(row, 8), pl.ds(value * lanes, lanes)] for value in range(8)]
        apart = [other[axis] - mine[axis] for axis in range(3)]
        square = apart[0] * apart[0] + apart[1] * apart[1] + apart[2] * apart[2] + epsilon_sq
        inverse = lax.rsqrt(square)
        reach = other[6] + mine[6]
        overlap = jnp.maximum(reach - square * inverse, 0.0)
        overlap = jnp.where(other[7] != mine[7], overlap, 0.0)
        closing = (
            (other[3] - mine[3]) * apart[0]
            + (other[4] - mine[4]) * apart[1]
            + (other[5] - mine[5]) * apart[2]
        )
        scaled = overlap * (other[6] * mine[6])
        root = scaled * lax.rsqrt(jnp.maximum(scaled * reach, 1e-30))
        factor = root * inverse * (stiffness / damping * overlap - closing * inverse)
        return [factor * apart[axis] for axis in range(3)]

    def pairs(step, wide_ref, next_ref, carry):
        last, running = carry
        spread(step + 1, next_ref)
        for unit in range(units):
            cell = cell_smem[0, step * units + unit]
            own = jnp.minimum(cell, cells - 1) * 8
            mine = [table_ref[pl.ds(own + value, 8, stride=0), :] for value in range(8)]
            running = [jnp.where(cell == last, running[axis], 0.0) for axis in range(3)]
            for block in range(GROUP // 8):
                force = block_force(wide_ref, unit * GROUP + block * 8, mine)
                running = [running[axis] + force[axis] for axis in range(3)]
            last = cell
            for axis in range(3):
                force_ref[cell, axis] = running[axis]
        return last, running

    spread(0, even_ref)

    def both(step, carry):
        carry = pairs(2 * step, even_ref, odd_ref, carry)
        return pairs(2 * step + 1, odd_ref, even_ref, carry)

    zero = jnp.zeros((8, lanes), jnp.float32)
    steps = lax.div(groups + (2 * units - 1), 2 * units)
    lax.fori_loop(0, steps, both, (jnp.int32(-1), [zero] * 3))


def forces(
    amount, near_of, sizes, code_ref, table_ref, near_table_ref, force_ref,
    slots_ref, where_ref, word_ref, cell_ref, where_smem, word_smem, cell_smem, sems,
    class_ref, member_ref, count_ref, near_ref, need_ref, own_ref,
    list_ref, even_ref, odd_ref, shift_ref,
):
    cells, _, lanes = table_ref.shape
    groups = list_tiles(
        amount, near_of, sizes, code_ref, near_table_ref, slots_ref, where_ref, word_ref, cell_ref,
        class_ref, member_ref, count_ref, near_ref, need_ref, own_ref,
    )
    copies = [
        pltpu.make_async_copy(where_ref, where_smem, sems.at[0]),
        pltpu.make_async_copy(word_ref, word_smem, sems.at[1]),
        pltpu.make_async_copy(cell_ref, cell_smem, sems.at[2]),
    ]
    for copy in copies:
        copy.start()
    for copy in copies:
        copy.wait()
    fill_lists(amount, where_smem, word_smem, near_table_ref, slots_ref, shift_ref, list_ref)
    flat = table_ref.reshape(cells * 8, lanes)
    pair_forces(groups, cell_smem, flat, list_ref, force_ref, even_ref, odd_ref)


def inner_kernel(near_of, sizes, amount_smem, code_ref, table_ref, force_ref, *scratch):
    forces(amount_smem[0], near_of, sizes, code_ref, table_ref, table_ref, force_ref, *scratch)


def outer_kernel(
    near_of, sizes, amount_smem, code_ref, table_ref, halo_ref, inner_ref, arms_ref, frag_ref,
    fixed_ref, out_ref, force_ref, loads_ref, *scratch,
):
    held = fixed_ref.shape[1] // 2
    forces(amount_smem[0], near_of, sizes, code_ref, table_ref, halo_ref, force_ref, *scratch)
    sums = fragment_sums(inner_ref, force_ref, arms_ref, frag_ref, loads_ref, held)
    out = fixed_ref[...] + jnp.concatenate([sums, jnp.zeros_like(sums)], axis=1)
    for brick in range(out_ref.shape[0]):
        out_ref[brick] = out


def fragment_sums(inner_ref, outer_ref, arms_ref, frag_ref, loads_ref, held):
    cells, lanes = frag_ref.shape
    tall = loads_ref.shape[0]
    label = lax.broadcasted_iota(jnp.int32, (held, lanes), 0)

    def gather_sums(block, total):
        rows = pl.ds(pl.multiple_of(block * tall, tall), tall)
        force = [
            -damping * jnp.sum(inner_ref[rows, axis] + outer_ref[rows, axis], axis=1)
            for axis in range(3)
        ]
        lever = [arms_ref[axis, rows, :] for axis in range(3)]
        torque = [
            lever[1] * force[2] - lever[2] * force[1],
            lever[2] * force[0] - lever[0] * force[2],
            lever[0] * force[1] - lever[1] * force[0],
        ]
        loads = force + torque + [jnp.zeros_like(force[0])] * 2
        for comp in range(8):
            loads_ref[:, comp, :] = loads[comp]
        frags = frag_ref[rows, :]
        hits = [
            (frags[unit : unit + 1, :] == label).astype(jnp.float32).astype(jnp.bfloat16)
            for unit in range(tall)
        ]
        values = [split_rows(loads_ref[unit]) for unit in range(tall)]
        return total + dot_lanes(jnp.concatenate(values, axis=1), jnp.concatenate(hits, axis=1))

    total = lax.fori_loop(0, cells // tall, gather_sums, jnp.zeros((24, held), jnp.float32))
    return joined_rows(total)


def move_kernel(
    owned, target_ref, known_ref, state_ref, arms_ref, frag_ref, spheres_ref, clumps_ref
):
    bricks, _, lanes = known_ref.shape
    held = lanes // 2
    cells = frag_ref.shape[0]
    targets = jnp.broadcast_to(target_ref[...], (lanes, lanes))
    lane = lax.broadcasted_iota(jnp.int32, (1, lanes), 1)

    def match(block, carry):
        sums, base = carry
        for unit in range(8):
            brick = block * 8 + unit
            known = known_ref[brick]
            values = split_rows(known)
            key = jnp.where(lane < held, known[6:7], -1.0)
            number = jnp.where(
                (lane >= held) & (lane < held + owned), brick * owned + lane - held, -1
            ).astype(jnp.float32)
            sums = sums + dot_lanes(values, (targets == key).astype(jnp.float32).astype(jnp.bfloat16))
            base = base + dot_lanes(values, (targets == number).astype(jnp.float32).astype(jnp.bfloat16))
        return sums, base

    zero = jnp.zeros((24, lanes), jnp.float32)
    sums, base = lax.fori_loop(0, bricks // 8, match, (zero, zero))
    sums = joined_rows(sums)
    base = joined_rows(base)
    rows = []
    for axis in range(3):
        pull = gravity if axis == 2 else 0.0
        rows.append(
            base[axis : axis + 1]
            + time_step * (sums[axis : axis + 1] * base[6:7] - pull)
        )
    for axis in range(3, 6):
        rows.append(base[axis : axis + 1] + time_step * sums[axis : axis + 1] * base[7:8])
    for comp in range(6):
        clumps_ref[comp : comp + 1, :] = rows[comp]
    tall = 32
    wide = [jnp.broadcast_to(value, (tall, lanes)) for value in rows]

    def cross(first, second):
        return [
            first[1] * second[2] - first[2] * second[1],
            first[2] * second[0] - first[0] * second[2],
            first[0] * second[1] - first[1] * second[0],
        ]

    def move(block, unused):
        at = pl.ds(pl.multiple_of(block * tall, tall), tall)
        index = frag_ref[at, :] + (lanes - held)
        motion = [lanes_of(value, index) for value in wide]
        velocity, spin = motion[0:3], motion[3:6]
        arm = [arms_ref[axis, at, :] for axis in range(3)]
        half = [0.5 * time_step * value for value in spin]
        turned = cross(half, arm)
        twice = cross(half, turned)
        scale = 2.0 / (1.0 + half[0] * half[0] + half[1] * half[1] + half[2] * half[2])
        change = [scale * (turned[axis] + twice[axis]) for axis in range(3)]
        new_arm = [arm[axis] + change[axis] for axis in range(3)]
        swing = cross(spin, new_arm)
        for axis in range(3):
            spheres_ref[axis, at, :] = (
                state_ref[axis, at, :] + time_step * velocity[axis] + (new_arm[axis] - arm[axis])
            )
            spheres_ref[3 + axis, at, :] = velocity[axis] + swing[axis]
        return unused

    lax.fori_loop(0, cells // tall, move, 0)


def local(
    state, arms, sphere_frag, frag_owner, frag_clump, tiles, clump_motion, inv_mass, inv_moment
):
    cells_x, cells_y, cells_z = (state.shape[1], state.shape[2], state.shape[3])
    lanes = state.shape[4]
    cells = cells_x * cells_y * cells_z
    owned = inv_mass.shape[0]
    held = frag_clump.shape[0]
    names = ("gx", "gy", "gz")
    vmem = pl.BlockSpec(memory_space=pltpu.VMEM)
    smem = pl.BlockSpec(memory_space=pltpu.SMEM)
    params = pltpu.CompilerParams(vmem_limit_bytes=VMEM)

    frag_key = (frag_owner[:, 0] * owned + frag_clump).astype(jnp.float32)
    flat_state = state.reshape(7, cells, lanes)
    flat_arms = arms.reshape(3, cells, lanes)
    flat_frag = sphere_frag.reshape(cells, lanes)

    fixed = jnp.concatenate(
        [
            jnp.concatenate([jnp.zeros((6, held)), frag_key[None], jnp.zeros((1, held))], axis=0),
            jnp.concatenate([clump_motion, inv_mass[None], inv_moment[None]], axis=0),
            jnp.zeros((8, lanes - held - owned)),
        ],
        axis=1,
    )

    table = pl.pallas_call(
        pack_kernel,
        out_shape=jax.ShapeDtypeStruct((cells, 8, lanes), jnp.float32),
        in_specs=[vmem] * 3,
        out_specs=vmem,
        compiler_params=params,
    )(flat_state, flat_frag, jnp.pad(frag_key, (0, lanes - held))[None])
    grid = table.reshape(cells_x, cells_y, cells_z, 8, lanes)
    z_before, z_after = exchange(grid[:, :, -1:], grid[:, :, :1], "gz")

    outside = 1 << 20
    span_z = cells_z + 2
    starts = [0, cells_x * cells_y, 2 * cells_x * cells_y]
    starts += [starts[-1] + cells_y * span_z, starts[-1] + 2 * cells_y * span_z]
    starts += [starts[-1] + (cells_x + 2) * span_z]

    def inside(codes):
        own, kind = (codes // 27, codes % 27)
        x = own // (cells_y * cells_z) + kind // 9 - 1
        y = own // cells_z % cells_y + kind // 3 % 3 - 1
        z = own % cells_z + kind % 3 - 1
        inner = (x >= 0) & (x < cells_x) & (y >= 0) & (y < cells_y)
        return inner & (z >= 0) & (z < cells_z)

    def near_inside(x, y, z):
        return (x * cells_y + y) * cells_z + z

    def near_outside(x, y, z):
        in_y = jnp.where(y < 0, starts[4], starts[5]) + (x + 1) * span_z + z + 1
        in_x = jnp.where(x < 0, starts[2], starts[3]) + y * span_z + z + 1
        in_z = jnp.where(z < 0, starts[0], starts[1]) + x * cells_y + y
        in_x = jnp.where((x < 0) | (x >= cells_x), in_x, in_z)
        return jnp.where((y < 0) | (y >= cells_y), in_y, in_x)

    sizes = (cells_x, cells_y, cells_z)
    codes = tiles[0]
    total = codes.shape[0]
    codes = codes + jnp.where(inside(codes), 0, outside)
    chunks = total + cells * GROUP // lanes + 3 * SPREAD
    group_top = -(-(chunks * (lanes // GROUP) + SLACK) // (8 * lanes)) * 8 * lanes + 8 * lanes
    force_shape = (cells + 8, 3, 8, lanes)

    def scratch(span):
        return [
            pltpu.VMEM((total, lanes), jnp.int32),
            pltpu.VMEM((1, total), jnp.int32),
            pltpu.VMEM((1, total), jnp.int32),
            pltpu.VMEM((1, group_top), jnp.int32),
            pltpu.SMEM((1, total), jnp.int32),
            pltpu.SMEM((1, total), jnp.int32),
            pltpu.SMEM((1, group_top), jnp.int32),
            pltpu.SemaphoreType.DMA((3,)),
            pltpu.VMEM((-(-span // lanes) * lanes, lanes), jnp.float32),
            pltpu.VMEM((lanes, total), jnp.float32),
            pltpu.VMEM((cells, lanes), jnp.float32),
            pltpu.VMEM((1, total), jnp.int32),
            pltpu.VMEM((1, total), jnp.int32),
            pltpu.VMEM((1, total), jnp.int32),
            pltpu.VMEM((chunks, 8, lanes), jnp.float32),
            pltpu.VMEM((SPREAD * lanes, 8 * lanes), jnp.float32),
            pltpu.VMEM((SPREAD * lanes, 8 * lanes), jnp.float32),
            pltpu.VMEM((27, 8, lanes), jnp.float32),
        ]

    z_before, z_after, codes = lax.optimization_barrier((z_before, z_after, codes))
    x_before, x_after = exchange(
        jnp.concatenate([z_before[-1:], grid[-1:], z_after[-1:]], axis=2),
        jnp.concatenate([z_before[:1], grid[:1], z_after[:1]], axis=2),
        "gx",
    )
    codes = jnp.sort(codes)
    inner_amount = jnp.sum((codes < outside).astype(jnp.int32))
    outer_amount = total - inner_amount
    outer_codes = lax.dynamic_slice(jnp.concatenate([codes, codes]), (inner_amount,), (total,))
    outer_codes = outer_codes & (outside - 1)
    x_before, x_after, codes, outer_codes = lax.optimization_barrier(
        (x_before, x_after, codes, outer_codes)
    )

    def face(at):
        middle = jnp.concatenate([z_before[:, at], grid[:, at], z_after[:, at]], axis=2)
        return jnp.concatenate([x_before[:, at], middle, x_after[:, at]], axis=0)

    y_before, y_after = exchange(face(slice(-1, None)), face(slice(0, 1)), "gy")
    inner = pl.pallas_call(
        functools.partial(inner_kernel, near_inside, sizes),
        out_shape=jax.ShapeDtypeStruct(force_shape, jnp.float32),
        in_specs=[smem] + [vmem] * 2,
        out_specs=vmem,
        scratch_shapes=scratch(cells),
        compiler_params=params,
    )(inner_amount[None], (codes & (outside - 1))[None], table)

    halo = jnp.concatenate(
        [
            part.reshape(-1, 8, lanes)
            for part in (z_before, z_after, x_before, x_after, y_before, y_after)
        ],
        axis=0,
    )
    bricks = lax.axis_size(names)
    known = pl.pallas_call(
        functools.partial(outer_kernel, near_outside, sizes),
        out_shape=jax.ShapeDtypeStruct((bricks, 8, lanes), jnp.float32),
        in_specs=[smem] + [vmem] * 7,
        out_specs=vmem,
        scratch_shapes=[
            pltpu.VMEM(force_shape, jnp.float32),
            pltpu.VMEM((16, 8, lanes), jnp.float32),
        ]
        + scratch(halo.shape[0]),
        compiler_params=params,
    )(outer_amount[None], outer_codes[None], table, halo, inner, flat_arms, flat_frag, fixed)
    known = lax.all_to_all(known, names, split_axis=0, concat_axis=0, tiled=True)

    brick = lax.axis_index(names)
    mine = jnp.where(
        jnp.arange(lanes - held) < owned, brick * owned + jnp.arange(lanes - held), -2
    ).astype(jnp.float32)
    target = jnp.concatenate([mine, frag_key])[:, None]
    spheres, clumps = pl.pallas_call(
        functools.partial(move_kernel, owned),
        out_shape=(
            jax.ShapeDtypeStruct((6, cells, lanes), jnp.float32),
            jax.ShapeDtypeStruct((6, lanes), jnp.float32),
        ),
        in_specs=[vmem] * 5,
        out_specs=(vmem, vmem),
        compiler_params=params,
    )(target, known, flat_state, flat_arms, flat_frag)
    return (spheres.reshape((6,) + state.shape[1:]), clumps[:, :owned])


def solution(mesh):
    return jax.shard_map(
        local,
        mesh=mesh,
        in_specs=(
            P(None, "gx", "gy", "gz", None),
            P(None, "gx", "gy", "gz", None),
            P("gx", "gy", "gz", None),
            P(("gx", "gy", "gz"), None),
            P(("gx", "gy", "gz")),
            P(("gx", "gy", "gz"), None),
            P(None, ("gx", "gy", "gz")),
            P(("gx", "gy", "gz")),
            P(("gx", "gy", "gz")),
        ),
        out_specs=(P(None, "gx", "gy", "gz", None), P(None, ("gx", "gy", "gz"))),
        check_vma=False,
    )
```

```python
import functools

import jax
import jax.numpy as jnp
from jax import lax
from jax.experimental import pallas as pl
from jax.experimental.pallas import tpu as pltpu
from jax.sharding import PartitionSpec as P

stiffness = 100.0
damping = 2.0
time_step = 0.01
gravity = 9.81
epsilon_sq = 1e-08
radius_top = 0.14

GROUP = 16
FILL = 32
SLACK = 256
SPREAD = 4
VMEM = 56 * 1024 * 1024


def lanes_of(values, index):
    return jnp.take_along_axis(values, index, axis=1, mode="promise_in_bounds")


def split_rows(values):
    high = values.astype(jnp.bfloat16).astype(jnp.float32)
    rest = values - high
    middle = rest.astype(jnp.bfloat16).astype(jnp.float32)
    low = rest - middle
    return jnp.concatenate([high, middle, low], axis=0).astype(jnp.bfloat16)


def joined_rows(stacked):
    rows = stacked.shape[0] // 3
    return stacked[0:rows] + stacked[rows : 2 * rows] + stacked[2 * rows :]


def dot_lanes(first, second):
    return lax.dot_general(
        first, second, (((1,), (1,)), ((), ())), preferred_element_type=jnp.float32
    )


def exchange(last, initial, axis):
    devices = lax.axis_size(axis)
    up = [(i, (i + 1) % devices) for i in range(devices)]
    down = [(j, i) for i, j in up]
    return lax.ppermute(last, axis, up), lax.ppermute(initial, axis, down)


def pack_kernel(deep, state_ref, frag_ref, key_ref, out_ref, last_ref, first_ref):
    cells, lanes = frag_ref.shape
    held = key_ref.shape[1]
    for comp in range(7):
        out_ref[:, comp, :] = state_ref[comp]
    keys = jnp.concatenate([key_ref[0:1, :], jnp.zeros((1, lanes - held), jnp.float32)], axis=1)
    keys = jnp.broadcast_to(keys, (8, lanes))
    for block in range(cells // 8):
        rows = pl.ds(block * 8, 8)
        out_ref[rows, 7, :] = lanes_of(keys, frag_ref[rows, :])
    for column in range(cells // deep):
        first_ref[column] = out_ref[column * deep]
        last_ref[column] = out_ref[column * deep + deep - 1]


def list_tiles(
    amount, near_of, sizes, code_ref, table_ref, slots_ref, where_ref, word_ref, cell_ref,
    class_ref, member_ref, count_ref, near_ref, need_ref, own_ref,
):
    tiles, lanes = slots_ref.shape
    span = table_ref.shape[0]
    padded = class_ref.shape[0]
    cells = count_ref.shape[0]
    wide = 256
    parts = 4
    flat = table_ref.reshape(span * 8, lanes)

    def plane(comp):
        return flat[pl.ds(comp, span, stride=8), :]

    def flag(value):
        return value.astype(jnp.float32).astype(jnp.bfloat16)

    def dot(first, second):
        return jnp.dot(first, second, preferred_element_type=jnp.float32)

    def ramp(shape, axis):
        return lax.broadcasted_iota(jnp.int32, shape, axis)

    def over(value, by):
        return jnp.floor((value.astype(jnp.float32) + 0.5) * (1.0 / by)).astype(jnp.int32)

    code = code_ref[...]
    own = over(code, 27)
    kind = code - 27 * own
    step_x = over(kind, 9)
    step_y = over(kind, 3) - 3 * step_x
    steps = (step_x - 1, step_y - 1, kind - 9 * step_x - 3 * step_y - 1)
    own_x = over(own, sizes[1] * sizes[2])
    row = over(own, sizes[2])
    near = near_of(
        own_x + steps[0], row - own_x * sizes[1] + steps[1], own - row * sizes[2] + steps[2]
    )
    need = sum(
        jnp.where(steps[axis] == 1, 1, jnp.where(steps[axis] == -1, 2, 0)) * (1 << (2 * axis))
        for axis in range(3)
    )
    live = ramp((1, tiles), 1) < amount
    near = jnp.where(live, near, 0)
    near_ref[...] = near
    word_ref[...] = near * 32 + jnp.where(live, kind, 0)
    need_ref[...] = jnp.where(live, need, 64)
    own_ref[...] = jnp.where(live, own, cells)

    radius = plane(6) + (radius_top + 1e-5)
    classes = jnp.zeros((span, lanes), jnp.float32)
    for axis in range(3):
        place = plane(axis)
        classes = classes + jnp.where(place < radius, 1.0 * (1 << (2 * axis)), 0.0)
        classes = classes + jnp.where(place > 1.0 - radius, 1.0 * (2 << (2 * axis)), 0.0)
    if padded > span:
        class_ref[...] = jnp.zeros(class_ref.shape, jnp.float32)
    class_ref[pl.ds(0, span), :] = classes
    codes = jnp.concatenate(
        [class_ref[pl.ds(at, lanes), :].T for at in range(0, padded, lanes)], axis=1
    ).astype(jnp.bfloat16)
    ones = jnp.ones((lanes, lanes), jnp.bfloat16)
    count_ref[...] = jnp.zeros(count_ref.shape, jnp.float32)
    blocks = lax.div(amount + (parts * wide - 1), parts * wide)

    def choose(block, unused):
        held = []
        for part in range(parts):
            at = pl.ds(pl.multiple_of((block * parts + part) * wide, wide), wide)
            hits = flag(ramp((padded, wide), 0) == near_ref[:, at])
            found = dot(codes, hits).astype(jnp.int32)
            need = need_ref[:, at]
            member = ((found & need) == need).astype(jnp.float32)
            member_ref[:, at] = member
            count = dot(ones, member.astype(jnp.bfloat16))
            mine = flag(ramp((cells, wide), 0) == own_ref[:, at])
            held.append(dot_lanes(mine, count.astype(jnp.bfloat16)))
        count_ref[...] += (held[0] + held[1]) + (held[2] + held[3])
        return unused

    lax.fori_loop(0, blocks, choose, 0)

    held = count_ref[...]
    high = jnp.floor(held * (1.0 / lanes))
    low = held - lanes * high
    taken = jnp.floor((held + (GROUP - 1)) * (1.0 / GROUP))
    upto = flag(ramp((cells, cells), 1) <= ramp((cells, cells), 0))
    ends = dot(upto, taken.astype(jnp.bfloat16))
    cell_ones = jnp.ones((8, cells), jnp.bfloat16)
    many = 8 * lanes
    wide_ends = jnp.concatenate([ends] * 8, axis=1)

    def name_groups(block, unused):
        group = (ramp((cells, many), 1) + block * many).astype(jnp.float32)
        at = pl.ds(pl.multiple_of(block * many, many), many)
        cell_ref[:, at] = dot(cell_ones, flag(wide_ends <= group))[0:1].astype(jnp.int32)
        return unused

    groups = jnp.max(ends).astype(jnp.int32)
    lax.fori_loop(0, lax.div(groups + SLACK, many) + 1, name_groups, 0)
    before_cell = jnp.concatenate(
        [value.T[0:8] for value in (taken, high, low)], axis=0
    ).astype(jnp.bfloat16)

    earlier = flag(ramp((lanes, lanes), 1) < ramp((lanes, lanes), 0))
    earlier_tile = flag(ramp((wide, wide), 0) < ramp((wide, wide), 1))

    def place(block, done):
        for part in range(parts):
            first = pl.multiple_of((block * parts + part) * wide, wide)
            at = pl.ds(first, wide)
            flags = member_ref[:, at].astype(jnp.bfloat16)
            count = dot(ones, flags)
            lower = flag(ramp((cells, wide), 0) < own_ref[:, at])
            before = dot(before_cell, lower)
            so_far = dot(count[0:8].astype(jnp.bfloat16), earlier_tile) + done
            start = GROUP * before[0:8] + so_far - (lanes * before[8:16] + before[16:24])
            start = start.astype(jnp.int32)[0:1]
            where_ref[:, at] = start * 256 + count[0:1].astype(jnp.int32)
            rank = dot(earlier, flags)
            slot = ramp((lanes, wide), 0)
            moves = slot - rank.astype(jnp.int32)
            word = jnp.where(member_ref[:, at] > 0.0, slot + lanes * moves, 0)
            bit = 1
            while bit < lanes:
                keep = jnp.where((word & (bit * lanes)) != 0, 0, word)
                gone = word ^ keep
                word = keep | jnp.concatenate([gone[bit:], gone[:bit]], axis=0)
                bit *= 2
            word = word & (lanes - 1)
            turn = jnp.broadcast_to(start, (lanes, wide))
            bit = 1
            while bit < lanes:
                moved = jnp.concatenate([word[lanes - bit :], word[: lanes - bit]], axis=0)
                word = jnp.where((turn & bit) != 0, moved, word)
                bit *= 2
            for half in range(wide // lanes):
                rows = pl.ds(pl.multiple_of(first + half * lanes, lanes), lanes)
                slots_ref[rows, :] = word[:, half * lanes : (half + 1) * lanes].T
            done = done + jnp.sum(count[0:8], axis=1, keepdims=True)
        return done

    lax.fori_loop(0, blocks, place, jnp.zeros((8, 1), jnp.float32))
    return groups


def fill_lists(amount, where_smem, near_smem, table_ref, slots_ref, shift_ref, list_ref):
    tiles, lanes = slots_ref.shape
    lane_bits = lanes.bit_length() - 1
    lane = lax.broadcasted_iota(jnp.int32, (8, lanes), 1)
    row = lax.broadcasted_iota(jnp.int32, (8, lanes), 0)
    absent = jnp.where(row == 6, -10.0, 0.0)
    for kind in range(27):
        steps = (kind // 9 - 1.0, kind // 3 % 3 - 1.0, kind % 3 - 1.0)
        shift_ref[kind] = sum(jnp.where(row == axis, steps[axis], 0.0) for axis in range(3))

    def fill(block, carry):
        last_chunk, last_new, last_held = carry
        units = range(FILL)
        where = [where_smem[0, block * FILL + unit] for unit in units]
        near = [near_smem[0, block * FILL + unit] for unit in units]
        found = []
        for unit in units:
            slots = slots_ref[pl.ds(block * FILL + unit, 8, stride=0), :]
            cell = table_ref[near[unit] >> 5]
            found.append(lanes_of(cell, slots) + shift_ref[near[unit] & 31])
        for unit in units:
            amount = where[unit] & 255
            chunk = where[unit] >> (8 + lane_bits)
            offset = (where[unit] >> 8) & (lanes - 1)
            new = jnp.where(((lane - offset) & (lanes - 1)) < amount, found[unit], absent)
            held_row = jnp.where(chunk != last_chunk, last_new, last_held)
            held_row = jnp.where(lane >= offset, new, held_row)
            new = jnp.where(lane >= offset, absent, new)
            list_ref[chunk] = held_row
            list_ref[chunk + 1] = new
            last_chunk, last_new, last_held = chunk, new, held_row
        return last_chunk, last_new, last_held

    blocks = lax.div(amount + (FILL - 1), FILL)
    lax.fori_loop(0, blocks, fill, (jnp.int32(0), absent, absent))


def pair_forces(groups, cell_smem, table_ref, list_ref, force_ref, even_ref, odd_ref):
    lanes = table_ref.shape[1]
    cells = table_ref.shape[0] // 8
    rows = even_ref.shape[0]
    chunks = rows // lanes
    units = rows // GROUP
    force_ref[...] = jnp.zeros(force_ref.shape, jnp.float32)
    part = lax.broadcasted_iota(jnp.int32, (32, 8 * lanes), 0)
    comp = lax.broadcasted_iota(jnp.int32, (32, 8 * lanes), 1) // lanes
    weights = jnp.where((part < 24) & (part % 8 == comp), 1.0, 0.0).astype(jnp.bfloat16)

    def turned(step):
        pieces = []
        for piece in range(chunks):
            values = list_ref[step * chunks + piece]
            high = values.astype(jnp.bfloat16).astype(jnp.float32)
            rest = values - high
            middle = rest.astype(jnp.bfloat16).astype(jnp.float32)
            parts = jnp.concatenate([high, middle, rest - middle, jnp.zeros_like(values)], axis=0)
            pieces.append(parts.astype(jnp.bfloat16).T)
        return jnp.concatenate(pieces, axis=0)

    def spread(step, out_ref):
        out_ref[...] = jnp.dot(turned(step), weights, preferred_element_type=jnp.float32)

    def block_force(wide_ref, row, mine):
        other = [wide_ref[pl.ds(row, 8), pl.ds(value * lanes, lanes)] for value in range(8)]
        apart = [other[axis] - mine[axis] for axis in range(3)]
        square = apart[0] * apart[0] + apart[1] * apart[1] + apart[2] * apart[2] + epsilon_sq
        inverse = lax.rsqrt(square)
        reach = other[6] + mine[6]
        overlap = jnp.maximum(reach - square * inverse, 0.0)
        overlap = jnp.where(other[7] != mine[7], overlap, 0.0)
        closing = (
            (other[3] - mine[3]) * apart[0]
            + (other[4] - mine[4]) * apart[1]
            + (other[5] - mine[5]) * apart[2]
        )
        scaled = overlap * (other[6] * mine[6])
        root = scaled * lax.rsqrt(jnp.maximum(scaled * reach, 1e-30))
        factor = root * inverse * (stiffness / damping * overlap - closing * inverse)
        return [factor * apart[axis] for axis in range(3)]

    def pairs(step, wide_ref, next_ref, carry):
        last, running = carry
        spread(step + 1, next_ref)
        for unit in range(units):
            cell = cell_smem[0, step * units + unit]
            own = jnp.minimum(cell, cells - 1) * 8
            mine = [table_ref[pl.ds(own + value, 8, stride=0), :] for value in range(8)]
            running = [jnp.where(cell == last, running[axis], 0.0) for axis in range(3)]
            for block in range(GROUP // 8):
                force = block_force(wide_ref, unit * GROUP + block * 8, mine)
                running = [running[axis] + force[axis] for axis in range(3)]
            last = cell
            for axis in range(3):
                force_ref[cell, axis] = running[axis]
        return last, running

    spread(0, even_ref)

    def both(step, carry):
        carry = pairs(2 * step, even_ref, odd_ref, carry)
        return pairs(2 * step + 1, odd_ref, even_ref, carry)

    zero = jnp.zeros((8, lanes), jnp.float32)
    steps = lax.div(groups + (2 * units - 1), 2 * units)
    lax.fori_loop(0, steps, both, (jnp.int32(-1), [zero] * 3))


def to_scalars(pairs, sems):
    copies = [
        pltpu.make_async_copy(source, target, sems.at[number])
        for number, (source, target) in enumerate(pairs)
    ]
    for copy in copies:
        copy.start()
    for copy in copies:
        copy.wait()


def list_kernel(
    near_of, sizes, amount_smem, code_ref, table_ref, slots_ref, where_ref, word_ref, cell_ref,
    groups_smem, *scratch,
):
    groups_smem[0] = list_tiles(
        amount_smem[0], near_of, sizes, code_ref, table_ref, slots_ref, where_ref, word_ref,
        cell_ref, *scratch,
    )


def inner_kernel(
    amount_smem, where_smem, word_smem, cell_smem, groups_smem, table_ref, slots_ref, force_ref,
    list_ref, even_ref, odd_ref, shift_ref,
):
    cells, _, lanes = table_ref.shape
    fill_lists(amount_smem[0], where_smem, word_smem, table_ref, slots_ref, shift_ref, list_ref)
    flat = table_ref.reshape(cells * 8, lanes)
    pair_forces(groups_smem[0], cell_smem, flat, list_ref, force_ref, even_ref, odd_ref)


def outer_kernel(
    near_of, sizes, amount_smem, code_ref, table_ref, halo_ref, inner_ref, arms_ref, frag_ref,
    fixed_ref, out_ref, force_ref, loads_ref, slots_ref, where_ref, word_ref, cell_ref,
    where_smem, word_smem, cell_smem, sems, list_ref, even_ref, odd_ref, shift_ref, *scratch,
):
    cells, _, lanes = table_ref.shape
    held = fixed_ref.shape[1] // 2
    amount = amount_smem[0]
    groups = list_tiles(
        amount, near_of, sizes, code_ref, halo_ref, slots_ref, where_ref, word_ref, cell_ref,
        *scratch,
    )
    to_scalars(
        [(where_ref, where_smem), (word_ref, word_smem), (cell_ref, cell_smem)], sems
    )
    fill_lists(amount, where_smem, word_smem, halo_ref, slots_ref, shift_ref, list_ref)
    flat = table_ref.reshape(cells * 8, lanes)
    pair_forces(groups, cell_smem, flat, list_ref, force_ref, even_ref, odd_ref)
    sums = fragment_sums(inner_ref, force_ref, arms_ref, frag_ref, loads_ref, held)
    out = fixed_ref[...] + jnp.concatenate([sums, jnp.zeros_like(sums)], axis=1)
    for brick in range(out_ref.shape[0]):
        out_ref[brick] = out


def fragment_sums(inner_ref, outer_ref, arms_ref, frag_ref, loads_ref, held):
    cells, lanes = frag_ref.shape
    tall = loads_ref.shape[0]
    label = lax.broadcasted_iota(jnp.int32, (held, lanes), 0)
    parts = [
        ref.reshape(ref.shape[0] * 24, lanes) for ref in (inner_ref, outer_ref)
    ]

    def total_force(block, axis):
        halves = []
        for half in range(tall // 8):
            first = (block * tall + half * 8) * 24 + axis * 8
            rows = [
                ref[pl.ds(first + part, 8, stride=24), :] for ref in parts for part in range(8)
            ]
            while len(rows) > 1:
                rows = [one + other for one, other in zip(rows[::2], rows[1::2])]
            halves.append(rows[0])
        return -damping * jnp.concatenate(halves, axis=0)

    def gather_sums(block, total):
        rows = pl.ds(pl.multiple_of(block * tall, tall), tall)
        force = [total_force(block, axis) for axis in range(3)]
        lever = [arms_ref[axis, rows, :] for axis in range(3)]
        torque = [
            lever[1] * force[2] - lever[2] * force[1],
            lever[2] * force[0] - lever[0] * force[2],
            lever[0] * force[1] - lever[1] * force[0],
        ]
        loads = force + torque + [jnp.zeros_like(force[0])] * 2
        for comp in range(8):
            loads_ref[:, comp, :] = loads[comp]
        frags = frag_ref[rows, :]
        hits = [
            (frags[unit : unit + 1, :] == label).astype(jnp.float32).astype(jnp.bfloat16)
            for unit in range(tall)
        ]
        values = [split_rows(loads_ref[unit]) for unit in range(tall)]
        return total + dot_lanes(jnp.concatenate(values, axis=1), jnp.concatenate(hits, axis=1))

    total = lax.fori_loop(0, cells // tall, gather_sums, jnp.zeros((24, held), jnp.float32))
    return joined_rows(total)


def move_kernel(
    owned, target_ref, known_ref, state_ref, arms_ref, frag_ref, spheres_ref, clumps_ref
):
    bricks, _, lanes = known_ref.shape
    held = lanes // 2
    cells = frag_ref.shape[0]
    targets = jnp.broadcast_to(target_ref[...], (lanes, lanes))
    lane = lax.broadcasted_iota(jnp.int32, (1, lanes), 1)

    def match(block, carry):
        sums, base = carry
        for unit in range(8):
            brick = block * 8 + unit
            known = known_ref[brick]
            values = split_rows(known)
            key = jnp.where(lane < held, known[6:7], -1.0)
            number = jnp.where(
                (lane >= held) & (lane < held + owned), brick * owned + lane - held, -1
            ).astype(jnp.float32)
            sums = sums + dot_lanes(values, (targets == key).astype(jnp.float32).astype(jnp.bfloat16))
            base = base + dot_lanes(values, (targets == number).astype(jnp.float32).astype(jnp.bfloat16))
        return sums, base

    zero = jnp.zeros((24, lanes), jnp.float32)
    sums, base = lax.fori_loop(0, bricks // 8, match, (zero, zero))
    sums = joined_rows(sums)
    base = joined_rows(base)
    rows = []
    for axis in range(3):
        pull = gravity if axis == 2 else 0.0
        rows.append(
            base[axis : axis + 1]
            + time_step * (sums[axis : axis + 1] * base[6:7] - pull)
        )
    for axis in range(3, 6):
        rows.append(base[axis : axis + 1] + time_step * sums[axis : axis + 1] * base[7:8])
    for comp in range(6):
        clumps_ref[comp : comp + 1, :] = rows[comp]
    tall = 32
    wide = [jnp.broadcast_to(value, (tall, lanes)) for value in rows]

    def cross(first, second):
        return [
            first[1] * second[2] - first[2] * second[1],
            first[2] * second[0] - first[0] * second[2],
            first[0] * second[1] - first[1] * second[0],
        ]

    def move(block, unused):
        at = pl.ds(pl.multiple_of(block * tall, tall), tall)
        index = frag_ref[at, :] + (lanes - held)
        motion = [lanes_of(value, index) for value in wide]
        velocity, spin = motion[0:3], motion[3:6]
        arm = [arms_ref[axis, at, :] for axis in range(3)]
        half = [0.5 * time_step * value for value in spin]
        turned = cross(half, arm)
        twice = cross(half, turned)
        scale = 2.0 / (1.0 + half[0] * half[0] + half[1] * half[1] + half[2] * half[2])
        change = [scale * (turned[axis] + twice[axis]) for axis in range(3)]
        new_arm = [arm[axis] + change[axis] for axis in range(3)]
        swing = cross(spin, new_arm)
        for axis in range(3):
            spheres_ref[axis, at, :] = (
                state_ref[axis, at, :] + time_step * velocity[axis] + (new_arm[axis] - arm[axis])
            )
            spheres_ref[3 + axis, at, :] = velocity[axis] + swing[axis]
        return unused

    lax.fori_loop(0, cells // tall, move, 0)


def local(
    state, arms, sphere_frag, frag_owner, frag_clump, tiles, clump_motion, inv_mass, inv_moment
):
    cells_x, cells_y, cells_z = (state.shape[1], state.shape[2], state.shape[3])
    lanes = state.shape[4]
    cells = cells_x * cells_y * cells_z
    owned = inv_mass.shape[0]
    held = frag_clump.shape[0]
    names = ("gx", "gy", "gz")
    vmem = pl.BlockSpec(memory_space=pltpu.VMEM)
    smem = pl.BlockSpec(memory_space=pltpu.SMEM)
    params = pltpu.CompilerParams(vmem_limit_bytes=VMEM)

    frag_key = (frag_owner[:, 0] * owned + frag_clump).astype(jnp.float32)
    flat_state = state.reshape(7, cells, lanes)
    flat_arms = arms.reshape(3, cells, lanes)
    flat_frag = sphere_frag.reshape(cells, lanes)

    fixed = jnp.concatenate(
        [
            jnp.concatenate([jnp.zeros((6, held)), frag_key[None], jnp.zeros((1, held))], axis=0),
            jnp.concatenate([clump_motion, inv_mass[None], inv_moment[None]], axis=0),
            jnp.zeros((8, lanes - held - owned)),
        ],
        axis=1,
    )

    face_shape = jax.ShapeDtypeStruct((cells_x * cells_y, 8, lanes), jnp.float32)
    table, z_last, z_first = pl.pallas_call(
        functools.partial(pack_kernel, cells_z),
        out_shape=(jax.ShapeDtypeStruct((cells, 8, lanes), jnp.float32), face_shape, face_shape),
        in_specs=[vmem] * 3,
        out_specs=(vmem,) * 3,
        compiler_params=params,
    )(flat_state, flat_frag, frag_key[None])
    grid = table.reshape(cells_x, cells_y, cells_z, 8, lanes)
    z_before, z_after = exchange(
        z_last.reshape(cells_x, cells_y, 1, 8, lanes),
        z_first.reshape(cells_x, cells_y, 1, 8, lanes),
        "gz",
    )

    outside = 1 << 20
    span_z = cells_z + 2
    starts = [0, cells_x * cells_y, 2 * cells_x * cells_y]
    starts += [starts[-1] + cells_y * span_z, starts[-1] + 2 * cells_y * span_z]
    starts += [starts[-1] + (cells_x + 2) * span_z]

    def inside(codes):
        own, kind = (codes // 27, codes % 27)
        x = own // (cells_y * cells_z) + kind // 9 - 1
        y = own // cells_z % cells_y + kind // 3 % 3 - 1
        z = own % cells_z + kind % 3 - 1
        inner = (x >= 0) & (x < cells_x) & (y >= 0) & (y < cells_y)
        return inner & (z >= 0) & (z < cells_z)

    def near_inside(x, y, z):
        return (x * cells_y + y) * cells_z + z

    def near_outside(x, y, z):
        in_y = jnp.where(y < 0, starts[4], starts[5]) + (x + 1) * span_z + z + 1
        in_x = jnp.where(x < 0, starts[2], starts[3]) + y * span_z + z + 1
        in_z = jnp.where(z < 0, starts[0], starts[1]) + x * cells_y + y
        in_x = jnp.where((x < 0) | (x >= cells_x), in_x, in_z)
        return jnp.where((y < 0) | (y >= cells_y), in_y, in_x)

    sizes = (cells_x, cells_y, cells_z)
    codes = tiles[0]
    total = codes.shape[0]
    codes = codes + jnp.where(inside(codes), 0, outside)
    chunks = total + cells * GROUP // lanes + 3 * SPREAD
    group_top = -(-(chunks * (lanes // GROUP) + SLACK) // (8 * lanes)) * 8 * lanes + 8 * lanes
    force_shape = (cells + 8, 3, 8, lanes)

    list_shapes = [(total, lanes), (1, total), (1, total), (1, group_top)]

    def list_scratch(span):
        return [
            pltpu.VMEM((-(-span // lanes) * lanes, lanes), jnp.float32),
            pltpu.VMEM((lanes, total), jnp.float32),
            pltpu.VMEM((cells, lanes), jnp.float32),
            pltpu.VMEM((1, total), jnp.int32),
            pltpu.VMEM((1, total), jnp.int32),
            pltpu.VMEM((1, total), jnp.int32),
        ]

    pair_scratch = [
        pltpu.VMEM((chunks, 8, lanes), jnp.float32),
        pltpu.VMEM((SPREAD * lanes, 8 * lanes), jnp.float32),
        pltpu.VMEM((SPREAD * lanes, 8 * lanes), jnp.float32),
        pltpu.VMEM((27, 8, lanes), jnp.float32),
    ]

    codes = jnp.sort(codes)
    inner_amount = jnp.sum((codes < outside).astype(jnp.int32))
    outer_amount = total - inner_amount
    z_before, z_after, codes, inner_amount = lax.optimization_barrier(
        (z_before, z_after, codes, inner_amount)
    )
    x_before, x_after = exchange(
        jnp.concatenate([z_before[-1:], grid[-1:], z_after[-1:]], axis=2),
        jnp.concatenate([z_before[:1], grid[:1], z_after[:1]], axis=2),
        "gx",
    )
    slots, where, word, cell_of, groups = pl.pallas_call(
        functools.partial(list_kernel, near_inside, sizes),
        out_shape=tuple(jax.ShapeDtypeStruct(shape, jnp.int32) for shape in list_shapes + [(1,)]),
        in_specs=[smem, vmem, vmem],
        out_specs=(vmem,) * 4 + (smem,),
        scratch_shapes=list_scratch(cells),
        compiler_params=params,
    )(inner_amount[None], (codes & (outside - 1))[None], table)
    x_before, x_after, slots, where, word, cell_of, groups = lax.optimization_barrier(
        (x_before, x_after, slots, where, word, cell_of, groups)
    )

    def face(at):
        middle = jnp.concatenate([z_before[:, at], grid[:, at], z_after[:, at]], axis=2)
        return jnp.concatenate([x_before[:, at], middle, x_after[:, at]], axis=0)

    y_before, y_after = exchange(face(slice(-1, None)), face(slice(0, 1)), "gy")
    inner = pl.pallas_call(
        inner_kernel,
        out_shape=jax.ShapeDtypeStruct(force_shape, jnp.float32),
        in_specs=[smem] * 5 + [vmem] * 2,
        out_specs=vmem,
        scratch_shapes=pair_scratch,
        compiler_params=params,
    )(inner_amount[None], where, word, cell_of, groups, table, slots)

    outer_codes = lax.dynamic_slice(jnp.concatenate([codes, codes]), (inner_amount,), (total,))
    outer_codes = outer_codes & (outside - 1)
    halo = jnp.concatenate(
        [
            part.reshape(-1, 8, lanes)
            for part in (z_before, z_after, x_before, x_after, y_before, y_after)
        ],
        axis=0,
    )
    bricks = lax.axis_size(names)
    known = pl.pallas_call(
        functools.partial(outer_kernel, near_outside, sizes),
        out_shape=jax.ShapeDtypeStruct((bricks, 8, lanes), jnp.float32),
        in_specs=[smem] + [vmem] * 7,
        out_specs=vmem,
        scratch_shapes=[
            pltpu.VMEM(force_shape, jnp.float32),
            pltpu.VMEM((16, 8, lanes), jnp.float32),
        ]
        + [pltpu.VMEM(shape, jnp.int32) for shape in list_shapes]
        + [pltpu.SMEM(shape, jnp.int32) for shape in list_shapes[1:]]
        + [pltpu.SemaphoreType.DMA((3,))]
        + pair_scratch
        + list_scratch(halo.shape[0]),
        compiler_params=params,
    )(outer_amount[None], outer_codes[None], table, halo, inner, flat_arms, flat_frag, fixed)
    known = lax.all_to_all(known, names, split_axis=0, concat_axis=0, tiled=True)

    brick = lax.axis_index(names)
    mine = jnp.where(
        jnp.arange(lanes - held) < owned, brick * owned + jnp.arange(lanes - held), -2
    ).astype(jnp.float32)
    target = jnp.concatenate([mine, frag_key])[:, None]
    spheres, clumps = pl.pallas_call(
        functools.partial(move_kernel, owned),
        out_shape=(
            jax.ShapeDtypeStruct((6, cells, lanes), jnp.float32),
            jax.ShapeDtypeStruct((6, lanes), jnp.float32),
        ),
        in_specs=[vmem] * 5,
        out_specs=(vmem, vmem),
        compiler_params=params,
    )(target, known, flat_state, flat_arms, flat_frag)
    return (spheres.reshape((6,) + state.shape[1:]), clumps[:, :owned])


def solution(mesh):
    return jax.shard_map(
        local,
        mesh=mesh,
        in_specs=(
            P(None, "gx", "gy", "gz", None),
            P(None, "gx", "gy", "gz", None),
            P("gx", "gy", "gz", None),
            P(("gx", "gy", "gz"), None),
            P(("gx", "gy", "gz")),
            P(("gx", "gy", "gz"), None),
            P(None, ("gx", "gy", "gz")),
            P(("gx", "gy", "gz")),
            P(("gx", "gy", "gz")),
        ),
        out_specs=(P(None, "gx", "gy", "gz", None), P(None, ("gx", "gy", "gz"))),
        check_vma=False,
    )
```

```python
import functools

import jax
import jax.numpy as jnp
from jax import lax
from jax.experimental import pallas as pl
from jax.experimental.pallas import tpu as pltpu
from jax.sharding import PartitionSpec as P

stiffness = 100.0
damping = 2.0
time_step = 0.01
gravity = 9.81
epsilon_sq = 1e-08
radius_top = 0.14

GROUP = 32
FILL = 32
SLACK = 256
SPREAD = 4
VMEM = 56 * 1024 * 1024


def lanes_of(values, index):
    return jnp.take_along_axis(values, index, axis=1, mode="promise_in_bounds")


def split_rows(values):
    high = values.astype(jnp.bfloat16).astype(jnp.float32)
    rest = values - high
    middle = rest.astype(jnp.bfloat16).astype(jnp.float32)
    low = rest - middle
    return jnp.concatenate([high, middle, low], axis=0).astype(jnp.bfloat16)


def joined_rows(stacked):
    rows = stacked.shape[0] // 3
    return stacked[0:rows] + stacked[rows : 2 * rows] + stacked[2 * rows :]


def dot_lanes(first, second):
    return lax.dot_general(
        first, second, (((1,), (1,)), ((), ())), preferred_element_type=jnp.float32
    )


def exchange(last, initial, axis):
    devices = lax.axis_size(axis)
    up = [(i, (i + 1) % devices) for i in range(devices)]
    down = [(j, i) for i, j in up]
    return lax.ppermute(last, axis, up), lax.ppermute(initial, axis, down)


def pack_kernel(deep, state_ref, frag_ref, key_ref, out_ref, last_ref, first_ref):
    cells, lanes = frag_ref.shape
    held = key_ref.shape[1]
    for comp in range(7):
        out_ref[:, comp, :] = state_ref[comp]
    keys = jnp.concatenate([key_ref[0:1, :], jnp.zeros((1, lanes - held), jnp.float32)], axis=1)
    keys = jnp.broadcast_to(keys, (8, lanes))
    for block in range(cells // 8):
        rows = pl.ds(block * 8, 8)
        out_ref[rows, 7, :] = lanes_of(keys, frag_ref[rows, :])
    for column in range(cells // deep):
        first_ref[column] = out_ref[column * deep]
        last_ref[column] = out_ref[column * deep + deep - 1]


def list_tiles(
    amount, near_of, sizes, code_ref, table_ref, slots_ref, where_ref, word_ref, cell_ref,
    class_ref, member_ref, count_ref, near_ref, need_ref, own_ref,
):
    tiles, lanes = slots_ref.shape
    span = table_ref.shape[0]
    padded = class_ref.shape[0]
    cells = count_ref.shape[0]
    wide = 256
    parts = 2
    flat = table_ref.reshape(span * 8, lanes)

    def plane(comp):
        return flat[pl.ds(comp, span, stride=8), :]

    def flag(value):
        return value.astype(jnp.float32).astype(jnp.bfloat16)

    def dot(first, second):
        return jnp.dot(first, second, preferred_element_type=jnp.float32)

    def ramp(shape, axis):
        return lax.broadcasted_iota(jnp.int32, shape, axis)

    def over(value, by):
        return jnp.floor((value.astype(jnp.float32) + 0.5) * (1.0 / by)).astype(jnp.int32)

    code = code_ref[...]
    own = over(code, 27)
    kind = code - 27 * own
    step_x = over(kind, 9)
    step_y = over(kind, 3) - 3 * step_x
    steps = (step_x - 1, step_y - 1, kind - 9 * step_x - 3 * step_y - 1)
    own_x = over(own, sizes[1] * sizes[2])
    row = over(own, sizes[2])
    near = near_of(
        own_x + steps[0], row - own_x * sizes[1] + steps[1], own - row * sizes[2] + steps[2]
    )
    need = sum(
        jnp.where(steps[axis] == 1, 1, jnp.where(steps[axis] == -1, 2, 0)) * (1 << (2 * axis))
        for axis in range(3)
    )
    live = ramp((1, tiles), 1) < amount
    near = jnp.where(live, near, 0)
    near_ref[...] = near
    word_ref[...] = near * 32 + jnp.where(live, kind, 0)
    need_ref[...] = jnp.where(live, need, 64)
    own_ref[...] = jnp.where(live, own, cells)

    radius = plane(6) + (radius_top + 1e-5)
    classes = jnp.zeros((span, lanes), jnp.float32)
    for axis in range(3):
        place = plane(axis)
        classes = classes + jnp.where(place < radius, 1.0 * (1 << (2 * axis)), 0.0)
        classes = classes + jnp.where(place > 1.0 - radius, 1.0 * (2 << (2 * axis)), 0.0)
    if padded > span:
        class_ref[...] = jnp.zeros(class_ref.shape, jnp.float32)
    class_ref[pl.ds(0, span), :] = classes
    codes = jnp.concatenate(
        [class_ref[pl.ds(at, lanes), :].T for at in range(0, padded, lanes)], axis=1
    ).astype(jnp.bfloat16)
    ones = jnp.ones((lanes, lanes), jnp.bfloat16)
    count_ref[...] = jnp.zeros(count_ref.shape, jnp.float32)
    blocks = lax.div(amount + (parts * wide - 1), parts * wide)

    def choose(block, unused):
        held = []
        for part in range(parts):
            at = pl.ds(pl.multiple_of((block * parts + part) * wide, wide), wide)
            hits = flag(ramp((padded, wide), 0) == near_ref[:, at])
            found = dot(codes, hits).astype(jnp.int32)
            need = need_ref[:, at]
            member = ((found & need) == need).astype(jnp.float32)
            member_ref[:, at] = member
            count = dot(ones, member.astype(jnp.bfloat16))
            mine = flag(ramp((cells, wide), 0) == own_ref[:, at])
            held.append(dot_lanes(mine, count[0:16].astype(jnp.bfloat16)))
        count_ref[:, 0:16] += held[0] + held[1]
        return unused

    lax.fori_loop(0, blocks, choose, 0)

    held = jnp.broadcast_to(count_ref[:, 0:1], count_ref.shape)
    high = jnp.floor(held * (1.0 / lanes))
    low = held - lanes * high
    taken = jnp.floor((held + (GROUP - 1)) * (1.0 / GROUP))
    upto = flag(ramp((cells, cells), 1) <= ramp((cells, cells), 0))
    ends = dot(upto, taken.astype(jnp.bfloat16))
    cell_ones = jnp.ones((8, cells), jnp.bfloat16)
    many = 8 * lanes
    wide_ends = jnp.concatenate([ends] * 8, axis=1)

    def name_groups(block, unused):
        group = (ramp((cells, many), 1) + block * many).astype(jnp.float32)
        at = pl.ds(pl.multiple_of(block * many, many), many)
        cell_ref[:, at] = dot(cell_ones, flag(wide_ends <= group))[0:1].astype(jnp.int32)
        return unused

    groups = jnp.max(ends).astype(jnp.int32)
    lax.fori_loop(0, lax.div(groups + SLACK, many) + 1, name_groups, 0)
    before_cell = jnp.concatenate(
        [value.T[0:8] for value in (taken, high, low)], axis=0
    ).astype(jnp.bfloat16)

    earlier = flag(ramp((lanes, lanes), 1) < ramp((lanes, lanes), 0))
    earlier_tile = flag(ramp((wide, wide), 0) < ramp((wide, wide), 1))

    def place(block, done):
        for part in range(parts):
            first = pl.multiple_of((block * parts + part) * wide, wide)
            at = pl.ds(first, wide)
            flags = member_ref[:, at].astype(jnp.bfloat16)
            count = dot(ones, flags)
            lower = flag(ramp((cells, wide), 0) < own_ref[:, at])
            before = dot(before_cell, lower)
            so_far = dot(count[0:8].astype(jnp.bfloat16), earlier_tile) + done
            start = GROUP * before[0:8] + so_far - (lanes * before[8:16] + before[16:24])
            start = start.astype(jnp.int32)[0:1]
            where_ref[:, at] = start * 256 + count[0:1].astype(jnp.int32)
            rank = dot(earlier, flags)
            slot = ramp((lanes, wide), 0)
            moves = slot - rank.astype(jnp.int32)
            word = jnp.where(member_ref[:, at] > 0.0, slot + lanes * moves, 0)
            bit = 1
            while bit < lanes:
                keep = jnp.where((word & (bit * lanes)) != 0, 0, word)
                gone = word ^ keep
                word = keep | jnp.concatenate([gone[bit:], gone[:bit]], axis=0)
                bit *= 2
            word = word & (lanes - 1)
            turn = jnp.broadcast_to(start, (lanes, wide))
            bit = 1
            while bit < lanes:
                moved = jnp.concatenate([word[lanes - bit :], word[: lanes - bit]], axis=0)
                word = jnp.where((turn & bit) != 0, moved, word)
                bit *= 2
            for half in range(wide // lanes):
                rows = pl.ds(pl.multiple_of(first + half * lanes, lanes), lanes)
                slots_ref[rows, :] = word[:, half * lanes : (half + 1) * lanes].T
            done = done + jnp.sum(count[0:8], axis=1, keepdims=True)
        return done

    lax.fori_loop(0, blocks, place, jnp.zeros((8, 1), jnp.float32))
    return groups


def fill_lists(amount, where_smem, near_smem, table_ref, slots_ref, shift_ref, list_ref):
    tiles, lanes = slots_ref.shape
    lane_bits = lanes.bit_length() - 1
    lane = lax.broadcasted_iota(jnp.int32, (8, lanes), 1)
    row = lax.broadcasted_iota(jnp.int32, (8, lanes), 0)
    absent = jnp.where(row == 6, -10.0, 0.0)
    for kind in range(27):
        steps = (kind // 9 - 1.0, kind // 3 % 3 - 1.0, kind % 3 - 1.0)
        shift_ref[kind] = sum(jnp.where(row == axis, steps[axis], 0.0) for axis in range(3))

    def fill(block, carry):
        last_chunk, last_new, last_held = carry
        units = range(FILL)
        where = [where_smem[0, block * FILL + unit] for unit in units]
        near = [near_smem[0, block * FILL + unit] for unit in units]
        found = []
        for unit in units:
            slots = slots_ref[pl.ds(block * FILL + unit, 8, stride=0), :]
            cell = table_ref[near[unit] >> 5]
            found.append(lanes_of(cell, slots) + shift_ref[near[unit] & 31])
        for unit in units:
            amount = where[unit] & 255
            chunk = where[unit] >> (8 + lane_bits)
            offset = (where[unit] >> 8) & (lanes - 1)
            new = jnp.where(((lane - offset) & (lanes - 1)) < amount, found[unit], absent)
            held_row = jnp.where(chunk != last_chunk, last_new, last_held)
            held_row = jnp.where(lane >= offset, new, held_row)
            new = jnp.where(lane >= offset, absent, new)
            list_ref[chunk] = held_row
            list_ref[chunk + 1] = new
            last_chunk, last_new, last_held = chunk, new, held_row
        return last_chunk, last_new, last_held

    blocks = lax.div(amount + (FILL - 1), FILL)
    lax.fori_loop(0, blocks, fill, (jnp.int32(0), absent, absent))


def pair_forces(groups, cell_smem, table_ref, list_ref, force_ref, even_ref, odd_ref):
    lanes = table_ref.shape[1]
    cells = table_ref.shape[0] // 8
    rows = even_ref.shape[0]
    chunks = rows // lanes
    units = rows // GROUP
    force_ref[...] = jnp.zeros(force_ref.shape, jnp.float32)
    part = lax.broadcasted_iota(jnp.int32, (32, 8 * lanes), 0)
    comp = lax.broadcasted_iota(jnp.int32, (32, 8 * lanes), 1) // lanes
    weights = jnp.where((part < 24) & (part % 8 == comp), 1.0, 0.0).astype(jnp.bfloat16)

    def turned(step):
        pieces = []
        for piece in range(chunks):
            values = list_ref[step * chunks + piece]
            high = values.astype(jnp.bfloat16).astype(jnp.float32)
            rest = values - high
            middle = rest.astype(jnp.bfloat16).astype(jnp.float32)
            parts = jnp.concatenate([high, middle, rest - middle, jnp.zeros_like(values)], axis=0)
            pieces.append(parts.astype(jnp.bfloat16).T)
        return jnp.concatenate(pieces, axis=0)

    def spread(step, out_ref):
        out_ref[...] = jnp.dot(turned(step), weights, preferred_element_type=jnp.float32)

    def block_force(wide_ref, row, mine):
        other = [wide_ref[pl.ds(row, 8), pl.ds(value * lanes, lanes)] for value in range(8)]
        apart = [other[axis] - mine[axis] for axis in range(3)]
        square = apart[0] * apart[0] + apart[1] * apart[1] + apart[2] * apart[2] + epsilon_sq
        inverse = lax.rsqrt(square)
        reach = other[6] + mine[6]
        overlap = jnp.maximum(reach - square * inverse, 0.0)
        overlap = jnp.where(other[7] != mine[7], overlap, 0.0)
        closing = (
            (other[3] - mine[3]) * apart[0]
            + (other[4] - mine[4]) * apart[1]
            + (other[5] - mine[5]) * apart[2]
        )
        scaled = overlap * (other[6] * mine[6])
        root = scaled * lax.rsqrt(jnp.maximum(scaled * reach, 1e-30))
        factor = root * inverse * (stiffness / damping * overlap - closing * inverse)
        return [factor * apart[axis] for axis in range(3)]

    def pairs(step, wide_ref, next_ref, carry):
        last, running = carry
        spread(step + 1, next_ref)
        for unit in range(units):
            cell = cell_smem[0, step * units + unit]
            own = jnp.minimum(cell, cells - 1) * 8
            mine = [table_ref[pl.ds(own + value, 8, stride=0), :] for value in range(8)]
            running = [jnp.where(cell == last, running[axis], 0.0) for axis in range(3)]
            for block in range(GROUP // 8):
                force = block_force(wide_ref, unit * GROUP + block * 8, mine)
                running = [running[axis] + force[axis] for axis in range(3)]
            last = cell
            for axis in range(3):
                force_ref[cell, axis] = running[axis]
        return last, running

    spread(0, even_ref)

    def both(step, carry):
        carry = pairs(2 * step, even_ref, odd_ref, carry)
        return pairs(2 * step + 1, odd_ref, even_ref, carry)

    zero = jnp.zeros((8, lanes), jnp.float32)
    steps = lax.div(groups + (2 * units - 1), 2 * units)
    lax.fori_loop(0, steps, both, (jnp.int32(-1), [zero] * 3))


def to_scalars(pairs, sems):
    copies = [
        pltpu.make_async_copy(source, target, sems.at[number])
        for number, (source, target) in enumerate(pairs)
    ]
    for copy in copies:
        copy.start()
    for copy in copies:
        copy.wait()


def list_kernel(
    near_of, sizes, amount_smem, code_ref, table_ref, slots_ref, where_ref, word_ref, cell_ref,
    groups_smem, *scratch,
):
    groups_smem[0] = list_tiles(
        amount_smem[0], near_of, sizes, code_ref, table_ref, slots_ref, where_ref, word_ref,
        cell_ref, *scratch,
    )


def inner_kernel(
    amount_smem, where_smem, word_smem, cell_smem, groups_smem, table_ref, slots_ref, force_ref,
    list_ref, even_ref, odd_ref, shift_ref,
):
    cells, _, lanes = table_ref.shape
    fill_lists(amount_smem[0], where_smem, word_smem, table_ref, slots_ref, shift_ref, list_ref)
    flat = table_ref.reshape(cells * 8, lanes)
    pair_forces(groups_smem[0], cell_smem, flat, list_ref, force_ref, even_ref, odd_ref)


def outer_kernel(
    near_of, sizes, amount_smem, code_ref, table_ref, halo_ref, inner_ref, arms_ref, frag_ref,
    fixed_ref, out_ref, force_ref, loads_ref, slots_ref, where_ref, word_ref, cell_ref,
    where_smem, word_smem, cell_smem, sems, list_ref, even_ref, odd_ref, shift_ref, *scratch,
):
    cells, _, lanes = table_ref.shape
    held = fixed_ref.shape[1] // 2
    amount = amount_smem[0]
    groups = list_tiles(
        amount, near_of, sizes, code_ref, halo_ref, slots_ref, where_ref, word_ref, cell_ref,
        *scratch,
    )
    to_scalars(
        [(where_ref, where_smem), (word_ref, word_smem), (cell_ref, cell_smem)], sems
    )
    fill_lists(amount, where_smem, word_smem, halo_ref, slots_ref, shift_ref, list_ref)
    flat = table_ref.reshape(cells * 8, lanes)
    pair_forces(groups, cell_smem, flat, list_ref, force_ref, even_ref, odd_ref)
    sums = fragment_sums(inner_ref, force_ref, arms_ref, frag_ref, loads_ref, held)
    out = fixed_ref[...] + jnp.concatenate([sums, jnp.zeros_like(sums)], axis=1)
    for brick in range(out_ref.shape[0]):
        out_ref[brick] = out


def fragment_sums(inner_ref, outer_ref, arms_ref, frag_ref, loads_ref, held):
    cells, lanes = frag_ref.shape
    tall = loads_ref.shape[0]
    label = lax.broadcasted_iota(jnp.int32, (held, lanes), 0)
    parts = [
        ref.reshape(ref.shape[0] * 24, lanes) for ref in (inner_ref, outer_ref)
    ]

    def total_force(block, axis):
        halves = []
        for half in range(tall // 8):
            first = (block * tall + half * 8) * 24 + axis * 8
            rows = [
                ref[pl.ds(first + part, 8, stride=24), :] for ref in parts for part in range(8)
            ]
            while len(rows) > 1:
                rows = [one + other for one, other in zip(rows[::2], rows[1::2])]
            halves.append(rows[0])
        return -damping * jnp.concatenate(halves, axis=0)

    def gather_sums(block, total):
        rows = pl.ds(pl.multiple_of(block * tall, tall), tall)
        force = [total_force(block, axis) for axis in range(3)]
        lever = [arms_ref[axis, rows, :] for axis in range(3)]
        torque = [
            lever[1] * force[2] - lever[2] * force[1],
            lever[2] * force[0] - lever[0] * force[2],
            lever[0] * force[1] - lever[1] * force[0],
        ]
        loads = force + torque + [jnp.zeros_like(force[0])] * 2
        for comp in range(8):
            loads_ref[:, comp, :] = loads[comp]
        frags = frag_ref[rows, :]
        hits = [
            (frags[unit : unit + 1, :] == label).astype(jnp.float32).astype(jnp.bfloat16)
            for unit in range(tall)
        ]
        values = [split_rows(loads_ref[unit]) for unit in range(tall)]
        return total + dot_lanes(jnp.concatenate(hits, axis=1), jnp.concatenate(values, axis=1))

    total = lax.fori_loop(0, cells // tall, gather_sums, jnp.zeros((held, 24), jnp.float32))
    return joined_rows(total.T)


def move_kernel(
    owned, target_ref, known_ref, state_ref, arms_ref, frag_ref, spheres_ref, clumps_ref
):
    bricks, _, lanes = known_ref.shape
    held = lanes // 2
    cells = frag_ref.shape[0]
    targets = jnp.broadcast_to(target_ref[...], (lanes, lanes))
    lane = lax.broadcasted_iota(jnp.int32, (1, lanes), 1)

    def match(block, carry):
        sums, base = carry
        for unit in range(8):
            brick = block * 8 + unit
            known = known_ref[brick]
            values = split_rows(known)
            key = jnp.where(lane < held, known[6:7], -1.0)
            number = jnp.where(
                (lane >= held) & (lane < held + owned), brick * owned + lane - held, -1
            ).astype(jnp.float32)
            sums = sums + dot_lanes((targets == key).astype(jnp.float32).astype(jnp.bfloat16), values)
            base = base + dot_lanes((targets == number).astype(jnp.float32).astype(jnp.bfloat16), values)
        return sums, base

    zero = jnp.zeros((lanes, 24), jnp.float32)
    sums, base = lax.fori_loop(0, bricks // 8, match, (zero, zero))
    sums = joined_rows(sums.T)
    base = joined_rows(base.T)
    rows = []
    for axis in range(3):
        pull = gravity if axis == 2 else 0.0
        rows.append(
            base[axis : axis + 1]
            + time_step * (sums[axis : axis + 1] * base[6:7] - pull)
        )
    for axis in range(3, 6):
        rows.append(base[axis : axis + 1] + time_step * sums[axis : axis + 1] * base[7:8])
    for comp in range(6):
        clumps_ref[comp : comp + 1, :] = rows[comp]
    tall = 32
    wide = [jnp.broadcast_to(value, (tall, lanes)) for value in rows]

    def cross(first, second):
        return [
            first[1] * second[2] - first[2] * second[1],
            first[2] * second[0] - first[0] * second[2],
            first[0] * second[1] - first[1] * second[0],
        ]

    def move(block, unused):
        at = pl.ds(pl.multiple_of(block * tall, tall), tall)
        index = frag_ref[at, :] + (lanes - held)
        motion = [lanes_of(value, index) for value in wide]
        velocity, spin = motion[0:3], motion[3:6]
        arm = [arms_ref[axis, at, :] for axis in range(3)]
        half = [0.5 * time_step * value for value in spin]
        turned = cross(half, arm)
        twice = cross(half, turned)
        scale = 2.0 / (1.0 + half[0] * half[0] + half[1] * half[1] + half[2] * half[2])
        change = [scale * (turned[axis] + twice[axis]) for axis in range(3)]
        new_arm = [arm[axis] + change[axis] for axis in range(3)]
        swing = cross(spin, new_arm)
        for axis in range(3):
            spheres_ref[axis, at, :] = (
                state_ref[axis, at, :] + time_step * velocity[axis] + (new_arm[axis] - arm[axis])
            )
            spheres_ref[3 + axis, at, :] = velocity[axis] + swing[axis]
        return unused

    lax.fori_loop(0, cells // tall, move, 0)


def local(
    state, arms, sphere_frag, frag_owner, frag_clump, tiles, clump_motion, inv_mass, inv_moment
):
    cells_x, cells_y, cells_z = (state.shape[1], state.shape[2], state.shape[3])
    lanes = state.shape[4]
    cells = cells_x * cells_y * cells_z
    owned = inv_mass.shape[0]
    held = frag_clump.shape[0]
    names = ("gx", "gy", "gz")
    vmem = pl.BlockSpec(memory_space=pltpu.VMEM)
    smem = pl.BlockSpec(memory_space=pltpu.SMEM)
    params = pltpu.CompilerParams(vmem_limit_bytes=VMEM)

    frag_key = (frag_owner[:, 0] * owned + frag_clump).astype(jnp.float32)
    flat_state = state.reshape(7, cells, lanes)
    flat_arms = arms.reshape(3, cells, lanes)
    flat_frag = sphere_frag.reshape(cells, lanes)

    fixed = jnp.concatenate(
        [
            jnp.concatenate([jnp.zeros((6, held)), frag_key[None], jnp.zeros((1, held))], axis=0),
            jnp.concatenate([clump_motion, inv_mass[None], inv_moment[None]], axis=0),
            jnp.zeros((8, lanes - held - owned)),
        ],
        axis=1,
    )

    face_shape = jax.ShapeDtypeStruct((cells_x * cells_y, 8, lanes), jnp.float32)
    table, z_last, z_first = pl.pallas_call(
        functools.partial(pack_kernel, cells_z),
        out_shape=(jax.ShapeDtypeStruct((cells, 8, lanes), jnp.float32), face_shape, face_shape),
        in_specs=[vmem] * 3,
        out_specs=(vmem,) * 3,
        compiler_params=params,
    )(flat_state, flat_frag, frag_key[None])
    grid = table.reshape(cells_x, cells_y, cells_z, 8, lanes)
    z_before, z_after = exchange(
        z_last.reshape(cells_x, cells_y, 1, 8, lanes),
        z_first.reshape(cells_x, cells_y, 1, 8, lanes),
        "gz",
    )

    outside = 1 << 20
    span_z = cells_z + 2
    starts = [0, cells_x * cells_y, 2 * cells_x * cells_y]
    starts += [starts[-1] + cells_y * span_z, starts[-1] + 2 * cells_y * span_z]
    starts += [starts[-1] + (cells_x + 2) * span_z]

    def inside(codes):
        own, kind = (codes // 27, codes % 27)
        x = own // (cells_y * cells_z) + kind // 9 - 1
        y = own // cells_z % cells_y + kind // 3 % 3 - 1
        z = own % cells_z + kind % 3 - 1
        inner = (x >= 0) & (x < cells_x) & (y >= 0) & (y < cells_y)
        return inner & (z >= 0) & (z < cells_z)

    def near_inside(x, y, z):
        return (x * cells_y + y) * cells_z + z

    def near_outside(x, y, z):
        in_y = jnp.where(y < 0, starts[4], starts[5]) + (x + 1) * span_z + z + 1
        in_x = jnp.where(x < 0, starts[2], starts[3]) + y * span_z + z + 1
        in_z = jnp.where(z < 0, starts[0], starts[1]) + x * cells_y + y
        in_x = jnp.where((x < 0) | (x >= cells_x), in_x, in_z)
        return jnp.where((y < 0) | (y >= cells_y), in_y, in_x)

    sizes = (cells_x, cells_y, cells_z)
    codes = tiles[0]
    total = codes.shape[0]
    codes = codes + jnp.where(inside(codes), 0, outside)
    chunks = total + cells * GROUP // lanes + 3 * SPREAD
    group_top = -(-(chunks * (lanes // GROUP) + SLACK) // (8 * lanes)) * 8 * lanes + 8 * lanes
    force_shape = (cells + 8, 3, 8, lanes)

    list_shapes = [(total, lanes), (1, total), (1, total), (1, group_top)]

    def list_scratch(span):
        return [
            pltpu.VMEM((-(-span // lanes) * lanes, lanes), jnp.float32),
            pltpu.VMEM((lanes, total), jnp.float32),
            pltpu.VMEM((cells, lanes), jnp.float32),
            pltpu.VMEM((1, total), jnp.int32),
            pltpu.VMEM((1, total), jnp.int32),
            pltpu.VMEM((1, total), jnp.int32),
        ]

    pair_scratch = [
        pltpu.VMEM((chunks, 8, lanes), jnp.float32),
        pltpu.VMEM((SPREAD * lanes, 8 * lanes), jnp.float32),
        pltpu.VMEM((SPREAD * lanes, 8 * lanes), jnp.float32),
        pltpu.VMEM((27, 8, lanes), jnp.float32),
    ]

    codes = jnp.sort(codes)
    inner_amount = jnp.sum((codes < outside).astype(jnp.int32))
    outer_amount = total - inner_amount
    z_before, z_after, codes, inner_amount = lax.optimization_barrier(
        (z_before, z_after, codes, inner_amount)
    )
    x_before, x_after = exchange(
        jnp.concatenate([z_before[-1:], grid[-1:], z_after[-1:]], axis=2),
        jnp.concatenate([z_before[:1], grid[:1], z_after[:1]], axis=2),
        "gx",
    )
    slots, where, word, cell_of, groups = pl.pallas_call(
        functools.partial(list_kernel, near_inside, sizes),
        out_shape=tuple(jax.ShapeDtypeStruct(shape, jnp.int32) for shape in list_shapes + [(1,)]),
        in_specs=[smem, vmem, vmem],
        out_specs=(vmem,) * 4 + (smem,),
        scratch_shapes=list_scratch(cells),
        compiler_params=params,
    )(inner_amount[None], (codes & (outside - 1))[None], table)
    x_before, x_after, slots, where, word, cell_of, groups = lax.optimization_barrier(
        (x_before, x_after, slots, where, word, cell_of, groups)
    )

    def face(at):
        middle = jnp.concatenate([z_before[:, at], grid[:, at], z_after[:, at]], axis=2)
        return jnp.concatenate([x_before[:, at], middle, x_after[:, at]], axis=0)

    y_before, y_after = exchange(face(slice(-1, None)), face(slice(0, 1)), "gy")
    inner = pl.pallas_call(
        inner_kernel,
        out_shape=jax.ShapeDtypeStruct(force_shape, jnp.float32),
        in_specs=[smem] * 5 + [vmem] * 2,
        out_specs=vmem,
        scratch_shapes=pair_scratch,
        compiler_params=params,
    )(inner_amount[None], where, word, cell_of, groups, table, slots)

    outer_codes = lax.dynamic_slice(jnp.concatenate([codes, codes]), (inner_amount,), (total,))
    outer_codes = outer_codes & (outside - 1)
    halo = jnp.concatenate(
        [
            part.reshape(-1, 8, lanes)
            for part in (z_before, z_after, x_before, x_after, y_before, y_after)
        ],
        axis=0,
    )
    bricks = lax.axis_size(names)
    known = pl.pallas_call(
        functools.partial(outer_kernel, near_outside, sizes),
        out_shape=jax.ShapeDtypeStruct((bricks, 8, lanes), jnp.float32),
        in_specs=[smem] + [vmem] * 7,
        out_specs=vmem,
        scratch_shapes=[
            pltpu.VMEM(force_shape, jnp.float32),
            pltpu.VMEM((16, 8, lanes), jnp.float32),
        ]
        + [pltpu.VMEM(shape, jnp.int32) for shape in list_shapes]
        + [pltpu.SMEM(shape, jnp.int32) for shape in list_shapes[1:]]
        + [pltpu.SemaphoreType.DMA((3,))]
        + pair_scratch
        + list_scratch(halo.shape[0]),
        compiler_params=params,
    )(outer_amount[None], outer_codes[None], table, halo, inner, flat_arms, flat_frag, fixed)
    known = lax.all_to_all(known, names, split_axis=0, concat_axis=0, tiled=True)

    brick = lax.axis_index(names)
    mine = jnp.where(
        jnp.arange(lanes - held) < owned, brick * owned + jnp.arange(lanes - held), -2
    ).astype(jnp.float32)
    target = jnp.concatenate([mine, frag_key])[:, None]
    spheres, clumps = pl.pallas_call(
        functools.partial(move_kernel, owned),
        out_shape=(
            jax.ShapeDtypeStruct((6, cells, lanes), jnp.float32),
            jax.ShapeDtypeStruct((6, lanes), jnp.float32),
        ),
        in_specs=[vmem] * 5,
        out_specs=(vmem, vmem),
        compiler_params=params,
    )(target, known, flat_state, flat_arms, flat_frag)
    return (spheres.reshape((6,) + state.shape[1:]), clumps[:, :owned])


def solution(mesh):
    return jax.shard_map(
        local,
        mesh=mesh,
        in_specs=(
            P(None, "gx", "gy", "gz", None),
            P(None, "gx", "gy", "gz", None),
            P("gx", "gy", "gz", None),
            P(("gx", "gy", "gz"), None),
            P(("gx", "gy", "gz")),
            P(("gx", "gy", "gz"), None),
            P(None, ("gx", "gy", "gz")),
            P(("gx", "gy", "gz")),
            P(("gx", "gy", "gz")),
        ),
        out_specs=(P(None, "gx", "gy", "gz", None), P(None, ("gx", "gy", "gz"))),
        check_vma=False,
    )
```

```python
import functools

import jax
import jax.numpy as jnp
from jax import lax
from jax.experimental import pallas as pl
from jax.experimental.pallas import tpu as pltpu
from jax.sharding import PartitionSpec as P

stiffness = 100.0
damping = 2.0
time_step = 0.01
gravity = 9.81
epsilon_sq = 1e-08
radius_top = 0.14

INNER_GROUP = 32
OUTER_GROUP = 16
FILL = 32
WORD_BITS = 16
SLACK = 256
SPREAD = 4
VMEM = 56 * 1024 * 1024


def lanes_of(values, index):
    return jnp.take_along_axis(values, index, axis=1, mode="promise_in_bounds")


def split_rows(values):
    high = values.astype(jnp.bfloat16).astype(jnp.float32)
    rest = values - high
    middle = rest.astype(jnp.bfloat16).astype(jnp.float32)
    low = rest - middle
    return jnp.concatenate([high, middle, low], axis=0).astype(jnp.bfloat16)


def joined_rows(stacked):
    rows = stacked.shape[0] // 3
    return stacked[0:rows] + stacked[rows : 2 * rows] + stacked[2 * rows :]


def dot_lanes(first, second):
    return lax.dot_general(
        first, second, (((1,), (1,)), ((), ())), preferred_element_type=jnp.float32
    )


def exchange(last, initial, axis):
    devices = lax.axis_size(axis)
    up = [(i, (i + 1) % devices) for i in range(devices)]
    down = [(j, i) for i, j in up]
    return lax.ppermute(last, axis, up), lax.ppermute(initial, axis, down)


def pack_kernel(deep, state_ref, frag_ref, key_ref, out_ref, last_ref, first_ref):
    cells, lanes = frag_ref.shape
    held = key_ref.shape[1]
    for comp in range(7):
        out_ref[:, comp, :] = state_ref[comp]
    keys = jnp.concatenate([key_ref[0:1, :], jnp.zeros((1, lanes - held), jnp.float32)], axis=1)
    keys = jnp.broadcast_to(keys, (8, lanes))
    for block in range(cells // 8):
        rows = pl.ds(block * 8, 8)
        out_ref[rows, 7, :] = lanes_of(keys, frag_ref[rows, :])
    for column in range(cells // deep):
        first_ref[column] = out_ref[column * deep]
        last_ref[column] = out_ref[column * deep + deep - 1]


def list_tiles(
    group, amount, near_of, sizes, code_ref, table_ref, slots_ref, word_ref, cell_ref,
    class_ref, member_ref, count_ref, near_ref, need_ref, own_ref, kind_ref,
):
    tiles, lanes = slots_ref.shape
    span = table_ref.shape[0]
    padded = class_ref.shape[0]
    cells = count_ref.shape[0]
    lane_bits = lanes.bit_length() - 1
    wide = 256
    parts = 2
    flat = table_ref.reshape(span * 8, lanes)

    def plane(comp):
        return flat[pl.ds(comp, span, stride=8), :]

    def flag(value):
        return value.astype(jnp.float32).astype(jnp.bfloat16)

    def dot(first, second):
        return jnp.dot(first, second, preferred_element_type=jnp.float32)

    def ramp(shape, axis):
        return lax.broadcasted_iota(jnp.int32, shape, axis)

    def over(value, by):
        return jnp.floor((value.astype(jnp.float32) + 0.5) * (1.0 / by)).astype(jnp.int32)

    code = code_ref[...]
    own = over(code, 27)
    kind = code - 27 * own
    step_x = over(kind, 9)
    step_y = over(kind, 3) - 3 * step_x
    steps = (step_x - 1, step_y - 1, kind - 9 * step_x - 3 * step_y - 1)
    own_x = over(own, sizes[1] * sizes[2])
    row = over(own, sizes[2])
    near = near_of(
        own_x + steps[0], row - own_x * sizes[1] + steps[1], own - row * sizes[2] + steps[2]
    )
    need = sum(
        jnp.where(steps[axis] == 1, 1, jnp.where(steps[axis] == -1, 2, 0)) * (1 << (2 * axis))
        for axis in range(3)
    )
    live = ramp((1, tiles), 1) < amount
    near = jnp.where(live, near, 0)
    near_ref[...] = near
    kind_ref[...] = near * 32 + jnp.where(live, kind, 0)
    need_ref[...] = jnp.where(live, need, 64)
    own_ref[...] = jnp.where(live, own, cells)

    radius = plane(6) + (radius_top + 1e-5)
    classes = jnp.zeros((span, lanes), jnp.float32)
    for axis in range(3):
        place = plane(axis)
        classes = classes + jnp.where(place < radius, 1.0 * (1 << (2 * axis)), 0.0)
        classes = classes + jnp.where(place > 1.0 - radius, 1.0 * (2 << (2 * axis)), 0.0)
    if padded > span:
        class_ref[...] = jnp.zeros(class_ref.shape, jnp.float32)
    class_ref[pl.ds(0, span), :] = classes
    codes = jnp.concatenate(
        [class_ref[pl.ds(at, lanes), :].T for at in range(0, padded, lanes)], axis=1
    ).astype(jnp.bfloat16)
    ones = jnp.ones((lanes, lanes), jnp.bfloat16)
    count_ref[...] = jnp.zeros(count_ref.shape, jnp.float32)
    blocks = lax.div(amount + (parts * wide - 1), parts * wide)

    def choose(block, unused):
        held = []
        for part in range(parts):
            at = pl.ds(pl.multiple_of((block * parts + part) * wide, wide), wide)
            hits = flag(ramp((padded, wide), 0) == near_ref[:, at])
            found = dot(codes, hits).astype(jnp.int32)
            need = need_ref[:, at]
            member = ((found & need) == need).astype(jnp.float32)
            member_ref[:, at] = member
            count = dot(ones, member.astype(jnp.bfloat16))
            mine = flag(ramp((cells, wide), 0) == own_ref[:, at])
            held.append(dot_lanes(mine, count[0:16].astype(jnp.bfloat16)))
        count_ref[:, 0:16] += held[0] + held[1]
        return unused

    lax.fori_loop(0, blocks, choose, 0)

    held = jnp.broadcast_to(count_ref[:, 0:1], count_ref.shape)
    high = jnp.floor(held * (1.0 / lanes))
    low = held - lanes * high
    taken = jnp.floor((held + (group - 1)) * (1.0 / group))
    upto = flag(ramp((cells, cells), 1) <= ramp((cells, cells), 0))
    ends = dot(upto, taken.astype(jnp.bfloat16))
    cell_ones = jnp.ones((8, cells), jnp.bfloat16)
    many = 8 * lanes
    wide_ends = jnp.concatenate([ends] * 8, axis=1)

    def name_groups(block, unused):
        number = (ramp((cells, many), 1) + block * many).astype(jnp.float32)
        at = pl.ds(pl.multiple_of(block * many, many), many)
        cell_ref[:, at] = dot(cell_ones, flag(wide_ends <= number))[0:1].astype(jnp.int32)
        return unused

    groups = jnp.max(ends).astype(jnp.int32)
    lax.fori_loop(0, lax.div(groups + SLACK, many) + 1, name_groups, 0)
    before_cell = jnp.concatenate(
        [value.T[0:8] for value in (taken, high, low)], axis=0
    ).astype(jnp.bfloat16)

    earlier = flag(ramp((lanes, lanes), 1) < ramp((lanes, lanes), 0))
    earlier_tile = flag(ramp((wide, wide), 0) < ramp((wide, wide), 1))

    def place(block, done):
        for part in range(parts):
            first = pl.multiple_of((block * parts + part) * wide, wide)
            at = pl.ds(first, wide)
            flags = member_ref[:, at].astype(jnp.bfloat16)
            count = dot(ones, flags)
            lower = flag(ramp((cells, wide), 0) < own_ref[:, at])
            before = dot(before_cell, lower)
            so_far = dot(count[0:8].astype(jnp.bfloat16), earlier_tile) + done
            start = group * before[0:8] + so_far - (lanes * before[8:16] + before[16:24])
            start = start.astype(jnp.int32)[0:1]
            offset = jnp.broadcast_to(start & (lanes - 1), (8, wide))
            word_ref[:, at] = (start >> lane_bits) * (1 << WORD_BITS) + kind_ref[:, at]
            rank = dot(earlier, flags)
            slot = ramp((lanes, wide), 0)
            moves = slot - rank.astype(jnp.int32)
            word = jnp.where(member_ref[:, at] > 0.0, slot + lanes * moves, 0)
            bit = 1
            while bit < lanes:
                keep = jnp.where((word & (bit * lanes)) != 0, 0, word)
                gone = word ^ keep
                word = keep | jnp.concatenate([gone[bit:], gone[:bit]], axis=0)
                bit *= 2
            word = word & (lanes - 1)
            line = ramp((8, wide), 0)
            within = offset & 7
            pick = (line - within) & 7
            slabs = [
                jnp.take_along_axis(
                    word[at_row : at_row + 8], pick, axis=0, mode="promise_in_bounds"
                )
                for at_row in range(0, lanes, 8)
            ]
            slabs = [
                jnp.where(line >= within, slabs[number], slabs[number - 1])
                for number in range(len(slabs))
            ]
            hop = 1
            while hop < len(slabs):
                chosen = (offset & (8 * hop)) != 0
                slabs = [
                    jnp.where(chosen, slabs[number - hop], slabs[number])
                    for number in range(len(slabs))
                ]
                hop *= 2
            count = count[0:8].astype(jnp.int32)
            for number in range(len(slabs)):
                lead = line + 8 * number - offset
                taken_lane = jnp.where((lead & (lanes - 1)) < count, lanes, 0)
                slabs[number] = slabs[number] | taken_lane | jnp.where(lead < 0, 2 * lanes, 0)
            word = jnp.concatenate(slabs, axis=0)
            for half in range(wide // lanes):
                rows = pl.ds(pl.multiple_of(first + half * lanes, lanes), lanes)
                slots_ref[rows, :] = word[:, half * lanes : (half + 1) * lanes].T
            done = done + jnp.sum(count.astype(jnp.float32), axis=1, keepdims=True)
        return done

    lax.fori_loop(0, blocks, place, jnp.zeros((8, 1), jnp.float32))
    return groups


def fill_lists(amount, word_smem, near_table_ref, slots_ref, shift_ref, list_ref):
    lanes = slots_ref.shape[1]
    row = lax.broadcasted_iota(jnp.int32, (8, lanes), 0)
    absent = jnp.where(row == 6, -10.0, 0.0)
    for kind in range(27):
        steps = (kind // 9 - 1.0, kind // 3 % 3 - 1.0, kind % 3 - 1.0)
        shift_ref[kind] = sum(jnp.where(row == axis, steps[axis], 0.0) for axis in range(3))

    def fill(block, carry):
        last_chunk, last_new, last_held = carry
        words = [word_smem[0, block * FILL + unit] for unit in range(FILL)]
        for unit, word in enumerate(words):
            slots = slots_ref[pl.ds(block * FILL + unit, 8, stride=0), :]
            cell = near_table_ref[(word >> 5) & ((1 << (WORD_BITS - 5)) - 1)]
            found = lanes_of(cell, slots & (lanes - 1)) + shift_ref[word & 31]
            chunk = word >> WORD_BITS
            new = jnp.where((slots & lanes) != 0, found, absent)
            later = (slots & (2 * lanes)) != 0
            held_row = jnp.where(chunk != last_chunk, last_new, last_held)
            held_row = jnp.where(later, held_row, new)
            new = jnp.where(later, new, absent)
            list_ref[chunk] = held_row
            list_ref[chunk + 1] = new
            last_chunk, last_new, last_held = chunk, new, held_row
        return last_chunk, last_new, last_held

    blocks = lax.div(amount + (FILL - 1), FILL)
    lax.fori_loop(0, blocks, fill, (jnp.int32(0), absent, absent))


def pair_forces(group, groups, cell_smem, table_ref, list_ref, force_ref, even_ref, odd_ref):
    lanes = table_ref.shape[1]
    cells = table_ref.shape[0] // 8
    rows = even_ref.shape[0]
    chunks = rows // lanes
    units = rows // group
    force_ref[...] = jnp.zeros(force_ref.shape, jnp.float32)
    part = lax.broadcasted_iota(jnp.int32, (32, 8 * lanes), 0)
    comp = lax.broadcasted_iota(jnp.int32, (32, 8 * lanes), 1) // lanes
    weights = jnp.where((part < 24) & (part % 8 == comp), 1.0, 0.0).astype(jnp.bfloat16)

    def turned(step):
        pieces = []
        for piece in range(chunks):
            values = list_ref[step * chunks + piece]
            high = values.astype(jnp.bfloat16).astype(jnp.float32)
            rest = values - high
            middle = rest.astype(jnp.bfloat16).astype(jnp.float32)
            parts = jnp.concatenate([high, middle, rest - middle, jnp.zeros_like(values)], axis=0)
            pieces.append(parts.astype(jnp.bfloat16).T)
        return jnp.concatenate(pieces, axis=0)

    def spread(step, out_ref):
        out_ref[...] = jnp.dot(turned(step), weights, preferred_element_type=jnp.float32)

    def block_force(wide_ref, row, mine):
        other = [wide_ref[pl.ds(row, 8), pl.ds(value * lanes, lanes)] for value in range(8)]
        apart = [other[axis] - mine[axis] for axis in range(3)]
        square = apart[0] * apart[0] + apart[1] * apart[1] + apart[2] * apart[2] + epsilon_sq
        inverse = lax.rsqrt(square)
        reach = other[6] + mine[6]
        overlap = jnp.maximum(reach - square * inverse, 0.0)
        overlap = jnp.where(other[7] != mine[7], overlap, 0.0)
        closing = (
            (other[3] - mine[3]) * apart[0]
            + (other[4] - mine[4]) * apart[1]
            + (other[5] - mine[5]) * apart[2]
        )
        scaled = overlap * (other[6] * mine[6])
        root = scaled * lax.rsqrt(jnp.maximum(scaled * reach, 1e-30))
        factor = root * inverse * (stiffness / damping * overlap - closing * inverse)
        return [factor * apart[axis] for axis in range(3)]

    def pairs(step, wide_ref, next_ref, carry):
        last, running = carry
        spread(step + 1, next_ref)
        for unit in range(units):
            cell = cell_smem[0, step * units + unit]
            own = jnp.minimum(cell, cells - 1) * 8
            mine = [table_ref[pl.ds(own + value, 8, stride=0), :] for value in range(8)]
            running = [jnp.where(cell == last, running[axis], 0.0) for axis in range(3)]
            for block in range(group // 8):
                force = block_force(wide_ref, unit * group + block * 8, mine)
                running = [running[axis] + force[axis] for axis in range(3)]
            last = cell
            for axis in range(3):
                force_ref[cell, axis] = running[axis]
        return last, running

    spread(0, even_ref)

    def both(step, carry):
        carry = pairs(2 * step, even_ref, odd_ref, carry)
        return pairs(2 * step + 1, odd_ref, even_ref, carry)

    zero = jnp.zeros((8, lanes), jnp.float32)
    steps = lax.div(groups + (2 * units - 1), 2 * units)
    lax.fori_loop(0, steps, both, (jnp.int32(-1), [zero] * 3))


def to_scalars(pairs, sems):
    copies = [
        pltpu.make_async_copy(source, target, sems.at[number])
        for number, (source, target) in enumerate(pairs)
    ]
    for copy in copies:
        copy.start()
    for copy in copies:
        copy.wait()


def list_kernel(
    near_of, sizes, amount_smem, code_ref, table_ref, slots_ref, word_ref, cell_ref,
    groups_smem, *scratch,
):
    groups_smem[0] = list_tiles(
        INNER_GROUP, amount_smem[0], near_of, sizes, code_ref, table_ref, slots_ref, word_ref, cell_ref, *scratch,
    )


def inner_kernel(
    amount_smem, word_smem, cell_smem, groups_smem, table_ref, slots_ref, force_ref,
    list_ref, even_ref, odd_ref, shift_ref,
):
    cells, _, lanes = table_ref.shape
    fill_lists(amount_smem[0], word_smem, table_ref, slots_ref, shift_ref, list_ref)
    flat = table_ref.reshape(cells * 8, lanes)
    pair_forces(INNER_GROUP, groups_smem[0], cell_smem, flat, list_ref, force_ref, even_ref, odd_ref)


def outer_kernel(
    near_of, sizes, amount_smem, code_ref, table_ref, halo_ref, inner_ref, arms_ref, frag_ref,
    fixed_ref, out_ref, force_ref, loads_ref, slots_ref, word_ref, cell_ref, word_smem, cell_smem, sems, list_ref, even_ref, odd_ref, shift_ref, *scratch,
):
    cells, _, lanes = table_ref.shape
    held = fixed_ref.shape[1] // 2
    amount = amount_smem[0]
    groups = list_tiles(
        OUTER_GROUP, amount, near_of, sizes, code_ref, halo_ref, slots_ref, word_ref, cell_ref, *scratch,
    )
    to_scalars([(word_ref, word_smem), (cell_ref, cell_smem)], sems)
    fill_lists(amount, word_smem, halo_ref, slots_ref, shift_ref, list_ref)
    flat = table_ref.reshape(cells * 8, lanes)
    pair_forces(OUTER_GROUP, groups, cell_smem, flat, list_ref, force_ref, even_ref, odd_ref)
    sums = fragment_sums(inner_ref, force_ref, arms_ref, frag_ref, loads_ref, held)
    out = fixed_ref[...] + jnp.concatenate([sums, jnp.zeros_like(sums)], axis=1)
    for brick in range(out_ref.shape[0]):
        out_ref[brick] = out


def fragment_sums(inner_ref, outer_ref, arms_ref, frag_ref, loads_ref, held):
    cells, lanes = frag_ref.shape
    tall = loads_ref.shape[0]
    label = lax.broadcasted_iota(jnp.int32, (held, lanes), 0)
    parts = [
        ref.reshape(ref.shape[0] * 24, lanes) for ref in (inner_ref, outer_ref)
    ]

    def total_force(block, axis):
        halves = []
        for half in range(tall // 8):
            first = (block * tall + half * 8) * 24 + axis * 8
            rows = [
                ref[pl.ds(first + part, 8, stride=24), :] for ref in parts for part in range(8)
            ]
            while len(rows) > 1:
                rows = [one + other for one, other in zip(rows[::2], rows[1::2])]
            halves.append(rows[0])
        return -damping * jnp.concatenate(halves, axis=0)

    def gather_sums(block, total):
        rows = pl.ds(pl.multiple_of(block * tall, tall), tall)
        force = [total_force(block, axis) for axis in range(3)]
        lever = [arms_ref[axis, rows, :] for axis in range(3)]
        torque = [
            lever[1] * force[2] - lever[2] * force[1],
            lever[2] * force[0] - lever[0] * force[2],
            lever[0] * force[1] - lever[1] * force[0],
        ]
        loads = force + torque + [jnp.zeros_like(force[0])] * 2
        for comp in range(8):
            loads_ref[:, comp, :] = loads[comp]
        frags = frag_ref[rows, :]
        hits = [
            (frags[unit : unit + 1, :] == label).astype(jnp.float32).astype(jnp.bfloat16)
            for unit in range(tall)
        ]
        values = [split_rows(loads_ref[unit]) for unit in range(tall)]
        return total + dot_lanes(jnp.concatenate(values, axis=1), jnp.concatenate(hits, axis=1))

    total = lax.fori_loop(0, cells // tall, gather_sums, jnp.zeros((24, held), jnp.float32))
    return joined_rows(total)


def move_kernel(
    owned, target_ref, known_ref, state_ref, arms_ref, frag_ref, spheres_ref, clumps_ref
):
    bricks, _, lanes = known_ref.shape
    held = lanes // 2
    cells = frag_ref.shape[0]
    targets = jnp.broadcast_to(target_ref[...], (lanes, lanes))
    lane = lax.broadcasted_iota(jnp.int32, (1, lanes), 1)

    def match(block, carry):
        sums, base = carry
        for unit in range(8):
            brick = block * 8 + unit
            known = known_ref[brick]
            values = split_rows(known)
            key = jnp.where(lane < held, known[6:7], -1.0)
            number = jnp.where(
                (lane >= held) & (lane < held + owned), brick * owned + lane - held, -1
            ).astype(jnp.float32)
            sums = sums + dot_lanes((targets == key).astype(jnp.float32).astype(jnp.bfloat16), values)
            base = base + dot_lanes((targets == number).astype(jnp.float32).astype(jnp.bfloat16), values)
        return sums, base

    zero = jnp.zeros((lanes, 24), jnp.float32)
    sums, base = lax.fori_loop(0, bricks // 8, match, (zero, zero))
    sums = joined_rows(sums.T)
    base = joined_rows(base.T)
    rows = []
    for axis in range(3):
        pull = gravity if axis == 2 else 0.0
        rows.append(
            base[axis : axis + 1]
            + time_step * (sums[axis : axis + 1] * base[6:7] - pull)
        )
    for axis in range(3, 6):
        rows.append(base[axis : axis + 1] + time_step * sums[axis : axis + 1] * base[7:8])
    for comp in range(6):
        clumps_ref[comp : comp + 1, :] = rows[comp]
    tall = 32
    wide = [jnp.broadcast_to(value, (tall, lanes)) for value in rows]

    def cross(first, second):
        return [
            first[1] * second[2] - first[2] * second[1],
            first[2] * second[0] - first[0] * second[2],
            first[0] * second[1] - first[1] * second[0],
        ]

    def move(block, unused):
        at = pl.ds(pl.multiple_of(block * tall, tall), tall)
        index = frag_ref[at, :] + (lanes - held)
        motion = [lanes_of(value, index) for value in wide]
        velocity, spin = motion[0:3], motion[3:6]
        arm = [arms_ref[axis, at, :] for axis in range(3)]
        half = [0.5 * time_step * value for value in spin]
        turned = cross(half, arm)
        twice = cross(half, turned)
        scale = 2.0 / (1.0 + half[0] * half[0] + half[1] * half[1] + half[2] * half[2])
        change = [scale * (turned[axis] + twice[axis]) for axis in range(3)]
        new_arm = [arm[axis] + change[axis] for axis in range(3)]
        swing = cross(spin, new_arm)
        for axis in range(3):
            spheres_ref[axis, at, :] = (
                state_ref[axis, at, :] + time_step * velocity[axis] + (new_arm[axis] - arm[axis])
            )
            spheres_ref[3 + axis, at, :] = velocity[axis] + swing[axis]
        return unused

    lax.fori_loop(0, cells // tall, move, 0)


def local(
    state, arms, sphere_frag, frag_owner, frag_clump, tiles, clump_motion, inv_mass, inv_moment
):
    cells_x, cells_y, cells_z = (state.shape[1], state.shape[2], state.shape[3])
    lanes = state.shape[4]
    cells = cells_x * cells_y * cells_z
    owned = inv_mass.shape[0]
    held = frag_clump.shape[0]
    names = ("gx", "gy", "gz")
    vmem = pl.BlockSpec(memory_space=pltpu.VMEM)
    smem = pl.BlockSpec(memory_space=pltpu.SMEM)
    params = pltpu.CompilerParams(vmem_limit_bytes=VMEM)

    frag_key = (frag_owner[:, 0] * owned + frag_clump).astype(jnp.float32)
    flat_state = state.reshape(7, cells, lanes)
    flat_arms = arms.reshape(3, cells, lanes)
    flat_frag = sphere_frag.reshape(cells, lanes)

    fixed = jnp.concatenate(
        [
            jnp.concatenate([jnp.zeros((6, held)), frag_key[None], jnp.zeros((1, held))], axis=0),
            jnp.concatenate([clump_motion, inv_mass[None], inv_moment[None]], axis=0),
            jnp.zeros((8, lanes - held - owned)),
        ],
        axis=1,
    )

    face_shape = jax.ShapeDtypeStruct((cells_x * cells_y, 8, lanes), jnp.float32)
    table, z_last, z_first = pl.pallas_call(
        functools.partial(pack_kernel, cells_z),
        out_shape=(jax.ShapeDtypeStruct((cells, 8, lanes), jnp.float32), face_shape, face_shape),
        in_specs=[vmem] * 3,
        out_specs=(vmem,) * 3,
        compiler_params=params,
    )(flat_state, flat_frag, frag_key[None])
    grid = table.reshape(cells_x, cells_y, cells_z, 8, lanes)
    z_before, z_after = exchange(
        z_last.reshape(cells_x, cells_y, 1, 8, lanes),
        z_first.reshape(cells_x, cells_y, 1, 8, lanes),
        "gz",
    )

    outside = 1 << 20
    span_z = cells_z + 2
    starts = [0, cells_x * cells_y, 2 * cells_x * cells_y]
    starts += [starts[-1] + cells_y * span_z, starts[-1] + 2 * cells_y * span_z]
    starts += [starts[-1] + (cells_x + 2) * span_z]

    def inside(codes):
        own, kind = (codes // 27, codes % 27)
        x = own // (cells_y * cells_z) + kind // 9 - 1
        y = own // cells_z % cells_y + kind // 3 % 3 - 1
        z = own % cells_z + kind % 3 - 1
        inner = (x >= 0) & (x < cells_x) & (y >= 0) & (y < cells_y)
        return inner & (z >= 0) & (z < cells_z)

    def near_inside(x, y, z):
        return (x * cells_y + y) * cells_z + z

    def near_outside(x, y, z):
        in_y = jnp.where(y < 0, starts[4], starts[5]) + (x + 1) * span_z + z + 1
        in_x = jnp.where(x < 0, starts[2], starts[3]) + y * span_z + z + 1
        in_z = jnp.where(z < 0, starts[0], starts[1]) + x * cells_y + y
        in_x = jnp.where((x < 0) | (x >= cells_x), in_x, in_z)
        return jnp.where((y < 0) | (y >= cells_y), in_y, in_x)

    sizes = (cells_x, cells_y, cells_z)
    codes = tiles[0]
    total = codes.shape[0]
    codes = codes + jnp.where(inside(codes), 0, outside)
    chunks = total + cells * INNER_GROUP // lanes + 3 * SPREAD
    group_top = -(-(chunks * (lanes // OUTER_GROUP) + SLACK) // (8 * lanes)) * 8 * lanes + 8 * lanes
    force_shape = (cells + 8, 3, 8, lanes)

    list_shapes = [(total, lanes), (1, total), (1, group_top)]

    def list_scratch(span):
        return [
            pltpu.VMEM((-(-span // lanes) * lanes, lanes), jnp.float32),
            pltpu.VMEM((lanes, total), jnp.float32),
            pltpu.VMEM((cells, lanes), jnp.float32),
            pltpu.VMEM((1, total), jnp.int32),
            pltpu.VMEM((1, total), jnp.int32),
            pltpu.VMEM((1, total), jnp.int32),
            pltpu.VMEM((1, total), jnp.int32),
        ]

    pair_scratch = [
        pltpu.VMEM((chunks, 8, lanes), jnp.float32),
        pltpu.VMEM((SPREAD * lanes, 8 * lanes), jnp.float32),
        pltpu.VMEM((SPREAD * lanes, 8 * lanes), jnp.float32),
        pltpu.VMEM((27, 8, lanes), jnp.float32),
    ]

    codes = jnp.sort(codes)
    inner_amount = jnp.sum((codes < outside).astype(jnp.int32))
    outer_amount = total - inner_amount
    z_before, z_after, codes, inner_amount = lax.optimization_barrier(
        (z_before, z_after, codes, inner_amount)
    )
    x_before, x_after = exchange(
        jnp.concatenate([z_before[-1:], grid[-1:], z_after[-1:]], axis=2),
        jnp.concatenate([z_before[:1], grid[:1], z_after[:1]], axis=2),
        "gx",
    )
    slots, word, cell_of, groups = pl.pallas_call(
        functools.partial(list_kernel, near_inside, sizes),
        out_shape=tuple(jax.ShapeDtypeStruct(shape, jnp.int32) for shape in list_shapes + [(1,)]),
        in_specs=[smem, vmem, vmem],
        out_specs=(vmem,) * 3 + (smem,),
        scratch_shapes=list_scratch(cells),
        compiler_params=params,
    )(inner_amount[None], (codes & (outside - 1))[None], table)
    x_before, x_after, slots, word, cell_of, groups = lax.optimization_barrier(
        (x_before, x_after, slots, word, cell_of, groups)
    )

    def face(at):
        middle = jnp.concatenate([z_before[:, at], grid[:, at], z_after[:, at]], axis=2)
        return jnp.concatenate([x_before[:, at], middle, x_after[:, at]], axis=0)

    y_before, y_after = exchange(face(slice(-1, None)), face(slice(0, 1)), "gy")
    inner = pl.pallas_call(
        inner_kernel,
        out_shape=jax.ShapeDtypeStruct(force_shape, jnp.float32),
        in_specs=[smem] * 4 + [vmem] * 2,
        out_specs=vmem,
        scratch_shapes=pair_scratch,
        compiler_params=params,
    )(inner_amount[None], word, cell_of, groups, table, slots)

    outer_codes = lax.dynamic_slice(jnp.concatenate([codes, codes]), (inner_amount,), (total,))
    outer_codes = outer_codes & (outside - 1)
    halo = jnp.concatenate(
        [
            part.reshape(-1, 8, lanes)
            for part in (z_before, z_after, x_before, x_after, y_before, y_after)
        ],
        axis=0,
    )
    bricks = lax.axis_size(names)
    known = pl.pallas_call(
        functools.partial(outer_kernel, near_outside, sizes),
        out_shape=jax.ShapeDtypeStruct((bricks, 8, lanes), jnp.float32),
        in_specs=[smem] + [vmem] * 7,
        out_specs=vmem,
        scratch_shapes=[
            pltpu.VMEM(force_shape, jnp.float32),
            pltpu.VMEM((16, 8, lanes), jnp.float32),
        ]
        + [pltpu.VMEM(shape, jnp.int32) for shape in list_shapes]
        + [pltpu.SMEM(shape, jnp.int32) for shape in list_shapes[1:]]
        + [pltpu.SemaphoreType.DMA((2,))]
        + pair_scratch
        + list_scratch(halo.shape[0]),
        compiler_params=params,
    )(outer_amount[None], outer_codes[None], table, halo, inner, flat_arms, flat_frag, fixed)
    known = lax.all_to_all(known, names, split_axis=0, concat_axis=0, tiled=True)

    brick = lax.axis_index(names)
    mine = jnp.where(
        jnp.arange(lanes - held) < owned, brick * owned + jnp.arange(lanes - held), -2
    ).astype(jnp.float32)
    target = jnp.concatenate([mine, frag_key])[:, None]
    spheres, clumps = pl.pallas_call(
        functools.partial(move_kernel, owned),
        out_shape=(
            jax.ShapeDtypeStruct((6, cells, lanes), jnp.float32),
            jax.ShapeDtypeStruct((6, lanes), jnp.float32),
        ),
        in_specs=[vmem] * 5,
        out_specs=(vmem, vmem),
        compiler_params=params,
    )(target, known, flat_state, flat_arms, flat_frag)
    return (spheres.reshape((6,) + state.shape[1:]), clumps[:, :owned])


def solution(mesh):
    return jax.shard_map(
        local,
        mesh=mesh,
        in_specs=(
            P(None, "gx", "gy", "gz", None),
            P(None, "gx", "gy", "gz", None),
            P("gx", "gy", "gz", None),
            P(("gx", "gy", "gz"), None),
            P(("gx", "gy", "gz")),
            P(("gx", "gy", "gz"), None),
            P(None, ("gx", "gy", "gz")),
            P(("gx", "gy", "gz")),
            P(("gx", "gy", "gz")),
        ),
        out_specs=(P(None, "gx", "gy", "gz", None), P(None, ("gx", "gy", "gz"))),
        check_vma=False,
    )
```

```python
import functools

import jax
import jax.numpy as jnp
from jax import lax
from jax.experimental import pallas as pl
from jax.experimental.pallas import tpu as pltpu
from jax.sharding import PartitionSpec as P

stiffness = 100.0
damping = 2.0
time_step = 0.01
gravity = 9.81
epsilon_sq = 1e-08
radius_top = 0.14

INNER_GROUP = 32
OUTER_GROUP = 16
FILL = 64
OUTSIDE = 1 << 20
WORD_BITS = 16
SLACK = 256
SPREAD = 4
VMEM = 56 * 1024 * 1024


def lanes_of(values, index):
    return jnp.take_along_axis(values, index, axis=1, mode="promise_in_bounds")


def split_rows(values):
    high = values.astype(jnp.bfloat16).astype(jnp.float32)
    rest = values - high
    middle = rest.astype(jnp.bfloat16).astype(jnp.float32)
    low = rest - middle
    return jnp.concatenate([high, middle, low], axis=0).astype(jnp.bfloat16)


def joined_rows(stacked):
    rows = stacked.shape[0] // 3
    return stacked[0:rows] + stacked[rows : 2 * rows] + stacked[2 * rows :]


def dot_lanes(first, second):
    return lax.dot_general(
        first, second, (((1,), (1,)), ((), ())), preferred_element_type=jnp.float32
    )


def exchange(last, initial, axis):
    devices = lax.axis_size(axis)
    up = [(i, (i + 1) % devices) for i in range(devices)]
    down = [(j, i) for i, j in up]
    return lax.ppermute(last, axis, up), lax.ppermute(initial, axis, down)


def pack_kernel(deep, state_ref, frag_ref, key_ref, out_ref, last_ref, first_ref):
    cells, lanes = frag_ref.shape
    held = key_ref.shape[1]
    for comp in range(7):
        out_ref[:, comp, :] = state_ref[comp] * (damping / stiffness if 3 <= comp < 6 else 1.0)
    keys = jnp.concatenate([key_ref[0:1, :], jnp.zeros((1, lanes - held), jnp.float32)], axis=1)
    keys = jnp.broadcast_to(keys, (8, lanes))
    for block in range(cells // 8):
        rows = pl.ds(block * 8, 8)
        out_ref[rows, 7, :] = lanes_of(keys, frag_ref[rows, :])
    for column in range(cells // deep):
        first_ref[column] = out_ref[column * deep]
        last_ref[column] = out_ref[column * deep + deep - 1]


def list_tiles(
    group, amount, near_of, sizes, code_ref, table_ref, slots_ref, word_ref, cell_ref,
    class_ref, member_ref, count_ref, near_ref, need_ref, own_ref, kind_ref,
):
    tiles, lanes = slots_ref.shape
    span = table_ref.shape[0]
    padded = class_ref.shape[0]
    cells = count_ref.shape[0]
    lane_bits = lanes.bit_length() - 1
    wide = 256
    parts = 2
    flat = table_ref.reshape(span * 8, lanes)

    def plane(comp):
        return flat[pl.ds(comp, span, stride=8), :]

    def flag(value):
        return value.astype(jnp.float32).astype(jnp.bfloat16)

    def dot(first, second):
        return jnp.dot(first, second, preferred_element_type=jnp.float32)

    def ramp(shape, axis):
        return lax.broadcasted_iota(jnp.int32, shape, axis)

    def over(value, by):
        return jnp.floor((value.astype(jnp.float32) + 0.5) * (1.0 / by)).astype(jnp.int32)

    code = code_ref[...] & (OUTSIDE - 1)
    own = over(code, 27)
    kind = code - 27 * own
    step_x = over(kind, 9)
    step_y = over(kind, 3) - 3 * step_x
    steps = (step_x - 1, step_y - 1, kind - 9 * step_x - 3 * step_y - 1)
    own_x = over(own, sizes[1] * sizes[2])
    row = over(own, sizes[2])
    near = near_of(
        own_x + steps[0], row - own_x * sizes[1] + steps[1], own - row * sizes[2] + steps[2]
    )
    need = sum(
        jnp.where(steps[axis] == 1, 1, jnp.where(steps[axis] == -1, 2, 0)) * (1 << (2 * axis))
        for axis in range(3)
    )
    live = ramp((1, tiles), 1) < amount
    near = jnp.where(live, near, 0)
    near_ref[...] = near
    kind_ref[...] = near * 32 + jnp.where(live, kind, 0)
    need_ref[...] = jnp.where(live, need, 64)
    own_ref[...] = jnp.where(live, own, cells)

    radius = plane(6) + (radius_top + 1e-5)
    classes = jnp.zeros((span, lanes), jnp.float32)
    for axis in range(3):
        place = plane(axis)
        classes = classes + jnp.where(place < radius, 1.0 * (1 << (2 * axis)), 0.0)
        classes = classes + jnp.where(place > 1.0 - radius, 1.0 * (2 << (2 * axis)), 0.0)
    if padded > span:
        class_ref[...] = jnp.zeros(class_ref.shape, jnp.float32)
    class_ref[pl.ds(0, span), :] = classes
    codes = jnp.concatenate(
        [class_ref[pl.ds(at, lanes), :].T for at in range(0, padded, lanes)], axis=1
    ).astype(jnp.bfloat16)
    ones = jnp.ones((lanes, lanes), jnp.bfloat16)
    count_ref[...] = jnp.zeros(count_ref.shape, jnp.float32)
    blocks = lax.div(amount + (parts * wide - 1), parts * wide)

    def choose(block, unused):
        held = []
        for part in range(parts):
            at = pl.ds(pl.multiple_of((block * parts + part) * wide, wide), wide)
            hits = flag(ramp((padded, wide), 0) == near_ref[:, at])
            found = dot(codes, hits).astype(jnp.int32)
            need = need_ref[:, at]
            member = ((found & need) == need).astype(jnp.float32)
            member_ref[:, at] = member
            count = dot(ones, member.astype(jnp.bfloat16))
            mine = flag(ramp((cells, wide), 0) == own_ref[:, at])
            held.append(dot_lanes(mine, count[0:16].astype(jnp.bfloat16)))
        count_ref[:, 0:16] += held[0] + held[1]
        return unused

    lax.fori_loop(0, blocks, choose, 0)

    held = jnp.broadcast_to(count_ref[:, 0:1], count_ref.shape)
    high = jnp.floor(held * (1.0 / lanes))
    low = held - lanes * high
    taken = jnp.floor((held + (group - 1)) * (1.0 / group))
    upto = flag(ramp((cells, cells), 1) <= ramp((cells, cells), 0))
    ends = dot(upto, taken.astype(jnp.bfloat16))
    cell_ones = jnp.ones((8, cells), jnp.bfloat16)
    many = 8 * lanes
    wide_ends = jnp.concatenate([ends] * 8, axis=1)

    def name_groups(block, unused):
        number = (ramp((cells, many), 1) + block * many).astype(jnp.float32)
        at = pl.ds(pl.multiple_of(block * many, many), many)
        cell_ref[:, at] = dot(cell_ones, flag(wide_ends <= number))[0:1].astype(jnp.int32)
        return unused

    groups = jnp.max(ends).astype(jnp.int32)
    lax.fori_loop(0, lax.div(groups + SLACK, many) + 1, name_groups, 0)
    before_cell = jnp.concatenate(
        [value.T[0:8] for value in (taken, high, low)], axis=0
    ).astype(jnp.bfloat16)

    earlier = flag(ramp((lanes, lanes), 1) < ramp((lanes, lanes), 0))
    earlier_tile = flag(ramp((wide, wide), 0) < ramp((wide, wide), 1))

    def place(block, done):
        for part in range(parts):
            first = pl.multiple_of((block * parts + part) * wide, wide)
            at = pl.ds(first, wide)
            flags = member_ref[:, at].astype(jnp.bfloat16)
            count = dot(ones, flags)
            lower = flag(ramp((cells, wide), 0) < own_ref[:, at])
            before = dot(before_cell, lower)
            so_far = dot(count[0:8].astype(jnp.bfloat16), earlier_tile) + done
            start = group * before[0:8] + so_far - (lanes * before[8:16] + before[16:24])
            start = start.astype(jnp.int32)[0:1]
            offset = jnp.broadcast_to(start & (lanes - 1), (8, wide))
            word_ref[:, at] = (start >> lane_bits) * (1 << WORD_BITS) + kind_ref[:, at]
            rank = dot(earlier, flags)
            slot = ramp((lanes, wide), 0)
            moves = slot - rank.astype(jnp.int32)
            word = jnp.where(member_ref[:, at] > 0.0, slot + lanes * moves, 0)
            bit = 1
            while bit < lanes:
                keep = jnp.where((word & (bit * lanes)) != 0, 0, word)
                gone = word ^ keep
                word = keep | jnp.concatenate([gone[bit:], gone[:bit]], axis=0)
                bit *= 2
            word = word & (lanes - 1)
            line = ramp((8, wide), 0)
            within = offset & 7
            pick = (line - within) & 7
            slabs = [
                jnp.take_along_axis(
                    word[at_row : at_row + 8], pick, axis=0, mode="promise_in_bounds"
                )
                for at_row in range(0, lanes, 8)
            ]
            slabs = [
                jnp.where(line >= within, slabs[number], slabs[number - 1])
                for number in range(len(slabs))
            ]
            hop = 1
            while hop < len(slabs):
                chosen = (offset & (8 * hop)) != 0
                slabs = [
                    jnp.where(chosen, slabs[number - hop], slabs[number])
                    for number in range(len(slabs))
                ]
                hop *= 2
            count = count[0:8].astype(jnp.int32)
            for number in range(len(slabs)):
                lead = line + 8 * number - offset
                taken_lane = jnp.where((lead & (lanes - 1)) < count, lanes, 0)
                slabs[number] = slabs[number] | taken_lane | jnp.where(lead < 0, 2 * lanes, 0)
            word = jnp.concatenate(slabs, axis=0)
            for half in range(wide // lanes):
                rows = pl.ds(pl.multiple_of(first + half * lanes, lanes), lanes)
                slots_ref[rows, :] = word[:, half * lanes : (half + 1) * lanes].T
            done = done + jnp.sum(count.astype(jnp.float32), axis=1, keepdims=True)
        return done

    lax.fori_loop(0, blocks, place, jnp.zeros((8, 1), jnp.float32))
    return groups


def fill_lists(amount, word_smem, near_table_ref, slots_ref, shift_ref, list_ref):
    lanes = slots_ref.shape[1]
    row = lax.broadcasted_iota(jnp.int32, (8, lanes), 0)
    absent = jnp.where(row == 6, -10.0, 0.0)
    for kind in range(27):
        steps = (kind // 9 - 1.0, kind // 3 % 3 - 1.0, kind % 3 - 1.0)
        shift_ref[kind] = sum(jnp.where(row == axis, steps[axis], 0.0) for axis in range(3))

    def fill(block, carry):
        last_chunk, last_new, last_held = carry
        words = [word_smem[0, block * FILL + unit] for unit in range(FILL)]
        for unit, word in enumerate(words):
            slots = slots_ref[pl.ds(block * FILL + unit, 8, stride=0), :]
            cell = near_table_ref[(word >> 5) & ((1 << (WORD_BITS - 5)) - 1)]
            found = lanes_of(cell, slots & (lanes - 1)) + shift_ref[word & 31]
            chunk = word >> WORD_BITS
            new = jnp.where((slots & lanes) != 0, found, absent)
            later = (slots & (2 * lanes)) != 0
            held_row = jnp.where(chunk != last_chunk, last_new, last_held)
            held_row = jnp.where(later, held_row, new)
            new = jnp.where(later, new, absent)
            list_ref[chunk] = held_row
            list_ref[chunk + 1] = new
            last_chunk, last_new, last_held = chunk, new, held_row
        return last_chunk, last_new, last_held

    blocks = lax.div(amount + (FILL - 1), FILL)
    lax.fori_loop(0, blocks, fill, (jnp.int32(0), absent, absent))


def pair_forces(group, groups, cell_smem, table_ref, list_ref, force_ref, even_ref, odd_ref):
    lanes = table_ref.shape[1]
    cells = table_ref.shape[0] // 8
    rows = even_ref.shape[0]
    chunks = rows // lanes
    units = rows // group
    force_ref[...] = jnp.zeros(force_ref.shape, jnp.float32)
    part = lax.broadcasted_iota(jnp.int32, (32, 8 * lanes), 0)
    comp = lax.broadcasted_iota(jnp.int32, (32, 8 * lanes), 1) // lanes
    weights = jnp.where((part < 24) & (part % 8 == comp), 1.0, 0.0).astype(jnp.bfloat16)

    def turned(step):
        pieces = []
        for piece in range(chunks):
            values = list_ref[step * chunks + piece]
            high = values.astype(jnp.bfloat16).astype(jnp.float32)
            rest = values - high
            middle = rest.astype(jnp.bfloat16).astype(jnp.float32)
            parts = jnp.concatenate([high, middle, rest - middle, jnp.zeros_like(values)], axis=0)
            pieces.append(parts.astype(jnp.bfloat16).T)
        return jnp.concatenate(pieces, axis=0)

    def spread(step, out_ref):
        out_ref[...] = jnp.dot(turned(step), weights, preferred_element_type=jnp.float32)

    def block_force(wide_ref, row, mine):
        other = [wide_ref[pl.ds(row, 8), pl.ds(value * lanes, lanes)] for value in range(8)]
        apart = [other[axis] - mine[axis] for axis in range(3)]
        square = apart[0] * apart[0] + apart[1] * apart[1] + apart[2] * apart[2] + epsilon_sq
        inverse = lax.rsqrt(square)
        reach = other[6] + mine[6]
        overlap = jnp.maximum(reach - square * inverse, 0.0)
        overlap = jnp.where(other[7] != mine[7], overlap, 0.0)
        closing = (
            (other[3] - mine[3]) * apart[0]
            + (other[4] - mine[4]) * apart[1]
            + (other[5] - mine[5]) * apart[2]
        )
        scaled = overlap * (other[6] * mine[6])
        root = scaled * lax.rsqrt(jnp.maximum(scaled * reach, 1e-30))
        factor = root * inverse * (overlap - closing * inverse)
        return [factor * apart[axis] for axis in range(3)]

    def pairs(step, wide_ref, next_ref, carry):
        last, running = carry
        spread(step + 1, next_ref)
        for unit in range(units):
            cell = cell_smem[0, step * units + unit]
            own = jnp.minimum(cell, cells - 1) * 8
            mine = [table_ref[pl.ds(own + value, 8, stride=0), :] for value in range(8)]
            running = [jnp.where(cell == last, running[axis], 0.0) for axis in range(3)]
            for block in range(group // 8):
                force = block_force(wide_ref, unit * group + block * 8, mine)
                running = [running[axis] + force[axis] for axis in range(3)]
            last = cell
            for axis in range(3):
                force_ref[cell, axis] = running[axis]
        return last, running

    spread(0, even_ref)

    def both(step, carry):
        carry = pairs(2 * step, even_ref, odd_ref, carry)
        return pairs(2 * step + 1, odd_ref, even_ref, carry)

    zero = jnp.zeros((8, lanes), jnp.float32)
    steps = lax.div(groups + (2 * units - 1), 2 * units)
    lax.fori_loop(0, steps, both, (jnp.int32(-1), [zero] * 3))


def to_scalars(pairs, sems):
    copies = [
        pltpu.make_async_copy(source, target, sems.at[number])
        for number, (source, target) in enumerate(pairs)
    ]
    for copy in copies:
        copy.start()
    for copy in copies:
        copy.wait()


def list_kernel(
    near_of, sizes, amount_smem, code_ref, table_ref, slots_ref, word_ref, cell_ref,
    groups_smem, *scratch,
):
    groups_smem[0] = list_tiles(
        INNER_GROUP, amount_smem[0], near_of, sizes, code_ref, table_ref, slots_ref, word_ref, cell_ref, *scratch,
    )


def inner_kernel(
    amount_smem, word_smem, cell_smem, groups_smem, table_ref, slots_ref, sums_ref, force_ref,
    list_ref, even_ref, odd_ref, shift_ref,
):
    cells, _, lanes = table_ref.shape
    fill_lists(amount_smem[0], word_smem, table_ref, slots_ref, shift_ref, list_ref)
    flat = table_ref.reshape(cells * 8, lanes)
    pair_forces(INNER_GROUP, groups_smem[0], cell_smem, flat, list_ref, force_ref, even_ref, odd_ref)
    parts = force_ref.reshape(force_ref.shape[0] * 24, lanes)

    def store_sums(block, unused):
        for half in range(4):
            at = pl.multiple_of(block * 32 + half * 8, 8)
            for axis in range(3):
                sums_ref[axis, pl.ds(at, 8), :] = sublane_sums(parts, at, axis)
        return unused

    lax.fori_loop(0, cells // 32, store_sums, 0)


def outer_kernel(
    near_of, sizes, amount_smem, code_ref, table_ref, halo_ref, inner_ref, arms_ref, frag_ref,
    key_ref, motion_ref, mass_ref, moment_ref, out_ref, fixed_ref, force_ref, loads_ref, slots_ref, word_ref, cell_ref, word_smem, cell_smem, sems, list_ref, even_ref, odd_ref, shift_ref, *scratch,
):
    cells, _, lanes = table_ref.shape
    held = key_ref.shape[1]
    owned = mass_ref.shape[1]
    fixed_ref[...] = jnp.zeros(fixed_ref.shape, jnp.float32)
    fixed_ref[6:7, 0:held] = key_ref[...]
    fixed_ref[0:6, held : held + owned] = motion_ref[...]
    fixed_ref[6:7, held : held + owned] = mass_ref[...]
    fixed_ref[7:8, held : held + owned] = moment_ref[...]
    amount = amount_smem[0]
    groups = list_tiles(
        OUTER_GROUP, amount, near_of, sizes, code_ref, halo_ref, slots_ref, word_ref, cell_ref, *scratch,
    )
    to_scalars([(word_ref, word_smem), (cell_ref, cell_smem)], sems)
    fill_lists(amount, word_smem, halo_ref, slots_ref, shift_ref, list_ref)
    flat = table_ref.reshape(cells * 8, lanes)
    pair_forces(OUTER_GROUP, groups, cell_smem, flat, list_ref, force_ref, even_ref, odd_ref)
    sums = fragment_sums(inner_ref, force_ref, arms_ref, frag_ref, loads_ref, held)
    out = fixed_ref[...] + jnp.concatenate([sums, jnp.zeros_like(sums)], axis=1)
    for brick in range(out_ref.shape[0]):
        out_ref[brick] = out


def sublane_sums(parts_ref, first, axis):
    rows = [parts_ref[pl.ds(first * 24 + axis * 8 + part, 8, stride=24), :] for part in range(8)]
    while len(rows) > 1:
        rows = [one + other for one, other in zip(rows[::2], rows[1::2])]
    return rows[0]


def fragment_sums(inner_ref, outer_ref, arms_ref, frag_ref, loads_ref, held):
    cells, lanes = frag_ref.shape
    tall = loads_ref.shape[0]
    label = lax.broadcasted_iota(jnp.int32, (held, lanes), 0)
    parts = outer_ref.reshape(outer_ref.shape[0] * 24, lanes)

    def total_force(block, axis):
        halves = []
        for half in range(tall // 8):
            at = pl.multiple_of(block * tall + half * 8, 8)
            halves.append(sublane_sums(parts, at, axis) + inner_ref[axis, pl.ds(at, 8), :])
        return -stiffness * jnp.concatenate(halves, axis=0)

    def gather_sums(block, total):
        rows = pl.ds(pl.multiple_of(block * tall, tall), tall)
        force = [total_force(block, axis) for axis in range(3)]
        lever = [arms_ref[axis, rows, :] for axis in range(3)]
        torque = [
            lever[1] * force[2] - lever[2] * force[1],
            lever[2] * force[0] - lever[0] * force[2],
            lever[0] * force[1] - lever[1] * force[0],
        ]
        loads = force + torque + [jnp.zeros_like(force[0])] * 2
        for comp in range(8):
            loads_ref[:, comp, :] = loads[comp]
        frags = frag_ref[rows, :]
        hits = [
            (frags[unit : unit + 1, :] == label).astype(jnp.float32).astype(jnp.bfloat16)
            for unit in range(tall)
        ]
        values = [split_rows(loads_ref[unit]) for unit in range(tall)]
        return total + dot_lanes(jnp.concatenate(values, axis=1), jnp.concatenate(hits, axis=1))

    total = lax.fori_loop(0, cells // tall, gather_sums, jnp.zeros((24, held), jnp.float32))
    return joined_rows(total)


def move_kernel(
    owned, target_ref, known_ref, state_ref, arms_ref, frag_ref, spheres_ref, clumps_ref
):
    bricks, _, lanes = known_ref.shape
    held = lanes // 2
    cells = frag_ref.shape[0]
    targets = jnp.broadcast_to(target_ref[...], (lanes, lanes))
    lane = lax.broadcasted_iota(jnp.int32, (1, lanes), 1)

    def match(block, carry):
        sums, base = carry
        for unit in range(8):
            brick = block * 8 + unit
            known = known_ref[brick]
            values = split_rows(known)
            key = jnp.where(lane < held, known[6:7], -1.0)
            number = jnp.where(
                (lane >= held) & (lane < held + owned), brick * owned + lane - held, -1
            ).astype(jnp.float32)
            sums = sums + dot_lanes((targets == key).astype(jnp.float32).astype(jnp.bfloat16), values)
            base = base + dot_lanes((targets == number).astype(jnp.float32).astype(jnp.bfloat16), values)
        return sums, base

    zero = jnp.zeros((lanes, 24), jnp.float32)
    sums, base = lax.fori_loop(0, bricks // 8, match, (zero, zero))
    sums = joined_rows(sums.T)
    base = joined_rows(base.T)
    rows = []
    for axis in range(3):
        pull = gravity if axis == 2 else 0.0
        rows.append(
            base[axis : axis + 1]
            + time_step * (sums[axis : axis + 1] * base[6:7] - pull)
        )
    for axis in range(3, 6):
        rows.append(base[axis : axis + 1] + time_step * sums[axis : axis + 1] * base[7:8])
    for comp in range(6):
        clumps_ref[comp : comp + 1, :] = rows[comp]
    tall = 32
    wide = [jnp.broadcast_to(value, (tall, lanes)) for value in rows]

    def cross(first, second):
        return [
            first[1] * second[2] - first[2] * second[1],
            first[2] * second[0] - first[0] * second[2],
            first[0] * second[1] - first[1] * second[0],
        ]

    def move(block, unused):
        at = pl.ds(pl.multiple_of(block * tall, tall), tall)
        index = frag_ref[at, :] + (lanes - held)
        motion = [lanes_of(value, index) for value in wide]
        velocity, spin = motion[0:3], motion[3:6]
        arm = [arms_ref[axis, at, :] for axis in range(3)]
        half = [0.5 * time_step * value for value in spin]
        turned = cross(half, arm)
        twice = cross(half, turned)
        scale = 2.0 / (1.0 + half[0] * half[0] + half[1] * half[1] + half[2] * half[2])
        change = [scale * (turned[axis] + twice[axis]) for axis in range(3)]
        new_arm = [arm[axis] + change[axis] for axis in range(3)]
        swing = cross(spin, new_arm)
        for axis in range(3):
            spheres_ref[axis, at, :] = (
                state_ref[axis, at, :] + time_step * velocity[axis] + (new_arm[axis] - arm[axis])
            )
            spheres_ref[3 + axis, at, :] = velocity[axis] + swing[axis]
        return unused

    lax.fori_loop(0, cells // tall, move, 0)


def local(
    state, arms, sphere_frag, frag_owner, frag_clump, tiles, clump_motion, inv_mass, inv_moment
):
    cells_x, cells_y, cells_z = (state.shape[1], state.shape[2], state.shape[3])
    lanes = state.shape[4]
    cells = cells_x * cells_y * cells_z
    owned = inv_mass.shape[0]
    held = frag_clump.shape[0]
    names = ("gx", "gy", "gz")
    vmem = pl.BlockSpec(memory_space=pltpu.VMEM)
    smem = pl.BlockSpec(memory_space=pltpu.SMEM)
    params = pltpu.CompilerParams(vmem_limit_bytes=VMEM)

    frag_key = (frag_owner[:, 0] * owned + frag_clump).astype(jnp.float32)
    flat_state = state.reshape(7, cells, lanes)
    flat_arms = arms.reshape(3, cells, lanes)
    flat_frag = sphere_frag.reshape(cells, lanes)

    face_shape = jax.ShapeDtypeStruct((cells_x * cells_y, 8, lanes), jnp.float32)
    table, z_last, z_first = pl.pallas_call(
        functools.partial(pack_kernel, cells_z),
        out_shape=(jax.ShapeDtypeStruct((cells, 8, lanes), jnp.float32), face_shape, face_shape),
        in_specs=[vmem] * 3,
        out_specs=(vmem,) * 3,
        compiler_params=params,
    )(flat_state, flat_frag, frag_key[None])
    grid = table.reshape(cells_x, cells_y, cells_z, 8, lanes)
    z_before, z_after = exchange(z_last, z_first, "gz")

    span_z = cells_z + 2
    starts = [0, cells_x * cells_y, 2 * cells_x * cells_y]
    starts += [starts[-1] + cells_y * span_z, starts[-1] + 2 * cells_y * span_z]
    starts += [starts[-1] + (cells_x + 2) * span_z]

    def inside(codes):
        own, kind = (codes // 27, codes % 27)
        x = own // (cells_y * cells_z) + kind // 9 - 1
        y = own // cells_z % cells_y + kind // 3 % 3 - 1
        z = own % cells_z + kind % 3 - 1
        inner = (x >= 0) & (x < cells_x) & (y >= 0) & (y < cells_y)
        return inner & (z >= 0) & (z < cells_z)

    def near_inside(x, y, z):
        return (x * cells_y + y) * cells_z + z

    def near_outside(x, y, z):
        in_y = jnp.where(y < 0, starts[4], starts[5]) + (x + 1) * span_z + z + 1
        in_x = jnp.where(x < 0, starts[2], starts[3]) + y * span_z + z + 1
        in_z = jnp.where(z < 0, starts[0], starts[1]) + x * cells_y + y
        in_x = jnp.where((x < 0) | (x >= cells_x), in_x, in_z)
        return jnp.where((y < 0) | (y >= cells_y), in_y, in_x)

    sizes = (cells_x, cells_y, cells_z)
    codes = tiles[0]
    total = codes.shape[0]
    codes = codes + jnp.where(inside(codes), 0, OUTSIDE)
    chunks = total + cells * INNER_GROUP // lanes + 3 * SPREAD
    group_top = -(-(chunks * (lanes // OUTER_GROUP) + SLACK) // (8 * lanes)) * 8 * lanes + 8 * lanes
    force_shape = (cells + 8, 3, 8, lanes)

    list_shapes = [(total, lanes), (1, total), (1, group_top)]

    def list_scratch(span):
        return [
            pltpu.VMEM((-(-span // lanes) * lanes, lanes), jnp.float32),
            pltpu.VMEM((lanes, total), jnp.float32),
            pltpu.VMEM((cells, lanes), jnp.float32),
            pltpu.VMEM((1, total), jnp.int32),
            pltpu.VMEM((1, total), jnp.int32),
            pltpu.VMEM((1, total), jnp.int32),
            pltpu.VMEM((1, total), jnp.int32),
        ]

    pair_scratch = [
        pltpu.VMEM((chunks, 8, lanes), jnp.float32),
        pltpu.VMEM((SPREAD * lanes, 8 * lanes), jnp.float32),
        pltpu.VMEM((SPREAD * lanes, 8 * lanes), jnp.float32),
        pltpu.VMEM((27, 8, lanes), jnp.float32),
    ]

    codes = jnp.sort(codes)
    inner_amount = jnp.sum((codes < OUTSIDE).astype(jnp.int32))
    outer_amount = total - inner_amount
    z_before, z_after, codes, inner_amount = lax.optimization_barrier(
        (z_before, z_after, codes, inner_amount)
    )
    z_before, z_after = (
        part.reshape(cells_x, cells_y, 1, 8, lanes) for part in (z_before, z_after)
    )
    x_before, x_after = exchange(
        jnp.concatenate([z_before[-1:], grid[-1:], z_after[-1:]], axis=2),
        jnp.concatenate([z_before[:1], grid[:1], z_after[:1]], axis=2),
        "gx",
    )
    slots, word, cell_of, groups = pl.pallas_call(
        functools.partial(list_kernel, near_inside, sizes),
        out_shape=tuple(jax.ShapeDtypeStruct(shape, jnp.int32) for shape in list_shapes + [(1,)]),
        in_specs=[smem, vmem, vmem],
        out_specs=(vmem,) * 3 + (smem,),
        scratch_shapes=list_scratch(cells),
        compiler_params=params,
    )(inner_amount[None], codes[None], table)
    x_before, x_after, slots, word, cell_of, groups = lax.optimization_barrier(
        (x_before, x_after, slots, word, cell_of, groups)
    )

    def face(at):
        middle = jnp.concatenate([z_before[:, at], grid[:, at], z_after[:, at]], axis=2)
        return jnp.concatenate([x_before[:, at], middle, x_after[:, at]], axis=0)

    y_before, y_after = exchange(face(slice(-1, None)), face(slice(0, 1)), "gy")
    inner = pl.pallas_call(
        inner_kernel,
        out_shape=jax.ShapeDtypeStruct((3, cells, lanes), jnp.float32),
        in_specs=[smem] * 4 + [vmem] * 2,
        out_specs=vmem,
        scratch_shapes=[pltpu.VMEM(force_shape, jnp.float32)] + pair_scratch,
        compiler_params=params,
    )(inner_amount[None], word, cell_of, groups, table, slots)

    outer_codes = lax.dynamic_slice(jnp.concatenate([codes, codes]), (inner_amount,), (total,))
    halo = jnp.concatenate(
        [
            part.reshape(-1, 8, lanes)
            for part in (z_before, z_after, x_before, x_after, y_before, y_after)
        ],
        axis=0,
    )
    bricks = lax.axis_size(names)
    known = pl.pallas_call(
        functools.partial(outer_kernel, near_outside, sizes),
        out_shape=jax.ShapeDtypeStruct((bricks, 8, lanes), jnp.float32),
        in_specs=[smem] + [vmem] * 10,
        out_specs=vmem,
        scratch_shapes=[
            pltpu.VMEM((8, lanes), jnp.float32),
            pltpu.VMEM(force_shape, jnp.float32),
            pltpu.VMEM((16, 8, lanes), jnp.float32),
        ]
        + [pltpu.VMEM(shape, jnp.int32) for shape in list_shapes]
        + [pltpu.SMEM(shape, jnp.int32) for shape in list_shapes[1:]]
        + [pltpu.SemaphoreType.DMA((2,))]
        + pair_scratch
        + list_scratch(halo.shape[0]),
        compiler_params=params,
    )(outer_amount[None], outer_codes[None], table, halo, inner, flat_arms, flat_frag,
        frag_key[None], clump_motion, inv_mass[None], inv_moment[None])
    known = lax.all_to_all(known, names, split_axis=0, concat_axis=0, tiled=True)

    brick = lax.axis_index(names)
    mine = jnp.where(
        jnp.arange(lanes - held) < owned, brick * owned + jnp.arange(lanes - held), -2
    ).astype(jnp.float32)
    target = jnp.concatenate([mine, frag_key])[:, None]
    spheres, clumps = pl.pallas_call(
        functools.partial(move_kernel, owned),
        out_shape=(
            jax.ShapeDtypeStruct((6, cells, lanes), jnp.float32),
            jax.ShapeDtypeStruct((6, lanes), jnp.float32),
        ),
        in_specs=[vmem] * 5,
        out_specs=(vmem, vmem),
        compiler_params=params,
    )(target, known, flat_state, flat_arms, flat_frag)
    return (spheres.reshape((6,) + state.shape[1:]), clumps[:, :owned])


def solution(mesh):
    return jax.shard_map(
        local,
        mesh=mesh,
        in_specs=(
            P(None, "gx", "gy", "gz", None),
            P(None, "gx", "gy", "gz", None),
            P("gx", "gy", "gz", None),
            P(("gx", "gy", "gz"), None),
            P(("gx", "gy", "gz")),
            P(("gx", "gy", "gz"), None),
            P(None, ("gx", "gy", "gz")),
            P(("gx", "gy", "gz")),
            P(("gx", "gy", "gz")),
        ),
        out_specs=(P(None, "gx", "gy", "gz", None), P(None, ("gx", "gy", "gz"))),
        check_vma=False,
    )
```

```python
import functools

import jax
import jax.numpy as jnp
from jax import lax
from jax.experimental import pallas as pl
from jax.experimental.pallas import tpu as pltpu
from jax.sharding import PartitionSpec as P

stiffness = 100.0
damping = 2.0
time_step = 0.01
gravity = 9.81
epsilon_sq = 1e-08
radius_top = 0.14

INNER_GROUP = 32
OUTER_GROUP = 16
FILL = 16
INNER_FILL = 48
OUTER_FILL = 88
OUTSIDE = 1 << 20
WORD_BITS = 16
SLACK = 256
SPREAD = 4
VMEM = 56 * 1024 * 1024


def lanes_of(values, index):
    return jnp.take_along_axis(values, index, axis=1, mode="promise_in_bounds")


def split_rows(values):
    high = values.astype(jnp.bfloat16).astype(jnp.float32)
    rest = values - high
    middle = rest.astype(jnp.bfloat16).astype(jnp.float32)
    low = rest - middle
    return jnp.concatenate([high, middle, low], axis=0).astype(jnp.bfloat16)


def joined_rows(stacked):
    rows = stacked.shape[0] // 3
    return stacked[0:rows] + stacked[rows : 2 * rows] + stacked[2 * rows :]


def dot_lanes(first, second):
    return lax.dot_general(
        first, second, (((1,), (1,)), ((), ())), preferred_element_type=jnp.float32
    )


def exchange(last, initial, axis):
    devices = lax.axis_size(axis)
    up = [(i, (i + 1) % devices) for i in range(devices)]
    down = [(j, i) for i, j in up]
    return lax.ppermute(last, axis, up), lax.ppermute(initial, axis, down)


def pack_kernel(deep, state_ref, frag_ref, key_ref, out_ref, last_ref, first_ref):
    cells, lanes = frag_ref.shape
    held = key_ref.shape[1]
    for comp in range(7):
        out_ref[:, comp, :] = state_ref[comp] * (damping / stiffness if 3 <= comp < 6 else 1.0)
    keys = jnp.concatenate([key_ref[0:1, :], jnp.zeros((1, lanes - held), jnp.float32)], axis=1)
    keys = jnp.broadcast_to(keys, (8, lanes))
    for block in range(cells // 8):
        rows = pl.ds(block * 8, 8)
        out_ref[rows, 7, :] = lanes_of(keys, frag_ref[rows, :])
    for column in range(cells // deep):
        first_ref[column] = out_ref[column * deep]
        last_ref[column] = out_ref[column * deep + deep - 1]


def list_tiles(
    group, amount, near_of, sizes, code_ref, table_ref, slots_ref, word_ref, cell_ref,
    class_ref, member_ref, count_ref, near_ref, need_ref, own_ref, kind_ref,
):
    tiles, lanes = slots_ref.shape
    span = table_ref.shape[0]
    padded = class_ref.shape[0]
    cells = count_ref.shape[0]
    lane_bits = lanes.bit_length() - 1
    wide = 256
    parts = 2
    flat = table_ref.reshape(span * 8, lanes)

    def plane(comp):
        return flat[pl.ds(comp, span, stride=8), :]

    def flag(value):
        return value.astype(jnp.float32).astype(jnp.bfloat16)

    def dot(first, second):
        return jnp.dot(first, second, preferred_element_type=jnp.float32)

    def ramp(shape, axis):
        return lax.broadcasted_iota(jnp.int32, shape, axis)

    def over(value, by):
        return jnp.floor((value.astype(jnp.float32) + 0.5) * (1.0 / by)).astype(jnp.int32)

    code = code_ref[...] & (OUTSIDE - 1)
    own = over(code, 27)
    kind = code - 27 * own
    step_x = over(kind, 9)
    step_y = over(kind, 3) - 3 * step_x
    steps = (step_x - 1, step_y - 1, kind - 9 * step_x - 3 * step_y - 1)
    own_x = over(own, sizes[1] * sizes[2])
    row = over(own, sizes[2])
    near = near_of(
        own_x + steps[0], row - own_x * sizes[1] + steps[1], own - row * sizes[2] + steps[2]
    )
    need = sum(
        jnp.where(steps[axis] == 1, 1, jnp.where(steps[axis] == -1, 2, 0)) * (1 << (2 * axis))
        for axis in range(3)
    )
    live = ramp((1, tiles), 1) < amount
    near = jnp.where(live, near, 0)
    near_ref[...] = near
    kind_ref[...] = near * 32 + jnp.where(live, kind, 0)
    need_ref[...] = jnp.where(live, need, 64)
    own_ref[...] = jnp.where(live, own, cells)

    radius = plane(6) + (radius_top + 1e-5)
    classes = jnp.zeros((span, lanes), jnp.float32)
    for axis in range(3):
        place = plane(axis)
        classes = classes + jnp.where(place < radius, 1.0 * (1 << (2 * axis)), 0.0)
        classes = classes + jnp.where(place > 1.0 - radius, 1.0 * (2 << (2 * axis)), 0.0)
    if padded > span:
        class_ref[...] = jnp.zeros(class_ref.shape, jnp.float32)
    class_ref[pl.ds(0, span), :] = classes
    codes = jnp.concatenate(
        [class_ref[pl.ds(at, lanes), :].T for at in range(0, padded, lanes)], axis=1
    ).astype(jnp.bfloat16)
    ones = jnp.ones((lanes, lanes), jnp.bfloat16)
    count_ref[...] = jnp.zeros(count_ref.shape, jnp.float32)
    blocks = lax.div(amount + (parts * wide - 1), parts * wide)

    def choose(block, unused):
        held = []
        for part in range(parts):
            at = pl.ds(pl.multiple_of((block * parts + part) * wide, wide), wide)
            hits = flag(ramp((padded, wide), 0) == near_ref[:, at])
            found = dot(codes, hits).astype(jnp.int32)
            need = need_ref[:, at]
            member = ((found & need) == need).astype(jnp.float32)
            member_ref[:, at] = member
            count = dot(ones, member.astype(jnp.bfloat16))
            mine = flag(ramp((cells, wide), 0) == own_ref[:, at])
            held.append(dot_lanes(mine, count[0:16].astype(jnp.bfloat16)))
        count_ref[:, 0:16] += held[0] + held[1]
        return unused

    lax.fori_loop(0, blocks, choose, 0)

    held = jnp.broadcast_to(count_ref[:, 0:1], count_ref.shape)
    high = jnp.floor(held * (1.0 / lanes))
    low = held - lanes * high
    taken = jnp.floor((held + (group - 1)) * (1.0 / group))
    upto = flag(ramp((cells, cells), 1) <= ramp((cells, cells), 0))
    ends = dot(upto, taken.astype(jnp.bfloat16))
    cell_ones = jnp.ones((8, cells), jnp.bfloat16)
    many = 8 * lanes
    wide_ends = jnp.concatenate([ends] * 8, axis=1)

    def name_groups(block, unused):
        number = (ramp((cells, many), 1) + block * many).astype(jnp.float32)
        at = pl.ds(pl.multiple_of(block * many, many), many)
        cell_ref[:, at] = dot(cell_ones, flag(wide_ends <= number))[0:1].astype(jnp.int32)
        return unused

    groups = jnp.max(ends).astype(jnp.int32)
    lax.fori_loop(0, lax.div(groups + SLACK, many) + 1, name_groups, 0)
    before_cell = jnp.concatenate(
        [value.T[0:8] for value in (taken, high, low)], axis=0
    ).astype(jnp.bfloat16)

    earlier = flag(ramp((lanes, lanes), 1) < ramp((lanes, lanes), 0))
    earlier_tile = flag(ramp((wide, wide), 0) < ramp((wide, wide), 1))

    def place(block, done):
        for part in range(parts):
            first = pl.multiple_of((block * parts + part) * wide, wide)
            at = pl.ds(first, wide)
            flags = member_ref[:, at].astype(jnp.bfloat16)
            count = dot(ones, flags)
            lower = flag(ramp((cells, wide), 0) < own_ref[:, at])
            before = dot(before_cell, lower)
            so_far = dot(count[0:8].astype(jnp.bfloat16), earlier_tile) + done
            start = group * before[0:8] + so_far - (lanes * before[8:16] + before[16:24])
            start = start.astype(jnp.int32)[0:1]
            offset = jnp.broadcast_to(start & (lanes - 1), (8, wide))
            word_ref[:, at] = (start >> lane_bits) * (1 << WORD_BITS) + kind_ref[:, at]
            rank = dot(earlier, flags)
            slot = ramp((lanes, wide), 0)
            moves = slot - rank.astype(jnp.int32)
            word = jnp.where(member_ref[:, at] > 0.0, slot + lanes * moves, 0)
            bit = 1
            while bit < lanes:
                keep = jnp.where((word & (bit * lanes)) != 0, 0, word)
                gone = word ^ keep
                word = keep | jnp.concatenate([gone[bit:], gone[:bit]], axis=0)
                bit *= 2
            word = word & (lanes - 1)
            line = ramp((8, wide), 0)
            within = offset & 7
            pick = (line - within) & 7
            slabs = [
                jnp.take_along_axis(
                    word[at_row : at_row + 8], pick, axis=0, mode="promise_in_bounds"
                )
                for at_row in range(0, lanes, 8)
            ]
            slabs = [
                jnp.where(line >= within, slabs[number], slabs[number - 1])
                for number in range(len(slabs))
            ]
            hop = 1
            while hop < len(slabs):
                chosen = (offset & (8 * hop)) != 0
                slabs = [
                    jnp.where(chosen, slabs[number - hop], slabs[number])
                    for number in range(len(slabs))
                ]
                hop *= 2
            count = count[0:8].astype(jnp.int32)
            for number in range(len(slabs)):
                lead = line + 8 * number - offset
                taken_lane = jnp.where((lead & (lanes - 1)) < count, lanes, 0)
                slabs[number] = slabs[number] | taken_lane | jnp.where(lead < 0, 2 * lanes, 0)
            word = jnp.concatenate(slabs, axis=0)
            for half in range(wide // lanes):
                rows = pl.ds(pl.multiple_of(first + half * lanes, lanes), lanes)
                slots_ref[rows, :] = word[:, half * lanes : (half + 1) * lanes].T
            done = done + jnp.sum(count.astype(jnp.float32), axis=1, keepdims=True)
        return done

    lax.fori_loop(0, blocks, place, jnp.zeros((8, 1), jnp.float32))
    return groups


def pair_forces(
    group, beside, amount, groups, word_smem, cell_smem, table_ref, near_table_ref, slots_ref,
    shift_ref, list_ref, force_ref, even_ref, odd_ref,
):
    lanes = table_ref.shape[1]
    cells = table_ref.shape[0] // 8
    rows = even_ref.shape[0]
    chunks = rows // lanes
    units = rows // group
    row = lax.broadcasted_iota(jnp.int32, (8, lanes), 0)
    absent = jnp.where(row == 6, -10.0, 0.0)
    for kind in range(27):
        steps = (kind // 9 - 1.0, kind // 3 % 3 - 1.0, kind % 3 - 1.0)
        shift_ref[kind] = sum(jnp.where(row == axis, steps[axis], 0.0) for axis in range(3))
    last_tile = jnp.maximum(amount - 1, 0)

    def fill(count, state):
        tile, _, last_chunk, last_new, last_held = state
        places = [jnp.minimum(tile + unit, last_tile) for unit in range(count + 1)]
        words = [word_smem[0, place] for place in places]
        for place, word in zip(places[:count], words):
            slots = slots_ref[pl.ds(place, 8, stride=0), :]
            cell = near_table_ref[(word >> 5) & ((1 << (WORD_BITS - 5)) - 1)]
            found = lanes_of(cell, slots & (lanes - 1)) + shift_ref[word & 31]
            chunk = word >> WORD_BITS
            new = jnp.where((slots & lanes) != 0, found, absent)
            later = (slots & (2 * lanes)) != 0
            held_row = jnp.where(chunk != last_chunk, last_new, last_held)
            held_row = jnp.where(later, held_row, new)
            new = jnp.where(later, new, absent)
            list_ref[chunk] = held_row
            list_ref[chunk + 1] = new
            last_chunk, last_new, last_held = chunk, new, held_row
        return tile + count, words[count] >> WORD_BITS, last_chunk, last_new, last_held

    def catch_up(limit, state):
        return lax.while_loop(
            lambda state: (state[0] < amount) & (state[1] <= limit), functools.partial(fill, FILL), state
        )

    force_ref[...] = jnp.zeros(force_ref.shape, jnp.float32)
    part = lax.broadcasted_iota(jnp.int32, (32, 8 * lanes), 0)
    comp = lax.broadcasted_iota(jnp.int32, (32, 8 * lanes), 1) // lanes
    weights = jnp.where((part < 24) & (part % 8 == comp), 1.0, 0.0).astype(jnp.bfloat16)

    def turned(step):
        pieces = []
        for piece in range(chunks):
            values = list_ref[step * chunks + piece]
            high = values.astype(jnp.bfloat16).astype(jnp.float32)
            rest = values - high
            middle = rest.astype(jnp.bfloat16).astype(jnp.float32)
            parts = jnp.concatenate([high, middle, rest - middle, jnp.zeros_like(values)], axis=0)
            pieces.append(parts.astype(jnp.bfloat16).T)
        return jnp.concatenate(pieces, axis=0)

    def spread(step, out_ref):
        out_ref[...] = jnp.dot(turned(step), weights, preferred_element_type=jnp.float32)

    def block_force(wide_ref, row, mine):
        other = [wide_ref[pl.ds(row, 8), pl.ds(value * lanes, lanes)] for value in range(8)]
        apart = [other[axis] - mine[axis] for axis in range(3)]
        square = apart[0] * apart[0] + apart[1] * apart[1] + apart[2] * apart[2] + epsilon_sq
        inverse = lax.rsqrt(square)
        reach = other[6] + mine[6]
        overlap = jnp.maximum(reach - square * inverse, 0.0)
        overlap = jnp.where(other[7] != mine[7], overlap, 0.0)
        closing = (
            (other[3] - mine[3]) * apart[0]
            + (other[4] - mine[4]) * apart[1]
            + (other[5] - mine[5]) * apart[2]
        )
        scaled = overlap * (other[6] * mine[6])
        root = scaled * lax.rsqrt(jnp.maximum(scaled * reach, 1e-30))
        factor = root * inverse * (overlap - closing * inverse)
        return [factor * apart[axis] for axis in range(3)]

    def pairs(step, wide_ref, carry):
        last, running = carry
        for unit in range(units):
            cell = cell_smem[0, step * units + unit]
            own = jnp.minimum(cell, cells - 1) * 8
            mine = [table_ref[pl.ds(own + value, 8, stride=0), :] for value in range(8)]
            running = [jnp.where(cell == last, running[axis], 0.0) for axis in range(3)]
            for block in range(group // 8):
                force = block_force(wide_ref, unit * group + block * 8, mine)
                running = [running[axis] + force[axis] for axis in range(3)]
            last = cell
            for axis in range(3):
                force_ref[cell, axis] = running[axis]
        return last, running

    def both(step, carry):
        state, carry = carry
        state = catch_up((2 * step + 3) * chunks - 1, state)
        spread(2 * step + 1, odd_ref)
        state = fill(beside, state)
        carry = pairs(2 * step, even_ref, carry)
        spread(2 * step + 2, even_ref)
        return state, pairs(2 * step + 1, odd_ref, carry)

    zero = jnp.zeros((8, lanes), jnp.float32)
    state = catch_up(3 * chunks - 1, (jnp.int32(0), jnp.int32(0), jnp.int32(0), absent, absent))
    spread(0, even_ref)
    steps = lax.div(groups + (2 * units - 1), 2 * units)
    lax.fori_loop(0, steps, both, (state, (jnp.int32(-1), [zero] * 3)))


def to_scalars(pairs, sems):
    copies = [
        pltpu.make_async_copy(source, target, sems.at[number])
        for number, (source, target) in enumerate(pairs)
    ]
    for copy in copies:
        copy.start()
    for copy in copies:
        copy.wait()


def list_kernel(
    near_of, sizes, amount_smem, code_ref, table_ref, slots_ref, word_ref, cell_ref,
    groups_smem, *scratch,
):
    groups_smem[0] = list_tiles(
        INNER_GROUP, amount_smem[0], near_of, sizes, code_ref, table_ref, slots_ref, word_ref, cell_ref, *scratch,
    )


def inner_kernel(
    amount_smem, word_smem, cell_smem, groups_smem, table_ref, slots_ref, sums_ref, force_ref,
    list_ref, even_ref, odd_ref, shift_ref,
):
    cells, _, lanes = table_ref.shape
    pair_forces(
        INNER_GROUP, INNER_FILL, amount_smem[0], groups_smem[0], word_smem, cell_smem,
        table_ref.reshape(cells * 8, lanes), table_ref, slots_ref, shift_ref, list_ref, force_ref,
        even_ref, odd_ref,
    )
    parts = force_ref.reshape(force_ref.shape[0] * 24, lanes)

    def store_sums(block, unused):
        for half in range(4):
            at = pl.multiple_of(block * 32 + half * 8, 8)
            for axis in range(3):
                sums_ref[axis, pl.ds(at, 8), :] = sublane_sums(parts, at, axis)
        return unused

    lax.fori_loop(0, cells // 32, store_sums, 0)


def outer_kernel(
    near_of, sizes, amount_smem, code_ref, table_ref, halo_ref, inner_ref, arms_ref, frag_ref,
    key_ref, motion_ref, mass_ref, moment_ref, out_ref, fixed_ref, force_ref, loads_ref, slots_ref, word_ref, cell_ref, word_smem, cell_smem, sems, list_ref, even_ref, odd_ref, shift_ref, *scratch,
):
    cells, _, lanes = table_ref.shape
    held = key_ref.shape[1]
    owned = mass_ref.shape[1]
    fixed_ref[...] = jnp.zeros(fixed_ref.shape, jnp.float32)
    fixed_ref[6:7, 0:held] = key_ref[...]
    fixed_ref[0:6, held : held + owned] = motion_ref[...]
    fixed_ref[6:7, held : held + owned] = mass_ref[...]
    fixed_ref[7:8, held : held + owned] = moment_ref[...]
    amount = amount_smem[0]
    groups = list_tiles(
        OUTER_GROUP, amount, near_of, sizes, code_ref, halo_ref, slots_ref, word_ref, cell_ref, *scratch,
    )
    to_scalars([(word_ref, word_smem), (cell_ref, cell_smem)], sems)
    pair_forces(
        OUTER_GROUP, OUTER_FILL, amount, groups, word_smem, cell_smem,
        table_ref.reshape(cells * 8, lanes), halo_ref, slots_ref, shift_ref, list_ref, force_ref,
        even_ref, odd_ref,
    )
    sums = fragment_sums(inner_ref, force_ref, arms_ref, frag_ref, loads_ref, held)
    out = fixed_ref[...] + jnp.concatenate([sums, jnp.zeros_like(sums)], axis=1)
    for brick in range(out_ref.shape[0]):
        out_ref[brick] = out


def sublane_sums(parts_ref, first, axis):
    rows = [parts_ref[pl.ds(first * 24 + axis * 8 + part, 8, stride=24), :] for part in range(8)]
    while len(rows) > 1:
        rows = [one + other for one, other in zip(rows[::2], rows[1::2])]
    return rows[0]


def fragment_sums(inner_ref, outer_ref, arms_ref, frag_ref, loads_ref, held):
    cells, lanes = frag_ref.shape
    tall = loads_ref.shape[0]
    label = lax.broadcasted_iota(jnp.int32, (held, lanes), 0)
    parts = outer_ref.reshape(outer_ref.shape[0] * 24, lanes)

    def total_force(block, axis):
        halves = []
        for half in range(tall // 8):
            at = pl.multiple_of(block * tall + half * 8, 8)
            halves.append(sublane_sums(parts, at, axis) + inner_ref[axis, pl.ds(at, 8), :])
        return -stiffness * jnp.concatenate(halves, axis=0)

    def gather_sums(block, total):
        rows = pl.ds(pl.multiple_of(block * tall, tall), tall)
        force = [total_force(block, axis) for axis in range(3)]
        lever = [arms_ref[axis, rows, :] for axis in range(3)]
        torque = [
            lever[1] * force[2] - lever[2] * force[1],
            lever[2] * force[0] - lever[0] * force[2],
            lever[0] * force[1] - lever[1] * force[0],
        ]
        loads = force + torque + [jnp.zeros_like(force[0])] * 2
        for comp in range(8):
            loads_ref[:, comp, :] = loads[comp]
        frags = frag_ref[rows, :]
        hits = [
            (frags[unit : unit + 1, :] == label).astype(jnp.float32).astype(jnp.bfloat16)
            for unit in range(tall)
        ]
        values = [split_rows(loads_ref[unit]) for unit in range(tall)]
        return total + dot_lanes(jnp.concatenate(values, axis=1), jnp.concatenate(hits, axis=1))

    total = lax.fori_loop(0, cells // tall, gather_sums, jnp.zeros((24, held), jnp.float32))
    return joined_rows(total)


def move_kernel(
    owned, target_ref, known_ref, state_ref, arms_ref, frag_ref, spheres_ref, clumps_ref
):
    bricks, _, lanes = known_ref.shape
    held = lanes // 2
    cells = frag_ref.shape[0]
    targets = jnp.broadcast_to(target_ref[...], (lanes, lanes))
    lane = lax.broadcasted_iota(jnp.int32, (1, lanes), 1)

    def match(block, carry):
        sums, base = carry
        for unit in range(8):
            brick = block * 8 + unit
            known = known_ref[brick]
            values = split_rows(known)
            key = jnp.where(lane < held, known[6:7], -1.0)
            number = jnp.where(
                (lane >= held) & (lane < held + owned), brick * owned + lane - held, -1
            ).astype(jnp.float32)
            sums = sums + dot_lanes((targets == key).astype(jnp.float32).astype(jnp.bfloat16), values)
            base = base + dot_lanes((targets == number).astype(jnp.float32).astype(jnp.bfloat16), values)
        return sums, base

    zero = jnp.zeros((lanes, 24), jnp.float32)
    sums, base = lax.fori_loop(0, bricks // 8, match, (zero, zero))
    sums = joined_rows(sums.T)
    base = joined_rows(base.T)
    rows = []
    for axis in range(3):
        pull = gravity if axis == 2 else 0.0
        rows.append(
            base[axis : axis + 1]
            + time_step * (sums[axis : axis + 1] * base[6:7] - pull)
        )
    for axis in range(3, 6):
        rows.append(base[axis : axis + 1] + time_step * sums[axis : axis + 1] * base[7:8])
    for comp in range(6):
        clumps_ref[comp : comp + 1, :] = rows[comp]
    tall = 32
    wide = [jnp.broadcast_to(value, (tall, lanes)) for value in rows]

    def cross(first, second):
        return [
            first[1] * second[2] - first[2] * second[1],
            first[2] * second[0] - first[0] * second[2],
            first[0] * second[1] - first[1] * second[0],
        ]

    def move(block, unused):
        at = pl.ds(pl.multiple_of(block * tall, tall), tall)
        index = frag_ref[at, :] + (lanes - held)
        motion = [lanes_of(value, index) for value in wide]
        velocity, spin = motion[0:3], motion[3:6]
        arm = [arms_ref[axis, at, :] for axis in range(3)]
        half = [0.5 * time_step * value for value in spin]
        turned = cross(half, arm)
        twice = cross(half, turned)
        scale = 2.0 / (1.0 + half[0] * half[0] + half[1] * half[1] + half[2] * half[2])
        change = [scale * (turned[axis] + twice[axis]) for axis in range(3)]
        new_arm = [arm[axis] + change[axis] for axis in range(3)]
        swing = cross(spin, new_arm)
        for axis in range(3):
            spheres_ref[axis, at, :] = (
                state_ref[axis, at, :] + time_step * velocity[axis] + (new_arm[axis] - arm[axis])
            )
            spheres_ref[3 + axis, at, :] = velocity[axis] + swing[axis]
        return unused

    lax.fori_loop(0, cells // tall, move, 0)


def local(
    state, arms, sphere_frag, frag_owner, frag_clump, tiles, clump_motion, inv_mass, inv_moment
):
    cells_x, cells_y, cells_z = (state.shape[1], state.shape[2], state.shape[3])
    lanes = state.shape[4]
    cells = cells_x * cells_y * cells_z
    owned = inv_mass.shape[0]
    held = frag_clump.shape[0]
    names = ("gx", "gy", "gz")
    vmem = pl.BlockSpec(memory_space=pltpu.VMEM)
    smem = pl.BlockSpec(memory_space=pltpu.SMEM)
    params = pltpu.CompilerParams(vmem_limit_bytes=VMEM)

    frag_key = (frag_owner[:, 0] * owned + frag_clump).astype(jnp.float32)
    flat_state = state.reshape(7, cells, lanes)
    flat_arms = arms.reshape(3, cells, lanes)
    flat_frag = sphere_frag.reshape(cells, lanes)

    face_shape = jax.ShapeDtypeStruct((cells_x * cells_y, 8, lanes), jnp.float32)
    table, z_last, z_first = pl.pallas_call(
        functools.partial(pack_kernel, cells_z),
        out_shape=(jax.ShapeDtypeStruct((cells, 8, lanes), jnp.float32), face_shape, face_shape),
        in_specs=[vmem] * 3,
        out_specs=(vmem,) * 3,
        compiler_params=params,
    )(flat_state, flat_frag, frag_key[None])
    grid = table.reshape(cells_x, cells_y, cells_z, 8, lanes)
    z_before, z_after = exchange(z_last, z_first, "gz")

    span_z = cells_z + 2
    starts = [0, cells_x * cells_y, 2 * cells_x * cells_y]
    starts += [starts[-1] + cells_y * span_z, starts[-1] + 2 * cells_y * span_z]
    starts += [starts[-1] + (cells_x + 2) * span_z]

    def inside(codes):
        own, kind = (codes // 27, codes % 27)
        x = own // (cells_y * cells_z) + kind // 9 - 1
        y = own // cells_z % cells_y + kind // 3 % 3 - 1
        z = own % cells_z + kind % 3 - 1
        inner = (x >= 0) & (x < cells_x) & (y >= 0) & (y < cells_y)
        return inner & (z >= 0) & (z < cells_z)

    def near_inside(x, y, z):
        return (x * cells_y + y) * cells_z + z

    def near_outside(x, y, z):
        in_y = jnp.where(y < 0, starts[4], starts[5]) + (x + 1) * span_z + z + 1
        in_x = jnp.where(x < 0, starts[2], starts[3]) + y * span_z + z + 1
        in_z = jnp.where(z < 0, starts[0], starts[1]) + x * cells_y + y
        in_x = jnp.where((x < 0) | (x >= cells_x), in_x, in_z)
        return jnp.where((y < 0) | (y >= cells_y), in_y, in_x)

    sizes = (cells_x, cells_y, cells_z)
    codes = tiles[0]
    total = codes.shape[0]
    codes = codes + jnp.where(inside(codes), 0, OUTSIDE)
    chunks = total + cells * INNER_GROUP // lanes + 3 * SPREAD
    group_top = -(-(chunks * (lanes // OUTER_GROUP) + SLACK) // (8 * lanes)) * 8 * lanes + 8 * lanes
    force_shape = (cells + 8, 3, 8, lanes)

    list_shapes = [(total, lanes), (1, total), (1, group_top)]

    def list_scratch(span):
        return [
            pltpu.VMEM((-(-span // lanes) * lanes, lanes), jnp.float32),
            pltpu.VMEM((lanes, total), jnp.float32),
            pltpu.VMEM((cells, lanes), jnp.float32),
            pltpu.VMEM((1, total), jnp.int32),
            pltpu.VMEM((1, total), jnp.int32),
            pltpu.VMEM((1, total), jnp.int32),
            pltpu.VMEM((1, total), jnp.int32),
        ]

    pair_scratch = [
        pltpu.VMEM((chunks, 8, lanes), jnp.float32),
        pltpu.VMEM((SPREAD * lanes, 8 * lanes), jnp.float32),
        pltpu.VMEM((SPREAD * lanes, 8 * lanes), jnp.float32),
        pltpu.VMEM((27, 8, lanes), jnp.float32),
    ]

    codes = jnp.sort(codes)
    inner_amount = jnp.sum((codes < OUTSIDE).astype(jnp.int32))
    outer_amount = total - inner_amount
    z_before, z_after, codes, inner_amount = lax.optimization_barrier(
        (z_before, z_after, codes, inner_amount)
    )
    z_before, z_after = (
        part.reshape(cells_x, cells_y, 1, 8, lanes) for part in (z_before, z_after)
    )
    x_before, x_after = exchange(
        jnp.concatenate([z_before[-1:], grid[-1:], z_after[-1:]], axis=2),
        jnp.concatenate([z_before[:1], grid[:1], z_after[:1]], axis=2),
        "gx",
    )
    slots, word, cell_of, groups = pl.pallas_call(
        functools.partial(list_kernel, near_inside, sizes),
        out_shape=tuple(jax.ShapeDtypeStruct(shape, jnp.int32) for shape in list_shapes + [(1,)]),
        in_specs=[smem, vmem, vmem],
        out_specs=(vmem,) * 3 + (smem,),
        scratch_shapes=list_scratch(cells),
        compiler_params=params,
    )(inner_amount[None], codes[None], table)
    x_before, x_after, slots, word, cell_of, groups = lax.optimization_barrier(
        (x_before, x_after, slots, word, cell_of, groups)
    )

    def face(at):
        middle = jnp.concatenate([z_before[:, at], grid[:, at], z_after[:, at]], axis=2)
        return jnp.concatenate([x_before[:, at], middle, x_after[:, at]], axis=0)

    y_before, y_after = exchange(face(slice(-1, None)), face(slice(0, 1)), "gy")
    inner = pl.pallas_call(
        inner_kernel,
        out_shape=jax.ShapeDtypeStruct((3, cells, lanes), jnp.float32),
        in_specs=[smem] * 4 + [vmem] * 2,
        out_specs=vmem,
        scratch_shapes=[pltpu.VMEM(force_shape, jnp.float32)] + pair_scratch,
        compiler_params=params,
    )(inner_amount[None], word, cell_of, groups, table, slots)

    outer_codes = lax.dynamic_slice(jnp.concatenate([codes, codes]), (inner_amount,), (total,))
    halo = jnp.concatenate(
        [
            part.reshape(-1, 8, lanes)
            for part in (z_before, z_after, x_before, x_after, y_before, y_after)
        ],
        axis=0,
    )
    bricks = lax.axis_size(names)
    known = pl.pallas_call(
        functools.partial(outer_kernel, near_outside, sizes),
        out_shape=jax.ShapeDtypeStruct((bricks, 8, lanes), jnp.float32),
        in_specs=[smem] + [vmem] * 10,
        out_specs=vmem,
        scratch_shapes=[
            pltpu.VMEM((8, lanes), jnp.float32),
            pltpu.VMEM(force_shape, jnp.float32),
            pltpu.VMEM((16, 8, lanes), jnp.float32),
        ]
        + [pltpu.VMEM(shape, jnp.int32) for shape in list_shapes]
        + [pltpu.SMEM(shape, jnp.int32) for shape in list_shapes[1:]]
        + [pltpu.SemaphoreType.DMA((2,))]
        + pair_scratch
        + list_scratch(halo.shape[0]),
        compiler_params=params,
    )(outer_amount[None], outer_codes[None], table, halo, inner, flat_arms, flat_frag,
        frag_key[None], clump_motion, inv_mass[None], inv_moment[None])
    known = lax.all_to_all(known, names, split_axis=0, concat_axis=0, tiled=True)

    brick = lax.axis_index(names)
    mine = jnp.where(
        jnp.arange(lanes - held) < owned, brick * owned + jnp.arange(lanes - held), -2
    ).astype(jnp.float32)
    target = jnp.concatenate([mine, frag_key])[:, None]
    spheres, clumps = pl.pallas_call(
        functools.partial(move_kernel, owned),
        out_shape=(
            jax.ShapeDtypeStruct((6, cells, lanes), jnp.float32),
            jax.ShapeDtypeStruct((6, lanes), jnp.float32),
        ),
        in_specs=[vmem] * 5,
        out_specs=(vmem, vmem),
        compiler_params=params,
    )(target, known, flat_state, flat_arms, flat_frag)
    return (spheres.reshape((6,) + state.shape[1:]), clumps[:, :owned])


def solution(mesh):
    return jax.shard_map(
        local,
        mesh=mesh,
        in_specs=(
            P(None, "gx", "gy", "gz", None),
            P(None, "gx", "gy", "gz", None),
            P("gx", "gy", "gz", None),
            P(("gx", "gy", "gz"), None),
            P(("gx", "gy", "gz")),
            P(("gx", "gy", "gz"), None),
            P(None, ("gx", "gy", "gz")),
            P(("gx", "gy", "gz")),
            P(("gx", "gy", "gz")),
        ),
        out_specs=(P(None, "gx", "gy", "gz", None), P(None, ("gx", "gy", "gz"))),
        check_vma=False,
    )
```

```python
import functools

import jax
import jax.numpy as jnp
from jax import lax
from jax.experimental import pallas as pl
from jax.experimental.pallas import tpu as pltpu
from jax.sharding import PartitionSpec as P

stiffness = 100.0
damping = 2.0
time_step = 0.01
gravity = 9.81
epsilon_sq = 1e-08
radius_top = 0.14

INNER_GROUP = 32
OUTER_GROUP = 16
FILL = 64
OUTSIDE = 1 << 20
WORD_BITS = 16
SLACK = 256
SPREAD = 4
VMEM = 56 * 1024 * 1024


def lanes_of(values, index):
    return jnp.take_along_axis(values, index, axis=1, mode="promise_in_bounds")


def split_rows(values):
    high = values.astype(jnp.bfloat16).astype(jnp.float32)
    rest = values - high
    middle = rest.astype(jnp.bfloat16).astype(jnp.float32)
    low = rest - middle
    return jnp.concatenate([high, middle, low], axis=0).astype(jnp.bfloat16)


def joined_rows(stacked):
    rows = stacked.shape[0] // 3
    return stacked[0:rows] + stacked[rows : 2 * rows] + stacked[2 * rows :]


def inverse_root(values):
    return jnp.exp2(-0.5 * jnp.log2(values))


def dot_lanes(first, second):
    return lax.dot_general(
        first, second, (((1,), (1,)), ((), ())), preferred_element_type=jnp.float32
    )


def exchange(last, initial, axis):
    devices = lax.axis_size(axis)
    up = [(i, (i + 1) % devices) for i in range(devices)]
    down = [(j, i) for i, j in up]
    return lax.ppermute(last, axis, up), lax.ppermute(initial, axis, down)


def pack_kernel(deep, state_ref, frag_ref, key_ref, out_ref, last_ref, first_ref):
    cells, lanes = frag_ref.shape
    held = key_ref.shape[1]
    for comp in range(7):
        out_ref[:, comp, :] = state_ref[comp] * (damping / stiffness if 3 <= comp < 6 else 1.0)
    keys = jnp.concatenate([key_ref[0:1, :], jnp.zeros((1, lanes - held), jnp.float32)], axis=1)
    keys = jnp.broadcast_to(keys, (8, lanes))
    for block in range(cells // 8):
        rows = pl.ds(block * 8, 8)
        out_ref[rows, 7, :] = lanes_of(keys, frag_ref[rows, :])
    for column in range(cells // deep):
        first_ref[column] = out_ref[column * deep]
        last_ref[column] = out_ref[column * deep + deep - 1]


def list_tiles(
    group, amount, near_of, sizes, code_ref, table_ref, slots_ref, word_ref, cell_ref,
    class_ref, member_ref, count_ref, near_ref, need_ref, own_ref, kind_ref,
):
    tiles, lanes = slots_ref.shape
    span = table_ref.shape[0]
    padded = class_ref.shape[0]
    cells = count_ref.shape[0]
    lane_bits = lanes.bit_length() - 1
    wide = 256
    parts = 2
    flat = table_ref.reshape(span * 8, lanes)

    def plane(comp):
        return flat[pl.ds(comp, span, stride=8), :]

    def flag(value):
        return value.astype(jnp.float32).astype(jnp.bfloat16)

    def dot(first, second):
        return jnp.dot(first, second, preferred_element_type=jnp.float32)

    def ramp(shape, axis):
        return lax.broadcasted_iota(jnp.int32, shape, axis)

    def over(value, by):
        return jnp.floor((value.astype(jnp.float32) + 0.5) * (1.0 / by)).astype(jnp.int32)

    code = code_ref[...] & (OUTSIDE - 1)
    own = over(code, 27)
    kind = code - 27 * own
    step_x = over(kind, 9)
    step_y = over(kind, 3) - 3 * step_x
    steps = (step_x - 1, step_y - 1, kind - 9 * step_x - 3 * step_y - 1)
    own_x = over(own, sizes[1] * sizes[2])
    row = over(own, sizes[2])
    near = near_of(
        own_x + steps[0], row - own_x * sizes[1] + steps[1], own - row * sizes[2] + steps[2]
    )
    need = sum(
        jnp.where(steps[axis] == 1, 1, jnp.where(steps[axis] == -1, 2, 0)) * (1 << (2 * axis))
        for axis in range(3)
    )
    live = ramp((1, tiles), 1) < amount
    near = jnp.where(live, near, 0)
    near_ref[...] = near
    kind_ref[...] = near * 32 + jnp.where(live, kind, 0)
    need_ref[...] = jnp.where(live, need, 64)
    own_ref[...] = jnp.where(live, own, cells)

    radius = plane(6) + (radius_top + 1e-5)
    classes = jnp.zeros((span, lanes), jnp.float32)
    for axis in range(3):
        place = plane(axis)
        classes = classes + jnp.where(place < radius, 1.0 * (1 << (2 * axis)), 0.0)
        classes = classes + jnp.where(place > 1.0 - radius, 1.0 * (2 << (2 * axis)), 0.0)
    if padded > span:
        class_ref[...] = jnp.zeros(class_ref.shape, jnp.float32)
    class_ref[pl.ds(0, span), :] = classes
    codes = jnp.concatenate(
        [class_ref[pl.ds(at, lanes), :].T for at in range(0, padded, lanes)], axis=1
    ).astype(jnp.bfloat16)
    ones = jnp.ones((lanes, lanes), jnp.bfloat16)
    count_ref[...] = jnp.zeros(count_ref.shape, jnp.float32)
    blocks = lax.div(amount + (parts * wide - 1), parts * wide)

    def choose(block, unused):
        held = []
        for part in range(parts):
            at = pl.ds(pl.multiple_of((block * parts + part) * wide, wide), wide)
            hits = flag(ramp((padded, wide), 0) == near_ref[:, at])
            found = dot(codes, hits).astype(jnp.int32)
            need = need_ref[:, at]
            member = ((found & need) == need).astype(jnp.float32)
            member_ref[:, at] = member
            count = dot(ones, member.astype(jnp.bfloat16))
            mine = flag(ramp((cells, wide), 0) == own_ref[:, at])
            held.append(dot_lanes(mine, count[0:16].astype(jnp.bfloat16)))
        count_ref[:, 0:16] += held[0] + held[1]
        return unused

    lax.fori_loop(0, blocks, choose, 0)

    held = jnp.broadcast_to(count_ref[:, 0:1], count_ref.shape)
    high = jnp.floor(held * (1.0 / lanes))
    low = held - lanes * high
    taken = jnp.floor((held + (group - 1)) * (1.0 / group))
    upto = flag(ramp((cells, cells), 1) <= ramp((cells, cells), 0))
    ends = dot(upto, taken.astype(jnp.bfloat16))
    cell_ones = jnp.ones((8, cells), jnp.bfloat16)
    many = 8 * lanes
    wide_ends = jnp.concatenate([ends] * 8, axis=1)

    def name_groups(block, unused):
        number = (ramp((cells, many), 1) + block * many).astype(jnp.float32)
        at = pl.ds(pl.multiple_of(block * many, many), many)
        cell_ref[:, at] = dot(cell_ones, flag(wide_ends <= number))[0:1].astype(jnp.int32)
        return unused

    groups = jnp.max(ends).astype(jnp.int32)
    lax.fori_loop(0, lax.div(groups + SLACK, many) + 1, name_groups, 0)
    before_cell = jnp.concatenate(
        [value.T[0:8] for value in (taken, high, low)], axis=0
    ).astype(jnp.bfloat16)

    earlier = flag(ramp((lanes, lanes), 1) < ramp((lanes, lanes), 0))
    earlier_tile = flag(ramp((wide, wide), 0) < ramp((wide, wide), 1))

    def place(block, done):
        for part in range(parts):
            first = pl.multiple_of((block * parts + part) * wide, wide)
            at = pl.ds(first, wide)
            flags = member_ref[:, at].astype(jnp.bfloat16)
            count = dot(ones, flags)
            lower = flag(ramp((cells, wide), 0) < own_ref[:, at])
            before = dot(before_cell, lower)
            so_far = dot(count[0:8].astype(jnp.bfloat16), earlier_tile) + done
            start = group * before[0:8] + so_far - (lanes * before[8:16] + before[16:24])
            start = start.astype(jnp.int32)[0:1]
            offset = jnp.broadcast_to(start & (lanes - 1), (8, wide))
            word_ref[:, at] = (start >> lane_bits) * (1 << WORD_BITS) + kind_ref[:, at]
            rank = dot(earlier, flags)
            slot = ramp((lanes, wide), 0)
            moves = slot - rank.astype(jnp.int32)
            word = jnp.where(member_ref[:, at] > 0.0, slot + lanes * moves, 0)
            bit = 1
            while bit < lanes:
                keep = jnp.where((word & (bit * lanes)) != 0, 0, word)
                gone = word ^ keep
                word = keep | jnp.concatenate([gone[bit:], gone[:bit]], axis=0)
                bit *= 2
            word = word & (lanes - 1)
            line = ramp((8, wide), 0)
            within = offset & 7
            pick = (line - within) & 7
            slabs = [
                jnp.take_along_axis(
                    word[at_row : at_row + 8], pick, axis=0, mode="promise_in_bounds"
                )
                for at_row in range(0, lanes, 8)
            ]
            slabs = [
                jnp.where(line >= within, slabs[number], slabs[number - 1])
                for number in range(len(slabs))
            ]
            hop = 1
            while hop < len(slabs):
                chosen = (offset & (8 * hop)) != 0
                slabs = [
                    jnp.where(chosen, slabs[number - hop], slabs[number])
                    for number in range(len(slabs))
                ]
                hop *= 2
            count = count[0:8].astype(jnp.int32)
            for number in range(len(slabs)):
                lead = line + 8 * number - offset
                taken_lane = jnp.where((lead & (lanes - 1)) < count, lanes, 0)
                slabs[number] = slabs[number] | taken_lane | jnp.where(lead < 0, 2 * lanes, 0)
            word = jnp.concatenate(slabs, axis=0)
            for half in range(wide // lanes):
                rows = pl.ds(pl.multiple_of(first + half * lanes, lanes), lanes)
                slots_ref[rows, :] = word[:, half * lanes : (half + 1) * lanes].T
            done = done + jnp.sum(count.astype(jnp.float32), axis=1, keepdims=True)
        return done

    lax.fori_loop(0, blocks, place, jnp.zeros((8, 1), jnp.float32))
    return groups


def fill_lists(amount, word_smem, near_table_ref, slots_ref, shift_ref, list_ref):
    lanes = slots_ref.shape[1]
    row = lax.broadcasted_iota(jnp.int32, (8, lanes), 0)
    absent = jnp.where(row == 6, -10.0, 0.0)
    for kind in range(27):
        steps = (kind // 9 - 1.0, kind // 3 % 3 - 1.0, kind % 3 - 1.0)
        shift_ref[kind] = sum(jnp.where(row == axis, steps[axis], 0.0) for axis in range(3))

    def fill(block, carry):
        last_chunk, last_new, last_held = carry
        words = [word_smem[0, block * FILL + unit] for unit in range(FILL)]
        for unit, word in enumerate(words):
            slots = slots_ref[pl.ds(block * FILL + unit, 8, stride=0), :]
            cell = near_table_ref[(word >> 5) & ((1 << (WORD_BITS - 5)) - 1)]
            found = lanes_of(cell, slots & (lanes - 1)) + shift_ref[word & 31]
            chunk = word >> WORD_BITS
            new = jnp.where((slots & lanes) != 0, found, absent)
            later = (slots & (2 * lanes)) != 0
            held_row = jnp.where(chunk != last_chunk, last_new, last_held)
            held_row = jnp.where(later, held_row, new)
            new = jnp.where(later, new, absent)
            list_ref[chunk] = held_row
            list_ref[chunk + 1] = new
            last_chunk, last_new, last_held = chunk, new, held_row
        return last_chunk, last_new, last_held

    blocks = lax.div(amount + (FILL - 1), FILL)
    lax.fori_loop(0, blocks, fill, (jnp.int32(0), absent, absent))


def pair_forces(group, groups, cell_smem, table_ref, list_ref, force_ref, even_ref, odd_ref):
    lanes = table_ref.shape[1]
    cells = table_ref.shape[0] // 8
    rows = even_ref.shape[0]
    chunks = rows // lanes
    units = rows // group
    force_ref[...] = jnp.zeros(force_ref.shape, jnp.float32)
    part = lax.broadcasted_iota(jnp.int32, (32, 8 * lanes), 0)
    comp = lax.broadcasted_iota(jnp.int32, (32, 8 * lanes), 1) // lanes
    weights = jnp.where((part < 24) & (part % 8 == comp), 1.0, 0.0).astype(jnp.bfloat16)

    def turned(step):
        pieces = []
        for piece in range(chunks):
            values = list_ref[step * chunks + piece]
            high = values.astype(jnp.bfloat16).astype(jnp.float32)
            rest = values - high
            middle = rest.astype(jnp.bfloat16).astype(jnp.float32)
            parts = jnp.concatenate([high, middle, rest - middle, jnp.zeros_like(values)], axis=0)
            pieces.append(parts.astype(jnp.bfloat16).T)
        return jnp.concatenate(pieces, axis=0)

    def spread(step, out_ref):
        out_ref[...] = jnp.dot(turned(step), weights, preferred_element_type=jnp.float32)

    def block_force(wide_ref, row, mine):
        other = [wide_ref[pl.ds(row, 8), pl.ds(value * lanes, lanes)] for value in range(8)]
        apart = [other[axis] - mine[axis] for axis in range(3)]
        square = apart[0] * apart[0] + apart[1] * apart[1] + apart[2] * apart[2] + epsilon_sq
        inverse = inverse_root(square)
        reach = other[6] + mine[6]
        overlap = jnp.maximum(reach - square * inverse, 0.0)
        overlap = jnp.where(other[7] != mine[7], overlap, 0.0)
        closing = (
            (other[3] - mine[3]) * apart[0]
            + (other[4] - mine[4]) * apart[1]
            + (other[5] - mine[5]) * apart[2]
        )
        scaled = overlap * (other[6] * mine[6])
        root = scaled * inverse_root(jnp.maximum(scaled * reach, 1e-30))
        factor = root * inverse * (overlap - closing * inverse)
        return [factor * apart[axis] for axis in range(3)]

    def pairs(step, wide_ref, next_ref, carry):
        last, running = carry
        spread(step + 1, next_ref)
        for unit in range(units):
            cell = cell_smem[0, step * units + unit]
            own = jnp.minimum(cell, cells - 1) * 8
            mine = [table_ref[pl.ds(own + value, 8, stride=0), :] for value in range(8)]
            running = [jnp.where(cell == last, running[axis], 0.0) for axis in range(3)]
            for block in range(group // 8):
                force = block_force(wide_ref, unit * group + block * 8, mine)
                running = [running[axis] + force[axis] for axis in range(3)]
            last = cell
            for axis in range(3):
                force_ref[cell, axis] = running[axis]
        return last, running

    spread(0, even_ref)

    def both(step, carry):
        carry = pairs(2 * step, even_ref, odd_ref, carry)
        return pairs(2 * step + 1, odd_ref, even_ref, carry)

    zero = jnp.zeros((8, lanes), jnp.float32)
    steps = lax.div(groups + (2 * units - 1), 2 * units)
    lax.fori_loop(0, steps, both, (jnp.int32(-1), [zero] * 3))


def to_scalars(pairs, sems):
    copies = [
        pltpu.make_async_copy(source, target, sems.at[number])
        for number, (source, target) in enumerate(pairs)
    ]
    for copy in copies:
        copy.start()
    for copy in copies:
        copy.wait()


def list_kernel(
    near_of, sizes, amount_smem, code_ref, table_ref, slots_ref, word_ref, cell_ref,
    groups_smem, *scratch,
):
    groups_smem[0] = list_tiles(
        INNER_GROUP, amount_smem[0], near_of, sizes, code_ref, table_ref, slots_ref, word_ref, cell_ref, *scratch,
    )


def inner_kernel(
    amount_smem, word_smem, cell_smem, groups_smem, table_ref, slots_ref, sums_ref, force_ref,
    list_ref, even_ref, odd_ref, shift_ref,
):
    cells, _, lanes = table_ref.shape
    fill_lists(amount_smem[0], word_smem, table_ref, slots_ref, shift_ref, list_ref)
    flat = table_ref.reshape(cells * 8, lanes)
    pair_forces(INNER_GROUP, groups_smem[0], cell_smem, flat, list_ref, force_ref, even_ref, odd_ref)
    parts = force_ref.reshape(force_ref.shape[0] * 24, lanes)

    def store_sums(block, unused):
        for half in range(4):
            at = pl.multiple_of(block * 32 + half * 8, 8)
            for axis in range(3):
                sums_ref[axis, pl.ds(at, 8), :] = sublane_sums(parts, at, axis)
        return unused

    lax.fori_loop(0, cells // 32, store_sums, 0)


def outer_kernel(
    near_of, sizes, amount_smem, code_ref, table_ref, halo_ref, inner_ref, arms_ref, frag_ref,
    key_ref, motion_ref, mass_ref, moment_ref, out_ref, fixed_ref, force_ref, loads_ref, slots_ref, word_ref, cell_ref, word_smem, cell_smem, sems, list_ref, even_ref, odd_ref, shift_ref, *scratch,
):
    cells, _, lanes = table_ref.shape
    held = key_ref.shape[1]
    owned = mass_ref.shape[1]
    fixed_ref[...] = jnp.zeros(fixed_ref.shape, jnp.float32)
    fixed_ref[6:7, 0:held] = key_ref[...]
    fixed_ref[0:6, held : held + owned] = motion_ref[...]
    fixed_ref[6:7, held : held + owned] = mass_ref[...]
    fixed_ref[7:8, held : held + owned] = moment_ref[...]
    amount = amount_smem[0]
    groups = list_tiles(
        OUTER_GROUP, amount, near_of, sizes, code_ref, halo_ref, slots_ref, word_ref, cell_ref, *scratch,
    )
    to_scalars([(word_ref, word_smem), (cell_ref, cell_smem)], sems)
    fill_lists(amount, word_smem, halo_ref, slots_ref, shift_ref, list_ref)
    flat = table_ref.reshape(cells * 8, lanes)
    pair_forces(OUTER_GROUP, groups, cell_smem, flat, list_ref, force_ref, even_ref, odd_ref)
    sums = fragment_sums(inner_ref, force_ref, arms_ref, frag_ref, loads_ref, held)
    out = fixed_ref[...] + jnp.concatenate([sums, jnp.zeros_like(sums)], axis=1)
    for brick in range(out_ref.shape[0]):
        out_ref[brick] = out


def sublane_sums(parts_ref, first, axis):
    rows = [parts_ref[pl.ds(first * 24 + axis * 8 + part, 8, stride=24), :] for part in range(8)]
    while len(rows) > 1:
        rows = [one + other for one, other in zip(rows[::2], rows[1::2])]
    return rows[0]


def fragment_sums(inner_ref, outer_ref, arms_ref, frag_ref, loads_ref, held):
    cells, lanes = frag_ref.shape
    tall = loads_ref.shape[0]
    label = lax.broadcasted_iota(jnp.int32, (held, lanes), 0)
    parts = outer_ref.reshape(outer_ref.shape[0] * 24, lanes)

    def total_force(block, axis):
        halves = []
        for half in range(tall // 8):
            at = pl.multiple_of(block * tall + half * 8, 8)
            halves.append(sublane_sums(parts, at, axis) + inner_ref[axis, pl.ds(at, 8), :])
        return -stiffness * jnp.concatenate(halves, axis=0)

    def gather_sums(block, total):
        rows = pl.ds(pl.multiple_of(block * tall, tall), tall)
        force = [total_force(block, axis) for axis in range(3)]
        lever = [arms_ref[axis, rows, :] for axis in range(3)]
        torque = [
            lever[1] * force[2] - lever[2] * force[1],
            lever[2] * force[0] - lever[0] * force[2],
            lever[0] * force[1] - lever[1] * force[0],
        ]
        loads = force + torque + [jnp.zeros_like(force[0])] * 2
        for comp in range(8):
            loads_ref[:, comp, :] = loads[comp]
        frags = frag_ref[rows, :]
        hits = [
            (frags[unit : unit + 1, :] == label).astype(jnp.float32).astype(jnp.bfloat16)
            for unit in range(tall)
        ]
        values = [split_rows(loads_ref[unit]) for unit in range(tall)]
        return total + dot_lanes(jnp.concatenate(values, axis=1), jnp.concatenate(hits, axis=1))

    total = lax.fori_loop(0, cells // tall, gather_sums, jnp.zeros((24, held), jnp.float32))
    return joined_rows(total)


def move_kernel(
    owned, target_ref, known_ref, state_ref, arms_ref, frag_ref, spheres_ref, clumps_ref
):
    bricks, _, lanes = known_ref.shape
    held = lanes // 2
    cells = frag_ref.shape[0]
    targets = jnp.broadcast_to(target_ref[...], (lanes, lanes))
    lane = lax.broadcasted_iota(jnp.int32, (1, lanes), 1)

    def match(block, carry):
        sums, base = carry
        for unit in range(8):
            brick = block * 8 + unit
            known = known_ref[brick]
            values = split_rows(known)
            key = jnp.where(lane < held, known[6:7], -1.0)
            number = jnp.where(
                (lane >= held) & (lane < held + owned), brick * owned + lane - held, -1
            ).astype(jnp.float32)
            sums = sums + dot_lanes((targets == key).astype(jnp.float32).astype(jnp.bfloat16), values)
            base = base + dot_lanes((targets == number).astype(jnp.float32).astype(jnp.bfloat16), values)
        return sums, base

    zero = jnp.zeros((lanes, 24), jnp.float32)
    sums, base = lax.fori_loop(0, bricks // 8, match, (zero, zero))
    sums = joined_rows(sums.T)
    base = joined_rows(base.T)
    rows = []
    for axis in range(3):
        pull = gravity if axis == 2 else 0.0
        rows.append(
            base[axis : axis + 1]
            + time_step * (sums[axis : axis + 1] * base[6:7] - pull)
        )
    for axis in range(3, 6):
        rows.append(base[axis : axis + 1] + time_step * sums[axis : axis + 1] * base[7:8])
    for comp in range(6):
        clumps_ref[comp : comp + 1, :] = rows[comp]
    tall = 32
    wide = [jnp.broadcast_to(value, (tall, lanes)) for value in rows]

    def cross(first, second):
        return [
            first[1] * second[2] - first[2] * second[1],
            first[2] * second[0] - first[0] * second[2],
            first[0] * second[1] - first[1] * second[0],
        ]

    def move(block, unused):
        at = pl.ds(pl.multiple_of(block * tall, tall), tall)
        index = frag_ref[at, :] + (lanes - held)
        motion = [lanes_of(value, index) for value in wide]
        velocity, spin = motion[0:3], motion[3:6]
        arm = [arms_ref[axis, at, :] for axis in range(3)]
        half = [0.5 * time_step * value for value in spin]
        turned = cross(half, arm)
        twice = cross(half, turned)
        scale = 2.0 / (1.0 + half[0] * half[0] + half[1] * half[1] + half[2] * half[2])
        change = [scale * (turned[axis] + twice[axis]) for axis in range(3)]
        new_arm = [arm[axis] + change[axis] for axis in range(3)]
        swing = cross(spin, new_arm)
        for axis in range(3):
            spheres_ref[axis, at, :] = (
                state_ref[axis, at, :] + time_step * velocity[axis] + (new_arm[axis] - arm[axis])
            )
            spheres_ref[3 + axis, at, :] = velocity[axis] + swing[axis]
        return unused

    lax.fori_loop(0, cells // tall, move, 0)


def local(
    state, arms, sphere_frag, frag_owner, frag_clump, tiles, clump_motion, inv_mass, inv_moment
):
    cells_x, cells_y, cells_z = (state.shape[1], state.shape[2], state.shape[3])
    lanes = state.shape[4]
    cells = cells_x * cells_y * cells_z
    owned = inv_mass.shape[0]
    held = frag_clump.shape[0]
    names = ("gx", "gy", "gz")
    vmem = pl.BlockSpec(memory_space=pltpu.VMEM)
    smem = pl.BlockSpec(memory_space=pltpu.SMEM)
    params = pltpu.CompilerParams(vmem_limit_bytes=VMEM)

    frag_key = (frag_owner[:, 0] * owned + frag_clump).astype(jnp.float32)
    flat_state = state.reshape(7, cells, lanes)
    flat_arms = arms.reshape(3, cells, lanes)
    flat_frag = sphere_frag.reshape(cells, lanes)

    face_shape = jax.ShapeDtypeStruct((cells_x * cells_y, 8, lanes), jnp.float32)
    table, z_last, z_first = pl.pallas_call(
        functools.partial(pack_kernel, cells_z),
        out_shape=(jax.ShapeDtypeStruct((cells, 8, lanes), jnp.float32), face_shape, face_shape),
        in_specs=[vmem] * 3,
        out_specs=(vmem,) * 3,
        compiler_params=params,
    )(flat_state, flat_frag, frag_key[None])
    grid = table.reshape(cells_x, cells_y, cells_z, 8, lanes)
    z_before, z_after = exchange(z_last, z_first, "gz")

    span_z = cells_z + 2
    starts = [0, cells_x * cells_y, 2 * cells_x * cells_y]
    starts += [starts[-1] + cells_y * span_z, starts[-1] + 2 * cells_y * span_z]
    starts += [starts[-1] + (cells_x + 2) * span_z]

    def inside(codes):
        own, kind = (codes // 27, codes % 27)
        x = own // (cells_y * cells_z) + kind // 9 - 1
        y = own // cells_z % cells_y + kind // 3 % 3 - 1
        z = own % cells_z + kind % 3 - 1
        inner = (x >= 0) & (x < cells_x) & (y >= 0) & (y < cells_y)
        return inner & (z >= 0) & (z < cells_z)

    def near_inside(x, y, z):
        return (x * cells_y + y) * cells_z + z

    def near_outside(x, y, z):
        in_y = jnp.where(y < 0, starts[4], starts[5]) + (x + 1) * span_z + z + 1
        in_x = jnp.where(x < 0, starts[2], starts[3]) + y * span_z + z + 1
        in_z = jnp.where(z < 0, starts[0], starts[1]) + x * cells_y + y
        in_x = jnp.where((x < 0) | (x >= cells_x), in_x, in_z)
        return jnp.where((y < 0) | (y >= cells_y), in_y, in_x)

    sizes = (cells_x, cells_y, cells_z)
    codes = tiles[0]
    total = codes.shape[0]
    codes = codes + jnp.where(inside(codes), 0, OUTSIDE)
    chunks = total + cells * INNER_GROUP // lanes + 3 * SPREAD
    group_top = -(-(chunks * (lanes // OUTER_GROUP) + SLACK) // (8 * lanes)) * 8 * lanes + 8 * lanes
    force_shape = (cells + 8, 3, 8, lanes)

    list_shapes = [(total, lanes), (1, total), (1, group_top)]

    def list_scratch(span):
        return [
            pltpu.VMEM((-(-span // lanes) * lanes, lanes), jnp.float32),
            pltpu.VMEM((lanes, total), jnp.float32),
            pltpu.VMEM((cells, lanes), jnp.float32),
            pltpu.VMEM((1, total), jnp.int32),
            pltpu.VMEM((1, total), jnp.int32),
            pltpu.VMEM((1, total), jnp.int32),
            pltpu.VMEM((1, total), jnp.int32),
        ]

    pair_scratch = [
        pltpu.VMEM((chunks, 8, lanes), jnp.float32),
        pltpu.VMEM((SPREAD * lanes, 8 * lanes), jnp.float32),
        pltpu.VMEM((SPREAD * lanes, 8 * lanes), jnp.float32),
        pltpu.VMEM((27, 8, lanes), jnp.float32),
    ]

    codes = jnp.sort(codes)
    inner_amount = jnp.sum((codes < OUTSIDE).astype(jnp.int32))
    outer_amount = total - inner_amount
    z_before, z_after, codes, inner_amount = lax.optimization_barrier(
        (z_before, z_after, codes, inner_amount)
    )
    z_before, z_after = (
        part.reshape(cells_x, cells_y, 1, 8, lanes) for part in (z_before, z_after)
    )
    x_before, x_after = exchange(
        jnp.concatenate([z_before[-1:], grid[-1:], z_after[-1:]], axis=2),
        jnp.concatenate([z_before[:1], grid[:1], z_after[:1]], axis=2),
        "gx",
    )
    slots, word, cell_of, groups = pl.pallas_call(
        functools.partial(list_kernel, near_inside, sizes),
        out_shape=tuple(jax.ShapeDtypeStruct(shape, jnp.int32) for shape in list_shapes + [(1,)]),
        in_specs=[smem, vmem, vmem],
        out_specs=(vmem,) * 3 + (smem,),
        scratch_shapes=list_scratch(cells),
        compiler_params=params,
    )(inner_amount[None], codes[None], table)
    x_before, x_after, slots, word, cell_of, groups = lax.optimization_barrier(
        (x_before, x_after, slots, word, cell_of, groups)
    )

    def face(at):
        middle = jnp.concatenate([z_before[:, at], grid[:, at], z_after[:, at]], axis=2)
        return jnp.concatenate([x_before[:, at], middle, x_after[:, at]], axis=0)

    y_before, y_after = exchange(face(slice(-1, None)), face(slice(0, 1)), "gy")
    inner = pl.pallas_call(
        inner_kernel,
        out_shape=jax.ShapeDtypeStruct((3, cells, lanes), jnp.float32),
        in_specs=[smem] * 4 + [vmem] * 2,
        out_specs=vmem,
        scratch_shapes=[pltpu.VMEM(force_shape, jnp.float32)] + pair_scratch,
        compiler_params=params,
    )(inner_amount[None], word, cell_of, groups, table, slots)

    outer_codes = lax.dynamic_slice(jnp.concatenate([codes, codes]), (inner_amount,), (total,))
    halo = jnp.concatenate(
        [
            part.reshape(-1, 8, lanes)
            for part in (z_before, z_after, x_before, x_after, y_before, y_after)
        ],
        axis=0,
    )
    bricks = lax.axis_size(names)
    known = pl.pallas_call(
        functools.partial(outer_kernel, near_outside, sizes),
        out_shape=jax.ShapeDtypeStruct((bricks, 8, lanes), jnp.float32),
        in_specs=[smem] + [vmem] * 10,
        out_specs=vmem,
        scratch_shapes=[
            pltpu.VMEM((8, lanes), jnp.float32),
            pltpu.VMEM(force_shape, jnp.float32),
            pltpu.VMEM((16, 8, lanes), jnp.float32),
        ]
        + [pltpu.VMEM(shape, jnp.int32) for shape in list_shapes]
        + [pltpu.SMEM(shape, jnp.int32) for shape in list_shapes[1:]]
        + [pltpu.SemaphoreType.DMA((2,))]
        + pair_scratch
        + list_scratch(halo.shape[0]),
        compiler_params=params,
    )(outer_amount[None], outer_codes[None], table, halo, inner, flat_arms, flat_frag,
        frag_key[None], clump_motion, inv_mass[None], inv_moment[None])
    known = lax.all_to_all(known, names, split_axis=0, concat_axis=0, tiled=True)

    brick = lax.axis_index(names)
    mine = jnp.where(
        jnp.arange(lanes - held) < owned, brick * owned + jnp.arange(lanes - held), -2
    ).astype(jnp.float32)
    target = jnp.concatenate([mine, frag_key])[:, None]
    spheres, clumps = pl.pallas_call(
        functools.partial(move_kernel, owned),
        out_shape=(
            jax.ShapeDtypeStruct((6, cells, lanes), jnp.float32),
            jax.ShapeDtypeStruct((6, lanes), jnp.float32),
        ),
        in_specs=[vmem] * 5,
        out_specs=(vmem, vmem),
        compiler_params=params,
    )(target, known, flat_state, flat_arms, flat_frag)
    return (spheres.reshape((6,) + state.shape[1:]), clumps[:, :owned])


def solution(mesh):
    return jax.shard_map(
        local,
        mesh=mesh,
        in_specs=(
            P(None, "gx", "gy", "gz", None),
            P(None, "gx", "gy", "gz", None),
            P("gx", "gy", "gz", None),
            P(("gx", "gy", "gz"), None),
            P(("gx", "gy", "gz")),
            P(("gx", "gy", "gz"), None),
            P(None, ("gx", "gy", "gz")),
            P(("gx", "gy", "gz")),
            P(("gx", "gy", "gz")),
        ),
        out_specs=(P(None, "gx", "gy", "gz", None), P(None, ("gx", "gy", "gz"))),
        check_vma=False,
    )
```

```python
import functools

import jax
import jax.numpy as jnp
from jax import lax
from jax.experimental import pallas as pl
from jax.experimental.pallas import tpu as pltpu
from jax.sharding import PartitionSpec as P

stiffness = 100.0
damping = 2.0
time_step = 0.01
gravity = 9.81
epsilon_sq = 1e-08
radius_top = 0.14

INNER_GROUP = 32
OUTER_GROUP = 16
FILL = 64
OUTSIDE = 1 << 20
WORD_BITS = 16
VALUES = 9
SLACK = 256
SPREAD = 4
VMEM = 56 * 1024 * 1024


def lanes_of(values, index):
    return jnp.take_along_axis(values, index, axis=1, mode="promise_in_bounds")


def split_rows(values):
    high = values.astype(jnp.bfloat16).astype(jnp.float32)
    rest = values - high
    middle = rest.astype(jnp.bfloat16).astype(jnp.float32)
    low = rest - middle
    return jnp.concatenate([high, middle, low], axis=0).astype(jnp.bfloat16)


def joined_rows(stacked):
    rows = stacked.shape[0] // 3
    return stacked[0:rows] + stacked[rows : 2 * rows] + stacked[2 * rows :]


def dot_lanes(first, second):
    return lax.dot_general(
        first, second, (((1,), (1,)), ((), ())), preferred_element_type=jnp.float32
    )


def exchange(last, initial, axis):
    devices = lax.axis_size(axis)
    up = [(i, (i + 1) % devices) for i in range(devices)]
    down = [(j, i) for i, j in up]
    return lax.ppermute(last, axis, up), lax.ppermute(initial, axis, down)


def decode(code, sizes):
    def over(value, by):
        return jnp.floor((value.astype(jnp.float32) + 0.5) * (1.0 / by)).astype(jnp.int32)

    own = over(code, 27)
    kind = code - 27 * own
    step_x = over(kind, 9)
    step_y = over(kind, 3) - 3 * step_x
    steps = (step_x - 1, step_y - 1, kind - 9 * step_x - 3 * step_y - 1)
    own_x = over(own, sizes[1] * sizes[2])
    row = over(own, sizes[2])
    place = (own_x + steps[0], row - own_x * sizes[1] + steps[1], own - row * sizes[2] + steps[2])
    return own, kind, steps, place


def pack_kernel(
    sizes, state_ref, frag_ref, key_ref, code_ref, out_ref, last_ref, first_ref, marked_ref
):
    deep = sizes[2]
    code = code_ref[...]
    place = decode(code, sizes)[3]
    within = [(place[axis] >= 0) & (place[axis] < sizes[axis]) for axis in range(3)]
    marked_ref[...] = jnp.where(within[0] & within[1] & within[2], code, code + OUTSIDE)
    cells, lanes = frag_ref.shape
    held = key_ref.shape[1]
    for comp in range(7):
        out_ref[:, comp, :] = state_ref[comp] * (damping / stiffness if 3 <= comp < 6 else 1.0)
    keys = jnp.concatenate([key_ref[0:1, :], jnp.zeros((1, lanes - held), jnp.float32)], axis=1)
    keys = jnp.broadcast_to(keys, (8, lanes))
    for block in range(cells // 8):
        rows = pl.ds(block * 8, 8)
        out_ref[rows, 7, :] = lanes_of(keys, frag_ref[rows, :])
    for column in range(cells // deep):
        first_ref[column] = out_ref[column * deep]
        last_ref[column] = out_ref[column * deep + deep - 1]


def list_tiles(
    group, amount, near_of, sizes, code_ref, table_ref, slots_ref, word_ref, cell_ref,
    class_ref, member_ref, count_ref, near_ref, need_ref, own_ref, kind_ref,
):
    tiles, lanes = slots_ref.shape
    span = table_ref.shape[0]
    padded = class_ref.shape[0]
    cells = count_ref.shape[0]
    lane_bits = lanes.bit_length() - 1
    wide = 256
    parts = 2
    flat = table_ref.reshape(span * 8, lanes)

    def plane(comp):
        return flat[pl.ds(comp, span, stride=8), :]

    def flag(value):
        return value.astype(jnp.float32).astype(jnp.bfloat16)

    def dot(first, second):
        return jnp.dot(first, second, preferred_element_type=jnp.float32)

    def ramp(shape, axis):
        return lax.broadcasted_iota(jnp.int32, shape, axis)

    code = code_ref[...] & (OUTSIDE - 1)
    own, kind, steps, place = decode(code, sizes)
    near = near_of(*place)
    need = sum(
        jnp.where(steps[axis] == 1, 1, jnp.where(steps[axis] == -1, 2, 0)) * (1 << (2 * axis))
        for axis in range(3)
    )
    live = ramp((1, tiles), 1) < amount
    near = jnp.where(live, near, 0)
    near_ref[...] = near
    kind_ref[...] = near * 32 + jnp.where(live, kind, 0)
    need_ref[...] = jnp.where(live, need, 64)
    own_ref[...] = jnp.where(live, own, cells)

    radius = plane(6) + (radius_top + 1e-5)
    classes = jnp.zeros((span, lanes), jnp.float32)
    for axis in range(3):
        place = plane(axis)
        classes = classes + jnp.where(place < radius, 1.0 * (1 << (2 * axis)), 0.0)
        classes = classes + jnp.where(place > 1.0 - radius, 1.0 * (2 << (2 * axis)), 0.0)
    if padded > span:
        class_ref[...] = jnp.zeros(class_ref.shape, jnp.float32)
    class_ref[pl.ds(0, span), :] = classes
    codes = jnp.concatenate(
        [class_ref[pl.ds(at, lanes), :].T for at in range(0, padded, lanes)], axis=1
    ).astype(jnp.bfloat16)
    ones = jnp.ones((lanes, lanes), jnp.bfloat16)
    count_ref[...] = jnp.zeros(count_ref.shape, jnp.float32)
    blocks = lax.div(amount + (parts * wide - 1), parts * wide)

    def choose(block, unused):
        held = []
        for part in range(parts):
            at = pl.ds(pl.multiple_of((block * parts + part) * wide, wide), wide)
            hits = flag(ramp((padded, wide), 0) == near_ref[:, at])
            found = dot(codes, hits).astype(jnp.int32)
            need = need_ref[:, at]
            member = ((found & need) == need).astype(jnp.float32)
            member_ref[:, at] = member
            count = dot(ones, member.astype(jnp.bfloat16))
            mine = flag(ramp((cells, wide), 0) == own_ref[:, at])
            held.append(dot_lanes(mine, count[0:16].astype(jnp.bfloat16)))
        count_ref[:, 0:16] += held[0] + held[1]
        return unused

    lax.fori_loop(0, blocks, choose, 0)

    held = jnp.broadcast_to(count_ref[:, 0:1], count_ref.shape)
    high = jnp.floor(held * (1.0 / lanes))
    low = held - lanes * high
    taken = jnp.floor((held + (group - 1)) * (1.0 / group))
    upto = flag(ramp((cells, cells), 1) <= ramp((cells, cells), 0))
    ends = dot(upto, taken.astype(jnp.bfloat16))
    cell_ones = jnp.ones((8, cells), jnp.bfloat16)
    many = 8 * lanes
    wide_ends = jnp.concatenate([ends] * 8, axis=1)

    def name_groups(block, unused):
        number = (ramp((cells, many), 1) + block * many).astype(jnp.float32)
        at = pl.ds(pl.multiple_of(block * many, many), many)
        cell_ref[:, at] = dot(cell_ones, flag(wide_ends <= number))[0:1].astype(jnp.int32)
        return unused

    groups = jnp.max(ends).astype(jnp.int32)
    lax.fori_loop(0, lax.div(groups + SLACK, many) + 1, name_groups, 0)
    before_cell = jnp.concatenate(
        [value.T[0:8] for value in (taken, high, low)], axis=0
    ).astype(jnp.bfloat16)

    earlier = flag(ramp((lanes, lanes), 1) < ramp((lanes, lanes), 0))
    earlier_tile = flag(ramp((wide, wide), 0) < ramp((wide, wide), 1))

    def place(block, done):
        for part in range(parts):
            first = pl.multiple_of((block * parts + part) * wide, wide)
            at = pl.ds(first, wide)
            flags = member_ref[:, at].astype(jnp.bfloat16)
            count = dot(ones, flags)
            lower = flag(ramp((cells, wide), 0) < own_ref[:, at])
            before = dot(before_cell, lower)
            so_far = dot(count[0:8].astype(jnp.bfloat16), earlier_tile) + done
            start = group * before[0:8] + so_far - (lanes * before[8:16] + before[16:24])
            start = start.astype(jnp.int32)[0:1]
            offset = jnp.broadcast_to(start & (lanes - 1), (8, wide))
            word_ref[:, at] = (start >> lane_bits) * (1 << WORD_BITS) + kind_ref[:, at]
            rank = dot(earlier, flags)
            slot = ramp((lanes, wide), 0)
            moves = slot - rank.astype(jnp.int32)
            word = jnp.where(member_ref[:, at] > 0.0, slot + lanes * moves, 0)
            bit = 1
            while bit < lanes:
                keep = jnp.where((word & (bit * lanes)) != 0, 0, word)
                gone = word ^ keep
                word = keep | jnp.concatenate([gone[bit:], gone[:bit]], axis=0)
                bit *= 2
            word = word & (lanes - 1)
            line = ramp((8, wide), 0)
            within = offset & 7
            pick = (line - within) & 7
            slabs = [
                jnp.take_along_axis(
                    word[at_row : at_row + 8], pick, axis=0, mode="promise_in_bounds"
                )
                for at_row in range(0, lanes, 8)
            ]
            slabs = [
                jnp.where(line >= within, slabs[number], slabs[number - 1])
                for number in range(len(slabs))
            ]
            hop = 1
            while hop < len(slabs):
                chosen = (offset & (8 * hop)) != 0
                slabs = [
                    jnp.where(chosen, slabs[number - hop], slabs[number])
                    for number in range(len(slabs))
                ]
                hop *= 2
            count = count[0:8].astype(jnp.int32)
            for number in range(len(slabs)):
                lead = line + 8 * number - offset
                taken_lane = jnp.where((lead & (lanes - 1)) < count, lanes, 0)
                slabs[number] = slabs[number] | taken_lane | jnp.where(lead < 0, 2 * lanes, 0)
            word = jnp.concatenate(slabs, axis=0)
            for half in range(wide // lanes):
                rows = pl.ds(pl.multiple_of(first + half * lanes, lanes), lanes)
                slots_ref[rows, :] = word[:, half * lanes : (half + 1) * lanes].T
            done = done + jnp.sum(count.astype(jnp.float32), axis=1, keepdims=True)
        return done

    lax.fori_loop(0, blocks, place, jnp.zeros((8, 1), jnp.float32))
    return groups


def fill_lists(amount, word_smem, near_table_ref, slots_ref, shift_ref, list_ref):
    lanes = slots_ref.shape[1]
    row = lax.broadcasted_iota(jnp.int32, (8, lanes), 0)
    absent = jnp.where(row == 6, -10.0, 0.0)
    for kind in range(27):
        steps = (kind // 9 - 1.0, kind // 3 % 3 - 1.0, kind % 3 - 1.0)
        shift_ref[kind] = sum(jnp.where(row == axis, steps[axis], 0.0) for axis in range(3))

    def fill(block, carry):
        last_chunk, last_new, last_held = carry
        words = [word_smem[0, block * FILL + unit] for unit in range(FILL)]
        for unit, word in enumerate(words):
            slots = slots_ref[pl.ds(block * FILL + unit, 8, stride=0), :]
            cell = near_table_ref[(word >> 5) & ((1 << (WORD_BITS - 5)) - 1)]
            found = lanes_of(cell, slots & (lanes - 1)) + shift_ref[word & 31]
            chunk = word >> WORD_BITS
            new = jnp.where((slots & lanes) != 0, found, absent)
            later = (slots & (2 * lanes)) != 0
            held_row = jnp.where(chunk != last_chunk, last_new, last_held)
            held_row = jnp.where(later, held_row, new)
            new = jnp.where(later, new, absent)
            list_ref[chunk] = held_row
            list_ref[chunk + 1] = new
            last_chunk, last_new, last_held = chunk, new, held_row
        return last_chunk, last_new, last_held

    blocks = lax.div(amount + (FILL - 1), FILL)
    lax.fori_loop(0, blocks, fill, (jnp.int32(0), absent, absent))


def pair_forces(group, groups, cell_smem, table_ref, list_ref, force_ref, even_ref, odd_ref):
    lanes = table_ref.shape[1]
    cells = table_ref.shape[0] // 8
    rows = even_ref.shape[0]
    chunks = rows // lanes
    units = rows // group
    force_ref[...] = jnp.zeros(force_ref.shape, jnp.float32)
    part = lax.broadcasted_iota(jnp.int32, (32, VALUES * lanes), 0)
    comp = lax.broadcasted_iota(jnp.int32, (32, VALUES * lanes), 1) // lanes
    chosen = ((part < 24) & (part % 8 == comp)) | ((part >= 24) & (part < 27) & (comp == 8))
    weights = jnp.where(chosen, 1.0, 0.0).astype(jnp.bfloat16)
    line = lax.broadcasted_iota(jnp.int32, (8, lanes), 0)

    def turned(step):
        pieces = []
        for piece in range(chunks):
            values = list_ref[step * chunks + piece]
            high = values.astype(jnp.bfloat16).astype(jnp.float32)
            rest = values - high
            middle = rest.astype(jnp.bfloat16).astype(jnp.float32)
            over = 1.0 / jnp.broadcast_to(values[6:7], (8, lanes))
            over_high = over.astype(jnp.bfloat16).astype(jnp.float32)
            over_rest = over - over_high
            over_middle = over_rest.astype(jnp.bfloat16).astype(jnp.float32)
            over = jnp.where(line == 2, over_rest - over_middle, 0.0)
            over = jnp.where(line == 1, over_middle, jnp.where(line == 0, over_high, over))
            parts = jnp.concatenate([high, middle, rest - middle, over], axis=0)
            pieces.append(parts.astype(jnp.bfloat16).T)
        return jnp.concatenate(pieces, axis=0)

    def spread(step, out_ref):
        out_ref[...] = jnp.dot(turned(step), weights, preferred_element_type=jnp.float32)

    def block_force(wide_ref, row, mine):
        other = [wide_ref[pl.ds(row, 8), pl.ds(value * lanes, lanes)] for value in range(VALUES)]
        apart = [other[axis] - mine[axis] for axis in range(3)]
        square = apart[0] * apart[0] + apart[1] * apart[1] + apart[2] * apart[2] + epsilon_sq
        inverse = lax.rsqrt(square)
        reach = other[6] + mine[6]
        overlap = jnp.maximum(reach - square * inverse, 0.0)
        overlap = jnp.where(other[7] != mine[7], overlap, 0.0)
        closing = (
            (other[3] - mine[3]) * apart[0]
            + (other[4] - mine[4]) * apart[1]
            + (other[5] - mine[5]) * apart[2]
        )
        root = overlap * lax.rsqrt(jnp.maximum(overlap * (other[8] + mine[8]), 1e-30))
        factor = root * inverse * (overlap - closing * inverse)
        return [factor * apart[axis] for axis in range(3)]

    def pairs(step, wide_ref, next_ref, carry):
        last, running = carry
        spread(step + 1, next_ref)
        for unit in range(units):
            cell = cell_smem[0, step * units + unit]
            own = jnp.minimum(cell, cells - 1) * 8
            mine = [table_ref[pl.ds(own + value, 8, stride=0), :] for value in range(8)]
            mine.append(1.0 / mine[6])
            running = [jnp.where(cell == last, running[axis], 0.0) for axis in range(3)]
            for block in range(group // 8):
                force = block_force(wide_ref, unit * group + block * 8, mine)
                running = [running[axis] + force[axis] for axis in range(3)]
            last = cell
            for axis in range(3):
                force_ref[cell, axis] = running[axis]
        return last, running

    spread(0, even_ref)

    def both(step, carry):
        carry = pairs(2 * step, even_ref, odd_ref, carry)
        return pairs(2 * step + 1, odd_ref, even_ref, carry)

    zero = jnp.zeros((8, lanes), jnp.float32)
    steps = lax.div(groups + (2 * units - 1), 2 * units)
    lax.fori_loop(0, steps, both, (jnp.int32(-1), [zero] * 3))


def to_scalars(pairs, sems):
    copies = [
        pltpu.make_async_copy(source, target, sems.at[number])
        for number, (source, target) in enumerate(pairs)
    ]
    for copy in copies:
        copy.start()
    for copy in copies:
        copy.wait()


def list_kernel(
    near_of, sizes, amount_smem, code_ref, table_ref, slots_ref, word_ref, cell_ref,
    groups_smem, *scratch,
):
    groups_smem[0] = list_tiles(
        INNER_GROUP, amount_smem[0], near_of, sizes, code_ref, table_ref, slots_ref, word_ref, cell_ref, *scratch,
    )


def inner_kernel(
    amount_smem, word_smem, cell_smem, groups_smem, table_ref, slots_ref, sums_ref, force_ref,
    list_ref, even_ref, odd_ref, shift_ref,
):
    cells, _, lanes = table_ref.shape
    fill_lists(amount_smem[0], word_smem, table_ref, slots_ref, shift_ref, list_ref)
    flat = table_ref.reshape(cells * 8, lanes)
    pair_forces(INNER_GROUP, groups_smem[0], cell_smem, flat, list_ref, force_ref, even_ref, odd_ref)
    parts = force_ref.reshape(force_ref.shape[0] * 24, lanes)

    def store_sums(block, unused):
        for half in range(4):
            at = pl.multiple_of(block * 32 + half * 8, 8)
            for axis in range(3):
                sums_ref[axis, pl.ds(at, 8), :] = sublane_sums(parts, at, axis)
        return unused

    lax.fori_loop(0, cells // 32, store_sums, 0)


def outer_kernel(
    near_of, sizes, amount_smem, code_ref, table_ref, halo_ref, inner_ref, arms_ref, frag_ref,
    key_ref, motion_ref, mass_ref, moment_ref, out_ref, fixed_ref, force_ref, loads_ref, slots_ref, word_ref, cell_ref, word_smem, cell_smem, sems, list_ref, even_ref, odd_ref, shift_ref, *scratch,
):
    cells, _, lanes = table_ref.shape
    held = key_ref.shape[1]
    owned = mass_ref.shape[1]
    fixed_ref[...] = jnp.zeros(fixed_ref.shape, jnp.float32)
    fixed_ref[6:7, 0:held] = key_ref[...]
    fixed_ref[0:6, held : held + owned] = motion_ref[...]
    fixed_ref[6:7, held : held + owned] = mass_ref[...]
    fixed_ref[7:8, held : held + owned] = moment_ref[...]
    amount = amount_smem[0]
    groups = list_tiles(
        OUTER_GROUP, amount, near_of, sizes, code_ref, halo_ref, slots_ref, word_ref, cell_ref, *scratch,
    )
    to_scalars([(word_ref, word_smem), (cell_ref, cell_smem)], sems)
    fill_lists(amount, word_smem, halo_ref, slots_ref, shift_ref, list_ref)
    flat = table_ref.reshape(cells * 8, lanes)
    pair_forces(OUTER_GROUP, groups, cell_smem, flat, list_ref, force_ref, even_ref, odd_ref)
    sums = fragment_sums(inner_ref, force_ref, arms_ref, frag_ref, loads_ref, held)
    out = fixed_ref[...] + jnp.concatenate([sums, jnp.zeros_like(sums)], axis=1)
    for brick in range(out_ref.shape[0]):
        out_ref[brick] = out


def sublane_sums(parts_ref, first, axis):
    rows = [parts_ref[pl.ds(first * 24 + axis * 8 + part, 8, stride=24), :] for part in range(8)]
    while len(rows) > 1:
        rows = [one + other for one, other in zip(rows[::2], rows[1::2])]
    return rows[0]


def fragment_sums(inner_ref, outer_ref, arms_ref, frag_ref, loads_ref, held):
    cells, lanes = frag_ref.shape
    tall = loads_ref.shape[0]
    label = lax.broadcasted_iota(jnp.int32, (held, lanes), 0)
    parts = outer_ref.reshape(outer_ref.shape[0] * 24, lanes)

    def total_force(block, axis):
        halves = []
        for half in range(tall // 8):
            at = pl.multiple_of(block * tall + half * 8, 8)
            halves.append(sublane_sums(parts, at, axis) + inner_ref[axis, pl.ds(at, 8), :])
        return -stiffness * jnp.concatenate(halves, axis=0)

    def gather_sums(block, total):
        rows = pl.ds(pl.multiple_of(block * tall, tall), tall)
        force = [total_force(block, axis) for axis in range(3)]
        lever = [arms_ref[axis, rows, :] for axis in range(3)]
        torque = [
            lever[1] * force[2] - lever[2] * force[1],
            lever[2] * force[0] - lever[0] * force[2],
            lever[0] * force[1] - lever[1] * force[0],
        ]
        loads = force + torque + [jnp.zeros_like(force[0])] * 2
        for comp in range(8):
            loads_ref[:, comp, :] = loads[comp]
        frags = frag_ref[rows, :]
        hits = [
            (frags[unit : unit + 1, :] == label).astype(jnp.float32).astype(jnp.bfloat16)
            for unit in range(tall)
        ]
        values = [split_rows(loads_ref[unit]) for unit in range(tall)]
        return total + dot_lanes(jnp.concatenate(values, axis=1), jnp.concatenate(hits, axis=1))

    total = lax.fori_loop(0, cells // tall, gather_sums, jnp.zeros((24, held), jnp.float32))
    return joined_rows(total)


def move_kernel(
    owned, target_ref, known_ref, state_ref, arms_ref, frag_ref, spheres_ref, clumps_ref
):
    bricks, _, lanes = known_ref.shape
    held = lanes // 2
    cells = frag_ref.shape[0]
    targets = jnp.broadcast_to(target_ref[...], (lanes, lanes))
    lane = lax.broadcasted_iota(jnp.int32, (1, lanes), 1)

    def match(block, carry):
        sums, base = carry
        for unit in range(8):
            brick = block * 8 + unit
            known = known_ref[brick]
            values = split_rows(known)
            key = jnp.where(lane < held, known[6:7], -1.0)
            number = jnp.where(
                (lane >= held) & (lane < held + owned), brick * owned + lane - held, -1
            ).astype(jnp.float32)
            sums = sums + dot_lanes((targets == key).astype(jnp.float32).astype(jnp.bfloat16), values)
            base = base + dot_lanes((targets == number).astype(jnp.float32).astype(jnp.bfloat16), values)
        return sums, base

    zero = jnp.zeros((lanes, 24), jnp.float32)
    sums, base = lax.fori_loop(0, bricks // 8, match, (zero, zero))
    sums = joined_rows(sums.T)
    base = joined_rows(base.T)
    rows = []
    for axis in range(3):
        pull = gravity if axis == 2 else 0.0
        rows.append(
            base[axis : axis + 1]
            + time_step * (sums[axis : axis + 1] * base[6:7] - pull)
        )
    for axis in range(3, 6):
        rows.append(base[axis : axis + 1] + time_step * sums[axis : axis + 1] * base[7:8])
    for comp in range(6):
        clumps_ref[comp : comp + 1, :] = rows[comp]
    tall = 32
    wide = [jnp.broadcast_to(value, (tall, lanes)) for value in rows]

    def cross(first, second):
        return [
            first[1] * second[2] - first[2] * second[1],
            first[2] * second[0] - first[0] * second[2],
            first[0] * second[1] - first[1] * second[0],
        ]

    def move(block, unused):
        at = pl.ds(pl.multiple_of(block * tall, tall), tall)
        index = frag_ref[at, :] + (lanes - held)
        motion = [lanes_of(value, index) for value in wide]
        velocity, spin = motion[0:3], motion[3:6]
        arm = [arms_ref[axis, at, :] for axis in range(3)]
        half = [0.5 * time_step * value for value in spin]
        turned = cross(half, arm)
        twice = cross(half, turned)
        scale = 2.0 / (1.0 + half[0] * half[0] + half[1] * half[1] + half[2] * half[2])
        change = [scale * (turned[axis] + twice[axis]) for axis in range(3)]
        new_arm = [arm[axis] + change[axis] for axis in range(3)]
        swing = cross(spin, new_arm)
        for axis in range(3):
            spheres_ref[axis, at, :] = (
                state_ref[axis, at, :] + time_step * velocity[axis] + (new_arm[axis] - arm[axis])
            )
            spheres_ref[3 + axis, at, :] = velocity[axis] + swing[axis]
        return unused

    lax.fori_loop(0, cells // tall, move, 0)


def local(
    state, arms, sphere_frag, frag_owner, frag_clump, tiles, clump_motion, inv_mass, inv_moment
):
    cells_x, cells_y, cells_z = (state.shape[1], state.shape[2], state.shape[3])
    lanes = state.shape[4]
    cells = cells_x * cells_y * cells_z
    owned = inv_mass.shape[0]
    held = frag_clump.shape[0]
    names = ("gx", "gy", "gz")
    vmem = pl.BlockSpec(memory_space=pltpu.VMEM)
    smem = pl.BlockSpec(memory_space=pltpu.SMEM)
    params = pltpu.CompilerParams(vmem_limit_bytes=VMEM)

    frag_key = (frag_owner[:, 0] * owned + frag_clump).astype(jnp.float32)
    flat_state = state.reshape(7, cells, lanes)
    flat_arms = arms.reshape(3, cells, lanes)
    flat_frag = sphere_frag.reshape(cells, lanes)

    face_shape = jax.ShapeDtypeStruct((cells_x * cells_y, 8, lanes), jnp.float32)
    sizes = (cells_x, cells_y, cells_z)
    total = tiles.shape[1]
    table, z_last, z_first, codes = pl.pallas_call(
        functools.partial(pack_kernel, sizes),
        out_shape=(
            jax.ShapeDtypeStruct((cells, 8, lanes), jnp.float32),
            face_shape,
            face_shape,
            jax.ShapeDtypeStruct((1, total), jnp.int32),
        ),
        in_specs=[vmem] * 4,
        out_specs=(vmem,) * 4,
        compiler_params=params,
    )(flat_state, flat_frag, frag_key[None], tiles)
    grid = table.reshape(cells_x, cells_y, cells_z, 8, lanes)
    z_before, z_after = exchange(z_last, z_first, "gz")

    span_z = cells_z + 2
    starts = [0, cells_x * cells_y, 2 * cells_x * cells_y]
    starts += [starts[-1] + cells_y * span_z, starts[-1] + 2 * cells_y * span_z]
    starts += [starts[-1] + (cells_x + 2) * span_z]

    def near_inside(x, y, z):
        return (x * cells_y + y) * cells_z + z

    def near_outside(x, y, z):
        in_y = jnp.where(y < 0, starts[4], starts[5]) + (x + 1) * span_z + z + 1
        in_x = jnp.where(x < 0, starts[2], starts[3]) + y * span_z + z + 1
        in_z = jnp.where(z < 0, starts[0], starts[1]) + x * cells_y + y
        in_x = jnp.where((x < 0) | (x >= cells_x), in_x, in_z)
        return jnp.where((y < 0) | (y >= cells_y), in_y, in_x)

    chunks = total + cells * INNER_GROUP // lanes + 3 * SPREAD
    group_top = -(-(chunks * (lanes // OUTER_GROUP) + SLACK) // (8 * lanes)) * 8 * lanes + 8 * lanes
    force_shape = (cells + 8, 3, 8, lanes)

    list_shapes = [(total, lanes), (1, total), (1, group_top)]

    def list_scratch(span):
        return [
            pltpu.VMEM((-(-span // lanes) * lanes, lanes), jnp.float32),
            pltpu.VMEM((lanes, total), jnp.float32),
            pltpu.VMEM((cells, lanes), jnp.float32),
            pltpu.VMEM((1, total), jnp.int32),
            pltpu.VMEM((1, total), jnp.int32),
            pltpu.VMEM((1, total), jnp.int32),
            pltpu.VMEM((1, total), jnp.int32),
        ]

    pair_scratch = [
        pltpu.VMEM((chunks, 8, lanes), jnp.float32),
        pltpu.VMEM((SPREAD * lanes, VALUES * lanes), jnp.float32),
        pltpu.VMEM((SPREAD * lanes, VALUES * lanes), jnp.float32),
        pltpu.VMEM((27, 8, lanes), jnp.float32),
    ]

    codes = jnp.sort(codes, axis=1)
    inner_amount = jnp.sum((codes < OUTSIDE).astype(jnp.int32))
    outer_amount = total - inner_amount
    z_before, z_after, codes, inner_amount = lax.optimization_barrier(
        (z_before, z_after, codes, inner_amount)
    )
    z_before, z_after = (
        part.reshape(cells_x, cells_y, 1, 8, lanes) for part in (z_before, z_after)
    )
    x_before, x_after = exchange(
        jnp.concatenate([z_before[-1:], grid[-1:], z_after[-1:]], axis=2),
        jnp.concatenate([z_before[:1], grid[:1], z_after[:1]], axis=2),
        "gx",
    )
    slots, word, cell_of, groups = pl.pallas_call(
        functools.partial(list_kernel, near_inside, sizes),
        out_shape=tuple(jax.ShapeDtypeStruct(shape, jnp.int32) for shape in list_shapes + [(1,)]),
        in_specs=[smem, vmem, vmem],
        out_specs=(vmem,) * 3 + (smem,),
        scratch_shapes=list_scratch(cells),
        compiler_params=params,
    )(inner_amount[None], codes, table)
    x_before, x_after, slots, word, cell_of, groups = lax.optimization_barrier(
        (x_before, x_after, slots, word, cell_of, groups)
    )

    def face(at):
        middle = jnp.concatenate([z_before[:, at], grid[:, at], z_after[:, at]], axis=2)
        return jnp.concatenate([x_before[:, at], middle, x_after[:, at]], axis=0)

    y_before, y_after = exchange(face(slice(-1, None)), face(slice(0, 1)), "gy")
    inner = pl.pallas_call(
        inner_kernel,
        out_shape=jax.ShapeDtypeStruct((3, cells, lanes), jnp.float32),
        in_specs=[smem] * 4 + [vmem] * 2,
        out_specs=vmem,
        scratch_shapes=[pltpu.VMEM(force_shape, jnp.float32)] + pair_scratch,
        compiler_params=params,
    )(inner_amount[None], word, cell_of, groups, table, slots)

    outer_codes = lax.dynamic_slice(
        jnp.concatenate([codes, codes], axis=1), (jnp.int32(0), inner_amount), (1, total)
    )
    halo = jnp.concatenate(
        [
            part.reshape(-1, 8, lanes)
            for part in (z_before, z_after, x_before, x_after, y_before, y_after)
        ],
        axis=0,
    )
    bricks = lax.axis_size(names)
    known = pl.pallas_call(
        functools.partial(outer_kernel, near_outside, sizes),
        out_shape=jax.ShapeDtypeStruct((bricks, 8, lanes), jnp.float32),
        in_specs=[smem] + [vmem] * 10,
        out_specs=vmem,
        scratch_shapes=[
            pltpu.VMEM((8, lanes), jnp.float32),
            pltpu.VMEM(force_shape, jnp.float32),
            pltpu.VMEM((16, 8, lanes), jnp.float32),
        ]
        + [pltpu.VMEM(shape, jnp.int32) for shape in list_shapes]
        + [pltpu.SMEM(shape, jnp.int32) for shape in list_shapes[1:]]
        + [pltpu.SemaphoreType.DMA((2,))]
        + pair_scratch
        + list_scratch(halo.shape[0]),
        compiler_params=params,
    )(outer_amount[None], outer_codes, table, halo, inner, flat_arms, flat_frag,
        frag_key[None], clump_motion, inv_mass[None], inv_moment[None])
    known = lax.all_to_all(known, names, split_axis=0, concat_axis=0, tiled=True)

    brick = lax.axis_index(names)
    mine = jnp.where(
        jnp.arange(lanes - held) < owned, brick * owned + jnp.arange(lanes - held), -2
    ).astype(jnp.float32)
    target = jnp.concatenate([mine, frag_key])[:, None]
    spheres, clumps = pl.pallas_call(
        functools.partial(move_kernel, owned),
        out_shape=(
            jax.ShapeDtypeStruct((6, cells, lanes), jnp.float32),
            jax.ShapeDtypeStruct((6, lanes), jnp.float32),
        ),
        in_specs=[vmem] * 5,
        out_specs=(vmem, vmem),
        compiler_params=params,
    )(target, known, flat_state, flat_arms, flat_frag)
    return (spheres.reshape((6,) + state.shape[1:]), clumps[:, :owned])


def solution(mesh):
    return jax.shard_map(
        local,
        mesh=mesh,
        in_specs=(
            P(None, "gx", "gy", "gz", None),
            P(None, "gx", "gy", "gz", None),
            P("gx", "gy", "gz", None),
            P(("gx", "gy", "gz"), None),
            P(("gx", "gy", "gz")),
            P(("gx", "gy", "gz"), None),
            P(None, ("gx", "gy", "gz")),
            P(("gx", "gy", "gz")),
            P(("gx", "gy", "gz")),
        ),
        out_specs=(P(None, "gx", "gy", "gz", None), P(None, ("gx", "gy", "gz"))),
        check_vma=False,
    )
```

```python
import functools

import jax
import jax.numpy as jnp
from jax import lax
from jax.experimental import pallas as pl
from jax.experimental.pallas import tpu as pltpu
from jax.sharding import PartitionSpec as P

stiffness = 100.0
damping = 2.0
time_step = 0.01
gravity = 9.81
epsilon_sq = 1e-08
radius_top = 0.14

INNER_GROUP = 32
OUTER_GROUP = 16
FILL = 64
OUTSIDE = 1 << 20
WORD_BITS = 16
VALUES = 9
SLACK = 256
SPREAD = 4
VMEM = 56 * 1024 * 1024


def lanes_of(values, index):
    return jnp.take_along_axis(values, index, axis=1, mode="promise_in_bounds")


def split_rows(values):
    high = values.astype(jnp.bfloat16).astype(jnp.float32)
    rest = values - high
    middle = rest.astype(jnp.bfloat16).astype(jnp.float32)
    low = rest - middle
    return jnp.concatenate([high, middle, low], axis=0).astype(jnp.bfloat16)


def joined_rows(stacked):
    rows = stacked.shape[0] // 3
    return stacked[0:rows] + stacked[rows : 2 * rows] + stacked[2 * rows :]


def dot_lanes(first, second):
    return lax.dot_general(
        first, second, (((1,), (1,)), ((), ())), preferred_element_type=jnp.float32
    )


def exchange(last, initial, axis):
    devices = lax.axis_size(axis)
    up = [(i, (i + 1) % devices) for i in range(devices)]
    down = [(j, i) for i, j in up]
    return lax.ppermute(last, axis, up), lax.ppermute(initial, axis, down)


def decode(code, sizes):
    def over(value, by):
        return jnp.floor((value.astype(jnp.float32) + 0.5) * (1.0 / by)).astype(jnp.int32)

    own = over(code, 27)
    kind = code - 27 * own
    step_x = over(kind, 9)
    step_y = over(kind, 3) - 3 * step_x
    steps = (step_x - 1, step_y - 1, kind - 9 * step_x - 3 * step_y - 1)
    own_x = over(own, sizes[1] * sizes[2])
    row = over(own, sizes[2])
    place = (own_x + steps[0], row - own_x * sizes[1] + steps[1], own - row * sizes[2] + steps[2])
    return own, kind, steps, place


def pack_kernel(
    sizes, state_ref, frag_ref, key_ref, code_ref, out_ref, last_ref, first_ref, marked_ref
):
    deep = sizes[2]
    code = code_ref[...]
    place = decode(code, sizes)[3]
    within = [(place[axis] >= 0) & (place[axis] < sizes[axis]) for axis in range(3)]
    marked_ref[...] = jnp.where(within[0] & within[1] & within[2], code, code + OUTSIDE)
    cells, lanes = frag_ref.shape
    held = key_ref.shape[1]
    for comp in range(7):
        out_ref[:, comp, :] = state_ref[comp] * (damping / stiffness if 3 <= comp < 6 else 1.0)
    keys = jnp.concatenate([key_ref[0:1, :], jnp.zeros((1, lanes - held), jnp.float32)], axis=1)
    keys = jnp.broadcast_to(keys, (8, lanes))
    for block in range(cells // 8):
        rows = pl.ds(block * 8, 8)
        out_ref[rows, 7, :] = lanes_of(keys, frag_ref[rows, :])
    for column in range(cells // deep):
        first_ref[column] = out_ref[column * deep]
        last_ref[column] = out_ref[column * deep + deep - 1]


def list_tiles(
    group, amount, near_of, sizes, code_ref, table_ref, slots_ref, word_ref, cell_ref,
    class_ref, member_ref, count_ref, near_ref, need_ref, own_ref, kind_ref,
):
    tiles, lanes = slots_ref.shape
    span = table_ref.shape[0]
    padded = class_ref.shape[0]
    cells = count_ref.shape[0]
    lane_bits = lanes.bit_length() - 1
    wide = 256
    parts = 2
    flat = table_ref.reshape(span * 8, lanes)

    def plane(comp):
        return flat[pl.ds(comp, span, stride=8), :]

    def flag(value):
        return value.astype(jnp.float32).astype(jnp.bfloat16)

    def dot(first, second):
        return jnp.dot(first, second, preferred_element_type=jnp.float32)

    def ramp(shape, axis):
        return lax.broadcasted_iota(jnp.int32, shape, axis)

    code = code_ref[...] & (OUTSIDE - 1)
    own, kind, steps, place = decode(code, sizes)
    near = near_of(*place)
    need = sum(
        jnp.where(steps[axis] == 1, 1, jnp.where(steps[axis] == -1, 2, 0)) * (1 << (2 * axis))
        for axis in range(3)
    )
    live = ramp((1, tiles), 1) < amount
    near = jnp.where(live, near, 0)
    near_ref[...] = near
    kind_ref[...] = near * 32 + jnp.where(live, kind, 0)
    need_ref[...] = jnp.where(live, need, 64)
    own_ref[...] = jnp.where(live, own, cells)

    radius = plane(6) + (radius_top + 1e-5)
    classes = jnp.zeros((span, lanes), jnp.float32)
    for axis in range(3):
        place = plane(axis)
        classes = classes + jnp.where(place < radius, 1.0 * (1 << (2 * axis)), 0.0)
        classes = classes + jnp.where(place > 1.0 - radius, 1.0 * (2 << (2 * axis)), 0.0)
    if padded > span:
        class_ref[...] = jnp.zeros(class_ref.shape, jnp.float32)
    class_ref[pl.ds(0, span), :] = classes
    codes = jnp.concatenate(
        [class_ref[pl.ds(at, lanes), :].T for at in range(0, padded, lanes)], axis=1
    ).astype(jnp.bfloat16)
    ones = jnp.ones((lanes, lanes), jnp.bfloat16)
    count_ref[...] = jnp.zeros(count_ref.shape, jnp.float32)
    blocks = lax.div(amount + (parts * wide - 1), parts * wide)

    def choose(block, unused):
        held = []
        for part in range(parts):
            at = pl.ds(pl.multiple_of((block * parts + part) * wide, wide), wide)
            hits = flag(ramp((padded, wide), 0) == near_ref[:, at])
            found = dot(codes, hits).astype(jnp.int32)
            need = need_ref[:, at]
            member = ((found & need) == need).astype(jnp.float32)
            member_ref[:, at] = member
            count = dot(ones, member.astype(jnp.bfloat16))
            mine = flag(ramp((cells, wide), 0) == own_ref[:, at])
            held.append(dot_lanes(mine, count[0:16].astype(jnp.bfloat16)))
        count_ref[:, 0:16] += held[0] + held[1]
        return unused

    lax.fori_loop(0, blocks, choose, 0)

    held = jnp.broadcast_to(count_ref[:, 0:1], count_ref.shape)
    high = jnp.floor(held * (1.0 / lanes))
    low = held - lanes * high
    taken = jnp.floor((held + (group - 1)) * (1.0 / group))
    upto = flag(ramp((cells, cells), 1) <= ramp((cells, cells), 0))
    ends = dot(upto, taken.astype(jnp.bfloat16))
    cell_ones = jnp.ones((8, cells), jnp.bfloat16)
    many = 8 * lanes
    wide_ends = jnp.concatenate([ends] * 8, axis=1)

    def name_groups(block, unused):
        number = (ramp((cells, many), 1) + block * many).astype(jnp.float32)
        at = pl.ds(pl.multiple_of(block * many, many), many)
        cell_ref[:, at] = dot(cell_ones, flag(wide_ends <= number))[0:1].astype(jnp.int32)
        return unused

    groups = jnp.max(ends).astype(jnp.int32)
    lax.fori_loop(0, lax.div(groups + SLACK, many) + 1, name_groups, 0)
    before_cell = jnp.concatenate(
        [value.T[0:8] for value in (taken, high, low)], axis=0
    ).astype(jnp.bfloat16)

    earlier = flag(ramp((lanes, lanes), 1) < ramp((lanes, lanes), 0))
    earlier_tile = flag(ramp((wide, wide), 0) < ramp((wide, wide), 1))

    def place(block, done):
        for part in range(parts):
            first = pl.multiple_of((block * parts + part) * wide, wide)
            at = pl.ds(first, wide)
            flags = member_ref[:, at].astype(jnp.bfloat16)
            count = dot(ones, flags)
            lower = flag(ramp((cells, wide), 0) < own_ref[:, at])
            before = dot(before_cell, lower)
            so_far = dot(count[0:8].astype(jnp.bfloat16), earlier_tile) + done
            start = group * before[0:8] + so_far - (lanes * before[8:16] + before[16:24])
            start = start.astype(jnp.int32)[0:1]
            offset = jnp.broadcast_to(start & (lanes - 1), (8, wide))
            word_ref[:, at] = (start >> lane_bits) * (1 << WORD_BITS) + kind_ref[:, at]
            rank = dot(earlier, flags)
            slot = ramp((lanes, wide), 0)
            moves = slot - rank.astype(jnp.int32)
            word = jnp.where(member_ref[:, at] > 0.0, slot + lanes * moves, 0)
            bit = 1
            while bit < lanes:
                keep = jnp.where((word & (bit * lanes)) != 0, 0, word)
                gone = word ^ keep
                word = keep | jnp.concatenate([gone[bit:], gone[:bit]], axis=0)
                bit *= 2
            word = word & (lanes - 1)
            line = ramp((8, wide), 0)
            within = offset & 7
            pick = (line - within) & 7
            slabs = [
                jnp.take_along_axis(
                    word[at_row : at_row + 8], pick, axis=0, mode="promise_in_bounds"
                )
                for at_row in range(0, lanes, 8)
            ]
            slabs = [
                jnp.where(line >= within, slabs[number], slabs[number - 1])
                for number in range(len(slabs))
            ]
            hop = 1
            while hop < len(slabs):
                chosen = (offset & (8 * hop)) != 0
                slabs = [
                    jnp.where(chosen, slabs[number - hop], slabs[number])
                    for number in range(len(slabs))
                ]
                hop *= 2
            count = count[0:8].astype(jnp.int32)
            for number in range(len(slabs)):
                lead = line + 8 * number - offset
                taken_lane = jnp.where((lead & (lanes - 1)) < count, lanes, 0)
                slabs[number] = slabs[number] | taken_lane | jnp.where(lead < 0, 2 * lanes, 0)
            word = jnp.concatenate(slabs, axis=0)
            for half in range(wide // lanes):
                rows = pl.ds(pl.multiple_of(first + half * lanes, lanes), lanes)
                slots_ref[rows, :] = word[:, half * lanes : (half + 1) * lanes].T
            done = done + jnp.sum(count.astype(jnp.float32), axis=1, keepdims=True)
        return done

    lax.fori_loop(0, blocks, place, jnp.zeros((8, 1), jnp.float32))
    return groups


def fill_lists(amount, word_smem, near_table_ref, slots_ref, shift_ref, list_ref):
    lanes = slots_ref.shape[1]
    row = lax.broadcasted_iota(jnp.int32, (8, lanes), 0)
    absent = jnp.where(row == 6, -10.0, 0.0)
    for kind in range(27):
        steps = (kind // 9 - 1.0, kind // 3 % 3 - 1.0, kind % 3 - 1.0)
        shift_ref[kind] = sum(jnp.where(row == axis, steps[axis], 0.0) for axis in range(3))

    def fill(block, carry):
        last_chunk, last_new, last_held = carry
        words = [word_smem[0, block * FILL + unit] for unit in range(FILL)]
        for unit, word in enumerate(words):
            slots = slots_ref[pl.ds(block * FILL + unit, 8, stride=0), :]
            cell = near_table_ref[(word >> 5) & ((1 << (WORD_BITS - 5)) - 1)]
            found = lanes_of(cell, slots & (lanes - 1)) + shift_ref[word & 31]
            chunk = word >> WORD_BITS
            new = jnp.where((slots & lanes) != 0, found, absent)
            later = (slots & (2 * lanes)) != 0
            held_row = jnp.where(chunk != last_chunk, last_new, last_held)
            held_row = jnp.where(later, held_row, new)
            new = jnp.where(later, new, absent)
            list_ref[chunk] = held_row
            list_ref[chunk + 1] = new
            last_chunk, last_new, last_held = chunk, new, held_row
        return last_chunk, last_new, last_held

    blocks = lax.div(amount + (FILL - 1), FILL)
    lax.fori_loop(0, blocks, fill, (jnp.int32(0), absent, absent))


def pair_forces(group, groups, cell_smem, table_ref, list_ref, force_ref, even_ref, odd_ref):
    lanes = table_ref.shape[1]
    cells = table_ref.shape[0] // 8
    rows = even_ref.shape[0]
    chunks = rows // lanes
    units = rows // group
    force_ref[...] = jnp.zeros(force_ref.shape, jnp.float32)
    part = lax.broadcasted_iota(jnp.int32, (32, VALUES * lanes), 0)
    comp = lax.broadcasted_iota(jnp.int32, (32, VALUES * lanes), 1) // lanes
    chosen = ((part < 24) & (part % 8 == comp)) | ((part >= 24) & (part < 27) & (comp == 8))
    weights = jnp.where(chosen, 1.0, 0.0).astype(jnp.bfloat16)
    line = lax.broadcasted_iota(jnp.int32, (8, lanes), 0)

    def turned(step):
        pieces = []
        for piece in range(chunks):
            values = list_ref[step * chunks + piece]
            high = values.astype(jnp.bfloat16).astype(jnp.float32)
            rest = values - high
            middle = rest.astype(jnp.bfloat16).astype(jnp.float32)
            over = 1.0 / jnp.broadcast_to(values[6:7], (8, lanes))
            over_high = over.astype(jnp.bfloat16).astype(jnp.float32)
            over_rest = over - over_high
            over_middle = over_rest.astype(jnp.bfloat16).astype(jnp.float32)
            over = jnp.where(line == 2, over_rest - over_middle, 0.0)
            over = jnp.where(line == 1, over_middle, jnp.where(line == 0, over_high, over))
            parts = jnp.concatenate([high, middle, rest - middle, over], axis=0)
            pieces.append(parts.astype(jnp.bfloat16).T)
        return jnp.concatenate(pieces, axis=0)

    def spread(step, out_ref):
        out_ref[...] = jnp.dot(turned(step), weights, preferred_element_type=jnp.float32)

    def block_force(wide_ref, row, mine):
        other = [wide_ref[pl.ds(row, 8), pl.ds(value * lanes, lanes)] for value in range(VALUES)]
        apart = [other[axis] - mine[axis] for axis in range(3)]
        square = apart[0] * apart[0] + apart[1] * apart[1] + apart[2] * apart[2] + epsilon_sq
        inverse = lax.rsqrt(square)
        reach = other[6] + mine[6]
        overlap = jnp.maximum(reach - square * inverse, 0.0)
        overlap = jnp.where(other[7] != mine[7], overlap, 0.0)
        closing = (
            (other[3] - mine[3]) * apart[0]
            + (other[4] - mine[4]) * apart[1]
            + (other[5] - mine[5]) * apart[2]
        )
        root = overlap * lax.rsqrt(jnp.maximum(overlap * (other[8] + mine[8]), 1e-30))
        factor = root * inverse * (overlap - closing * inverse)
        return [factor * apart[axis] for axis in range(3)]

    def pairs(step, wide_ref, next_ref, carry):
        last, running = carry
        spread(step + 1, next_ref)
        for unit in range(units):
            cell = cell_smem[0, step * units + unit]
            own = jnp.minimum(cell, cells - 1) * 8
            mine = [table_ref[pl.ds(own + value, 8, stride=0), :] for value in range(8)]
            mine.append(1.0 / mine[6])
            running = [jnp.where(cell == last, running[axis], 0.0) for axis in range(3)]
            for block in range(group // 8):
                force = block_force(wide_ref, unit * group + block * 8, mine)
                running = [running[axis] + force[axis] for axis in range(3)]
            last = cell
            for axis in range(3):
                force_ref[cell, axis] = running[axis]
        return last, running

    spread(0, even_ref)

    def both(step, carry):
        carry = pairs(2 * step, even_ref, odd_ref, carry)
        return pairs(2 * step + 1, odd_ref, even_ref, carry)

    zero = jnp.zeros((8, lanes), jnp.float32)
    steps = lax.div(groups + (2 * units - 1), 2 * units)
    lax.fori_loop(0, steps, both, (jnp.int32(-1), [zero] * 3))


def to_scalars(pairs, sems):
    copies = [
        pltpu.make_async_copy(source, target, sems.at[number])
        for number, (source, target) in enumerate(pairs)
    ]
    for copy in copies:
        copy.start()
    for copy in copies:
        copy.wait()


def list_kernel(
    near_of, sizes, amount_smem, code_ref, table_ref, slots_ref, word_ref, cell_ref,
    groups_smem, *scratch,
):
    groups_smem[0] = list_tiles(
        INNER_GROUP, amount_smem[0], near_of, sizes, code_ref, table_ref, slots_ref, word_ref, cell_ref, *scratch,
    )


def inner_kernel(
    amount_smem, word_smem, cell_smem, groups_smem, table_ref, slots_ref, sums_ref, force_ref,
    list_ref, even_ref, odd_ref, shift_ref,
):
    cells, _, lanes = table_ref.shape
    fill_lists(amount_smem[0], word_smem, table_ref, slots_ref, shift_ref, list_ref)
    flat = table_ref.reshape(cells * 8, lanes)
    pair_forces(INNER_GROUP, groups_smem[0], cell_smem, flat, list_ref, force_ref, even_ref, odd_ref)
    parts = force_ref.reshape(force_ref.shape[0] * 24, lanes)

    def store_sums(block, unused):
        for half in range(4):
            at = pl.multiple_of(block * 32 + half * 8, 8)
            for axis in range(3):
                sums_ref[axis, pl.ds(at, 8), :] = sublane_sums(parts, at, axis)
        return unused

    lax.fori_loop(0, cells // 32, store_sums, 0)


def outer_kernel(
    near_of, sizes, amount_smem, code_ref, table_ref, halo_ref, inner_ref, arms_ref, frag_ref,
    key_ref, motion_ref, mass_ref, moment_ref, out_ref, fixed_ref, force_ref, loads_ref, slots_ref, word_ref, cell_ref, word_smem, cell_smem, sems, list_ref, even_ref, odd_ref, shift_ref, *scratch,
):
    cells, _, lanes = table_ref.shape
    held = key_ref.shape[1]
    owned = mass_ref.shape[1]
    fixed_ref[...] = jnp.zeros(fixed_ref.shape, jnp.float32)
    fixed_ref[6:7, 0:held] = key_ref[...]
    fixed_ref[0:6, held : held + owned] = motion_ref[...]
    fixed_ref[6:7, held : held + owned] = mass_ref[...]
    fixed_ref[7:8, held : held + owned] = moment_ref[...]
    amount = amount_smem[0]
    groups = list_tiles(
        OUTER_GROUP, amount, near_of, sizes, code_ref, halo_ref, slots_ref, word_ref, cell_ref, *scratch,
    )
    to_scalars([(word_ref, word_smem), (cell_ref, cell_smem)], sems)
    fill_lists(amount, word_smem, halo_ref, slots_ref, shift_ref, list_ref)
    flat = table_ref.reshape(cells * 8, lanes)
    pair_forces(OUTER_GROUP, groups, cell_smem, flat, list_ref, force_ref, even_ref, odd_ref)
    sums = fragment_sums(inner_ref, force_ref, arms_ref, frag_ref, loads_ref, held)
    out = fixed_ref[...] + jnp.concatenate([sums, jnp.zeros_like(sums)], axis=1)
    for brick in range(out_ref.shape[0]):
        out_ref[brick] = out


def sublane_sums(parts_ref, first, axis):
    rows = [parts_ref[pl.ds(first * 24 + axis * 8 + part, 8, stride=24), :] for part in range(8)]
    while len(rows) > 1:
        rows = [one + other for one, other in zip(rows[::2], rows[1::2])]
    return rows[0]


def fragment_sums(inner_ref, outer_ref, arms_ref, frag_ref, loads_ref, held):
    cells, lanes = frag_ref.shape
    tall = loads_ref.shape[0]
    label = lax.broadcasted_iota(jnp.int32, (held, lanes), 0)
    parts = outer_ref.reshape(outer_ref.shape[0] * 24, lanes)

    def total_force(block, axis):
        halves = []
        for half in range(tall // 8):
            at = pl.multiple_of(block * tall + half * 8, 8)
            halves.append(sublane_sums(parts, at, axis) + inner_ref[axis, pl.ds(at, 8), :])
        return -stiffness * jnp.concatenate(halves, axis=0)

    def gather_sums(block, total):
        rows = pl.ds(pl.multiple_of(block * tall, tall), tall)
        force = [total_force(block, axis) for axis in range(3)]
        lever = [arms_ref[axis, rows, :] for axis in range(3)]
        torque = [
            lever[1] * force[2] - lever[2] * force[1],
            lever[2] * force[0] - lever[0] * force[2],
            lever[0] * force[1] - lever[1] * force[0],
        ]
        loads = force + torque + [jnp.zeros_like(force[0])] * 2
        for comp in range(8):
            loads_ref[:, comp, :] = loads[comp]
        frags = frag_ref[rows, :]
        hits = [
            (frags[unit : unit + 1, :] == label).astype(jnp.float32).astype(jnp.bfloat16)
            for unit in range(tall)
        ]
        values = [split_rows(loads_ref[unit]) for unit in range(tall)]
        return total + dot_lanes(jnp.concatenate(values, axis=1), jnp.concatenate(hits, axis=1))

    total = lax.fori_loop(0, cells // tall, gather_sums, jnp.zeros((24, held), jnp.float32))
    return joined_rows(total)


def move_kernel(
    owned, target_ref, known_ref, state_ref, arms_ref, frag_ref, spheres_ref, clumps_ref
):
    bricks, _, lanes = known_ref.shape
    held = lanes // 2
    cells = frag_ref.shape[0]
    targets = jnp.broadcast_to(target_ref[...], (lanes, lanes))
    lane = lax.broadcasted_iota(jnp.int32, (1, lanes), 1)

    def match(block, carry):
        sums, base = carry
        for unit in range(8):
            brick = block * 8 + unit
            known = known_ref[brick]
            values = split_rows(known)
            key = jnp.where(lane < held, known[6:7], -1.0)
            number = jnp.where(
                (lane >= held) & (lane < held + owned), brick * owned + lane - held, -1
            ).astype(jnp.float32)
            sums = sums + dot_lanes((targets == key).astype(jnp.float32).astype(jnp.bfloat16), values)
            base = base + dot_lanes((targets == number).astype(jnp.float32).astype(jnp.bfloat16), values)
        return sums, base

    zero = jnp.zeros((lanes, 24), jnp.float32)
    sums, base = lax.fori_loop(0, bricks // 8, match, (zero, zero))
    sums = joined_rows(sums.T)
    base = joined_rows(base.T)
    rows = []
    for axis in range(3):
        pull = gravity if axis == 2 else 0.0
        rows.append(
            base[axis : axis + 1]
            + time_step * (sums[axis : axis + 1] * base[6:7] - pull)
        )
    for axis in range(3, 6):
        rows.append(base[axis : axis + 1] + time_step * sums[axis : axis + 1] * base[7:8])
    for comp in range(6):
        clumps_ref[comp : comp + 1, :] = rows[comp]
    tall = 32
    wide = [jnp.broadcast_to(value, (tall, lanes)) for value in rows]

    def cross(first, second):
        return [
            first[1] * second[2] - first[2] * second[1],
            first[2] * second[0] - first[0] * second[2],
            first[0] * second[1] - first[1] * second[0],
        ]

    def move(block, unused):
        at = pl.ds(pl.multiple_of(block * tall, tall), tall)
        index = frag_ref[at, :] + (lanes - held)
        motion = [lanes_of(value, index) for value in wide]
        velocity, spin = motion[0:3], motion[3:6]
        arm = [arms_ref[axis, at, :] for axis in range(3)]
        half = [0.5 * time_step * value for value in spin]
        turned = cross(half, arm)
        twice = cross(half, turned)
        scale = 2.0 / (1.0 + half[0] * half[0] + half[1] * half[1] + half[2] * half[2])
        change = [scale * (turned[axis] + twice[axis]) for axis in range(3)]
        new_arm = [arm[axis] + change[axis] for axis in range(3)]
        swing = cross(spin, new_arm)
        for axis in range(3):
            spheres_ref[axis, at, :] = (
                state_ref[axis, at, :] + time_step * velocity[axis] + (new_arm[axis] - arm[axis])
            )
            spheres_ref[3 + axis, at, :] = velocity[axis] + swing[axis]
        return unused

    lax.fori_loop(0, cells // tall, move, 0)


def local(
    state, arms, sphere_frag, frag_owner, frag_clump, tiles, clump_motion, inv_mass, inv_moment
):
    cells_x, cells_y, cells_z = (state.shape[1], state.shape[2], state.shape[3])
    lanes = state.shape[4]
    cells = cells_x * cells_y * cells_z
    owned = inv_mass.shape[0]
    held = frag_clump.shape[0]
    names = ("gx", "gy", "gz")
    vmem = pl.BlockSpec(memory_space=pltpu.VMEM)
    smem = pl.BlockSpec(memory_space=pltpu.SMEM)
    params = pltpu.CompilerParams(vmem_limit_bytes=VMEM)

    frag_key = (frag_owner[:, 0] * owned + frag_clump).astype(jnp.float32)
    flat_state = state.reshape(7, cells, lanes)
    flat_arms = arms.reshape(3, cells, lanes)
    flat_frag = sphere_frag.reshape(cells, lanes)

    face_shape = jax.ShapeDtypeStruct((cells_x * cells_y, 8, lanes), jnp.float32)
    sizes = (cells_x, cells_y, cells_z)
    total = tiles.shape[1]
    table, z_last, z_first, codes = pl.pallas_call(
        functools.partial(pack_kernel, sizes),
        out_shape=(
            jax.ShapeDtypeStruct((cells, 8, lanes), jnp.float32),
            face_shape,
            face_shape,
            jax.ShapeDtypeStruct((1, total), jnp.int32),
        ),
        in_specs=[vmem] * 4,
        out_specs=(vmem,) * 4,
        compiler_params=params,
    )(flat_state, flat_frag, frag_key[None], tiles)
    grid = table.reshape(cells_x, cells_y, cells_z, 8, lanes)
    z_before, z_after = exchange(z_last, z_first, "gz")

    span_z = cells_z + 2
    starts = [0, cells_x * cells_y, 2 * cells_x * cells_y]
    starts += [starts[-1] + cells_y * span_z, starts[-1] + 2 * cells_y * span_z]
    starts += [starts[-1] + (cells_x + 2) * span_z]

    def near_inside(x, y, z):
        return (x * cells_y + y) * cells_z + z

    def near_outside(x, y, z):
        in_y = jnp.where(y < 0, starts[4], starts[5]) + (x + 1) * span_z + z + 1
        in_x = jnp.where(x < 0, starts[2], starts[3]) + y * span_z + z + 1
        in_z = jnp.where(z < 0, starts[0], starts[1]) + x * cells_y + y
        in_x = jnp.where((x < 0) | (x >= cells_x), in_x, in_z)
        return jnp.where((y < 0) | (y >= cells_y), in_y, in_x)

    chunks = total + cells * INNER_GROUP // lanes + 3 * SPREAD
    group_top = -(-(chunks * (lanes // OUTER_GROUP) + SLACK) // (8 * lanes)) * 8 * lanes + 8 * lanes
    force_shape = (cells + 8, 3, 8, lanes)

    list_shapes = [(total, lanes), (1, total), (1, group_top)]

    def list_scratch(span):
        return [
            pltpu.VMEM((-(-span // lanes) * lanes, lanes), jnp.float32),
            pltpu.VMEM((lanes, total), jnp.float32),
            pltpu.VMEM((cells, lanes), jnp.float32),
            pltpu.VMEM((1, total), jnp.int32),
            pltpu.VMEM((1, total), jnp.int32),
            pltpu.VMEM((1, total), jnp.int32),
            pltpu.VMEM((1, total), jnp.int32),
        ]

    pair_scratch = [
        pltpu.VMEM((chunks, 8, lanes), jnp.float32),
        pltpu.VMEM((SPREAD * lanes, VALUES * lanes), jnp.float32),
        pltpu.VMEM((SPREAD * lanes, VALUES * lanes), jnp.float32),
        pltpu.VMEM((27, 8, lanes), jnp.float32),
    ]

    codes = jnp.sort(codes[0])
    inner_amount = jnp.sum((codes < OUTSIDE).astype(jnp.int32))
    outer_amount = total - inner_amount
    z_before, z_after, codes, inner_amount = lax.optimization_barrier(
        (z_before, z_after, codes, inner_amount)
    )
    z_before, z_after = (
        part.reshape(cells_x, cells_y, 1, 8, lanes) for part in (z_before, z_after)
    )
    x_before, x_after = exchange(
        jnp.concatenate([z_before[-1:], grid[-1:], z_after[-1:]], axis=2),
        jnp.concatenate([z_before[:1], grid[:1], z_after[:1]], axis=2),
        "gx",
    )
    slots, word, cell_of, groups = pl.pallas_call(
        functools.partial(list_kernel, near_inside, sizes),
        out_shape=tuple(jax.ShapeDtypeStruct(shape, jnp.int32) for shape in list_shapes + [(1,)]),
        in_specs=[smem, vmem, vmem],
        out_specs=(vmem,) * 3 + (smem,),
        scratch_shapes=list_scratch(cells),
        compiler_params=params,
    )(inner_amount[None], codes[None], table)
    x_before, x_after, slots, word, cell_of, groups = lax.optimization_barrier(
        (x_before, x_after, slots, word, cell_of, groups)
    )

    def face(at):
        middle = jnp.concatenate([z_before[:, at], grid[:, at], z_after[:, at]], axis=2)
        return jnp.concatenate([x_before[:, at], middle, x_after[:, at]], axis=0)

    y_before, y_after = exchange(face(slice(-1, None)), face(slice(0, 1)), "gy")
    inner = pl.pallas_call(
        inner_kernel,
        out_shape=jax.ShapeDtypeStruct((3, cells, lanes), jnp.float32),
        in_specs=[smem] * 4 + [vmem] * 2,
        out_specs=vmem,
        scratch_shapes=[pltpu.VMEM(force_shape, jnp.float32)] + pair_scratch,
        compiler_params=params,
    )(inner_amount[None], word, cell_of, groups, table, slots)

    outer_codes = lax.dynamic_slice(jnp.concatenate([codes, codes]), (inner_amount,), (total,))
    halo = jnp.concatenate(
        [
            part.reshape(-1, 8, lanes)
            for part in (z_before, z_after, x_before, x_after, y_before, y_after)
        ],
        axis=0,
    )
    bricks = lax.axis_size(names)
    known = pl.pallas_call(
        functools.partial(outer_kernel, near_outside, sizes),
        out_shape=jax.ShapeDtypeStruct((bricks, 8, lanes), jnp.float32),
        in_specs=[smem] + [vmem] * 10,
        out_specs=vmem,
        scratch_shapes=[
            pltpu.VMEM((8, lanes), jnp.float32),
            pltpu.VMEM(force_shape, jnp.float32),
            pltpu.VMEM((16, 8, lanes), jnp.float32),
        ]
        + [pltpu.VMEM(shape, jnp.int32) for shape in list_shapes]
        + [pltpu.SMEM(shape, jnp.int32) for shape in list_shapes[1:]]
        + [pltpu.SemaphoreType.DMA((2,))]
        + pair_scratch
        + list_scratch(halo.shape[0]),
        compiler_params=params,
    )(outer_amount[None], outer_codes[None], table, halo, inner, flat_arms, flat_frag,
        frag_key[None], clump_motion, inv_mass[None], inv_moment[None])
    known = lax.all_to_all(known, names, split_axis=0, concat_axis=0, tiled=True)

    brick = lax.axis_index(names)
    mine = jnp.where(
        jnp.arange(lanes - held) < owned, brick * owned + jnp.arange(lanes - held), -2
    ).astype(jnp.float32)
    target = jnp.concatenate([mine, frag_key])[:, None]
    spheres, clumps = pl.pallas_call(
        functools.partial(move_kernel, owned),
        out_shape=(
            jax.ShapeDtypeStruct((6, cells, lanes), jnp.float32),
            jax.ShapeDtypeStruct((6, lanes), jnp.float32),
        ),
        in_specs=[vmem] * 5,
        out_specs=(vmem, vmem),
        compiler_params=params,
    )(target, known, flat_state, flat_arms, flat_frag)
    return (spheres.reshape((6,) + state.shape[1:]), clumps[:, :owned])


def solution(mesh):
    return jax.shard_map(
        local,
        mesh=mesh,
        in_specs=(
            P(None, "gx", "gy", "gz", None),
            P(None, "gx", "gy", "gz", None),
            P("gx", "gy", "gz", None),
            P(("gx", "gy", "gz"), None),
            P(("gx", "gy", "gz")),
            P(("gx", "gy", "gz"), None),
            P(None, ("gx", "gy", "gz")),
            P(("gx", "gy", "gz")),
            P(("gx", "gy", "gz")),
        ),
        out_specs=(P(None, "gx", "gy", "gz", None), P(None, ("gx", "gy", "gz"))),
        check_vma=False,
    )
```

```python
import functools

import jax
import jax.numpy as jnp
from jax import lax
from jax.experimental import pallas as pl
from jax.experimental.pallas import tpu as pltpu
from jax.sharding import PartitionSpec as P

stiffness = 100.0
damping = 2.0
time_step = 0.01
gravity = 9.81
epsilon_sq = 1e-08
radius_top = 0.14

INNER_GROUP = 32
OUTER_GROUP = 16
FILL = 64
OUTSIDE = 1 << 20
WORD_BITS = 16
VALUES = 9
SLACK = 256
SPREAD = 4
VMEM = 56 * 1024 * 1024


def lanes_of(values, index):
    return jnp.take_along_axis(values, index, axis=1, mode="promise_in_bounds")


def split_rows(values):
    high = values.astype(jnp.bfloat16).astype(jnp.float32)
    rest = values - high
    middle = rest.astype(jnp.bfloat16).astype(jnp.float32)
    low = rest - middle
    return jnp.concatenate([high, middle, low], axis=0).astype(jnp.bfloat16)


def joined_rows(stacked):
    rows = stacked.shape[0] // 3
    return stacked[0:rows] + stacked[rows : 2 * rows] + stacked[2 * rows :]


def dot_lanes(first, second):
    return lax.dot_general(
        first, second, (((1,), (1,)), ((), ())), preferred_element_type=jnp.float32
    )


def exchange(last, initial, axis):
    devices = lax.axis_size(axis)
    up = [(i, (i + 1) % devices) for i in range(devices)]
    down = [(j, i) for i, j in up]
    return lax.ppermute(last, axis, up), lax.ppermute(initial, axis, down)


def decode(code, sizes):
    def over(value, by):
        return jnp.floor((value.astype(jnp.float32) + 0.5) * (1.0 / by)).astype(jnp.int32)

    own = over(code, 27)
    kind = code - 27 * own
    step_x = over(kind, 9)
    step_y = over(kind, 3) - 3 * step_x
    steps = (step_x - 1, step_y - 1, kind - 9 * step_x - 3 * step_y - 1)
    own_x = over(own, sizes[1] * sizes[2])
    row = over(own, sizes[2])
    place = (own_x + steps[0], row - own_x * sizes[1] + steps[1], own - row * sizes[2] + steps[2])
    return own, kind, steps, place


def pack_kernel(
    sizes, state_ref, frag_ref, key_ref, code_ref, out_ref, last_ref, first_ref, marked_ref
):
    deep = sizes[2]
    code = code_ref[...]
    place = decode(code, sizes)[3]
    within = [(place[axis] >= 0) & (place[axis] < sizes[axis]) for axis in range(3)]
    marked_ref[...] = jnp.where(within[0] & within[1] & within[2], code, code + OUTSIDE)
    cells, lanes = frag_ref.shape
    held = key_ref.shape[1]
    for comp in range(7):
        out_ref[:, comp, :] = state_ref[comp] * (damping / stiffness if 3 <= comp < 6 else 1.0)
    keys = jnp.concatenate([key_ref[0:1, :], jnp.zeros((1, lanes - held), jnp.float32)], axis=1)
    keys = jnp.broadcast_to(keys, (8, lanes))
    for block in range(cells // 8):
        rows = pl.ds(block * 8, 8)
        out_ref[rows, 7, :] = lanes_of(keys, frag_ref[rows, :])
    for column in range(cells // deep):
        first_ref[column] = out_ref[column * deep]
        last_ref[column] = out_ref[column * deep + deep - 1]


def list_tiles(
    group, amount, near_of, sizes, code_ref, table_ref, slots_ref, word_ref, cell_ref,
    class_ref, member_ref, count_ref, near_ref, need_ref, own_ref, kind_ref,
):
    tiles, lanes = slots_ref.shape
    span = table_ref.shape[0]
    padded = class_ref.shape[0]
    cells = count_ref.shape[0]
    lane_bits = lanes.bit_length() - 1
    wide = 256
    parts = 2
    flat = table_ref.reshape(span * 8, lanes)

    def plane(comp):
        return flat[pl.ds(comp, span, stride=8), :]

    def flag(value):
        return value.astype(jnp.float32).astype(jnp.bfloat16)

    def dot(first, second):
        return jnp.dot(first, second, preferred_element_type=jnp.float32)

    def ramp(shape, axis):
        return lax.broadcasted_iota(jnp.int32, shape, axis)

    code = code_ref[...] & (OUTSIDE - 1)
    own, kind, steps, place = decode(code, sizes)
    near = near_of(*place)
    need = sum(
        jnp.where(steps[axis] == 1, 1, jnp.where(steps[axis] == -1, 2, 0)) * (1 << (2 * axis))
        for axis in range(3)
    )
    live = ramp((1, tiles), 1) < amount
    near = jnp.where(live, near, 0)
    near_ref[...] = near
    kind_ref[...] = near * 32 + jnp.where(live, kind, 0)
    need_ref[...] = jnp.where(live, need, 64)
    own_ref[...] = jnp.where(live, own, cells)

    radius = plane(6) + (radius_top + 1e-5)
    classes = jnp.zeros((span, lanes), jnp.float32)
    for axis in range(3):
        place = plane(axis)
        classes = classes + jnp.where(place < radius, 1.0 * (1 << (2 * axis)), 0.0)
        classes = classes + jnp.where(place > 1.0 - radius, 1.0 * (2 << (2 * axis)), 0.0)
    if padded > span:
        class_ref[...] = jnp.zeros(class_ref.shape, jnp.float32)
    class_ref[pl.ds(0, span), :] = classes
    codes = jnp.concatenate(
        [class_ref[pl.ds(at, lanes), :].T for at in range(0, padded, lanes)], axis=1
    ).astype(jnp.bfloat16)
    ones = jnp.ones((lanes, lanes), jnp.bfloat16)
    count_ref[...] = jnp.zeros(count_ref.shape, jnp.float32)
    blocks = lax.div(amount + (parts * wide - 1), parts * wide)

    def choose(block, unused):
        held = []
        for part in range(parts):
            at = pl.ds(pl.multiple_of((block * parts + part) * wide, wide), wide)
            hits = flag(ramp((padded, wide), 0) == near_ref[:, at])
            found = dot(codes, hits).astype(jnp.int32)
            need = need_ref[:, at]
            member = ((found & need) == need).astype(jnp.float32)
            member_ref[:, at] = member
            count = dot(ones, member.astype(jnp.bfloat16))
            mine = flag(ramp((cells, wide), 0) == own_ref[:, at])
            held.append(dot_lanes(mine, count[0:16].astype(jnp.bfloat16)))
        count_ref[:, 0:16] += held[0] + held[1]
        return unused

    lax.fori_loop(0, blocks, choose, 0)

    held = jnp.broadcast_to(count_ref[:, 0:1], count_ref.shape)
    high = jnp.floor(held * (1.0 / lanes))
    low = held - lanes * high
    taken = jnp.floor((held + (group - 1)) * (1.0 / group))
    upto = flag(ramp((cells, cells), 1) <= ramp((cells, cells), 0))
    ends = dot(upto, taken.astype(jnp.bfloat16))
    cell_ones = jnp.ones((8, cells), jnp.bfloat16)
    many = 8 * lanes
    wide_ends = jnp.concatenate([ends] * 8, axis=1)

    def name_groups(block, unused):
        number = (ramp((cells, many), 1) + block * many).astype(jnp.float32)
        at = pl.ds(pl.multiple_of(block * many, many), many)
        cell_ref[:, at] = dot(cell_ones, flag(wide_ends <= number))[0:1].astype(jnp.int32)
        return unused

    groups = jnp.max(ends).astype(jnp.int32)
    lax.fori_loop(0, lax.div(groups + SLACK, many) + 1, name_groups, 0)
    before_cell = jnp.concatenate(
        [value.T[0:8] for value in (taken, high, low)], axis=0
    ).astype(jnp.bfloat16)

    earlier = flag(ramp((lanes, lanes), 1) < ramp((lanes, lanes), 0))
    earlier_tile = flag(ramp((wide, wide), 0) < ramp((wide, wide), 1))

    def place(block, done):
        for part in range(parts):
            first = pl.multiple_of((block * parts + part) * wide, wide)
            at = pl.ds(first, wide)
            flags = member_ref[:, at].astype(jnp.bfloat16)
            count = dot(ones, flags)
            lower = flag(ramp((cells, wide), 0) < own_ref[:, at])
            before = dot(before_cell, lower)
            so_far = dot(count[0:8].astype(jnp.bfloat16), earlier_tile) + done
            start = group * before[0:8] + so_far - (lanes * before[8:16] + before[16:24])
            start = start.astype(jnp.int32)[0:1]
            offset = jnp.broadcast_to(start & (lanes - 1), (8, wide))
            word_ref[:, at] = (start >> lane_bits) * (1 << WORD_BITS) + kind_ref[:, at]
            rank = dot(earlier, flags)
            slot = ramp((lanes, wide), 0)
            moves = slot - rank.astype(jnp.int32)
            word = jnp.where(member_ref[:, at] > 0.0, slot + lanes * moves, 0)
            bit = 1
            while bit < lanes:
                keep = jnp.where((word & (bit * lanes)) != 0, 0, word)
                gone = word ^ keep
                word = keep | jnp.concatenate([gone[bit:], gone[:bit]], axis=0)
                bit *= 2
            word = word & (lanes - 1)
            line = ramp((8, wide), 0)
            within = offset & 7
            pick = (line - within) & 7
            slabs = [
                jnp.take_along_axis(
                    word[at_row : at_row + 8], pick, axis=0, mode="promise_in_bounds"
                )
                for at_row in range(0, lanes, 8)
            ]
            slabs = [
                jnp.where(line >= within, slabs[number], slabs[number - 1])
                for number in range(len(slabs))
            ]
            hop = 1
            while hop < len(slabs):
                chosen = (offset & (8 * hop)) != 0
                slabs = [
                    jnp.where(chosen, slabs[number - hop], slabs[number])
                    for number in range(len(slabs))
                ]
                hop *= 2
            count = count[0:8].astype(jnp.int32)
            for number in range(len(slabs)):
                lead = line + 8 * number - offset
                taken_lane = jnp.where((lead & (lanes - 1)) < count, lanes, 0)
                slabs[number] = slabs[number] | taken_lane | jnp.where(lead < 0, 2 * lanes, 0)
            word = jnp.concatenate(slabs, axis=0)
            for half in range(wide // lanes):
                rows = pl.ds(pl.multiple_of(first + half * lanes, lanes), lanes)
                slots_ref[rows, :] = word[:, half * lanes : (half + 1) * lanes].T
            done = done + jnp.sum(count.astype(jnp.float32), axis=1, keepdims=True)
        return done

    lax.fori_loop(0, blocks, place, jnp.zeros((8, 1), jnp.float32))
    return groups


def fill_lists(amount, word_smem, near_table_ref, slots_ref, shift_ref, list_ref):
    lanes = slots_ref.shape[1]
    row = lax.broadcasted_iota(jnp.int32, (8, lanes), 0)
    absent = jnp.where(row == 6, -10.0, 0.0)
    for kind in range(27):
        steps = (kind // 9 - 1.0, kind // 3 % 3 - 1.0, kind % 3 - 1.0)
        shift_ref[kind] = sum(jnp.where(row == axis, steps[axis], 0.0) for axis in range(3))

    def fill(block, carry):
        last_chunk, last_new, last_held = carry
        words = [word_smem[0, block * FILL + unit] for unit in range(FILL)]
        for unit, word in enumerate(words):
            slots = slots_ref[pl.ds(block * FILL + unit, 8, stride=0), :]
            cell = near_table_ref[(word >> 5) & ((1 << (WORD_BITS - 5)) - 1)]
            found = lanes_of(cell, slots & (lanes - 1)) + shift_ref[word & 31]
            chunk = word >> WORD_BITS
            new = jnp.where((slots & lanes) != 0, found, absent)
            later = (slots & (2 * lanes)) != 0
            held_row = jnp.where(chunk != last_chunk, last_new, last_held)
            held_row = jnp.where(later, held_row, new)
            new = jnp.where(later, new, absent)
            list_ref[chunk] = held_row
            list_ref[chunk + 1] = new
            last_chunk, last_new, last_held = chunk, new, held_row
        return last_chunk, last_new, last_held

    blocks = lax.div(amount + (FILL - 1), FILL)
    lax.fori_loop(0, blocks, fill, (jnp.int32(0), absent, absent))


def pair_forces(group, groups, cell_smem, table_ref, list_ref, force_ref, even_ref, odd_ref):
    lanes = table_ref.shape[1]
    cells = table_ref.shape[0] // 8
    rows = even_ref.shape[0]
    chunks = rows // lanes
    units = rows // group
    force_ref[...] = jnp.zeros(force_ref.shape, jnp.float32)
    part = lax.broadcasted_iota(jnp.int32, (32, VALUES * lanes), 0)
    comp = lax.broadcasted_iota(jnp.int32, (32, VALUES * lanes), 1) // lanes
    chosen = ((part < 24) & (part % 8 == comp)) | ((part >= 24) & (part < 27) & (comp == 8))
    weights = jnp.where(chosen, 1.0, 0.0).astype(jnp.bfloat16)
    line = lax.broadcasted_iota(jnp.int32, (8, lanes), 0)

    def turned(step):
        pieces = []
        for piece in range(chunks):
            values = list_ref[step * chunks + piece]
            high = values.astype(jnp.bfloat16).astype(jnp.float32)
            rest = values - high
            middle = rest.astype(jnp.bfloat16).astype(jnp.float32)
            over = 1.0 / jnp.broadcast_to(values[6:7], (8, lanes))
            over_high = over.astype(jnp.bfloat16).astype(jnp.float32)
            over_rest = over - over_high
            over_middle = over_rest.astype(jnp.bfloat16).astype(jnp.float32)
            over = jnp.where(line == 2, over_rest - over_middle, 0.0)
            over = jnp.where(line == 1, over_middle, jnp.where(line == 0, over_high, over))
            parts = jnp.concatenate([high, middle, rest - middle, over], axis=0)
            pieces.append(parts.astype(jnp.bfloat16).T)
        return jnp.concatenate(pieces, axis=0)

    def spread(step, out_ref):
        out_ref[...] = jnp.dot(turned(step), weights, preferred_element_type=jnp.float32)

    def block_force(wide_ref, row, mine):
        other = [wide_ref[pl.ds(row, 8), pl.ds(value * lanes, lanes)] for value in range(VALUES)]
        apart = [other[axis] - mine[axis] for axis in range(3)]
        square = apart[0] * apart[0] + apart[1] * apart[1] + apart[2] * apart[2] + epsilon_sq
        inverse = lax.rsqrt(square)
        reach = other[6] + mine[6]
        overlap = jnp.maximum(reach - square * inverse, 0.0)
        overlap = jnp.where(other[7] != mine[7], overlap, 0.0)
        closing = (
            (other[3] - mine[3]) * apart[0]
            + (other[4] - mine[4]) * apart[1]
            + (other[5] - mine[5]) * apart[2]
        )
        root = overlap * lax.rsqrt(jnp.maximum(overlap * (other[8] + mine[8]), 1e-30))
        factor = root * inverse * (overlap - closing * inverse)
        return [factor * apart[axis] for axis in range(3)]

    def pairs(step, wide_ref, next_ref, carry):
        last, running = carry
        spread(step + 1, next_ref)
        for unit in range(units):
            cell = cell_smem[0, step * units + unit]
            own = jnp.minimum(cell, cells - 1) * 8
            mine = [table_ref[pl.ds(own + value, 8, stride=0), :] for value in range(8)]
            mine.append(1.0 / mine[6])
            running = [jnp.where(cell == last, running[axis], 0.0) for axis in range(3)]
            for block in range(group // 8):
                force = block_force(wide_ref, unit * group + block * 8, mine)
                running = [running[axis] + force[axis] for axis in range(3)]
            last = cell
            for axis in range(3):
                force_ref[cell, axis] = running[axis]
        return last, running

    spread(0, even_ref)

    def both(step, carry):
        carry = pairs(2 * step, even_ref, odd_ref, carry)
        return pairs(2 * step + 1, odd_ref, even_ref, carry)

    zero = jnp.zeros((8, lanes), jnp.float32)
    steps = lax.div(groups + (2 * units - 1), 2 * units)
    lax.fori_loop(0, steps, both, (jnp.int32(-1), [zero] * 3))


def to_scalars(pairs, sems):
    copies = [
        pltpu.make_async_copy(source, target, sems.at[number])
        for number, (source, target) in enumerate(pairs)
    ]
    for copy in copies:
        copy.start()
    for copy in copies:
        copy.wait()


def list_kernel(
    near_of, sizes, amount_smem, code_ref, table_ref, slots_ref, word_ref, cell_ref,
    groups_smem, *scratch,
):
    groups_smem[0] = list_tiles(
        INNER_GROUP, amount_smem[0], near_of, sizes, code_ref, table_ref, slots_ref, word_ref, cell_ref, *scratch,
    )


def inner_kernel(
    amount_smem, word_smem, cell_smem, groups_smem, table_ref, slots_ref, sums_ref, force_ref,
    list_ref, even_ref, odd_ref, shift_ref,
):
    cells, _, lanes = table_ref.shape
    fill_lists(amount_smem[0], word_smem, table_ref, slots_ref, shift_ref, list_ref)
    flat = table_ref.reshape(cells * 8, lanes)
    pair_forces(INNER_GROUP, groups_smem[0], cell_smem, flat, list_ref, force_ref, even_ref, odd_ref)
    parts = force_ref.reshape(force_ref.shape[0] * 24, lanes)

    def store_sums(block, unused):
        for half in range(4):
            at = pl.multiple_of(block * 32 + half * 8, 8)
            for axis in range(3):
                sums_ref[axis, pl.ds(at, 8), :] = sublane_sums(parts, at, axis)
        return unused

    lax.fori_loop(0, cells // 32, store_sums, 0)


def outer_kernel(
    near_of, sizes, amount_smem, code_ref, table_ref, halo_ref, inner_ref, arms_ref, frag_ref,
    key_ref, motion_ref, mass_ref, moment_ref, out_ref, fixed_ref, force_ref, loads_ref, slots_ref, word_ref, cell_ref, word_smem, cell_smem, sems, list_ref, even_ref, odd_ref, shift_ref, *scratch,
):
    cells, _, lanes = table_ref.shape
    held = key_ref.shape[1]
    owned = mass_ref.shape[1]
    fixed_ref[...] = jnp.zeros(fixed_ref.shape, jnp.float32)
    fixed_ref[6:7, 0:held] = key_ref[...]
    fixed_ref[0:6, held : held + owned] = motion_ref[...]
    fixed_ref[6:7, held : held + owned] = mass_ref[...]
    fixed_ref[7:8, held : held + owned] = moment_ref[...]
    amount = amount_smem[0]
    groups = list_tiles(
        OUTER_GROUP, amount, near_of, sizes, code_ref, halo_ref, slots_ref, word_ref, cell_ref, *scratch,
    )
    to_scalars([(word_ref, word_smem), (cell_ref, cell_smem)], sems)
    fill_lists(amount, word_smem, halo_ref, slots_ref, shift_ref, list_ref)
    flat = table_ref.reshape(cells * 8, lanes)
    pair_forces(OUTER_GROUP, groups, cell_smem, flat, list_ref, force_ref, even_ref, odd_ref)
    sums = fragment_sums(inner_ref, force_ref, arms_ref, frag_ref, loads_ref, held)
    out = fixed_ref[...] + jnp.concatenate([sums, jnp.zeros_like(sums)], axis=1)
    for brick in range(out_ref.shape[0]):
        out_ref[brick] = out


def sublane_sums(parts_ref, first, axis):
    rows = [parts_ref[pl.ds(first * 24 + axis * 8 + part, 8, stride=24), :] for part in range(8)]
    while len(rows) > 1:
        rows = [one + other for one, other in zip(rows[::2], rows[1::2])]
    return rows[0]


def fragment_sums(inner_ref, outer_ref, arms_ref, frag_ref, loads_ref, held):
    cells, lanes = frag_ref.shape
    tall = loads_ref.shape[0]
    label = lax.broadcasted_iota(jnp.int32, (held, lanes), 0)
    parts = outer_ref.reshape(outer_ref.shape[0] * 24, lanes)

    def total_force(block, axis):
        halves = []
        for half in range(tall // 8):
            at = pl.multiple_of(block * tall + half * 8, 8)
            halves.append(sublane_sums(parts, at, axis) + inner_ref[axis, pl.ds(at, 8), :])
        return -stiffness * jnp.concatenate(halves, axis=0)

    def gather_sums(block, total):
        rows = pl.ds(pl.multiple_of(block * tall, tall), tall)
        force = [total_force(block, axis) for axis in range(3)]
        lever = [arms_ref[axis, rows, :] for axis in range(3)]
        torque = [
            lever[1] * force[2] - lever[2] * force[1],
            lever[2] * force[0] - lever[0] * force[2],
            lever[0] * force[1] - lever[1] * force[0],
        ]
        loads = force + torque + [jnp.zeros_like(force[0])] * 2
        for comp in range(8):
            loads_ref[:, comp, :] = loads[comp]
        frags = frag_ref[rows, :]
        hits = [
            (frags[unit : unit + 1, :] == label).astype(jnp.float32).astype(jnp.bfloat16)
            for unit in range(tall)
        ]
        values = [split_rows(loads_ref[unit]) for unit in range(tall)]
        return total + dot_lanes(jnp.concatenate(values, axis=1), jnp.concatenate(hits, axis=1))

    total = lax.fori_loop(0, cells // tall, gather_sums, jnp.zeros((24, held), jnp.float32))
    return joined_rows(total)


def move_kernel(
    owned, target_ref, known_ref, state_ref, arms_ref, frag_ref, spheres_ref, clumps_ref
):
    bricks, _, lanes = known_ref.shape
    held = lanes // 2
    cells = frag_ref.shape[0]
    targets = jnp.broadcast_to(target_ref[...], (lanes, lanes))
    lane = lax.broadcasted_iota(jnp.int32, (1, lanes), 1)

    def match(block, carry):
        sums, base = carry
        for unit in range(8):
            brick = block * 8 + unit
            known = known_ref[brick]
            values = split_rows(known)
            key = jnp.where(lane < held, known[6:7], -1.0)
            number = jnp.where(
                (lane >= held) & (lane < held + owned), brick * owned + lane - held, -1
            ).astype(jnp.float32)
            sums = sums + dot_lanes((targets == key).astype(jnp.float32).astype(jnp.bfloat16), values)
            base = base + dot_lanes((targets == number).astype(jnp.float32).astype(jnp.bfloat16), values)
        return sums, base

    zero = jnp.zeros((lanes, 24), jnp.float32)
    sums, base = lax.fori_loop(0, bricks // 8, match, (zero, zero))
    sums = joined_rows(sums.T)
    base = joined_rows(base.T)
    rows = []
    for axis in range(3):
        pull = gravity if axis == 2 else 0.0
        rows.append(
            base[axis : axis + 1]
            + time_step * (sums[axis : axis + 1] * base[6:7] - pull)
        )
    for axis in range(3, 6):
        rows.append(base[axis : axis + 1] + time_step * sums[axis : axis + 1] * base[7:8])
    for comp in range(6):
        clumps_ref[comp : comp + 1, :] = rows[comp]
    tall = 64
    wide = [jnp.broadcast_to(value, (tall, lanes)) for value in rows]

    def cross(first, second):
        return [
            first[1] * second[2] - first[2] * second[1],
            first[2] * second[0] - first[0] * second[2],
            first[0] * second[1] - first[1] * second[0],
        ]

    def move(block, unused):
        at = pl.ds(pl.multiple_of(block * tall, tall), tall)
        index = frag_ref[at, :] + (lanes - held)
        motion = [lanes_of(value, index) for value in wide]
        velocity, spin = motion[0:3], motion[3:6]
        arm = [arms_ref[axis, at, :] for axis in range(3)]
        half = [0.5 * time_step * value for value in spin]
        turned = cross(half, arm)
        twice = cross(half, turned)
        scale = 2.0 / (1.0 + half[0] * half[0] + half[1] * half[1] + half[2] * half[2])
        change = [scale * (turned[axis] + twice[axis]) for axis in range(3)]
        new_arm = [arm[axis] + change[axis] for axis in range(3)]
        swing = cross(spin, new_arm)
        for axis in range(3):
            spheres_ref[axis, at, :] = (
                state_ref[axis, at, :] + time_step * velocity[axis] + (new_arm[axis] - arm[axis])
            )
            spheres_ref[3 + axis, at, :] = velocity[axis] + swing[axis]
        return unused

    lax.fori_loop(0, cells // tall, move, 0)


def local(
    state, arms, sphere_frag, frag_owner, frag_clump, tiles, clump_motion, inv_mass, inv_moment
):
    cells_x, cells_y, cells_z = (state.shape[1], state.shape[2], state.shape[3])
    lanes = state.shape[4]
    cells = cells_x * cells_y * cells_z
    owned = inv_mass.shape[0]
    held = frag_clump.shape[0]
    names = ("gx", "gy", "gz")
    vmem = pl.BlockSpec(memory_space=pltpu.VMEM)
    smem = pl.BlockSpec(memory_space=pltpu.SMEM)
    params = pltpu.CompilerParams(vmem_limit_bytes=VMEM)

    frag_key = (frag_owner[:, 0] * owned + frag_clump).astype(jnp.float32)
    flat_state = state.reshape(7, cells, lanes)
    flat_arms = arms.reshape(3, cells, lanes)
    flat_frag = sphere_frag.reshape(cells, lanes)

    face_shape = jax.ShapeDtypeStruct((cells_x * cells_y, 8, lanes), jnp.float32)
    sizes = (cells_x, cells_y, cells_z)
    total = tiles.shape[1]
    table, z_last, z_first, codes = pl.pallas_call(
        functools.partial(pack_kernel, sizes),
        out_shape=(
            jax.ShapeDtypeStruct((cells, 8, lanes), jnp.float32),
            face_shape,
            face_shape,
            jax.ShapeDtypeStruct((1, total), jnp.int32),
        ),
        in_specs=[vmem] * 4,
        out_specs=(vmem,) * 4,
        compiler_params=params,
    )(flat_state, flat_frag, frag_key[None], tiles)
    grid = table.reshape(cells_x, cells_y, cells_z, 8, lanes)
    z_before, z_after = exchange(z_last, z_first, "gz")

    span_z = cells_z + 2
    starts = [0, cells_x * cells_y, 2 * cells_x * cells_y]
    starts += [starts[-1] + cells_y * span_z, starts[-1] + 2 * cells_y * span_z]
    starts += [starts[-1] + (cells_x + 2) * span_z]

    def near_inside(x, y, z):
        return (x * cells_y + y) * cells_z + z

    def near_outside(x, y, z):
        in_y = jnp.where(y < 0, starts[4], starts[5]) + (x + 1) * span_z + z + 1
        in_x = jnp.where(x < 0, starts[2], starts[3]) + y * span_z + z + 1
        in_z = jnp.where(z < 0, starts[0], starts[1]) + x * cells_y + y
        in_x = jnp.where((x < 0) | (x >= cells_x), in_x, in_z)
        return jnp.where((y < 0) | (y >= cells_y), in_y, in_x)

    chunks = total + cells * INNER_GROUP // lanes + 3 * SPREAD
    group_top = -(-(chunks * (lanes // OUTER_GROUP) + SLACK) // (8 * lanes)) * 8 * lanes + 8 * lanes
    force_shape = (cells + 8, 3, 8, lanes)

    list_shapes = [(total, lanes), (1, total), (1, group_top)]

    def list_scratch(span):
        return [
            pltpu.VMEM((-(-span // lanes) * lanes, lanes), jnp.float32),
            pltpu.VMEM((lanes, total), jnp.float32),
            pltpu.VMEM((cells, lanes), jnp.float32),
            pltpu.VMEM((1, total), jnp.int32),
            pltpu.VMEM((1, total), jnp.int32),
            pltpu.VMEM((1, total), jnp.int32),
            pltpu.VMEM((1, total), jnp.int32),
        ]

    pair_scratch = [
        pltpu.VMEM((chunks, 8, lanes), jnp.float32),
        pltpu.VMEM((SPREAD * lanes, VALUES * lanes), jnp.float32),
        pltpu.VMEM((SPREAD * lanes, VALUES * lanes), jnp.float32),
        pltpu.VMEM((27, 8, lanes), jnp.float32),
    ]

    codes = jnp.sort(codes[0])
    inner_amount = jnp.sum((codes < OUTSIDE).astype(jnp.int32))
    outer_amount = total - inner_amount
    z_before, z_after, codes, inner_amount = lax.optimization_barrier(
        (z_before, z_after, codes, inner_amount)
    )
    z_before, z_after = (
        part.reshape(cells_x, cells_y, 1, 8, lanes) for part in (z_before, z_after)
    )
    x_before, x_after = exchange(
        jnp.concatenate([z_before[-1:], grid[-1:], z_after[-1:]], axis=2),
        jnp.concatenate([z_before[:1], grid[:1], z_after[:1]], axis=2),
        "gx",
    )
    slots, word, cell_of, groups = pl.pallas_call(
        functools.partial(list_kernel, near_inside, sizes),
        out_shape=tuple(jax.ShapeDtypeStruct(shape, jnp.int32) for shape in list_shapes + [(1,)]),
        in_specs=[smem, vmem, vmem],
        out_specs=(vmem,) * 3 + (smem,),
        scratch_shapes=list_scratch(cells),
        compiler_params=params,
    )(inner_amount[None], codes[None], table)
    x_before, x_after, slots, word, cell_of, groups = lax.optimization_barrier(
        (x_before, x_after, slots, word, cell_of, groups)
    )

    def face(at):
        middle = jnp.concatenate([z_before[:, at], grid[:, at], z_after[:, at]], axis=2)
        return jnp.concatenate([x_before[:, at], middle, x_after[:, at]], axis=0)

    y_before, y_after = exchange(face(slice(-1, None)), face(slice(0, 1)), "gy")
    inner = pl.pallas_call(
        inner_kernel,
        out_shape=jax.ShapeDtypeStruct((3, cells, lanes), jnp.float32),
        in_specs=[smem] * 4 + [vmem] * 2,
        out_specs=vmem,
        scratch_shapes=[pltpu.VMEM(force_shape, jnp.float32)] + pair_scratch,
        compiler_params=params,
    )(inner_amount[None], word, cell_of, groups, table, slots)

    outer_codes = lax.dynamic_slice(jnp.concatenate([codes, codes]), (inner_amount,), (total,))
    halo = jnp.concatenate(
        [
            part.reshape(-1, 8, lanes)
            for part in (z_before, z_after, x_before, x_after, y_before, y_after)
        ],
        axis=0,
    )
    bricks = lax.axis_size(names)
    known = pl.pallas_call(
        functools.partial(outer_kernel, near_outside, sizes),
        out_shape=jax.ShapeDtypeStruct((bricks, 8, lanes), jnp.float32),
        in_specs=[smem] + [vmem] * 10,
        out_specs=vmem,
        scratch_shapes=[
            pltpu.VMEM((8, lanes), jnp.float32),
            pltpu.VMEM(force_shape, jnp.float32),
            pltpu.VMEM((32, 8, lanes), jnp.float32),
        ]
        + [pltpu.VMEM(shape, jnp.int32) for shape in list_shapes]
        + [pltpu.SMEM(shape, jnp.int32) for shape in list_shapes[1:]]
        + [pltpu.SemaphoreType.DMA((2,))]
        + pair_scratch
        + list_scratch(halo.shape[0]),
        compiler_params=params,
    )(outer_amount[None], outer_codes[None], table, halo, inner, flat_arms, flat_frag,
        frag_key[None], clump_motion, inv_mass[None], inv_moment[None])
    known = lax.all_to_all(known, names, split_axis=0, concat_axis=0, tiled=True)

    brick = lax.axis_index(names)
    mine = jnp.where(
        jnp.arange(lanes - held) < owned, brick * owned + jnp.arange(lanes - held), -2
    ).astype(jnp.float32)
    target = jnp.concatenate([mine, frag_key])[:, None]
    spheres, clumps = pl.pallas_call(
        functools.partial(move_kernel, owned),
        out_shape=(
            jax.ShapeDtypeStruct((6, cells, lanes), jnp.float32),
            jax.ShapeDtypeStruct((6, lanes), jnp.float32),
        ),
        in_specs=[vmem] * 5,
        out_specs=(vmem, vmem),
        compiler_params=params,
    )(target, known, flat_state, flat_arms, flat_frag)
    return (spheres.reshape((6,) + state.shape[1:]), clumps[:, :owned])


def solution(mesh):
    return jax.shard_map(
        local,
        mesh=mesh,
        in_specs=(
            P(None, "gx", "gy", "gz", None),
            P(None, "gx", "gy", "gz", None),
            P("gx", "gy", "gz", None),
            P(("gx", "gy", "gz"), None),
            P(("gx", "gy", "gz")),
            P(("gx", "gy", "gz"), None),
            P(None, ("gx", "gy", "gz")),
            P(("gx", "gy", "gz")),
            P(("gx", "gy", "gz")),
        ),
        out_specs=(P(None, "gx", "gy", "gz", None), P(None, ("gx", "gy", "gz"))),
        check_vma=False,
    )
```
